32 devices in a mesh: seq: 8 (over z, y), dp: 4 (over x, core).
Axes of the slice: x: 2, y: 2, z: 4, core: 2. Of those that a mesh axis runs over, the one named last changes fastest.
Arguments:
- tokens: bfloat16 [4, 4096, 1024], P('dp', 'seq'), may hold values from -6 to 6
- cotangent: bfloat16 [4, 4096, 1024], P('dp', 'seq'), may hold values from -6 to 6
- segment_ids: int32 [4, 4096], P('dp'), may hold values from 0 to 15, never falling along the last dimension, each value on 1 to 2048 neighbouring positions
- pad_mask: int32 [4, 4096], P('dp'), may hold values 0 or 1
- w_z: float32 [1024, 256], P(('seq', 'dp')), may hold values from -0.4375 to 0.4375
- w_v: float32 [1024, 2048], P(('seq', 'dp')), may hold values from -0.1875 to 0.1875
- w_r: float32 [1024, 2048], P(('seq', 'dp')), may hold values from -0.1875 to 0.1875
- w_h: float32 [2048, 1024], P(('seq', 'dp')), may hold values from -0.5 to 0.5
- w_gate: float32 [1024, 2560], P(('seq', 'dp')), may hold values from -0.1875 to 0.1875
- w_up: float32 [1024, 2560], P(('seq', 'dp')), may hold values from -0.1875 to 0.1875
- w_down: float32 [2560, 1024], P(('seq', 'dp')), may hold values from -0.25 to 0.25
- q_gain: float32 [256], P(('seq', 'dp')), may hold values from 0.5 to 1.5
- q_bias: float32 [256], P(('seq', 'dp')), may hold values from -3 to 3
- k_gain: float32 [256], P(('seq', 'dp')), may hold values from 0.5 to 1.5
- ffn_gain: float32 [1024], P(('seq', 'dp')), may hold values from 0.5 to 1.5
- norm_gain: float32 [1024], P('seq'), may hold values from 0.5 to 1.5
- ema_rate: float32 [1024, 16], P('seq'), may hold values from 1e-05 to 0.03
- ema_angle: float32 [1024, 16], P('seq'), may hold values from -3.140625 to 3.140625
- ema_input: float32 [1024, 16], P('seq'), may hold values from -4 to 4
- ema_output: float32 [1024, 16], P('seq'), may hold values from -1.5 to 1.5
- ema_skip: float32 [1024], P('seq'), may hold values from -3 to 3
Outputs:
- output: bfloat16 [4, 4096, 1024], P('dp', 'seq')
- input_grad: float32 [4, 4096, 1024], P('dp', 'seq')
- grad_w_z: float32 [1024, 256], P(('seq', 'dp'))
- grad_w_v: float32 [1024, 2048], P(('seq', 'dp'))
- grad_w_r: float32 [1024, 2048], P(('seq', 'dp'))
- grad_w_h: float32 [2048, 1024], P(('seq', 'dp'))
- grad_w_gate: float32 [1024, 2560], P(('seq', 'dp'))
- grad_w_up: float32 [1024, 2560], P(('seq', 'dp'))
- grad_w_down: float32 [2560, 1024], P(('seq', 'dp'))
- grad_q_gain: float32 [256], P(('seq', 'dp'))
- grad_q_bias: float32 [256], P(('seq', 'dp'))
- grad_k_gain: float32 [256], P(('seq', 'dp'))
- grad_ffn_gain: float32 [1024], P(('seq', 'dp'))
- grad_norm_gain: float32 [1024], P('seq')
- grad_ema_rate: float32 [1024, 16], P('seq')
- grad_ema_angle: float32 [1024, 16], P('seq')
- grad_ema_input: float32 [1024, 16], P('seq')
- grad_ema_output: float32 [1024, 16], P('seq')
- grad_ema_skip: float32 [1024], P('seq')
The draws below stay inside these ranges and needn't reach their ends.
Inputs may be any that keep to these rules, and one draw needn't show every extreme that they name: `segment_ids`: along each group's 4096 tokens the ids never fall; each of the 16 documents covers 1 to 2048 consecutive tokens, one exactly that many.
All inputs are finite; a program needn't handle non-finite values. No bound on the sum of `pad_mask` on one device may be relied on, other than what follows from the above.
Results may differ from the reference program's by a relative error of at most 0.04.
Values may be sent and summed in bfloat16 or wider, within the bound.
No kernel may reach another device: no remote copies, remote signals or barrier semaphores. Data moves between devices by JAX's collectives and lax.ppermute only.
A program may use at most 320 MiB of HBM per device.

```python
import math
import jax
import jax.numpy as jnp
import numpy as np
from jax import lax

D = 1024
Z = 256
E = 2048
FF = 2560
NDIM = 16
GROUP = 64
ROWS = 512
DOCS = 16
GROUP_TOK = 4096
GROUPS = 4


def place_ends(values, key, low, top_value):
    spot = [jax.random.randint(jax.random.fold_in(key, axis), (), 0, length) for axis, length in enumerate(values.shape)]
    main_axis = values.shape.index(max(values.shape))
    neighbour = spot[:main_axis] + [(spot[main_axis] + 1) % values.shape[main_axis]] + spot[main_axis + 1:]
    return values.at[tuple(spot)].set(low).at[tuple(neighbour)].set(top_value)


def levels(key, extent, cuts, low, largest):
    level, own = 1.0, jax.random.fold_in(key, 6)
    for position, parts in cuts:
        steps = jnp.exp(jax.random.uniform(jax.random.fold_in(own, position), (parts,), jnp.float32, low / len(cuts), largest / len(cuts)))
        level = level * jnp.repeat(steps, extent[position] // parts).reshape([-1 if axis == position else 1 for axis in range(len(extent))])
    return level


def length_profile(number_of, total, bound, slope):
    loads = [(1 << 20) // math.isqrt(standing ** slope) + 1 for standing in range(2, number_of + 1)]
    rest, given = total - bound - (number_of - 1), [1] * (number_of - 1)
    while rest > 0:
        movable = [i for i in range(number_of - 1) if given[i] < bound]
        mass, budget = sum([loads[i] for i in movable]), rest
        for i in movable:
            extra = min(bound - given[i], max(1, budget * loads[i] // mass), rest)
            given[i] = given[i] + extra
            rest = rest - extra
    return np.array([bound] + given)


def ragged(stream_key, number_of, total, bound, lean):
    if number_of == 2:
        one = jax.random.randint(stream_key, (), max(1, total - bound), min(bound, total - 1) + 1)
        return jnp.stack([one, total - one])
    tallies = jnp.asarray(length_profile(number_of, total, bound, lean), jnp.int32)
    pairs = (number_of - 1) // 2
    source_of, sink = tallies[1:1 + 2 * pairs:2], tallies[2:2 + 2 * pairs:2]
    margin = jnp.minimum(source_of - 1, bound - sink)
    shifted = jax.random.randint(jax.random.fold_in(stream_key, 1), (pairs,), 0, 1 << 20) % (margin + 1)
    tallies = tallies.at[1:1 + 2 * pairs:2].set(source_of - shifted).at[2:2 + 2 * pairs:2].set(sink + shifted)
    return tallies[jax.random.permutation(jax.random.fold_in(stream_key, 2), number_of)]


def gaussian(key, shape, deviation, reach, shards=(), dtype=jnp.bfloat16):
    values = jax.random.normal(key, shape, jnp.float32) * deviation
    if len(shards) > 0:
        values = levels(key, shape, shards, -0.22, 0.18) * values
    return jnp.clip(values, min=-reach, max=reach).astype(dtype)


def setup_inputs(seed: int = 0) -> dict:
    streams_of = jax.random.split(jax.random.key(seed), 22)
    return {
        "tokens": gaussian(streams_of[0], (GROUPS, GROUP_TOK, D), 1.0, 6.0, ((0, 4), (1, 8))),
        "cotangent": gaussian(streams_of[1], (GROUPS, GROUP_TOK, D), 1.0, 6.0, ((0, 4), (1, 8))),
        "segment_ids": jax.vmap(lambda own: jnp.searchsorted(jnp.cumsum(ragged(own, DOCS, GROUP_TOK, GROUP_TOK // 2, 2)), jnp.arange(GROUP_TOK), side="right"))(jax.random.split(streams_of[2], GROUPS)).reshape((GROUPS, GROUP_TOK)).astype(jnp.int32),
        "pad_mask": place_ends((jax.random.randint(streams_of[3], (GROUPS, GROUP_TOK), 0, 8) < 7).astype(jnp.int32), jax.random.fold_in(streams_of[3], 1), 0, 1),
        "w_z": gaussian(streams_of[4], (D, Z), (D // 6) ** -0.5, 0.4375, ((0, 32),), jnp.float32),
        "w_v": gaussian(streams_of[5], (D, E), D ** -0.5, 0.1875, ((0, 32),), jnp.float32),
        "w_r": gaussian(streams_of[6], (D, E), D ** -0.5, 0.1875, ((0, 32),), jnp.float32),
        "w_h": gaussian(streams_of[7], (E, D), (E // 16) ** -0.5, 0.5, ((0, 32),), jnp.float32),
        "w_gate": gaussian(streams_of[8], (D, FF), D ** -0.5, 0.1875, ((0, 32),), jnp.float32),
        "w_up": gaussian(streams_of[9], (D, FF), D ** -0.5, 0.1875, ((0, 32),), jnp.float32),
        "w_down": gaussian(streams_of[10], (FF, D), (FF // 4) ** -0.5, 0.25, ((0, 32),), jnp.float32),
        "q_gain": jnp.clip(1.0 + 0.1 * jax.random.normal(streams_of[11], (Z,), jnp.float32), 0.5, 1.5),
        "q_bias": gaussian(streams_of[12], (Z,), 0.5, 3.0, ((0, 32),), jnp.float32),
        "k_gain": jnp.clip(1.0 + 0.1 * jax.random.normal(streams_of[13], (Z,), jnp.float32), 0.5, 1.5),
        "ffn_gain": jnp.clip(1.0 + 0.1 * jax.random.normal(streams_of[14], (D,), jnp.float32), 0.5, 1.5),
        "norm_gain": jnp.clip(1.0 + 0.1 * jax.random.normal(streams_of[15], (D,), jnp.float32), 0.5, 1.5),
        "ema_rate": jnp.clip(jnp.exp(math.log(0.03) - 8.006368 * jax.random.uniform(streams_of[16], (D, NDIM), jnp.float32) ** levels(streams_of[16], (D, NDIM), ((0, 8),), -0.2, 0.2)), 9.999999747378752e-06, 0.03),
        "ema_angle": jnp.clip(jax.random.uniform(streams_of[17], (D, NDIM), jnp.float32, -3.140625, 3.140625), -3.140625, 3.140625),
        "ema_input": gaussian(streams_of[18], (D, NDIM), 1.0, 4.0, ((0, 8),), jnp.float32),
        "ema_output": gaussian(streams_of[19], (D, NDIM), NDIM ** -0.5, 1.5, ((0, 8),), jnp.float32),
        "ema_skip": gaussian(streams_of[20], (D,), 0.5, 3.0, ((0, 8),), jnp.float32),
    }


@jax.custom_vjp
def low(v):
    return lax.optimization_barrier(v.astype(jnp.bfloat16)).astype(jnp.float32)

@jax.custom_vjp
def low_back(v):
    return v

def low_keep(v):
    return (low(v), None)

def low_pass(kept, grad):
    return (grad,)

def back_keep(v):
    return (v, None)

def back_low(kept, grad):
    return (low(grad),)
low.defvjp(low_keep, low_pass)
low_back.defvjp(back_keep, back_low)

def matmul_high(left, right):
    return jnp.dot(left, right, precision=lax.Precision.HIGHEST, preferred_element_type=jnp.float32)

def segment_cumsum(values, flags):

    def combine(earlier, later):
        return (later[0] + (1.0 - later[1]) * earlier[0], jnp.maximum(earlier[1], later[1]))
    return lax.associative_scan(combine, (values, flags), axis=0)[0]

def step_norm(inputs, flags, valid, gain):
    length, width = inputs.shape
    groups = width // GROUP
    grouped = inputs.reshape(length, groups, GROUP)
    totals = jnp.concatenate([lax.optimization_barrier(jnp.sum(grouped, axis=2)), lax.optimization_barrier(jnp.sum(grouped * grouped, axis=2)), valid[:, None]], axis=1)
    running = segment_cumsum(totals, flags)
    counts = jnp.maximum(running[:, 2 * groups:], 1.0) * GROUP
    means = running[:, :groups] / counts
    variance = running[:, groups:2 * groups] / counts - means * means
    scaled = (grouped - means[:, :, None]) * lax.rsqrt(variance + 1e-05)[:, :, None]
    return scaled.reshape(length, width) * gain[None, :]

def complex_combine(earlier, later):
    return (later[0] * earlier[0] - later[1] * earlier[1], later[0] * earlier[1] + later[1] * earlier[0], later[0] * earlier[2] - later[1] * earlier[3] + later[2], later[0] * earlier[3] + later[1] * earlier[2] + later[3])

def ema_scan(normed, rate, angle, input_w, output_w, skip_w):
    magnitude = 1.0 - rate
    coeff = jnp.sqrt(rate * (2.0 - rate)) * input_w
    shape = (normed.shape[0],) + rate.shape
    decay_re = jnp.broadcast_to(magnitude * jnp.cos(angle), shape)
    decay_im = jnp.broadcast_to(magnitude * jnp.sin(angle), shape)
    drive_re = coeff[None] * normed[:, :, None]
    drive_im = jnp.zeros_like(drive_re)
    states = lax.associative_scan(complex_combine, (decay_re, decay_im, drive_re, drive_im), axis=0)
    return lax.optimization_barrier(jnp.sum(states[2] * output_w[None], axis=2)) + skip_w[None] * normed

def block_attention(queries, keys, values, segs, valid):
    length = queries.shape[0]
    scale_factor = queries.shape[1] ** (-0.5)
    scores = low_back(matmul_high(queries, keys.T) * scale_factor)
    places = jnp.arange(length)
    allowed = (places[None, :] <= places[:, None]) & (segs[None, :] == segs[:, None]) & ((valid[None, :] > 0.5) | (places[None, :] == places[:, None]))
    masked = jnp.where(allowed, scores, -1e+30)
    top = lax.optimization_barrier(jnp.max(masked, axis=1, keepdims=True))
    weights = jnp.exp(masked - top)
    probs = weights / lax.optimization_barrier(jnp.sum(weights, axis=1, keepdims=True))
    return low_back(matmul_high(low(probs), values))

def layer_group(params, inputs, segs, valid):
    w_z, w_v, w_r, w_h, w_gate, w_up, w_down, q_gain, q_bias, k_gain, ffn_gain, norm_gain, ema_rate, ema_angle, ema_input, ema_output, ema_skip = params
    length, width = inputs.shape
    masked_in = inputs * valid[:, None]
    flags = jnp.concatenate([jnp.ones((1,), jnp.float32), (segs[1:] != segs[:-1]).astype(jnp.float32)])[:, None]
    normed = step_norm(masked_in, flags, valid, norm_gain)
    piece_width = 64
    pieces = width // piece_width

    def ema_piece(items):
        return ema_scan(items[0], items[1], items[2], items[3], items[4], items[5])
    sliced = (jnp.transpose(normed.reshape(length, pieces, piece_width), (1, 0, 2)), ema_rate.reshape(pieces, piece_width, -1), ema_angle.reshape(pieces, piece_width, -1), ema_input.reshape(pieces, piece_width, -1), ema_output.reshape(pieces, piece_width, -1), ema_skip.reshape(pieces, piece_width))
    mixed = jnp.transpose(lax.map(jax.checkpoint(ema_piece), sliced), (1, 0, 2)).reshape(length, width)
    sent_norm = low(low_back(normed))
    sent_mix = low(low_back(jax.nn.silu(mixed)))
    shared = low_back(matmul_high(sent_mix, low(w_z)))
    queries = low(shared * low(q_gain)[None] + low(q_bias)[None])
    keys = low(shared * low(k_gain)[None])
    value_pre = low_back(matmul_high(sent_norm, low(w_v)))
    values = low(jax.nn.silu(value_pre))
    gate_pre = low_back(matmul_high(sent_mix, low(w_r)))
    reset_gate = jax.nn.silu(gate_pre)
    blocks = length // ROWS

    def attend(items):
        return block_attention(items[0], items[1], items[2], items[3], items[4])
    attended = lax.map(jax.checkpoint(attend), (queries.reshape(blocks, ROWS, -1), keys.reshape(blocks, ROWS, -1), values.reshape(blocks, ROWS, -1), segs.reshape(blocks, ROWS), valid.reshape(blocks, ROWS)))
    attended = attended.reshape(length, -1)
    gated = low(low_back(attended * reset_gate))
    middle = masked_in + low_back(matmul_high(gated, low(w_h)))
    inverse = lax.rsqrt(lax.optimization_barrier(jnp.mean(middle * middle, axis=1, keepdims=True)) + 1e-05)
    ffn_in = low(middle * inverse * low(ffn_gain)[None])
    gate_ffn = low_back(matmul_high(ffn_in, low(w_gate)))
    up_ffn = low_back(matmul_high(ffn_in, low(w_up)))
    hidden = low(jax.nn.silu(gate_ffn) * up_ffn)
    return middle + low_back(matmul_high(hidden, low(w_down)))

def reference(tokens, cotangent, segment_ids, pad_mask, w_z, w_v, w_r, w_h, w_gate, w_up, w_down, q_gain, q_bias, k_gain, ffn_gain, norm_gain, ema_rate, ema_angle, ema_input, ema_output, ema_skip):
    params = (w_z, w_v, w_r, w_h, w_gate, w_up, w_down, q_gain, q_bias, k_gain, ffn_gain, norm_gain, ema_rate, ema_angle, ema_input, ema_output, ema_skip)
    inputs = tokens.astype(jnp.float32)
    valid = pad_mask.astype(jnp.float32)

    def forward(weights, features):

        def one_group(items):
            return layer_group(weights, items[0], items[1], items[2])
        return lax.map(jax.checkpoint(one_group), (features, segment_ids, valid))
    result, pullback = jax.vjp(forward, params, inputs)
    grads, input_grad = pullback(cotangent.astype(jnp.float32))
    return (result.astype(jnp.bfloat16), input_grad, grads[0], grads[1], grads[2], grads[3], grads[4], grads[5], grads[6], grads[7], grads[8], grads[9], grads[10], grads[11], grads[12], grads[13], grads[14], grads[15], grads[16])
```

```python
import functools
import math

import jax
import jax.numpy as jnp
from jax import lax
from jax.experimental import pallas as pl
from jax.experimental.pallas import tpu as pltpu
from jax.sharding import PartitionSpec as P

GROUP = 64
DOCS = 16
LANES = 128
SUB = 8
SPAN = 32
BAND = 64
bf16 = jnp.bfloat16
f32 = jnp.float32
VMEM_LIMIT = 60 * 1024 * 1024


def split3(value):
    first = value.astype(bf16)
    rest = value - first.astype(f32)
    second = rest.astype(bf16)
    third = (rest - second.astype(f32)).astype(bf16)
    return first, second, third


def dot(left, right):
    return jnp.dot(left, right, preferred_element_type=f32)


def dot3(left, parts):
    return dot(left, parts[0]) + dot(left, parts[1]) + dot(left, parts[2])


def dot3_left(parts, right):
    return dot(parts[0], right) + dot(parts[1], right) + dot(parts[2], right)


def iota(shape, axis):
    return lax.broadcasted_iota(jnp.int32, shape, axis)


def group_pick(width, shift):
    own = lax.shift_right_logical(iota((width, LANES), 0), GROUP.bit_length() - 1)
    return (own + shift == iota((width, LANES), 1)).astype(bf16)


def group_spread(groups, width):
    own = lax.shift_right_logical(iota((groups, width), 1), GROUP.bit_length() - 1)
    return (own == iota((groups, width), 0)).astype(bf16)


ANY = pl.BlockSpec(memory_space=pl.ANY)
VM = pl.BlockSpec(memory_space=pltpu.VMEM)
SM = pl.BlockSpec(memory_space=pltpu.SMEM)


def kernel_call(body, outs, args, specs=None, scratch=(), name=None, micros=10, after=(), grid=None, out_specs=None):
    specs = [VM] * len(args) if specs is None else specs
    count = len(args)

    def run(*refs):
        body(*refs[:count], *refs[count + len(after) :])

    more = {} if grid is None else dict(grid=grid, out_specs=tuple(out_specs))
    return pl.pallas_call(
        run,
        out_shape=tuple(jax.ShapeDtypeStruct(shape, dtype) for shape, dtype in outs),
        in_specs=list(specs) + [ANY] * len(after),
        scratch_shapes=list(scratch),
        compiler_params=pltpu.CompilerParams(vmem_limit_bytes=VMEM_LIMIT),
        cost_estimate=pl.CostEstimate(
            flops=int(micros * 1.0e9), bytes_accessed=int(micros * 3.0e6), transcendentals=0
        ),
        name=name,
        **more,
    )(*args, *after)


def tie(value, *after):
    def nothing(*refs):
        return None

    return pl.pallas_call(
        nothing,
        out_shape=jax.ShapeDtypeStruct(value.shape, value.dtype),
        in_specs=[ANY] * (1 + len(after)),
        out_specs=ANY,
        input_output_aliases={0: 0},
        name="tie",
    )(value, *after)


def split_wide(value):
    return jnp.concatenate(split3(value), axis=1)


def spread_wide(groups, width, start):
    own = lax.shift_right_logical(iota((3 * groups, LANES), 1) + start, GROUP.bit_length() - 1)
    return (own == lax.rem(iota((3 * groups, LANES), 0), groups)).astype(bf16)


def moments(total, groups):
    counts = jnp.maximum(total[:, 2 * groups : 2 * groups + 1], 1.0) * float(GROUP)
    means = total[:, :groups] / counts
    variance = total[:, groups : 2 * groups] / counts - means * means
    return means, lax.rsqrt(variance + 1e-05), counts


def stats_kernel(tok_ref, valid_ref, segc_ref, segr_ref, prefix_ref, totals_ref):
    rows, width = tok_ref.shape
    groups = width // GROUP
    valid = valid_ref[...]
    masked = tok_ref[...].astype(f32) * valid
    low = masked.astype(bf16)
    square = masked * masked
    high = square.astype(bf16)
    rest = (square - high.astype(f32)).astype(bf16)
    second = group_pick(width, groups)
    sums = dot(low, group_pick(width, 0)) + dot(high, second) + dot(rest, second)
    sums = sums + jnp.where(iota((rows, LANES), 1) == 2 * groups, valid, 0.0)
    parts = split3(sums)
    earlier = (iota((rows, rows), 1) <= iota((rows, rows), 0)) & (segc_ref[...] == segr_ref[...])
    prefix_ref[...] = dot3(earlier.astype(f32).astype(bf16), parts)
    member = (iota((DOCS, rows), 0) == segr_ref[...]).astype(f32).astype(bf16)
    totals_ref[...] = dot3(member, parts)


def scan_ends(src_ref, a_ref, b_ref, end_ref, rows, ndim, reverse):
    half = ndim // 2
    for start in range(0, ndim, half):
        a = [a_ref[pl.ds((start + n) * SUB, SUB), :] for n in range(half)]
        b = [b_ref[pl.ds((start + n) * SUB, SUB), :] for n in range(half)]

        def step(i, state, a=a, b=b):
            t = rows - 1 - i if reverse else i
            x = src_ref[pl.ds(pl.multiple_of(t * SUB, SUB), SUB), :]
            fresh = []
            for n in range(half):
                re, im = state[2 * n], state[2 * n + 1]
                if reverse:
                    fresh += [a[n] * re + b[n] * im + x, a[n] * im - b[n] * re]
                else:
                    fresh += [a[n] * re - b[n] * im + x, a[n] * im + b[n] * re]
            return tuple(fresh)

        zero = jnp.zeros((SUB, LANES), f32)
        state = lax.fori_loop(0, rows, step, (zero,) * (2 * half), unroll=8)
        for n in range(half):
            end_ref[pl.ds((start + n) * SUB, SUB), :] = state[2 * n]
            end_ref[pl.ds((ndim + start + n) * SUB, SUB), :] = state[2 * n + 1]


def all_moments(prefix_ref, segc_ref, carry_ref, groups):
    total = prefix_ref[...] + jnp.where(segc_ref[...] == segc_ref[0:1, :], carry_ref[...], 0.0)
    return moments(total, groups)


def lane_rows(j, rows):
    return pl.ds(j, rows, stride=SUB)


def norm_kernel(tok_ref, valid_ref, segc_ref, prefix_ref, carry_ref, gain_ref, a_ref, b_ref,
                sent_ref, xs_ref, end_ref):
    rows, width = tok_ref.shape
    groups = width // GROUP
    ndim = a_ref.shape[0] // SUB
    means, scale, _ = all_moments(prefix_ref, segc_ref, carry_ref, groups)
    means, scale, valid = split_wide(means), split_wide(scale), valid_ref[...]
    for j in range(SUB):
        at = slice(j * LANES, (j + 1) * LANES)
        spread = spread_wide(groups, width, j * LANES)
        normed = (tok_ref[:, at].astype(f32) * valid - dot(means, spread)) * dot(scale, spread) * gain_ref[:, at]
        sent_ref[:, at] = normed.astype(bf16)
        xs_ref[lane_rows(j, rows), :] = normed
    scan_ends(xs_ref, a_ref, b_ref, end_ref, rows, ndim, False)


def mix_kernel(xs_ref, start_ref, a_ref, b_ref, g_ref, skip_ref, mixed_ref, sent_ref, keep_ref, state_ref):
    rows = xs_ref.shape[0] // SUB
    ndim = a_ref.shape[0] // SUB
    half = ndim // 2
    state_ref[...] = start_ref[...]

    def chunk(i, _):
        keep_ref[i] = state_ref[...]
        for start in range(0, ndim, half):
            re_at = [pl.ds((start + n) * SUB, SUB) for n in range(half)]
            im_at = [pl.ds((ndim + start + n) * SUB, SUB) for n in range(half)]
            a = [a_ref[at, :] for at in re_at]
            b = [b_ref[at, :] for at in re_at]
            g = [g_ref[at, :] for at in re_at]

            def step(k, state, start=start, a=a, b=b, g=g):
                at = pl.ds(pl.multiple_of((i * SPAN + k) * SUB, SUB), SUB)
                x = xs_ref[at, :]
                fresh, terms = [], []
                for n in range(half):
                    re, im = state[2 * n], state[2 * n + 1]
                    now = a[n] * re - b[n] * im + x
                    fresh += [now, a[n] * im + b[n] * re]
                    terms.append(g[n] * now)
                terms.append(skip_ref[...] * x if start == 0 else mixed_ref[at, :])
                while len(terms) > 1:
                    terms = [sum(terms[p : p + 2][1:], terms[p]) for p in range(0, len(terms), 2)]
                mixed_ref[at, :] = terms[0]
                return tuple(fresh)

            state = []
            for n in range(half):
                state += [state_ref[re_at[n], :], state_ref[im_at[n], :]]
            state = lax.fori_loop(0, SPAN, step, tuple(state), unroll=8)
            for n in range(half):
                state_ref[re_at[n], :] = state[2 * n]
                state_ref[im_at[n], :] = state[2 * n + 1]
        return 0

    lax.fori_loop(0, rows // SPAN, chunk, 0)

    def band(i, _):
        at = pl.ds(pl.multiple_of(i * BAND, BAND), BAND)
        for j in range(SUB):
            mixed = mixed_ref[pl.ds(i * (BAND * SUB) + j, BAND, stride=SUB), :]
            sent_ref[at, j * LANES : (j + 1) * LANES] = (mixed * jax.nn.sigmoid(mixed)).astype(bf16)
        return 0

    lax.fori_loop(0, rows // BAND, band, 0)


def back_ends_kernel(grad_ref, mixed_ref, a_ref, b_ref, drive_ref, end_ref):
    rows = grad_ref.shape[0]
    ndim = a_ref.shape[0] // SUB

    def band(i, _):
        at = pl.ds(pl.multiple_of(i * BAND, BAND), BAND)
        for j in range(SUB):
            where = pl.ds(i * (BAND * SUB) + j, BAND, stride=SUB)
            mixed = mixed_ref[where, :]
            sigma = jax.nn.sigmoid(mixed)
            slope = sigma * (1.0 + mixed * (1.0 - sigma))
            drive_ref[where, :] = grad_ref[at, j * LANES : (j + 1) * LANES].astype(f32) * slope
        return 0

    lax.fori_loop(0, rows // BAND, band, 0)
    scan_ends(drive_ref, a_ref, b_ref, end_ref, rows, ndim, True)


def back_scan_kernel(xs_ref, drive_ref, keep_ref, start_ref, sums_in_ref, a_ref, b_ref, g_ref, skip_ref,
                     dxs_ref, state_ref, sums_ref, hist_ref):
    ndim = a_ref.shape[0] // SUB
    rows = xs_ref.shape[0] // SUB
    part = 4
    count = rows // SPAN
    state_ref[...] = start_ref[...]
    sums_ref[...] = sums_in_ref[...]

    def chunk(c, _):
        i = count - 1 - c
        for start in range(0, ndim, part):
            re_at = [pl.ds((start + n) * SUB, SUB) for n in range(part)]
            im_at = [pl.ds((ndim + start + n) * SUB, SUB) for n in range(part)]
            last_at = [pl.ds((2 * ndim + start + n) * SUB, SUB) for n in range(part)]
            a = [a_ref[at, :] for at in re_at]
            b = [b_ref[at, :] for at in re_at]
            g = [g_ref[at, :] for at in re_at]

            def forward(k, state, a=a, b=b):
                x = xs_ref[pl.ds(pl.multiple_of((i * SPAN + k) * SUB, SUB), SUB), :]
                fresh = []
                for n in range(part):
                    re, im = state[2 * n], state[2 * n + 1]
                    hist_ref[k, pl.ds(2 * n * SUB, SUB), :] = re
                    hist_ref[k, pl.ds((2 * n + 1) * SUB, SUB), :] = im
                    fresh += [a[n] * re - b[n] * im + x, a[n] * im + b[n] * re]
                return tuple(fresh)

            state = []
            for n in range(part):
                state += [keep_ref[i, re_at[n], :], keep_ref[i, im_at[n], :]]
            lax.fori_loop(0, SPAN, forward, tuple(state), unroll=8)

            def backward(k, held, start=start, a=a, b=b, g=g):
                t = SPAN - 1 - k
                at = pl.ds(pl.multiple_of((i * SPAN + t) * SUB, SUB), SUB)
                x, drive = xs_ref[at, :], drive_ref[at, :]
                fresh, terms = [], []
                for n in range(part):
                    re, im, m_re, m_im, same = held[5 * n : 5 * n + 5]
                    now_re = a[n] * re + b[n] * im + drive
                    now_im = a[n] * im - b[n] * re
                    old_re = hist_ref[t, pl.ds(2 * n * SUB, SUB), :]
                    old_im = hist_ref[t, pl.ds((2 * n + 1) * SUB, SUB), :]
                    fresh += [
                        now_re,
                        now_im,
                        m_re + (now_re * old_re + now_im * old_im),
                        m_im + (now_im * old_re - now_re * old_im),
                        same + x * now_re,
                    ]
                    terms.append(g[n] * now_re)
                total = (terms[0] + terms[1]) + (terms[2] + terms[3])
                if start == 0:
                    dxs_ref[at, :] = total + skip_ref[...] * drive
                else:
                    dxs_ref[at, :] = total + dxs_ref[at, :]
                return tuple(fresh)

            held = []
            for n in range(part):
                held += [state_ref[re_at[n], :], state_ref[im_at[n], :]]
                held += [sums_ref[re_at[n], :], sums_ref[im_at[n], :], sums_ref[last_at[n], :]]
            held = lax.fori_loop(0, SPAN, backward, tuple(held), unroll=8)
            for n in range(part):
                state_ref[re_at[n], :] = held[5 * n]
                state_ref[im_at[n], :] = held[5 * n + 1]
                sums_ref[re_at[n], :] = held[5 * n + 2]
                sums_ref[im_at[n], :] = held[5 * n + 3]
                sums_ref[last_at[n], :] = held[5 * n + 4]
        return 0

    lax.fori_loop(0, count, chunk, 0)

    def skip_step(k, total):
        at = pl.ds(pl.multiple_of(k * SUB, SUB), SUB)
        return total + xs_ref[at, :] * drive_ref[at, :]

    last = pl.ds(3 * ndim * SUB, SUB)
    sums_ref[last, :] = lax.fori_loop(0, rows, skip_step, sums_ref[last, :], unroll=8)


def back_norm_kernel(*refs):
    dxs_refs, refs = refs[:-12], refs[-12:]
    (grad_ref, tok_ref, valid_ref, segc_ref, segr_ref, prefix_ref, carry_ref, gain_ref,
     dn_ref, dgain_ref, suffix_ref, totals_ref) = refs
    rows, width = tok_ref.shape
    groups = width // GROUP
    means, scale, counts = all_moments(prefix_ref, segc_ref, carry_ref, groups)
    wide_means, wide_scale, valid = split_wide(means), split_wide(scale), valid_ref[...]
    plain, leaning = jnp.zeros((rows, LANES), f32), jnp.zeros((rows, LANES), f32)
    for j in range(SUB):
        at = slice(j * LANES, (j + 1) * LANES)
        spread = spread_wide(groups, width, j * LANES)
        own = lax.shift_right_logical(iota((LANES, LANES), 0) + j * LANES, GROUP.bit_length() - 1)
        pick = (own == iota((LANES, LANES), 1)).astype(bf16)
        centred = tok_ref[:, at].astype(f32) * valid - dot(wide_means, spread)
        ema = [ref[lane_rows(j, ref.shape[0] // SUB), :] for ref in dxs_refs]
        dn = grad_ref[:, at].astype(f32) + jnp.concatenate(ema, axis=0)
        dgain_ref[:, at] = jnp.sum(dn * centred * dot(wide_scale, spread), axis=0, keepdims=True)
        dn = dn * gain_ref[:, at]
        dn_ref[:, at] = dn
        plain = plain + dot3_left(split3(dn), pick)
        leaning = leaning + dot3_left(split3(dn * centred), pick)
    plain, leaning = plain[:, :groups], leaning[:, :groups]
    d_variance = -0.5 * leaning * scale * scale * scale
    d_second = d_variance / counts
    d_first = (-scale * plain - 2.0 * means * d_variance) / counts
    flow = jnp.concatenate([d_first, d_second, jnp.zeros((rows, LANES - 2 * groups), f32)], axis=1)
    parts = split3(flow)
    later = (iota((rows, rows), 1) >= iota((rows, rows), 0)) & (segc_ref[...] == segr_ref[...])
    suffix_ref[...] = dot3(later.astype(f32).astype(bf16), parts)
    member = (iota((DOCS, rows), 0) == segr_ref[...]).astype(f32).astype(bf16)
    totals_ref[...] = dot3(member, parts)


def input_kernel(dn_ref, suffix_ref, back_ref, tok_ref, valid_ref, segc_ref, prefix_ref, carry_ref, middle_ref, out_ref):
    rows, width = tok_ref.shape
    groups = width // GROUP
    _, scale, _ = all_moments(prefix_ref, segc_ref, carry_ref, groups)
    flow = suffix_ref[...] + jnp.where(segc_ref[...] == segc_ref[rows - 1 : rows, :], back_ref[...], 0.0)
    scale, valid = split_wide(scale), valid_ref[...]
    first, second = split_wide(flow[:, :groups]), split_wide(flow[:, groups : 2 * groups])
    for j in range(SUB):
        at = slice(j * LANES, (j + 1) * LANES)
        spread = spread_wide(groups, width, j * LANES)
        masked = tok_ref[:, at].astype(f32) * valid
        grad = dn_ref[:, at] * dot(scale, spread) + dot(first, spread) + 2.0 * masked * dot(second, spread)
        out_ref[:, at] = valid * (middle_ref[:, at] + grad)


def swap(value, axis, bit):
    count = lax.axis_size(axis)
    return lax.ppermute(value, axis, [(i, i ^ bit) for i in range(count)])


def gather_small(value, axis):
    index, count = lax.axis_index(axis), lax.axis_size(axis)
    value, bit = value[None], 1
    while bit < count:
        other = swap(value, axis, bit)
        upper = (index & bit) != 0
        value = jnp.concatenate([jnp.where(upper, other, value), jnp.where(upper, value, other)], axis=0)
        bit *= 2
    return value


def cmul(left, right):
    return (left[0] * right[0] - left[1] * right[1], left[0] * right[1] + left[1] * right[0])


def state_before(ends, hop, axis, reverse):
    index, count = lax.axis_index(axis), lax.axis_size(axis)
    if reverse:
        index = count - 1 - index
    half = ends.shape[0] // 2
    before = (jnp.zeros_like(ends[:half]), jnp.zeros_like(ends[:half]))
    reach = (jnp.ones_like(hop[0]), jnp.zeros_like(hop[1]))
    bit = 1
    while bit < count:
        other = swap(ends, axis, bit)
        upper = (index & bit) != 0
        far, own = (other[:half], other[half:]), (ends[:half], ends[half:])
        moved = cmul(reach, far)
        before = tuple(v + jnp.where(upper, w, 0.0) for v, w in zip(before, moved))
        if bit * 2 < count:
            lower = tuple(jnp.where(upper, v, w) for v, w in zip(far, own))
            higher = tuple(jnp.where(upper, w, v) for v, w in zip(far, own))
            carried = cmul(hop, lower)
            ends = jnp.concatenate([carried[0] + higher[0], carried[1] + higher[1]], axis=0)
            longer = cmul(reach, hop)
            reach = tuple(jnp.where(upper, v, w) for v, w in zip(longer, reach))
            hop = cmul(hop, hop)
        bit *= 2
    return jnp.concatenate(before, axis=0)


def ema_params(full, ndim, rows):
    full = jnp.transpose(full, (1, 0, 2))
    full = full.reshape(full.shape[0], SUB, -1)
    rate, angle, input_w, output_w = (full[i * ndim : (i + 1) * ndim] for i in range(4))
    gain, skip = full[4 * ndim], full[4 * ndim + 1]
    base = jnp.sqrt(rate * (2.0 - rate))
    cos, sin = jnp.cos(angle), jnp.sin(angle)
    a, b = (1.0 - rate) * cos, (1.0 - rate) * sin
    hop, steps = (a, b), 1
    while steps < rows:
        hop, steps = cmul(hop, hop), steps * 2
    return dict(rate=rate, input_w=input_w, output_w=output_w, gain=gain, skip=skip, base=base,
                cos=cos, sin=sin, a=a, b=b, coeff=base * input_w, hop=hop)


def ema_param_grads(par, sums):
    ndim = par["rate"].shape[0]
    m_re, m_im, same = sums[:ndim], sums[ndim : 2 * ndim], sums[2 * ndim : 3 * ndim]
    weight = par["output_w"] * par["coeff"]
    d_a, d_b = weight * m_re, weight * m_im
    d_coeff = par["output_w"] * same
    d_output = par["coeff"] * same
    d_input = par["base"] * d_coeff
    d_rate = d_coeff * par["input_w"] * (1.0 - par["rate"]) / par["base"] - par["cos"] * d_a - par["sin"] * d_b
    d_angle = par["a"] * d_b - par["b"] * d_a
    return d_rate, d_angle, d_input, d_output


def mul_t(left, right):
    return lax.dot_general(left, right, (((1,), (1,)), ((), ())), preferred_element_type=f32)


def t_mul(left, right):
    return lax.dot_general(left, right, (((0,), (0,)), ((), ())), preferred_element_type=f32)


def silu_grad(value):
    sigma = jax.nn.sigmoid(value)
    return sigma * (1.0 + value * (1.0 - sigma))


def bits_of(count):
    return count.bit_length() - 1


class Pieces:
    def __init__(self, arrays, owners):
        self.arrays, self.owners = arrays, owners

    def copies(self, refs, where, column, me, sem):
        made = []
        for ref, owners in zip(refs, self.owners):
            block = ref.shape[1]
            for slot, owner in enumerate(owners):
                start = pl.multiple_of((me ^ owner) * block, block)
                to = where.at[pl.ds(start, block), column : column + ref.shape[2]]
                made.append(pltpu.make_async_copy(ref.at[slot], to, sem))
        return made


class Columns:
    def __init__(self, parts, starts):
        self.parts, self.starts = parts, starts
        self.arrays = [array for part in parts for array in part.arrays]

    def copies(self, refs, where, me, sem):
        made, refs = [], list(refs)
        for part, start in zip(self.parts, self.starts):
            own = [refs.pop(0) for _ in part.arrays]
            made += part.copies(own, where, start, me, sem)
        return made


class Gather:
    def __init__(self, shard, order):
        self.order = order
        if order is None:
            full = lax.all_gather(shard, ("seq", "dp"), axis=0, tiled=True)
            self.arrays, self.owners = [full[None]], [[0]]
            return
        self.arrays, self.owners, self.place = [shard[None]], [[0]], 0

    def step(self, after=()):
        if self.order is None:
            return ()
        bit = self.order[self.place]
        mine = [tie(value, *after) for value in self.arrays] if after else self.arrays
        others = [swap_bit(value, bit) for value in mine]
        moved = [[owner ^ (1 << bit) for owner in row] for row in self.owners]
        if self.place < len(self.order) - 2:
            self.arrays = [jnp.concatenate([mine[0], others[0]], axis=0)]
            self.owners = [self.owners[0] + moved[0]]
        else:
            self.arrays, self.owners = mine + others, self.owners + moved
        self.place += 1
        return (self.arrays[-1],)

    @property
    def pieces(self):
        return Pieces(self.arrays, self.owners)


def swap_bit(value, bit):
    dp_bits = bits_of(lax.axis_size("dp"))
    if bit < dp_bits:
        return swap(value, "dp", 1 << bit)
    return swap(value, "seq", 1 << (bit - dp_bits))


class Reduce:
    def __init__(self, blocks, order):
        self.keep, self.send = blocks
        self.order = order
        self.left = list(order or ())
        self.other = None
        self.begin()

    def begin(self):
        if self.left:
            self.other = swap_bit(self.send, self.left.pop(0))

    def step(self):
        if self.order is None:
            return ()
        if not self.left:
            self.keep = self.keep.astype(f32) + self.other.astype(f32)
            return (self.keep,)
        half = self.keep.shape[0] // 2
        self.send = (self.keep[half:].astype(f32) + self.other[half:].astype(f32)).astype(bf16)
        self.keep = (self.keep[:half].astype(f32) + self.other[:half].astype(f32)).astype(bf16)
        self.begin()
        return (self.send,)

    def finish(self, core, widths):
        if self.order is None:
            outs, at = [], 0
            for width in widths:
                part = self.keep[0, :, at : at + width]
                zero = jnp.zeros_like(part)
                full = jnp.concatenate([jnp.where(core == 0, part, zero), jnp.where(core == 0, zero, part)], axis=1)
                outs.append(lax.psum_scatter(full, ("seq", "dp"), scatter_dimension=0, tiled=True).astype(f32))
                at += width
            return outs
        chip_rows = self.keep[0]
        rows = chip_rows.shape[0] // 2
        lower, upper = chip_rows[:rows], chip_rows[rows:]
        own = jnp.where(core == 0, lower, upper)
        other = swap_bit(jnp.where(core == 0, upper, lower).astype(bf16), 0).astype(f32)
        outs, at = [], 0
        for width in widths:
            mine, theirs = own[:, at : at + width], other[:, at : at + width]
            outs.append(
                jnp.concatenate([jnp.where(core == 0, mine, theirs), jnp.where(core == 0, theirs, mine)], axis=1)
            )
            at += width
        return outs


def allowed_pairs(segc_ref, segr_ref, validr_ref):
    rows = segc_ref.shape[0]
    query, key = iota((rows, rows), 0), iota((rows, rows), 1)
    same = segc_ref[...] == segr_ref[...]
    usable = validr_ref[...] > 0.5
    return (key <= query) & same & (usable | (key == query))


def attention_kernel(pieces1, tile, *refs):
    n1 = len(pieces1.arrays)
    me_ref, norm_ref, mix_ref, segc_ref, segr_ref, validr_ref, qg_ref, qb_ref, kg_ref = refs[:9]
    w1_refs = refs[9 : 9 + n1]
    shared_ref, q_ref, k_ref, lse_ref, vpre_ref, values_ref, gpre_ref, att_ref, gated_ref, w1, probs_ref, sem1 = refs[9 + n1 :]
    me = me_ref[0]
    values_width = values_ref.shape[1]
    copies1 = pieces1.copies(w1_refs, w1, me, sem1)
    for copy in copies1:
        copy.start()
    for copy in copies1:
        copy.wait()
    shared = dot(mix_ref[...], w1[:, 2 * values_width :])
    shared_ref[...] = shared
    queries = (shared * qg_ref[...] + qb_ref[...]).astype(bf16)
    keys = (shared * kg_ref[...]).astype(bf16)
    q_ref[...] = queries
    k_ref[...] = keys
    scores = mul_t(queries, keys) * (queries.shape[1] ** -0.5)
    masked = jnp.where(allowed_pairs(segc_ref, segr_ref, validr_ref), scores, -1e30)
    top = jnp.max(masked, axis=1, keepdims=True)
    weights = jnp.exp(masked - top)
    total = jnp.sum(weights, axis=1, keepdims=True)
    probs_ref[...] = (weights / total).astype(bf16)
    lse_ref[...] = top + jnp.log(total)

    def columns(i, _):
        at = pl.ds(pl.multiple_of(i * tile, tile), tile)
        value_pre = dot(norm_ref[...], w1[:, at])
        vpre_ref[:, at] = value_pre.astype(bf16)
        values = (value_pre * jax.nn.sigmoid(value_pre)).astype(bf16)
        values_ref[:, at] = values
        gate_pre = dot(mix_ref[...], w1[:, pl.ds(pl.multiple_of(values_width + i * tile, tile), tile)])
        gpre_ref[:, at] = gate_pre.astype(bf16)
        attended = dot(probs_ref[...], values)
        att_ref[:, at] = attended.astype(bf16)
        gated_ref[:, at] = (attended * (gate_pre * jax.nn.sigmoid(gate_pre))).astype(bf16)
        return 0

    lax.fori_loop(0, values_width // tile, columns, 0)


def project_kernel(pieces2, tile, *refs):
    n2 = len(pieces2.arrays)
    me_ref, gated_ref, tok_ref, valid_ref, fg_ref = refs[:5]
    middle_ref, ffn_ref, inv_ref, w2, sem2 = refs[5 + n2 :]
    width = tok_ref.shape[1]
    copies2 = pieces2.copies(refs[5 : 5 + n2], w2, me_ref[0], sem2)
    for copy in copies2:
        copy.start()
    for copy in copies2:
        copy.wait()

    def out_columns(i, square):
        at = pl.ds(pl.multiple_of(i * tile, tile), tile)
        middle = tok_ref[:, at].astype(f32) * valid_ref[...] + dot(gated_ref[...], w2[:, at])
        middle_ref[:, at] = middle
        return square + jnp.sum(middle * middle, axis=1, keepdims=True)

    square = lax.fori_loop(0, width // tile, out_columns, jnp.zeros((tok_ref.shape[0], 1), f32))
    inverse = lax.rsqrt(square * (1.0 / width) + 1e-05)
    inv_ref[...] = inverse
    ffn_ref[...] = (middle_ref[...] * inverse * fg_ref[...]).astype(bf16)


def hidden_kernel(pieces3, pieces4, tile, *refs):
    n3, n4 = len(pieces3.arrays), len(pieces4.arrays)
    me_ref, ffn_ref, cot_ref = refs[:3]
    w3_refs, w4_refs = refs[3 : 3 + n3], refs[3 + n3 : 3 + n3 + n4]
    hid_ref, gg0, gu0, far_ref, w3, w4, sem3, sem4 = refs[3 + n3 + n4 :]
    me = me_ref[0]
    half = gg0.shape[1]
    copies3 = pieces3.copies(w3_refs, w3, me, sem3)
    copies4 = pieces4.copies(w4_refs, w4, me, sem4)
    for copy in copies3 + copies4:
        copy.start()
    for copy in copies3 + copies4:
        copy.wait()
    for rel in range(2):
        base = ((me_ref[1] ^ rel) * half)

        def columns(i, _, base=base, rel=rel):
            at = pl.ds(pl.multiple_of(i * tile, tile), tile)
            gate = dot(ffn_ref[...], w3[:, pl.ds(pl.multiple_of(base + i * tile, tile), tile)])
            up = dot(ffn_ref[...], w3[:, pl.ds(pl.multiple_of(2 * half + base + i * tile, tile), tile)])
            sigma = jax.nn.sigmoid(gate)
            act = gate * sigma
            hid_ref[:, pl.ds(pl.multiple_of(rel * half + i * tile, tile), tile)] = (act * up).astype(bf16)
            grad = mul_t(cot_ref[...], w4[pl.ds(pl.multiple_of(base + i * tile, tile), tile), :])
            grad_gate = (grad * up * (sigma * (1.0 + gate * (1.0 - sigma)))).astype(bf16)
            grad_up = (grad * act).astype(bf16)
            if rel == 0:
                gg0[:, at] = grad_gate
                gu0[:, at] = grad_up
            else:
                far_ref[:, at] = grad_gate
                far_ref[:, pl.ds(pl.multiple_of(half + i * tile, tile), tile)] = grad_up
            return 0

        lax.fori_loop(0, half // tile, columns, 0)


def ffn_back_kernel(pieces3, pieces4, tile, *refs):
    n3, n4 = len(pieces3.arrays), len(pieces4.arrays)
    me_ref, hid_ref, gg0, gu0, far_ref, middle_ref, inv_ref, cot_ref, fg_ref = refs[:9]
    w3_refs, w4_refs = refs[9 : 9 + n3], refs[9 + n3 : 9 + n3 + n4]
    out_ref, gmid_ref, low_own, low_oth, low_ref, dfg_ref, w3, w4, gin_ref, sem3, sem4 = refs[9 + n3 + n4 :]
    me, core = me_ref[0], me_ref[1]
    half = gg0.shape[1]
    rows, width = middle_ref.shape
    copies3 = pieces3.copies(w3_refs, w3, me, sem3)
    copies4 = pieces4.copies(w4_refs, w4, me, sem4)
    for copy in copies3 + copies4:
        copy.start()
    for copy in copies3:
        copy.wait()
    starts = [pl.multiple_of((core ^ rel) * half, half) for rel in range(2)]

    def grad_columns(i, carry):
        lean = carry
        at = pl.ds(pl.multiple_of(i * tile, tile), tile)
        grad = jnp.zeros((rows, tile), f32)
        for rel, (gg, gu) in enumerate(((gg0[...], gu0[...]), (far_ref[:, :half], far_ref[:, half:]))):
            grad = grad + mul_t(gg, w3[at, pl.ds(starts[rel], half)])
            up_start = pl.multiple_of(starts[rel] + 2 * half, half)
            grad = grad + mul_t(gu, w3[at, pl.ds(up_start, half)])
        normal = middle_ref[:, at] * inv_ref[...]
        dfg_ref[:, at] = jnp.sum(grad * normal, axis=0, keepdims=True)
        grad = grad * fg_ref[:, at]
        gin_ref[:, at] = grad
        return lean + jnp.sum(grad * normal, axis=1, keepdims=True)

    lean = lax.fori_loop(0, width // tile, grad_columns, jnp.zeros((rows, 1), f32)) * (1.0 / width)
    inverse = inv_ref[...]
    grad_middle = cot_ref[...].astype(f32) + inverse * (gin_ref[...] - middle_ref[...] * inverse * lean)
    gmid_ref[...] = grad_middle
    low_ref[...] = grad_middle.astype(bf16)
    part = width // 2
    low_own[...] = low_ref[:, pl.ds(pl.multiple_of(core * part, part), part)]
    low_oth[...] = low_ref[:, pl.ds(pl.multiple_of((1 - core) * part, part), part)]
    for copy in copies4:
        copy.wait()

    def out_columns(i, _):
        at = pl.ds(pl.multiple_of(i * tile, tile), tile)
        total = middle_ref[:, at]
        for rel in range(2):
            total = total + dot(hid_ref[:, rel * half : (rel + 1) * half], w4[pl.ds(starts[rel], half), at])
        out_ref[:, at] = total.astype(bf16)
        return 0

    lax.fori_loop(0, width // tile, out_columns, 0)


def attention_back_kernel(pieces1, pieces2, tile, *refs):
    n1, n2 = len(pieces1.arrays), len(pieces2.arrays)
    (me_ref, low_ref, q_ref, k_ref, lse_ref, shared_ref, vpre_ref, values_ref, gpre_ref, att_ref, segc_ref, segr_ref,
     validr_ref, qg_ref, kg_ref) = refs[:15]
    w1_refs, w2_refs = refs[15 : 15 + n1], refs[15 + n1 : 15 + n1 + n2]
    (gmix_ref, gnorm_ref, gv_own, gv_oth, gr_own, gr_oth, dgain_ref,
     w1, w2, probs_ref, low_probs_ref, gprobs_ref, ggp_ref, gvp_ref, gsh_ref, sem1, sem2) = refs[15 + n1 + n2 :]
    me, core = me_ref[0], me_ref[1]
    rows, width = low_ref.shape
    values_width = values_ref.shape[1]
    copies1 = pieces1.copies(w1_refs, w1, me, sem1)
    copies2 = pieces2.copies(w2_refs, w2, me, sem2)
    for copy in copies2 + copies1:
        copy.start()
    queries, keys = q_ref[...], k_ref[...]
    factor = queries.shape[1] ** -0.5
    scores = mul_t(queries, keys) * factor
    masked = jnp.where(allowed_pairs(segc_ref, segr_ref, validr_ref), scores, -1e30)
    probs = jnp.exp(masked - lse_ref[...])
    probs_ref[...] = probs
    low_probs_ref[...] = probs.astype(bf16)
    gprobs_ref[...] = jnp.zeros((rows, rows), f32)
    for copy in copies2:
        copy.wait()

    def columns(i, _):
        at = pl.ds(pl.multiple_of(i * tile, tile), tile)
        grad = mul_t(low_ref[...], w2[at, :]).astype(bf16).astype(f32)
        gate_pre = gpre_ref[:, at].astype(f32)
        sigma = jax.nn.sigmoid(gate_pre)
        grad_att = (grad * (gate_pre * sigma)).astype(bf16)
        slope = sigma * (1.0 + gate_pre * (1.0 - sigma))
        ggp_ref[:, at] = (grad * att_ref[:, at].astype(f32) * slope).astype(bf16)
        gprobs_ref[...] += mul_t(grad_att, values_ref[:, at])
        grad_values = t_mul(low_probs_ref[...], grad_att)
        gvp_ref[:, at] = (grad_values * silu_grad(vpre_ref[:, at].astype(f32))).astype(bf16)
        return 0

    lax.fori_loop(0, values_width // tile, columns, 0)
    probs, grad_probs = probs_ref[...], gprobs_ref[...]
    grad_scores = (probs * (grad_probs - jnp.sum(probs * grad_probs, axis=1, keepdims=True))).astype(bf16)
    grad_queries = dot(grad_scores, keys) * factor
    grad_keys = t_mul(grad_scores, queries) * factor
    shared = shared_ref[...]
    dgain_ref[0:1, :] = jnp.sum(grad_queries * shared, axis=0, keepdims=True)
    dgain_ref[1:2, :] = jnp.sum(grad_queries, axis=0, keepdims=True)
    dgain_ref[2:3, :] = jnp.sum(grad_keys * shared, axis=0, keepdims=True)
    gsh_ref[...] = (grad_queries * qg_ref[...] + grad_keys * kg_ref[...]).astype(bf16)
    for source, own, other, start in (
        (gvp_ref, gv_own, gv_oth, 0), (ggp_ref, gr_own, gr_oth, 0), (gsh_ref, gr_own, gr_oth, values_width // 2)
    ):
        part = source.shape[1] // 2
        own[:, start : start + part] = source[:, pl.ds(pl.multiple_of(core * part, part), part)]
        other[:, start : start + part] = source[:, pl.ds(pl.multiple_of((1 - core) * part, part), part)]
    for copy in copies1:
        copy.wait()

    def in_columns(i, _):
        at = pl.ds(pl.multiple_of(i * tile, tile), tile)
        gmix_ref[:, at] = (
            mul_t(gsh_ref[...], w1[at, 2 * values_width :])
            + mul_t(ggp_ref[...], w1[at, values_width : 2 * values_width])
        ).astype(bf16)
        gnorm_ref[:, at] = mul_t(gvp_ref[...], w1[at, :values_width]).astype(bf16)
        return 0

    lax.fori_loop(0, width // tile, in_columns, 0)


def weight_grad_kernel(halves, offset, order, blocks, me_ref, own, other, mine, theirs, *outs):
    chip, core = lax.shift_right_logical(me_ref[0], 1), me_ref[1]
    keep, send = outs if order is not None else (outs[0], None)
    block = keep.shape[1]
    half = own.shape[1] // halves
    span = mine.shape[1]
    if order is None:
        tile = math.gcd(half, 512)
    else:
        tile = math.lcm(block, LANES)
        while tile < 256 and half % (2 * tile) == 0:
            tile *= 2
    step = span if span <= 640 else math.gcd(span, 640) if math.gcd(span, 640) >= 256 else math.gcd(span, 512)
    if step < 256:
        step = 384 if span % 384 == 0 else step
    for rel in range(halves):
        base = (core ^ rel) * half if halves == 2 else 0

        def strip(i, _, base=base, rel=rel):
            left = own[:, pl.ds(pl.multiple_of(rel * half + i * tile, tile), tile)]
            far = rel if halves == 1 else 1 - rel
            right = other[:, pl.ds(pl.multiple_of(far * half + i * tile, tile), tile)]
            for c in range(0, span, step):
                cols = slice(c, c + step)
                out = t_mul(left, mine[:, cols]) + t_mul(right, theirs[:, offset + c : offset + c + step])
                out = out.astype(keep.dtype)
                if order is None:
                    keep[0, pl.ds(pl.multiple_of(base + i * tile, tile), tile), cols] = out
                    continue
                for s in range(tile // block):
                    rel_chip = (lax.div(base + i * tile, block) + s) ^ chip
                    slot = 0
                    for p, bit in enumerate(order):
                        up = len(order) - 1 - p
                        slot = slot | ((lax.shift_right_logical(rel_chip, bit - 1) & 1) << up)
                    piece = out[s * block : (s + 1) * block, :]
                    lower = slot < blocks // 2
                    index = slot & (blocks // 2 - 1)

                    @pl.when(lower)
                    def _():
                        keep[index, :, cols] = piece

                    @pl.when(jnp.logical_not(lower))
                    def _():
                        send[index, :, cols] = piece

            return 0

        lax.fori_loop(0, half // tile, strip, 0)


def weight_grad(left, right, order, me, chips, name, halves=1, offset=0, micros=8, after=()):
    total, span = left[0].shape[1], right[0].shape[1]
    if order is None:
        outs = [((1, total, span), bf16)]
    else:
        outs = [((chips // 2, total // chips, span), bf16)] * 2
    body = functools.partial(weight_grad_kernel, halves, offset, order, chips)
    given = kernel_call(body, outs, [me, *left, *right], [SM] + [VM] * 4, name=name, micros=micros, after=after)
    return (given[0], None) if order is None else tuple(given)


def exchange_start(pack, totals, axis):
    index, count = lax.axis_index(axis), lax.axis_size(axis)
    lanes = pack.shape[1]
    rows = pack.shape[0]
    full, totals_shape = pack, totals.shape
    totals = totals.reshape(-1, lanes)
    before, bit = jnp.zeros_like(totals), 1
    while bit < count:
        other = swap(jnp.concatenate([totals, full], axis=0), axis, bit)
        upper = (index & bit) != 0
        far_totals, far = other[: totals.shape[0]], other[totals.shape[0] :]
        before = before + jnp.where(upper, far_totals, 0.0)
        totals = totals + far_totals
        full = jnp.concatenate([jnp.where(upper, far, full), jnp.where(upper, full, far)], axis=0)
        bit *= 2
    return full.reshape(count, rows, lanes), before.reshape(totals_shape)


def exchange_end(pack, totals, axis):
    index, count = lax.axis_index(axis), lax.axis_size(axis)
    lanes = pack.shape[2]
    totals_shape = totals.shape
    totals = totals.reshape(-1, lanes)
    rows = totals.shape[0]
    after, bit = jnp.zeros_like(totals), 1
    while bit < count:
        upper = (index & bit) != 0
        pairs = pack.reshape((pack.shape[0] // 2, 2) + pack.shape[1:])
        goes = jnp.where(upper, pairs[:, 0], pairs[:, 1])
        stays = jnp.where(upper, pairs[:, 1], pairs[:, 0])
        other = swap(jnp.concatenate([totals, goes.reshape(-1, lanes)], axis=0), axis, bit)
        after = after + jnp.where(upper, 0.0, other[:rows])
        totals = totals + other[:rows]
        pack = stays + other[rows:].reshape(stays.shape)
        bit *= 2
    return pack[0], after.reshape(totals_shape)


def sum_over(value, axis):
    bit = 1
    while bit < lax.axis_size(axis):
        value = value + swap(value, axis, bit)
        bit *= 2
    return value


def on_device(tokens, cotangent, segment_ids, pad_mask, w_z, w_v, w_r, w_h, w_gate, w_up, w_down, q_gain, q_bias,
              k_gain, ffn_gain, norm_gain, ema_rate, ema_angle, ema_input, ema_output, ema_skip):
    rows, width = tokens.shape[1:]
    seq_count, dp_count = lax.axis_size("seq"), lax.axis_size("dp")
    seq_index, dp_index = lax.axis_index("seq"), lax.axis_index("dp")
    devices = seq_count * dp_count
    chips = devices // 2
    core = dp_index & 1
    fits = all(value.shape[0] % 16 == 0 for value in (w_z, w_h, w_down))
    dp_bits, all_bits = bits_of(dp_count), bits_of(devices)
    inner = list(range(1, dp_bits))
    first_seq, rest_seq = [dp_bits], list(range(all_bits - 1, dp_bits, -1))
    if fits:
        gather_a = rest_seq + first_seq + inner + [0]
        gather_b = rest_seq + inner + first_seq + [0]
        gather_c = inner + first_seq + rest_seq + [0]
        reduce_a, reduce_b = gather_a[-2::-1], gather_b[-2::-1]
        me = jnp.stack([seq_index * dp_count + dp_index, core]).astype(jnp.int32)
    else:
        gather_a = gather_b = gather_c = reduce_a = reduce_b = None
        me = jnp.stack([core * 0, core]).astype(jnp.int32)
    values_width, hidden_width = w_v.shape[1], w_gate.shape[1]
    z_width = w_z.shape[1]
    get_v = Gather(w_v.astype(bf16), gather_a)
    get_r = Gather(jnp.concatenate([w_r, w_z], axis=1).astype(bf16), gather_b)
    get_down = Gather(w_down.astype(bf16), gather_c)
    get_h = Gather(w_h.astype(bf16), gather_a)
    get_gate = Gather(w_gate.astype(bf16), gather_a)
    get_up = Gather(w_up.astype(bf16), gather_b)
    first_v, first_r, first_down = get_v.step(), get_r.step(), get_down.step()
    first_h = get_h.step(first_v)

    row_segs = lax.dynamic_slice_in_dim(segment_ids[0], seq_index * rows, rows)
    row_valid = lax.dynamic_slice_in_dim(pad_mask[0], seq_index * rows, rows).astype(f32)
    valid_col, seg_col, seg_row, valid_row = row_valid[:, None], row_segs[:, None], row_segs[None], row_valid[None]
    prefix, totals = kernel_call(
        stats_kernel, [((rows, LANES), f32), ((DOCS, LANES), f32)], [tokens[0], valid_col, seg_col, seg_row],
        name="stats", micros=5,
    )

    ndim, lanes = ema_rate.shape[1], norm_gain.shape[0]
    gains = jnp.concatenate([q_gain, q_bias, k_gain, ffn_gain])[None].astype(bf16).astype(f32)
    gains = gather_small(gains, "dp").reshape(-1)
    size = gains.shape[0]
    extra = -(-size // lanes)
    gains = jnp.pad(gains, (0, extra * lanes - size)).reshape(extra, lanes)
    pack = jnp.concatenate(
        [ema_rate.T, ema_angle.T, ema_input.T, ema_output.T, norm_gain[None], ema_skip[None], gains], axis=0
    )
    full, before = exchange_start(pack, totals, "seq")
    carry = lax.dynamic_slice_in_dim(before, row_segs[0], 1)
    gains = full[:, 4 * ndim + 2 :].reshape(seq_count, -1)[:, :size].reshape(devices, -1)
    zs, fs = q_gain.shape[0], ffn_gain.shape[0]
    full_qg = gains[:, :zs].reshape(1, -1)
    full_qb = gains[:, zs : 2 * zs].reshape(1, -1)
    full_kg = gains[:, 2 * zs : 3 * zs].reshape(1, -1)
    full_fg = gains[:, 3 * zs :].reshape(1, -1)
    par = ema_params(full[:, : 4 * ndim + 2], ndim, rows)
    flat = lambda value: value.reshape(-1, LANES)
    a_flat, b_flat, g_flat = flat(par["a"]), flat(par["b"]), flat(par["output_w"] * par["coeff"])
    gain_row = par["gain"].reshape(1, width)
    sent_norm, xs, ends = kernel_call(
        norm_kernel,
        [((rows, width), bf16), ((rows * SUB, LANES), f32), ((2 * ndim * SUB, LANES), f32)],
        [tokens[0], valid_col, seg_col, prefix, carry, gain_row, a_flat, b_flat],
        name="norm", micros=13, after=first_v + first_r + first_down,
    )
    seq_steps = len(rest_seq)
    for _ in range(seq_steps - 1):
        deep_v, deep_r = get_v.step(), get_r.step()
    first_gate, first_up = get_gate.step(deep_v), get_up.step(deep_r)
    middle_v, middle_r, second_down = get_v.step(), get_r.step(), get_down.step()
    start_state = state_before(ends.reshape(2 * ndim, SUB, LANES), par["hop"], "seq", False)
    mixed, sent_mix, kept = kernel_call(
        mix_kernel,
        [((rows * SUB, LANES), f32), ((rows, width), bf16), ((rows // SPAN, 2 * ndim * SUB, LANES), f32)],
        [xs, flat(start_state), a_flat, b_flat, g_flat, par["skip"]],
        scratch=[pltpu.VMEM((2 * ndim * SUB, LANES), f32)],
        name="mix", micros=16, after=middle_v + middle_r + first_h + second_down,
    )
    for getter in (get_v, get_r):
        while getter.order is not None and getter.place < all_bits:
            getter.step()
    for _ in range(seq_steps - 1):
        get_h.step()
        deep_gate, deep_up = get_gate.step(), get_up.step()
    third_h = get_h.step((mixed,))
    third_gate, third_up = get_gate.step((mixed,)), get_up.step((mixed,))
    third_down = get_down.step(deep_gate + deep_up)
    while get_h.order is not None and get_h.place < all_bits:
        get_h.step()
    pieces1 = Columns((get_v.pieces, get_r.pieces), (0, values_width))
    pieces2 = Columns((get_h.pieces,), (0,))

    tile = 256
    w1_shape, w2_shape = (width, 2 * values_width + z_width), (values_width, width)
    w3_shape, w4_shape = (width, 2 * hidden_width), (hidden_width, width)
    dma = pltpu.SemaphoreType.DMA
    wide = ((rows, values_width), bf16)

    def any_of(*groups):
        return [ANY] * sum(len(group.arrays) for group in groups)

    shared, queries, keys, log_total, value_pre, values, gate_pre, attended, gated = kernel_call(
        functools.partial(attention_kernel, pieces1, tile),
        [((rows, z_width), f32), ((rows, z_width), bf16), ((rows, z_width), bf16), ((rows, 1), f32), wide, wide, wide,
         wide, wide],
        [me, sent_norm, sent_mix, seg_col, seg_row, valid_row, full_qg, full_qb, full_kg, *pieces1.arrays],
        [SM] + [VM] * 8 + any_of(pieces1),
        scratch=[pltpu.VMEM(w1_shape, bf16), pltpu.VMEM((rows, rows), bf16), dma],
        name="attention", micros=20, after=third_h + third_gate + third_up,
    )
    for getter in (get_gate, get_up, get_down):
        while getter.order is not None and getter.place < all_bits - 1:
            getter.step()
        getter.step((gated,))
    pieces3 = Columns((get_gate.pieces, get_up.pieces), (0, hidden_width))
    pieces4 = Columns((get_down.pieces,), (0,))
    middle, ffn_in, inverse = kernel_call(
        functools.partial(project_kernel, pieces2, tile),
        [((rows, width), f32), ((rows, width), bf16), ((rows, 1), f32)],
        [me, gated, tokens[0], valid_col, full_fg, *pieces2.arrays],
        [SM] + [VM] * 4 + any_of(pieces2),
        scratch=[pltpu.VMEM(w2_shape, bf16), dma],
        name="project", micros=6,
    )

    def other_core(value):
        return swap_bit(value, 0)

    grad_low = cotangent[0]
    part = width // 2
    cot_own = lax.dynamic_slice_in_dim(grad_low, core * part, part, axis=1)
    cot_oth = other_core(lax.dynamic_slice_in_dim(grad_low, (1 - core) * part, part, axis=1))
    half_hidden = ((rows, hidden_width // 2), bf16)
    hid, gg_own, gu_own, far = kernel_call(
        functools.partial(hidden_kernel, pieces3, pieces4, tile),
        [((rows, hidden_width), bf16), half_hidden, half_hidden, ((rows, hidden_width), bf16)],
        [me, ffn_in, grad_low, *pieces3.arrays, *pieces4.arrays],
        [SM, VM, VM] + any_of(pieces3, pieces4),
        scratch=[pltpu.VMEM(w3_shape, bf16), pltpu.VMEM(w4_shape, bf16), dma, dma],
        name="hidden", micros=20, after=(cot_oth,),
    )
    output, grad_middle, low_own, low_oth, middle_low, dfg = kernel_call(
        functools.partial(ffn_back_kernel, pieces3, pieces4, tile),
        [((rows, width), bf16), ((rows, width), f32), ((rows, part), bf16), ((rows, part), bf16), ((rows, width), bf16),
         ((1, width), f32)],
        [me, hid, gg_own, gu_own, far, middle, inverse, grad_low, full_fg, *pieces3.arrays, *pieces4.arrays],
        [SM] + [VM] * 8 + any_of(pieces3, pieces4),
        scratch=[pltpu.VMEM(w3_shape, bf16), pltpu.VMEM(w4_shape, bf16), pltpu.VMEM((rows, width), f32), dma, dma],
        name="ffn_back", micros=22,
    )
    hid_pair, ffn_pair = (hid, other_core(hid)), (ffn_in, other_core(ffn_in))
    far_other = other_core(far)
    down = Reduce(
        weight_grad(hid_pair, (cot_own, cot_oth), reduce_a, me, chips, "grad_down", halves=2, after=(output,)), reduce_a
    )
    gate = Reduce(
        weight_grad(ffn_pair, (gg_own, far_other), reduce_b, me, chips, "grad_gate", after=(down.keep,)), reduce_b
    )
    up = Reduce(
        weight_grad(ffn_pair, (gu_own, far_other), reduce_a, me, chips, "grad_up", offset=hidden_width // 2,
                    after=(gate.keep,)),
        reduce_a,
    )
    gated_pair, mix_pair, norm_pair = ((value, other_core(value)) for value in (gated, sent_mix, sent_norm))
    half_values = ((rows, values_width // 2), bf16)
    half_mixed = ((rows, (values_width + z_width) // 2), bf16)
    grad_mix_rows, grad_norm_rows, gv_own, gv_oth, gr_own, gr_oth, dgains = kernel_call(
        functools.partial(attention_back_kernel, pieces1, pieces2, tile),
        [((rows, width), bf16)] * 2 + [half_values] * 2 + [half_mixed] * 2 + [((3, z_width), f32)],
        [me, middle_low, queries, keys, log_total, shared, value_pre, values, gate_pre, attended, seg_col, seg_row,
         valid_row, full_qg, full_kg, *pieces1.arrays, *pieces2.arrays],
        [SM] + [VM] * 14 + any_of(pieces1, pieces2),
        scratch=[pltpu.VMEM(w1_shape, bf16), pltpu.VMEM(w2_shape, bf16), pltpu.VMEM((rows, rows), f32),
                 pltpu.VMEM((rows, rows), bf16), pltpu.VMEM((rows, rows), f32), pltpu.VMEM((rows, values_width), bf16),
                 pltpu.VMEM((rows, values_width), bf16), pltpu.VMEM((rows, z_width), bf16), dma, dma],
        name="attention_back", micros=28,
        after=(up.keep, gated_pair[1], mix_pair[1], norm_pair[1]),
    )
    pins = down.step() + gate.step()
    drive, back_ends = kernel_call(
        back_ends_kernel, [((rows * SUB, LANES), f32), ((2 * ndim * SUB, LANES), f32)],
        [grad_mix_rows, mixed, a_flat, b_flat], name="back_ends", micros=12, after=pins,
    )
    heads = Reduce(
        weight_grad(gated_pair, (low_own, other_core(low_oth)), reduce_b, me, chips, "grad_h", after=(back_ends,)), reduce_b
    )
    pins = up.step() + down.step()
    value = Reduce(
        weight_grad(norm_pair, (gv_own, other_core(gv_oth)), reduce_a, me, chips, "grad_v", after=(heads.keep,) + pins),
        reduce_a,
    )
    pins = gate.step()
    reset = Reduce(
        weight_grad(mix_pair, (gr_own, other_core(gr_oth)), reduce_b, me, chips, "grad_r", after=(value.keep,) + pins),
        reduce_b,
    )
    hop_back = (par["hop"][0], -par["hop"][1])
    back_state = flat(state_before(back_ends.reshape(2 * ndim, SUB, LANES), hop_back, "seq", True))
    sums = jnp.zeros(((3 * ndim + 1) * SUB, LANES), f32)
    cuts = 4
    plan = [
        lambda: (reset.keep,) + down.step() + up.step(),
        lambda: down.step() + gate.step(),
        lambda: heads.step() + value.step() + up.step(),
        lambda: gate.step() + up.step(),
    ]
    long = rows * SUB // cuts
    pieces_dx = []
    for cut in range(cuts - 1, -1, -1):
        block = pl.BlockSpec((long, LANES), lambda i, cut=cut: (cut, 0))
        keep_block = pl.BlockSpec((rows // SPAN // cuts, 2 * ndim * SUB, LANES), lambda i, cut=cut: (cut, 0, 0))
        dxs, back_state, sums = kernel_call(
            back_scan_kernel,
            [((long, LANES), f32), ((2 * ndim * SUB, LANES), f32), (((3 * ndim + 1) * SUB, LANES), f32)],
            [xs, drive, kept, back_state, sums, a_flat, b_flat, g_flat, par["skip"]],
            [block, block, keep_block] + [VM] * 6,
            scratch=[pltpu.VMEM((SPAN, 8 * SUB, LANES), f32)],
            name="back", micros=10, after=plan.pop(0)(), grid=(1,), out_specs=[VM] * 3,
        )
        pieces_dx.insert(0, dxs)
    pins = heads.step() + reset.step()
    dn, dgain, suffix, back_totals = kernel_call(
        back_norm_kernel,
        [((rows, width), f32), ((1, width), f32), ((rows, LANES), f32), ((DOCS, LANES), f32)],
        [*pieces_dx, grad_norm_rows, tokens[0], valid_col, seg_col, seg_row, prefix, carry, gain_row],
        name="back_norm", micros=6, after=pins,
    )
    sums = sums.reshape(3 * ndim + 1, SUB, LANES)
    d_params = ema_param_grads(par, sums)
    d_pack = jnp.concatenate(list(d_params) + [dgain.reshape(1, SUB, LANES), sums[3 * ndim :]], axis=0)
    d_pack = jnp.transpose(d_pack.reshape(4 * ndim + 2, seq_count, lanes), (1, 0, 2))
    owned = [dgains[i].reshape(devices, zs) for i in range(3)] + [dfg.reshape(devices, fs)]
    owned = jnp.concatenate(owned, axis=1).reshape(seq_count, -1)
    owned = jnp.pad(owned, ((0, 0), (0, extra * lanes - size))).reshape(seq_count, extra, lanes)
    own_pack, after_totals = exchange_end(jnp.concatenate([d_pack, owned], axis=1), back_totals, "seq")
    back_carry = lax.dynamic_slice_in_dim(after_totals, row_segs[rows - 1], 1)
    (input_grad,) = kernel_call(
        input_kernel, [((rows, width), f32)],
        [dn, suffix, back_carry, tokens[0], valid_col, seg_col, prefix, carry, grad_middle], name="input", micros=6,
        after=value.step(),
    )
    total = sum_over(own_pack, "dp")
    mine = lax.dynamic_index_in_dim(total[4 * ndim + 2 :].reshape(-1)[:size].reshape(dp_count, -1), dp_index, 0, keepdims=False)
    while any(message.left or message.keep.dtype == bf16 for message in (heads, value, reset)) and fits:
        for message in (heads, value, reset):
            if message.left or message.keep.dtype == bf16:
                message.step()
    (shard_down,) = down.finish(core, [part])
    (shard_gate,) = gate.finish(core, [hidden_width // 2])
    (shard_up,) = up.finish(core, [hidden_width // 2])
    (shard_h,) = heads.finish(core, [part])
    (shard_v,) = value.finish(core, [values_width // 2])
    shard_r, shard_z = reset.finish(core, [values_width // 2, z_width // 2])
    return (
        output[None], input_grad[None], shard_z, shard_v, shard_r, shard_h, shard_gate, shard_up, shard_down,
        mine[:zs], mine[zs : 2 * zs], mine[2 * zs : 3 * zs], mine[3 * zs :],
        total[4 * ndim], total[:ndim].T, total[ndim : 2 * ndim].T, total[2 * ndim : 3 * ndim].T,
        total[3 * ndim : 4 * ndim].T, total[4 * ndim + 1],
    )


def solution(mesh):
    by_token, by_group = P("dp", "seq", None), P("dp", None)
    by_row, by_owner = P(("seq", "dp"), None), P(("seq", "dp"))
    params = (by_row,) * 7 + (by_owner,) * 4 + (P("seq"),) + (P("seq", None),) * 4 + (P("seq"),)
    return jax.shard_map(
        on_device,
        mesh=mesh,
        in_specs=(by_token, by_token, by_group, by_group) + params,
        out_specs=(by_token, by_token) + params,
        check_vma=False,
    )
```

```python
import functools
import math

import jax
import jax.numpy as jnp
from jax import lax
from jax.experimental import pallas as pl
from jax.experimental.pallas import tpu as pltpu
from jax.sharding import Mesh, PartitionSpec as P

AXES = ("seq", "chip", "core")
GROUP = 64
DOCS = 16
LANES = 128
SUB = 8
SPAN = 32
BAND = 64
bf16 = jnp.bfloat16
f32 = jnp.float32
VMEM_LIMIT = 60 * 1024 * 1024
PACE = 0.05


def split3(value):
    first = value.astype(bf16)
    rest = value - first.astype(f32)
    second = rest.astype(bf16)
    third = (rest - second.astype(f32)).astype(bf16)
    return first, second, third


def dot(left, right):
    return jnp.dot(left, right, preferred_element_type=f32)


def dot3(left, parts):
    return dot(left, parts[0]) + dot(left, parts[1]) + dot(left, parts[2])


def dot3_left(parts, right):
    return dot(parts[0], right) + dot(parts[1], right) + dot(parts[2], right)


def sigmoid(value):
    return 0.5 * jnp.tanh(0.5 * value) + 0.5


def iota(shape, axis):
    return lax.broadcasted_iota(jnp.int32, shape, axis)


def group_pick(width, shift):
    own = lax.shift_right_logical(iota((width, LANES), 0), GROUP.bit_length() - 1)
    return (own + shift == iota((width, LANES), 1)).astype(bf16)


def group_spread(groups, width):
    own = lax.shift_right_logical(iota((groups, width), 1), GROUP.bit_length() - 1)
    return (own == iota((groups, width), 0)).astype(bf16)


ANY = pl.BlockSpec(memory_space=pl.ANY)
VM = pl.BlockSpec(memory_space=pltpu.VMEM)
SM = pl.BlockSpec(memory_space=pltpu.SMEM)


def kernel_call(body, outs, args, specs=None, scratch=(), name=None, micros=10, after=(), grid=None, out_specs=None):
    specs = [VM] * len(args) if specs is None else specs
    count = len(args)

    def run(*refs):
        body(*refs[:count], *refs[count + len(after) :])

    more = {} if grid is None else dict(grid=grid, out_specs=tuple(out_specs))
    return pl.pallas_call(
        run,
        out_shape=tuple(jax.ShapeDtypeStruct(shape, dtype) for shape, dtype in outs),
        in_specs=list(specs) + [ANY] * len(after),
        scratch_shapes=list(scratch),
        compiler_params=pltpu.CompilerParams(vmem_limit_bytes=VMEM_LIMIT),
        cost_estimate=pl.CostEstimate(
            flops=int(micros * PACE * 1.0e9), bytes_accessed=int(micros * PACE * 3.0e6), transcendentals=0
        ),
        name=name,
        **more,
    )(*args, *after)


def grid_call(body, outs, args, steps, me, scratch=(), name=None, micros=10, after=()):
    def spec(shape, block, index):
        if block is None:
            return ANY
        if index is None:
            return pl.BlockSpec(shape, lambda g, me: (0,) * len(shape))
        return pl.BlockSpec(block, index)

    count = len(args)

    def run(*refs):
        body(*refs[: 1 + count], *refs[1 + count + len(after) :])

    return pl.pallas_call(
        run,
        out_shape=tuple(jax.ShapeDtypeStruct(shape, dtype) for shape, dtype, _, _ in outs),
        grid_spec=pltpu.PrefetchScalarGridSpec(
            num_scalar_prefetch=1,
            grid=(steps,),
            in_specs=[spec(array.shape, block, index) for array, block, index in args] + [ANY] * len(after),
            out_specs=tuple(spec(shape, block, index) for shape, _, block, index in outs),
            scratch_shapes=list(scratch),
        ),
        compiler_params=pltpu.CompilerParams(vmem_limit_bytes=VMEM_LIMIT),
        cost_estimate=pl.CostEstimate(
            flops=int(micros * PACE * 1.0e9), bytes_accessed=int(micros * PACE * 3.0e6), transcendentals=0
        ),
        name=name,
    )(me, *(array for array, _, _ in args), *after)


WHOLE = (1,)


def whole(array):
    return (array, WHOLE, None)


def columns_of(array, width, index=lambda g, me: (0, g)):
    return (array, (array.shape[0], width), index)


def tie(value, *after):
    def nothing(*refs):
        return None

    return pl.pallas_call(
        nothing,
        out_shape=jax.ShapeDtypeStruct(value.shape, value.dtype),
        in_specs=[ANY] * (1 + len(after)),
        out_specs=ANY,
        input_output_aliases={0: 0},
        name="tie",
    )(value, *after)


def zero_after(*after):
    return tie(jnp.zeros((1, 1, 1), bf16), *after)


def split_wide(value):
    return jnp.concatenate(split3(value), axis=1)


def spread_wide(groups, width, start):
    own = lax.shift_right_logical(iota((3 * groups, LANES), 1) + start, GROUP.bit_length() - 1)
    return (own == lax.rem(iota((3 * groups, LANES), 0), groups)).astype(bf16)


def moments(total, groups):
    counts = jnp.maximum(total[:, 2 * groups : 2 * groups + 1], 1.0) * float(GROUP)
    means = total[:, :groups] / counts
    variance = total[:, groups : 2 * groups] / counts - means * means
    return means, lax.rsqrt(variance + 1e-05), counts


def stats_kernel(tok_ref, valid_ref, segc_ref, segr_ref, prefix_ref, totals_ref):
    rows, width = tok_ref.shape
    groups = width // GROUP
    valid = valid_ref[...]
    masked = tok_ref[...].astype(f32) * valid
    low = masked.astype(bf16)
    square = masked * masked
    high = square.astype(bf16)
    rest = (square - high.astype(f32)).astype(bf16)
    second = group_pick(width, groups)
    sums = dot(low, group_pick(width, 0)) + dot(high, second) + dot(rest, second)
    sums = sums + jnp.where(iota((rows, LANES), 1) == 2 * groups, valid, 0.0)
    parts = split3(sums)
    earlier = (iota((rows, rows), 1) <= iota((rows, rows), 0)) & (segc_ref[...] == segr_ref[...])
    prefix_ref[...] = dot3(earlier.astype(f32).astype(bf16), parts)
    member = (iota((DOCS, rows), 0) == segr_ref[...]).astype(f32).astype(bf16)
    totals_ref[...] = dot3(member, parts)


def scan_ends(src_ref, a_ref, b_ref, end_ref, rows, ndim, reverse):
    half = ndim // 2
    for start in range(0, ndim, half):
        a = [a_ref[pl.ds((start + n) * SUB, SUB), :] for n in range(half)]
        b = [b_ref[pl.ds((start + n) * SUB, SUB), :] for n in range(half)]

        def step(i, state, a=a, b=b):
            t = rows - 1 - i if reverse else i
            x = src_ref[pl.ds(pl.multiple_of(t * SUB, SUB), SUB), :]
            fresh = []
            for n in range(half):
                re, im = state[2 * n], state[2 * n + 1]
                if reverse:
                    fresh += [a[n] * re + b[n] * im + x, a[n] * im - b[n] * re]
                else:
                    fresh += [a[n] * re - b[n] * im + x, a[n] * im + b[n] * re]
            return tuple(fresh)

        zero = jnp.zeros((SUB, LANES), f32)
        state = lax.fori_loop(0, rows, step, (zero,) * (2 * half), unroll=8)
        for n in range(half):
            end_ref[pl.ds((start + n) * SUB, SUB), :] = state[2 * n]
            end_ref[pl.ds((ndim + start + n) * SUB, SUB), :] = state[2 * n + 1]


def all_moments(prefix_ref, segc_ref, carry_ref, groups):
    total = prefix_ref[...] + jnp.where(segc_ref[...] == segc_ref[0:1, :], carry_ref[...], 0.0)
    return moments(total, groups)


def lane_rows(j, rows):
    return pl.ds(j, rows, stride=SUB)


def norm_kernel(tok_ref, valid_ref, segc_ref, prefix_ref, carry_ref, gain_ref, a_ref, b_ref,
                sent_ref, xs_ref, end_ref):
    rows, width = tok_ref.shape
    groups = width // GROUP
    ndim = a_ref.shape[0] // SUB
    means, scale, _ = all_moments(prefix_ref, segc_ref, carry_ref, groups)
    means, scale, valid = split_wide(means), split_wide(scale), valid_ref[...]
    for j in range(SUB):
        at = slice(j * LANES, (j + 1) * LANES)
        spread = spread_wide(groups, width, j * LANES)
        normed = (tok_ref[:, at].astype(f32) * valid - dot(means, spread)) * dot(scale, spread) * gain_ref[:, at]
        sent_ref[:, at] = normed.astype(bf16)
        xs_ref[lane_rows(j, rows), :] = normed
    scan_ends(xs_ref, a_ref, b_ref, end_ref, rows, ndim, False)


def mix_kernel(xs_ref, start_ref, a_ref, b_ref, g_ref, skip_ref, mixed_ref, sent_ref, keep_ref, state_ref):
    rows = xs_ref.shape[0] // SUB
    ndim = a_ref.shape[0] // SUB
    half = ndim // 2
    state_ref[...] = start_ref[...]

    def chunk(i, _):
        keep_ref[i] = state_ref[...]
        for start in range(0, ndim, half):
            re_at = [pl.ds((start + n) * SUB, SUB) for n in range(half)]
            im_at = [pl.ds((ndim + start + n) * SUB, SUB) for n in range(half)]
            a = [a_ref[at, :] for at in re_at]
            b = [b_ref[at, :] for at in re_at]
            g = [g_ref[at, :] for at in re_at]

            def step(k, state, start=start, a=a, b=b, g=g):
                at = pl.ds(pl.multiple_of((i * SPAN + k) * SUB, SUB), SUB)
                x = xs_ref[at, :]
                fresh, terms = [], []
                for n in range(half):
                    re, im = state[2 * n], state[2 * n + 1]
                    now = a[n] * re - b[n] * im + x
                    fresh += [now, a[n] * im + b[n] * re]
                    terms.append(g[n] * now)
                terms.append(skip_ref[...] * x if start == 0 else mixed_ref[at, :])
                while len(terms) > 1:
                    terms = [sum(terms[p : p + 2][1:], terms[p]) for p in range(0, len(terms), 2)]
                mixed_ref[at, :] = terms[0]
                return tuple(fresh)

            state = []
            for n in range(half):
                state += [state_ref[re_at[n], :], state_ref[im_at[n], :]]
            state = lax.fori_loop(0, SPAN, step, tuple(state), unroll=8)
            for n in range(half):
                state_ref[re_at[n], :] = state[2 * n]
                state_ref[im_at[n], :] = state[2 * n + 1]
        return 0

    lax.fori_loop(0, rows // SPAN, chunk, 0)

    def band(i, _):
        at = pl.ds(pl.multiple_of(i * BAND, BAND), BAND)
        for j in range(SUB):
            mixed = mixed_ref[pl.ds(i * (BAND * SUB) + j, BAND, stride=SUB), :]
            sent_ref[at, j * LANES : (j + 1) * LANES] = (mixed * sigmoid(mixed)).astype(bf16)
        return 0

    lax.fori_loop(0, rows // BAND, band, 0)


def back_ends_kernel(grad_ref, mixed_ref, a_ref, b_ref, drive_ref, end_ref):
    rows = grad_ref.shape[0]
    ndim = a_ref.shape[0] // SUB

    def band(i, _):
        at = pl.ds(pl.multiple_of(i * BAND, BAND), BAND)
        for j in range(SUB):
            where = pl.ds(i * (BAND * SUB) + j, BAND, stride=SUB)
            mixed = mixed_ref[where, :]
            sigma = sigmoid(mixed)
            slope = sigma * (1.0 + mixed * (1.0 - sigma))
            drive_ref[where, :] = grad_ref[at, j * LANES : (j + 1) * LANES].astype(f32) * slope
        return 0

    lax.fori_loop(0, rows // BAND, band, 0)
    scan_ends(drive_ref, a_ref, b_ref, end_ref, rows, ndim, True)


def back_scan_kernel(xs_ref, drive_ref, keep_ref, start_ref, sums_in_ref, a_ref, b_ref, g_ref, skip_ref,
                     dxs_ref, state_ref, sums_ref, hist_ref):
    ndim = a_ref.shape[0] // SUB
    rows = xs_ref.shape[0] // SUB
    part = 4
    count = rows // SPAN
    state_ref[...] = start_ref[...]
    sums_ref[...] = sums_in_ref[...]

    def chunk(c, _):
        i = count - 1 - c
        for start in range(0, ndim, part):
            re_at = [pl.ds((start + n) * SUB, SUB) for n in range(part)]
            im_at = [pl.ds((ndim + start + n) * SUB, SUB) for n in range(part)]
            last_at = [pl.ds((2 * ndim + start + n) * SUB, SUB) for n in range(part)]
            a = [a_ref[at, :] for at in re_at]
            b = [b_ref[at, :] for at in re_at]
            g = [g_ref[at, :] for at in re_at]

            def forward(k, state, a=a, b=b):
                x = xs_ref[pl.ds(pl.multiple_of((i * SPAN + k) * SUB, SUB), SUB), :]
                fresh = []
                for n in range(part):
                    re, im = state[2 * n], state[2 * n + 1]
                    hist_ref[k, pl.ds(2 * n * SUB, SUB), :] = re
                    hist_ref[k, pl.ds((2 * n + 1) * SUB, SUB), :] = im
                    fresh += [a[n] * re - b[n] * im + x, a[n] * im + b[n] * re]
                return tuple(fresh)

            state = []
            for n in range(part):
                state += [keep_ref[i, re_at[n], :], keep_ref[i, im_at[n], :]]
            lax.fori_loop(0, SPAN, forward, tuple(state), unroll=8)

            def backward(k, held, start=start, a=a, b=b, g=g):
                t = SPAN - 1 - k
                at = pl.ds(pl.multiple_of((i * SPAN + t) * SUB, SUB), SUB)
                x, drive = xs_ref[at, :], drive_ref[at, :]
                fresh, terms = [], []
                for n in range(part):
                    re, im, m_re, m_im, same = held[5 * n : 5 * n + 5]
                    now_re = a[n] * re + b[n] * im + drive
                    now_im = a[n] * im - b[n] * re
                    old_re = hist_ref[t, pl.ds(2 * n * SUB, SUB), :]
                    old_im = hist_ref[t, pl.ds((2 * n + 1) * SUB, SUB), :]
                    fresh += [
                        now_re,
                        now_im,
                        m_re + (now_re * old_re + now_im * old_im),
                        m_im + (now_im * old_re - now_re * old_im),
                        same + x * now_re,
                    ]
                    terms.append(g[n] * now_re)
                total = (terms[0] + terms[1]) + (terms[2] + terms[3])
                if start == 0:
                    dxs_ref[at, :] = total + skip_ref[...] * drive
                else:
                    dxs_ref[at, :] = total + dxs_ref[at, :]
                return tuple(fresh)

            held = []
            for n in range(part):
                held += [state_ref[re_at[n], :], state_ref[im_at[n], :]]
                held += [sums_ref[re_at[n], :], sums_ref[im_at[n], :], sums_ref[last_at[n], :]]
            held = lax.fori_loop(0, SPAN, backward, tuple(held), unroll=8)
            for n in range(part):
                state_ref[re_at[n], :] = held[5 * n]
                state_ref[im_at[n], :] = held[5 * n + 1]
                sums_ref[re_at[n], :] = held[5 * n + 2]
                sums_ref[im_at[n], :] = held[5 * n + 3]
                sums_ref[last_at[n], :] = held[5 * n + 4]
        return 0

    lax.fori_loop(0, count, chunk, 0)

    def skip_step(k, total):
        at = pl.ds(pl.multiple_of(k * SUB, SUB), SUB)
        return total + xs_ref[at, :] * drive_ref[at, :]

    last = pl.ds(3 * ndim * SUB, SUB)
    sums_ref[last, :] = lax.fori_loop(0, rows, skip_step, sums_ref[last, :], unroll=8)


def back_norm_kernel(*refs):
    dxs_refs, refs = refs[:-12], refs[-12:]
    (grad_ref, tok_ref, valid_ref, segc_ref, segr_ref, prefix_ref, carry_ref, gain_ref,
     dn_ref, dgain_ref, suffix_ref, totals_ref) = refs
    rows, width = tok_ref.shape
    groups = width // GROUP
    means, scale, counts = all_moments(prefix_ref, segc_ref, carry_ref, groups)
    wide_means, wide_scale, valid = split_wide(means), split_wide(scale), valid_ref[...]
    plain, leaning = jnp.zeros((rows, LANES), f32), jnp.zeros((rows, LANES), f32)
    for j in range(SUB):
        at = slice(j * LANES, (j + 1) * LANES)
        spread = spread_wide(groups, width, j * LANES)
        own = lax.shift_right_logical(iota((LANES, LANES), 0) + j * LANES, GROUP.bit_length() - 1)
        pick = (own == iota((LANES, LANES), 1)).astype(bf16)
        centred = tok_ref[:, at].astype(f32) * valid - dot(wide_means, spread)
        ema = [ref[lane_rows(j, ref.shape[0] // SUB), :] for ref in dxs_refs]
        dn = grad_ref[:, at].astype(f32) + jnp.concatenate(ema, axis=0)
        dgain_ref[:, at] = jnp.sum(dn * centred * dot(wide_scale, spread), axis=0, keepdims=True)
        dn = dn * gain_ref[:, at]
        dn_ref[:, at] = dn
        plain = plain + dot3_left(split3(dn), pick)
        leaning = leaning + dot3_left(split3(dn * centred), pick)
    plain, leaning = plain[:, :groups], leaning[:, :groups]
    d_variance = -0.5 * leaning * scale * scale * scale
    d_second = d_variance / counts
    d_first = (-scale * plain - 2.0 * means * d_variance) / counts
    flow = jnp.concatenate([d_first, d_second, jnp.zeros((rows, LANES - 2 * groups), f32)], axis=1)
    parts = split3(flow)
    later = (iota((rows, rows), 1) >= iota((rows, rows), 0)) & (segc_ref[...] == segr_ref[...])
    suffix_ref[...] = dot3(later.astype(f32).astype(bf16), parts)
    member = (iota((DOCS, rows), 0) == segr_ref[...]).astype(f32).astype(bf16)
    totals_ref[...] = dot3(member, parts)


def input_kernel(dn_ref, suffix_ref, back_ref, tok_ref, valid_ref, segc_ref, prefix_ref, carry_ref, middle_ref, out_ref):
    rows, width = tok_ref.shape
    groups = width // GROUP
    _, scale, _ = all_moments(prefix_ref, segc_ref, carry_ref, groups)
    flow = suffix_ref[...] + jnp.where(segc_ref[...] == segc_ref[rows - 1 : rows, :], back_ref[...], 0.0)
    scale, valid = split_wide(scale), valid_ref[...]
    first, second = split_wide(flow[:, :groups]), split_wide(flow[:, groups : 2 * groups])
    for j in range(SUB):
        at = slice(j * LANES, (j + 1) * LANES)
        spread = spread_wide(groups, width, j * LANES)
        masked = tok_ref[:, at].astype(f32) * valid
        grad = dn_ref[:, at] * dot(scale, spread) + dot(first, spread) + 2.0 * masked * dot(second, spread)
        out_ref[:, at] = valid * (middle_ref[:, at] + grad)


def swap(value, axis, bit):
    count = lax.axis_size(axis)
    return lax.ppermute(value, axis, [(i, i ^ bit) for i in range(count)])


def gather_small(value, axis):
    index, count = lax.axis_index(axis), lax.axis_size(axis)
    value, bit = value[None], 1
    while bit < count:
        other = swap(value, axis, bit)
        upper = (index & bit) != 0
        value = jnp.concatenate([jnp.where(upper, other, value), jnp.where(upper, value, other)], axis=0)
        bit *= 2
    return value


def cmul(left, right):
    return (left[0] * right[0] - left[1] * right[1], left[0] * right[1] + left[1] * right[0])


def state_before(ends, hop, axis, reverse, hold=None):
    index, count = lax.axis_index(axis), lax.axis_size(axis)
    if reverse:
        index = count - 1 - index
    half = ends.shape[0] // 2
    before = (jnp.zeros_like(ends[:half]), jnp.zeros_like(ends[:half]))
    reach = (jnp.ones_like(hop[0]), jnp.zeros_like(hop[1]))
    bit = 1
    while bit < count:
        waits = hold[bit]() if hold and bit in hold else ()
        other = swap(tie(ends, *waits) if waits else ends, axis, bit)
        upper = (index & bit) != 0
        far, own = (other[:half], other[half:]), (ends[:half], ends[half:])
        moved = cmul(reach, far)
        before = tuple(v + jnp.where(upper, w, 0.0) for v, w in zip(before, moved))
        if bit * 2 < count:
            lower = tuple(jnp.where(upper, v, w) for v, w in zip(far, own))
            higher = tuple(jnp.where(upper, w, v) for v, w in zip(far, own))
            carried = cmul(hop, lower)
            ends = jnp.concatenate([carried[0] + higher[0], carried[1] + higher[1]], axis=0)
            longer = cmul(reach, hop)
            reach = tuple(jnp.where(upper, v, w) for v, w in zip(longer, reach))
            hop = cmul(hop, hop)
        bit *= 2
    return jnp.concatenate(before, axis=0)


def ema_params(full, ndim, rows):
    full = jnp.transpose(full, (1, 0, 2))
    full = full.reshape(full.shape[0], SUB, -1)
    rate, angle, input_w, output_w = (full[i * ndim : (i + 1) * ndim] for i in range(4))
    gain, skip = full[4 * ndim], full[4 * ndim + 1]
    base = jnp.sqrt(rate * (2.0 - rate))
    cos, sin = jnp.cos(angle), jnp.sin(angle)
    a, b = (1.0 - rate) * cos, (1.0 - rate) * sin
    hop, steps = (a, b), 1
    while steps < rows:
        hop, steps = cmul(hop, hop), steps * 2
    return dict(rate=rate, input_w=input_w, output_w=output_w, gain=gain, skip=skip, base=base,
                cos=cos, sin=sin, a=a, b=b, coeff=base * input_w, hop=hop)


def ema_param_grads(par, sums):
    ndim = par["rate"].shape[0]
    m_re, m_im, same = sums[:ndim], sums[ndim : 2 * ndim], sums[2 * ndim : 3 * ndim]
    weight = par["output_w"] * par["coeff"]
    d_a, d_b = weight * m_re, weight * m_im
    d_coeff = par["output_w"] * same
    d_output = par["coeff"] * same
    d_input = par["base"] * d_coeff
    d_rate = d_coeff * par["input_w"] * (1.0 - par["rate"]) / par["base"] - par["cos"] * d_a - par["sin"] * d_b
    d_angle = par["a"] * d_b - par["b"] * d_a
    return d_rate, d_angle, d_input, d_output


def mul_t(left, right):
    return lax.dot_general(left, right, (((1,), (1,)), ((), ())), preferred_element_type=f32)


def t_mul(left, right):
    return lax.dot_general(left, right, (((0,), (0,)), ((), ())), preferred_element_type=f32)


def silu_grad(value):
    sigma = sigmoid(value)
    return sigma * (1.0 + value * (1.0 - sigma))


def bits_of(count):
    return count.bit_length() - 1


class Part:
    def __init__(self, source, take, width, rows, lower=0, column=0):
        self.arrays, self.owners, self.top = source.arrays, source.owners, source.top
        self.take, self.width, self.rows, self.lower, self.column = take, width, rows, lower, column

    def copies(self, refs, where, me, sem, span=None, near=None):
        made = []
        first, width = (0, self.width) if span is None else span
        for ref, owners in zip(refs, self.owners):
            block = ref.shape[1]
            for slot, owner in enumerate(owners):
                if near is not None and near != (owner < (1 << self.top)):
                    continue
                start = (me ^ owner) * self.rows + self.lower
                start = pl.multiple_of(start, math.gcd(self.rows, block)) if len(owners) > 1 else 0
                source = ref.at[slot, :, pl.ds(self.take + first, width)]
                to = where.at[pl.ds(start, block), pl.ds(self.column + first, width)]
                made.append(pltpu.make_async_copy(source, to, sem))
        return made


class Weight:
    def __init__(self, *parts):
        self.parts, self.arrays, self.places = parts, [], []
        self.split, self.top = len(parts[0].owners[0]) > 1, parts[0].top
        self.nears = (True, False) if self.split else (None,)
        for part in parts:
            place = []
            for array in part.arrays:
                same = [n for n, known in enumerate(self.arrays) if known is array]
                if not same:
                    self.arrays.append(array)
                place.append(same[0] if same else len(self.arrays) - 1)
            self.places.append(place)

    def copies(self, refs, where, me, sem, which=None, span=None, near=None):
        made = []
        for n, (part, place) in enumerate(zip(self.parts, self.places)):
            if which is None or which == n:
                made += part.copies([refs[n] for n in place], where, me, sem, span, near)
        return made


class Gather:
    def __init__(self, shard, order):
        self.order = order
        self.top = max(order or (0,))
        if order is None:
            full = lax.all_gather(shard, AXES, axis=0, tiled=True)
            self.arrays, self.owners = [full[None]], [[0]]
            return
        self.arrays, self.owners, self.place = [shard[None]], [[0]], 0

    def step(self, after=()):
        if self.order is None:
            return ()
        bit = self.order[self.place]
        mine = [tie(value, *after) for value in self.arrays] if after else self.arrays
        others = [swap_bit(value, bit) for value in mine]
        moved = [[owner ^ (1 << bit) for owner in row] for row in self.owners]
        if self.place < len(self.order) - 2:
            self.arrays = [jnp.concatenate([mine[0], others[0]], axis=0)]
            self.owners = [self.owners[0] + moved[0]]
        else:
            self.arrays, self.owners = mine + others, self.owners + moved
        self.place += 1
        return (self.arrays[-1],)

def swap_bit(value, bit):
    dp_bits = bits_of(lax.axis_size("chip")) + 1
    if bit == 0:
        return swap(value, "core", 1)
    if bit < dp_bits:
        return swap(value, "chip", 1 << (bit - 1))
    return swap(value, "seq", 1 << (bit - dp_bits))


def add_low(left, right, zero):
    return left + right + zero


class Reduce:
    def __init__(self, keep, send, order):
        self.keep, self.send, self.order, self.sent = keep, send, order, keep
        self.pins = () if order is None else (send,)
        self.left = list(order or ())
        self.other = None
        if order is None:
            self.keep = lax.psum_scatter(keep[0], ("seq", "chip"), scatter_dimension=0, tiled=True)[None]
        else:
            self.begin()

    def begin(self):
        self.other = swap_bit(self.send, self.left.pop(0)) if self.left else None

    def halves(self, after=()):
        half = self.keep.shape[0] // 2
        zero = zero_after(*after) if after else jnp.zeros((1, 1, 1), bf16)
        return add_low(self.keep[:half], self.other[:half], zero), add_low(self.keep[half:], self.other[half:], zero)

    def step(self, *after):
        if self.other is None:
            return ()
        if not self.left:
            zero = zero_after(*after) if after else 0.0
            self.keep = self.keep.astype(f32) + self.other.astype(f32) + zero
            self.other = None
            return (self.keep,)
        self.keep, self.send = self.halves(after)
        self.begin()
        return (self.send,)

    def finish(self, core, widths, *after):
        while self.other is not None:
            self.step(*after)
        chip_rows = self.keep[0].astype(f32)
        rows = chip_rows.shape[0] // 2
        lower, upper = chip_rows[:rows], chip_rows[rows:]
        own = jnp.where(core == 0, lower, upper)
        other = swap_bit(jnp.where(core == 0, upper, lower).astype(bf16), 0).astype(f32)
        outs, at = [], 0
        for width in widths:
            mine, theirs = own[:, at : at + width], other[:, at : at + width]
            outs.append(
                jnp.concatenate([jnp.where(core == 0, mine, theirs), jnp.where(core == 0, theirs, mine)], axis=1)
            )
            at += width
        return outs


def merge(first, second, *after):
    if first.order is None:
        both = Reduce.__new__(Reduce)
        both.keep = jnp.concatenate([first.keep, second.keep], axis=2)
        both.order, both.left, both.other, both.pins = None, [], None, ()
        return both
    parts = [first.halves(after), second.halves(after)]
    keep = jnp.concatenate([part[0] for part in parts], axis=2)
    send = jnp.concatenate([part[1] for part in parts], axis=2)
    return Reduce(keep, send, first.left)


def allowed_pairs(segc_ref, segr_ref, validr_ref):
    rows = segc_ref.shape[0]
    query, key = iota((rows, rows), 0), iota((rows, rows), 1)
    same = segc_ref[...] == segr_ref[...]
    usable = validr_ref[...] > 0.5
    return (key <= query) & same & (usable | (key == query))


def attention_kernel(weight1, tile, *refs):
    n1 = len(weight1.arrays)
    me_ref, norm_ref, mix_ref, segc_ref, segr_ref, validr_ref, qg_ref, qb_ref, kg_ref = refs[:9]
    w1_refs = refs[9 : 9 + n1]
    shared_ref, q_ref, k_ref, lse_ref, vpre_ref, values_ref, gpre_ref, att_ref, gated_ref, w1, probs_ref, sem1 = refs[9 + n1 :]
    me = me_ref[0]
    values_width = values_ref.shape[1]
    copies1 = weight1.copies(w1_refs, w1, me, sem1)
    for copy in copies1:
        copy.start()
    for copy in copies1:
        copy.wait()
    shared = dot(mix_ref[...], w1[:, 2 * values_width :])
    shared_ref[...] = shared
    queries = (shared * qg_ref[...] + qb_ref[...]).astype(bf16)
    keys = (shared * kg_ref[...]).astype(bf16)
    q_ref[...] = queries
    k_ref[...] = keys
    scores = mul_t(queries, keys) * (queries.shape[1] ** -0.5)
    masked = jnp.where(allowed_pairs(segc_ref, segr_ref, validr_ref), scores, -1e30)
    top = jnp.max(masked, axis=1, keepdims=True)
    weights = jnp.exp(masked - top)
    total = jnp.sum(weights, axis=1, keepdims=True)
    probs_ref[...] = (weights / total).astype(bf16)
    lse_ref[...] = top + jnp.log(total)

    def columns(i, _):
        at = pl.ds(pl.multiple_of(i * tile, tile), tile)
        value_pre = dot(norm_ref[...], w1[:, at])
        vpre_ref[:, at] = value_pre.astype(bf16)
        values = (value_pre * sigmoid(value_pre)).astype(bf16)
        values_ref[:, at] = values
        gate_pre = dot(mix_ref[...], w1[:, pl.ds(pl.multiple_of(values_width + i * tile, tile), tile)])
        gpre_ref[:, at] = gate_pre.astype(bf16)
        attended = dot(probs_ref[...], values)
        att_ref[:, at] = attended.astype(bf16)
        gated_ref[:, at] = (attended * (gate_pre * sigmoid(gate_pre))).astype(bf16)
        return 0

    lax.fori_loop(0, values_width // tile, columns, 0)


def project_kernel(weight2, *refs):
    n2 = len(weight2.arrays)
    me_ref, gated_ref, tok_ref, valid_ref, fg_ref = refs[:5]
    middle_ref, ffn_ref, inv_ref, w2, sems = refs[5 + n2 :]
    width = tok_ref.shape[1]
    edge = width // 2
    for part in range(2):
        for copy in weight2.copies(refs[5 : 5 + n2], w2, me_ref[0], sems.at[part], span=(part * edge, edge)):
            copy.start()
    square = jnp.zeros((tok_ref.shape[0], 1), f32)
    for part in range(2):
        for copy in weight2.copies(refs[5 : 5 + n2], w2, me_ref[0], sems.at[part], span=(part * edge, edge)):
            copy.wait()
        at = slice(part * edge, (part + 1) * edge)
        middle = tok_ref[:, at].astype(f32) * valid_ref[...] + dot(gated_ref[...], w2[:, at])
        middle_ref[:, at] = middle
        square = square + jnp.sum(middle * middle, axis=1, keepdims=True)
    inverse = lax.rsqrt(square * (1.0 / width) + 1e-05)
    inv_ref[...] = inverse
    ffn_ref[...] = (middle_ref[...] * inverse * fg_ref[...]).astype(bf16)


def hidden_kernel(weight3, weight4, me_ref, ffn_ref, cot_ref, *refs):
    n3, n4 = len(weight3.arrays), len(weight4.arrays)
    hid_ref, near_ref, far_ref, w3, w4, sems = refs[n3 + n4 :]
    step, core = pl.program_id(0), me_ref[1]
    half = hid_ref.shape[1]

    def copies(rel, n):
        base = pl.multiple_of((core ^ rel) * half, half)
        if n < 2:
            return weight3.copies(refs[:n3], w3, me_ref[0], sems.at[rel, n], n, (base, half))
        return weight4.copies(refs[n3 : n3 + n4], w4, me_ref[0], sems.at[rel, n], near=None)

    @pl.when(step == 0)
    def _():
        for rel, n in ((0, 0), (0, 1), (0, 2), (1, 0), (1, 1)):
            for copy in copies(rel, n):
                copy.start()

    def arrived(n):
        for rel in range(2):
            if (rel, n) != (1, 2):
                @pl.when(step == rel)
                def _():
                    for copy in copies(rel, n):
                        copy.wait()

    base = pl.multiple_of((core ^ step) * half, half)
    arrived(0)
    gate = dot(ffn_ref[...], w3[:, pl.ds(base, half)])
    sigma = sigmoid(gate)
    act = gate * sigma
    slope = sigma + act * (1.0 - sigma)
    arrived(1)
    up = dot(ffn_ref[...], w3[:, pl.ds(pl.multiple_of(base + 2 * half, half), half)])
    hid_ref[...] = (act * up).astype(bf16)
    arrived(2)
    grad = mul_t(cot_ref[...], w4[pl.ds(base, half), :])
    grad_gate = (grad * up * slope).astype(bf16)
    grad_up = (grad * act).astype(bf16)

    @pl.when(step == 0)
    def _():
        near_ref[:, :half] = grad_gate
        near_ref[:, half:] = grad_up

    @pl.when(step == 1)
    def _():
        far_ref[:, :half] = grad_gate
        far_ref[:, half:] = grad_up


def out_kernel(weight4, me_ref, hid_ref, middle_ref, *refs):
    n4 = len(weight4.arrays)
    out_ref, w4, sems = refs[n4:]
    width, half = middle_ref.shape[1], hid_ref.shape[1] // 2
    starts = [pl.multiple_of((me_ref[1] ^ rel) * half, half) for rel in range(2)]
    edge = width // 2
    for part in range(2):
        for copy in weight4.copies(refs[:n4], w4, me_ref[0], sems.at[part], span=(part * edge, edge)):
            copy.start()
    for part in range(2):
        for copy in weight4.copies(refs[:n4], w4, me_ref[0], sems.at[part], span=(part * edge, edge)):
            copy.wait()
        at = slice(part * edge, (part + 1) * edge)
        total = middle_ref[:, at]
        for rel in range(2):
            total = total + dot(hid_ref[:, rel * half : (rel + 1) * half], w4[pl.ds(starts[rel], half), at])
        out_ref[:, at] = total.astype(bf16)


def ffn_back_kernel(weight3, *refs):
    n3 = len(weight3.arrays)
    me_ref, near_ref, far_ref, middle_ref, inv_ref, cot_ref, fg_ref = refs[:7]
    gmid_ref, low_own, low_oth, low_ref, dfg_ref, w3, gin_ref, sems = refs[7 + n3 :]
    me, core = me_ref[0], me_ref[1]
    rows, width = middle_ref.shape
    half = near_ref.shape[1] // 2
    parts, edge = (2, width // 2) if weight3.split else (1, width)
    for part in range(parts):
        for copy in weight3.copies(refs[7 : 7 + n3], w3, me, sems.at[part], near=weight3.nears[part]):
            copy.start()
    starts = [pl.multiple_of((core ^ rel) * half, half) for rel in range(2)]
    lean = jnp.zeros((rows, 1), f32)
    for part in range(parts):
        for copy in weight3.copies(refs[7 : 7 + n3], w3, me, sems.at[part], near=weight3.nears[part]):
            copy.wait()
        base = pl.multiple_of((lax.shift_right_logical(me, weight3.top) ^ part) * edge, edge) if parts == 2 else 0
        at = pl.ds(base, edge)
        grad = jnp.zeros((rows, edge), f32)
        for rel, ref in enumerate((near_ref, far_ref)):
            grad = grad + mul_t(ref[:, :half], w3[at, pl.ds(starts[rel], half)])
            grad = grad + mul_t(ref[:, half:], w3[at, pl.ds(pl.multiple_of(starts[rel] + 2 * half, half), half)])
        normal = middle_ref[:, at] * inv_ref[...]
        dfg_ref[:, at] = jnp.sum(grad * normal, axis=0, keepdims=True)
        grad = grad * fg_ref[:, at]
        gin_ref[:, at] = grad
        lean = lean + jnp.sum(grad * normal, axis=1, keepdims=True)
    lean = lean * (1.0 / width)
    inverse = inv_ref[...]
    grad_middle = cot_ref[...].astype(f32) + inverse * (gin_ref[...] - middle_ref[...] * inverse * lean)
    gmid_ref[...] = grad_middle
    low_ref[...] = grad_middle.astype(bf16)
    part = width // 2
    low_own[...] = low_ref[:, pl.ds(pl.multiple_of(core * part, part), part)]
    low_oth[...] = low_ref[:, pl.ds(pl.multiple_of((1 - core) * part, part), part)]


def attention_back_kernel(weight2, tile, *refs):
    n2 = len(weight2.arrays)
    (me_ref, low_ref, q_ref, k_ref, lse_ref, shared_ref, vpre_ref, values_ref, gpre_ref, att_ref, segc_ref, segr_ref,
     validr_ref, qg_ref, kg_ref) = refs[:15]
    (gv_ref, gr_ref, gv_own, gv_oth, gr_own, gr_oth, dgain_ref, w2, low_probs_ref, gprobs_ref, gsh_ref, sem2) = refs[15 + n2 :]
    core = me_ref[1]
    rows = low_ref.shape[0]
    values_width = values_ref.shape[1]
    copies2 = weight2.copies(refs[15 : 15 + n2], w2, me_ref[0], sem2)
    for copy in copies2:
        copy.start()
    queries, keys = q_ref[...], k_ref[...]
    factor = queries.shape[1] ** -0.5
    scores = mul_t(queries, keys) * factor
    masked = jnp.where(allowed_pairs(segc_ref, segr_ref, validr_ref), scores, -1e30)
    probs = jnp.exp(masked - lse_ref[...])
    low_probs_ref[...] = probs.astype(bf16)
    gprobs_ref[...] = jnp.zeros((rows, rows), f32)
    for copy in copies2:
        copy.wait()

    def columns(i, _):
        at = pl.ds(pl.multiple_of(i * tile, tile), tile)
        grad = mul_t(low_ref[...], w2[at, :]).astype(bf16).astype(f32)
        gate_pre = gpre_ref[:, at].astype(f32)
        sigma = sigmoid(gate_pre)
        act = gate_pre * sigma
        grad_att = (grad * act).astype(bf16)
        gr_ref[:, at] = (grad * att_ref[:, at].astype(f32) * (sigma + act * (1.0 - sigma))).astype(bf16)
        gprobs_ref[...] += mul_t(grad_att, values_ref[:, at])
        grad_values = t_mul(low_probs_ref[...], grad_att)
        gv_ref[:, at] = (grad_values * silu_grad(vpre_ref[:, at].astype(f32))).astype(bf16)
        return 0

    lax.fori_loop(0, values_width // tile, columns, 0)
    grad_probs = gprobs_ref[...]
    grad_scores = (probs * (grad_probs - jnp.sum(probs * grad_probs, axis=1, keepdims=True))).astype(bf16)
    grad_queries = dot(grad_scores, keys) * factor
    grad_keys = t_mul(grad_scores, queries) * factor
    shared = shared_ref[...]
    dgain_ref[0:1, :] = jnp.sum(grad_queries * shared, axis=0, keepdims=True)
    dgain_ref[1:2, :] = jnp.sum(grad_queries, axis=0, keepdims=True)
    dgain_ref[2:3, :] = jnp.sum(grad_keys * shared, axis=0, keepdims=True)
    gsh_ref[...] = (grad_queries * qg_ref[...] + grad_keys * kg_ref[...]).astype(bf16)
    gr_ref[:, values_width:] = gsh_ref[...]
    for source, own, other, start in (
        (gv_ref, gv_own, gv_oth, 0), (gr_ref, gr_own, gr_oth, 0), (gsh_ref, gr_own, gr_oth, values_width // 2)
    ):
        part = (values_width if start == 0 else source.shape[1]) // 2
        own[:, start : start + part] = source[:, pl.ds(pl.multiple_of(core * part, part), part)]
        other[:, start : start + part] = source[:, pl.ds(pl.multiple_of((1 - core) * part, part), part)]


def sent_back_kernel(weight1, *refs):
    n1 = len(weight1.arrays)
    me_ref, gv_ref, gr_ref = refs[:3]
    gmix_ref, gnorm_ref, w1, sems = refs[3 + n1 :]
    me, width, values_width = me_ref[0], gmix_ref.shape[1], gv_ref.shape[1]
    parts, edge = (2, width // 2) if weight1.split else (1, width)
    for part in range(parts):
        for copy in weight1.copies(refs[3 : 3 + n1], w1, me, sems.at[part], near=weight1.nears[part]):
            copy.start()
    for part in range(parts):
        for copy in weight1.copies(refs[3 : 3 + n1], w1, me, sems.at[part], near=weight1.nears[part]):
            copy.wait()
        base = pl.multiple_of((lax.shift_right_logical(me, weight1.top) ^ part) * edge, edge) if parts == 2 else 0
        at = pl.ds(base, edge)
        gmix_ref[:, at] = mul_t(gr_ref[...], w1[at, values_width:]).astype(bf16)
        gnorm_ref[:, at] = mul_t(gv_ref[...], w1[at, :values_width]).astype(bf16)


def weight_grad_kernel(halves, order, blocks, block, me_ref, own, other, mine, theirs, *refs):
    keep, send = refs[0], refs[1]
    held, sems = refs[-2:]
    chip, core = lax.shift_right_logical(me_ref[0], 1), me_ref[1]
    tile, span = own.shape[1], mine.shape[1]
    step, steps = pl.program_id(0), pl.num_programs(0)
    strips = lax.div(steps, halves)
    rel = lax.div(step, strips)
    base = ((core ^ rel) if halves == 2 else rel) * (strips * tile) + lax.rem(step, strips) * tile
    slot = lax.rem(step, 2)
    parts = tile // block

    def done(slot):
        for s in range(parts):
            pltpu.make_async_copy(held.at[slot, pl.ds(s * block, block)], keep.at[0], sems.at[slot]).wait()

    @pl.when(step >= 2)
    def _():
        done(slot)

    out = t_mul(own[...], mine[...]) + t_mul(other[...], theirs[...])
    held[slot] = out.astype(bf16)
    for s in range(parts):
        rel_chip = (lax.div(base, block) + s) ^ chip
        place = 0
        for p, bit in enumerate(order):
            place = place | ((lax.shift_right_logical(rel_chip, bit - 1) & 1) << (len(order) - 1 - p))
        index = place & (blocks // 2 - 1)
        source = held.at[slot, pl.ds(s * block, block)]

        @pl.when(place < blocks // 2)
        def _():
            pltpu.make_async_copy(source, keep.at[index], sems.at[slot]).start()

        @pl.when(place >= blocks // 2)
        def _():
            pltpu.make_async_copy(source, send.at[index], sems.at[slot]).start()

    @pl.when(step == steps - 1)
    def _():
        done(slot)
        done(1 - slot)


def plain_grad_kernel(halves, me_ref, own, other, mine, theirs, keep):
    keep[0] = (t_mul(own[...], mine[...]) + t_mul(other[...], theirs[...])).astype(bf16)


def weight_grad(left, right, order, me, chips, name, halves=1, part=(0, 1), micros=6, after=()):
    total, span = left[0].shape[1], right[0].shape[1] // part[1]
    rows = left[0].shape[0]
    half = total // halves
    block = total // chips
    if order is None:
        tile = math.gcd(half, 256)
    else:
        tile = math.lcm(block, LANES)
        while tile < 512 and half % (2 * tile) == 0 and half // (2 * tile) >= 2 // halves:
            tile *= 2
    strips = half // tile
    far = (lambda g, me: (0, g)) if halves == 1 else (lambda g, me: (0, lax.rem(g + strips, 2 * strips)))
    args = [
        columns_of(left[0], tile), columns_of(left[1], tile, far), columns_of(right[0], span, lambda g, me: (0, part[0])),
        columns_of(right[1], span, lambda g, me: (0, part[0])),
    ]
    if order is None:
        place = (lambda g, me: (0, g, 0)) if halves == 1 else (
            lambda g, me: (0, (me[1] ^ lax.div(g, strips)) * strips + lax.rem(g, strips), 0))
        (keep,) = grid_call(
            functools.partial(plain_grad_kernel, halves), [((1, total, span), bf16, (1, tile, span), place)], args,
            halves * strips, me, name=name, micros=micros, after=after)
        return Reduce(keep, None, None)
    keep, send = grid_call(
        functools.partial(weight_grad_kernel, halves, order, chips, block),
        [((chips // 2, block, span), bf16, None, None)] * 2, args, halves * strips, me,
        scratch=[pltpu.VMEM((2, tile, span), bf16), pltpu.SemaphoreType.DMA((2,))], name=name, micros=micros, after=after)
    return Reduce(keep, send, order)


def exchange_start(pack, totals, axis, hold):
    index, count = lax.axis_index(axis), lax.axis_size(axis)
    lanes = pack.shape[1]
    rows = pack.shape[0]
    full, totals_shape = pack, totals.shape
    totals = totals.reshape(-1, lanes)
    before, bit = jnp.zeros_like(totals), 1
    while bit < count:
        goes = jnp.concatenate([totals, full], axis=0)
        other = swap(tie(goes, *hold) if hold and bit == 2 else goes, axis, bit)
        upper = (index & bit) != 0
        far_totals, far = other[: totals.shape[0]], other[totals.shape[0] :]
        before = before + jnp.where(upper, far_totals, 0.0)
        totals = totals + far_totals
        full = jnp.concatenate([jnp.where(upper, far, full), jnp.where(upper, full, far)], axis=0)
        bit *= 2
    return full.reshape(count, rows, lanes), before.reshape(totals_shape)


def exchange_end(pack, totals, axis):
    index, count = lax.axis_index(axis), lax.axis_size(axis)
    lanes = pack.shape[2]
    totals_shape = totals.shape
    totals = totals.reshape(-1, lanes)
    rows = totals.shape[0]
    after, bit = jnp.zeros_like(totals), 1
    while bit < count:
        upper = (index & bit) != 0
        pairs = pack.reshape((pack.shape[0] // 2, 2) + pack.shape[1:])
        goes = jnp.where(upper, pairs[:, 0], pairs[:, 1])
        stays = jnp.where(upper, pairs[:, 1], pairs[:, 0])
        other = swap(jnp.concatenate([totals, goes.reshape(-1, lanes)], axis=0), axis, bit)
        after = after + jnp.where(upper, 0.0, other[:rows])
        totals = totals + other[:rows]
        pack = stays + other[rows:].reshape(stays.shape)
        bit *= 2
    return pack[0], after.reshape(totals_shape)


def sum_over(value, axis):
    bit = 1
    while bit < lax.axis_size(axis):
        value = value + swap(value, axis, bit)
        bit *= 2
    return value


def on_device(tokens, cotangent, segment_ids, pad_mask, w_z, w_v, w_r, w_h, w_gate, w_up, w_down, q_gain, q_bias,
              k_gain, ffn_gain, norm_gain, ema_rate, ema_angle, ema_input, ema_output, ema_skip):
    rows, width = tokens.shape[1:]
    seq_count, dp_count = lax.axis_size("seq"), 2 * lax.axis_size("chip")
    seq_index, core = lax.axis_index("seq"), lax.axis_index("core")
    dp_index = lax.axis_index("chip") * 2 + core
    devices = seq_count * dp_count
    chips = devices // 2
    fits = all(value.shape[0] % 16 == 0 for value in (w_z, w_h, w_down))
    dp_bits, all_bits = bits_of(dp_count), bits_of(devices)
    inner = list(range(1, dp_bits))
    first_seq, rest_seq = [dp_bits], list(range(all_bits - 1, dp_bits, -1))
    if fits:
        gather_a = rest_seq + first_seq + inner + [0]
        gather_b = rest_seq + inner + first_seq + [0]
        gather_c = inner + first_seq + rest_seq + [0]
        reduce_a, reduce_b = gather_a[-2::-1], gather_b[-2::-1]
        me = jnp.stack([seq_index * dp_count + dp_index, core]).astype(jnp.int32)
    else:
        gather_a = gather_b = gather_c = reduce_a = reduce_b = None
        me = jnp.stack([core * 0, core]).astype(jnp.int32)
    values_width, hidden_width = w_v.shape[1], w_gate.shape[1]
    z_width = w_z.shape[1]
    low = lambda *parts: jnp.concatenate([part.astype(bf16) for part in parts], axis=1)
    short = w_v.shape[0]
    if fits:
        get_v = Gather(low(w_v, w_h[:short]), gather_a)
        get_r = Gather(low(w_r, w_z, w_h[short:]), gather_b)
    else:
        get_v, get_r = Gather(low(w_v), None), Gather(low(w_r, w_z), None)
    get_gate, get_up = Gather(low(w_gate), gather_a), Gather(low(w_up), gather_b)
    first_v, first_r = get_v.step(), get_r.step()
    get_down = Gather(low(w_down), gather_c)
    first_down = get_down.step()

    row_segs = lax.dynamic_slice_in_dim(segment_ids[0], seq_index * rows, rows)
    row_valid = lax.dynamic_slice_in_dim(pad_mask[0], seq_index * rows, rows).astype(f32)
    valid_col, seg_col, seg_row, valid_row = row_valid[:, None], row_segs[:, None], row_segs[None], row_valid[None]
    prefix, totals = kernel_call(
        stats_kernel, [((rows, LANES), f32), ((DOCS, LANES), f32)], [tokens[0], valid_col, seg_col, seg_row],
        name="stats", micros=5,
    )

    ndim, lanes = ema_rate.shape[1], norm_gain.shape[0]
    gains = jnp.concatenate([q_gain, q_bias, k_gain, ffn_gain])[None].astype(bf16).astype(f32)
    gains = gather_small(gather_small(gains, "core"), "chip").reshape(-1)
    size = gains.shape[0]
    extra = -(-size // lanes)
    gains = jnp.pad(gains, (0, extra * lanes - size)).reshape(extra, lanes)
    pack = jnp.concatenate(
        [ema_rate.T, ema_angle.T, ema_input.T, ema_output.T, norm_gain[None], ema_skip[None], gains], axis=0
    )
    full, before = exchange_start(pack, totals, "seq", first_v + first_r)
    carry = lax.dynamic_slice_in_dim(before, row_segs[0], 1)
    gains = full[:, 4 * ndim + 2 :].reshape(seq_count, -1)[:, :size].reshape(devices, -1)
    zs, fs = q_gain.shape[0], ffn_gain.shape[0]
    full_qg = gains[:, :zs].reshape(1, -1)
    full_qb = gains[:, zs : 2 * zs].reshape(1, -1)
    full_kg = gains[:, 2 * zs : 3 * zs].reshape(1, -1)
    full_fg = gains[:, 3 * zs :].reshape(1, -1)
    par = ema_params(full[:, : 4 * ndim + 2], ndim, rows)
    flat = lambda value: value.reshape(-1, LANES)
    a_flat, b_flat, g_flat = flat(par["a"]), flat(par["b"]), flat(par["output_w"] * par["coeff"])
    gain_row = par["gain"].reshape(1, width)
    seq_steps = len(rest_seq)
    for _ in range(seq_steps - 1):
        deep_v, deep_r = get_v.step(), get_r.step()
    for _ in inner[1:]:
        get_down.step()
    second_down = get_down.step(first_v)
    sent_norm, xs, ends = kernel_call(
        norm_kernel,
        [((rows, width), bf16), ((rows * SUB, LANES), f32), ((2 * ndim * SUB, LANES), f32)],
        [tokens[0], valid_col, seg_col, prefix, carry, gain_row, a_flat, b_flat],
        name="norm", micros=13, after=first_v + first_r + first_down,
    )
    middle_v, middle_r = get_v.step((ends,)), get_r.step((ends,))
    first_gate, first_up = get_gate.step(deep_v + (ends,)), get_up.step(deep_r + (ends,))
    start_state = state_before(ends.reshape(2 * ndim, SUB, LANES), par["hop"], "seq", False)
    start_state = tie(start_state, *middle_v, *middle_r, *first_gate, *first_up)
    for _ in range(seq_steps - 1):
        deep_gate, deep_up = get_gate.step((start_state,)), get_up.step((start_state,))
    mixed, sent_mix, kept = kernel_call(
        mix_kernel,
        [((rows * SUB, LANES), f32), ((rows, width), bf16), ((rows // SPAN, 2 * ndim * SUB, LANES), f32)],
        [xs, flat(start_state), a_flat, b_flat, g_flat, par["skip"]],
        scratch=[pltpu.VMEM((2 * ndim * SUB, LANES), f32)],
        name="mix", micros=16,
    )
    third_gate, third_up = get_gate.step((mixed,)), get_up.step((mixed,))
    get_down.step((mixed,))
    for getter in (get_v, get_r):
        getter.step((start_state,))
        while getter.order is not None and getter.place < all_bits:
            getter.step()
    weight1 = Weight(Part(get_v, 0, values_width, short), Part(get_r, 0, values_width + z_width, short, 0, values_width))
    if fits:
        tall = w_h.shape[0]
        weight2 = Weight(
            Part(get_v, values_width, width, tall), Part(get_r, values_width + z_width, width, tall, short)
        )
    else:
        weight2 = Weight(Part(Gather(low(w_h), None), 0, width, w_h.shape[0]))

    tile = 256
    w1_shape, w2_shape = (width, 2 * values_width + z_width), (values_width, width)
    w3_shape, w4_shape = (width, 2 * hidden_width), (hidden_width, width)
    dma = pltpu.SemaphoreType.DMA
    wide = ((rows, values_width), bf16)

    def other_core(value):
        return swap_bit(value, 0)

    norm_other = other_core(tie(sent_norm, mixed))

    def any_of(*groups):
        return [ANY] * sum(len(group.arrays) for group in groups)

    shared, queries, keys, log_total, value_pre, values, gate_pre, attended, gated = kernel_call(
        functools.partial(attention_kernel, weight1, tile),
        [((rows, z_width), f32), ((rows, z_width), bf16), ((rows, z_width), bf16), ((rows, 1), f32), wide, wide, wide,
         wide, wide],
        [me, sent_norm, sent_mix, seg_col, seg_row, valid_row, full_qg, full_qb, full_kg, *weight1.arrays],
        [SM] + [VM] * 8 + any_of(weight1),
        scratch=[pltpu.VMEM(w1_shape, bf16), pltpu.VMEM((rows, rows), bf16), dma],
        name="attention", micros=18, after=third_gate + third_up + (norm_other,),
    )
    for getter in (get_gate, get_up, get_down):
        while getter.order is not None and getter.place < all_bits - 1:
            getter.step()
        getter.step((gated,))
    weight4 = Weight(Part(get_down, 0, width, w_down.shape[0]))
    weight3 = Weight(Part(get_gate, 0, hidden_width, short), Part(get_up, 0, hidden_width, short, 0, hidden_width))
    middle, ffn_in, inverse = kernel_call(
        functools.partial(project_kernel, weight2),
        [((rows, width), f32), ((rows, width), bf16), ((rows, 1), f32)],
        [me, gated, tokens[0], valid_col, full_fg, *weight2.arrays],
        [SM] + [VM] * 4 + any_of(weight2),
        scratch=[pltpu.VMEM(w2_shape, bf16), pltpu.SemaphoreType.DMA((2,))],
        name="project", micros=6,
    )

    grad_low = cotangent[0]
    part = width // 2
    cot_own = lax.dynamic_slice_in_dim(grad_low, core * part, part, axis=1)
    cot_oth = other_core(tie(lax.dynamic_slice_in_dim(grad_low, (1 - core) * part, part, axis=1), mixed))
    gated_other, mix_other = other_core(gated), other_core(sent_mix)
    half = hidden_width // 2
    pair = ((rows, hidden_width), bf16, (rows, hidden_width), lambda g, me: (0, 0))
    hid, near, far = grid_call(
        functools.partial(hidden_kernel, weight3, weight4),
        [((rows, hidden_width), bf16, (rows, half), lambda g, me: (0, g)), pair, pair],
        [whole(ffn_in), whole(grad_low)] + [(array, None, None) for array in weight3.arrays + weight4.arrays],
        2, me,
        scratch=[pltpu.VMEM(w3_shape, bf16), pltpu.VMEM(w4_shape, bf16), pltpu.SemaphoreType.DMA((2, 3))],
        name="hidden", micros=15, after=(cot_oth, gated_other, mix_other),
    )
    ffn_other = other_core(ffn_in)
    (output,) = kernel_call(
        functools.partial(out_kernel, weight4),
        [((rows, width), bf16)],
        [me, hid, middle, *weight4.arrays],
        [SM, VM, VM] + any_of(weight4),
        scratch=[pltpu.VMEM(w4_shape, bf16), pltpu.SemaphoreType.DMA((2,))],
        name="out", micros=7,
    )
    hid_pair, ffn_pair = (hid, other_core(hid)), (ffn_in, ffn_other)
    far_other = other_core(far)
    down = weight_grad(hid_pair, (cot_own, cot_oth), reduce_a, me, chips, "grad_down", halves=2, after=(output,))
    gate = weight_grad(ffn_pair, (near, far_other), reduce_b, me, chips, "grad_gate", part=(0, 2), after=(down.sent,))
    up = weight_grad(
        ffn_pair, (near, far_other), reduce_a, me, chips, "grad_up", part=(1, 2), after=(gate.sent,)
    )
    grad_middle, low_own, low_oth, middle_low, dfg = kernel_call(
        functools.partial(ffn_back_kernel, weight3),
        [((rows, width), f32), ((rows, part), bf16), ((rows, part), bf16), ((rows, width), bf16), ((1, width), f32)],
        [me, near, far, middle, inverse, grad_low, full_fg, *weight3.arrays],
        [SM] + [VM] * 6 + any_of(weight3),
        scratch=[pltpu.VMEM(w3_shape, bf16), pltpu.VMEM((rows, width), f32), pltpu.SemaphoreType.DMA((2,))],
        name="ffn_back", micros=17, after=(up.sent,),
    )
    heads = weight_grad(
        (gated, gated_other), (low_own, other_core(low_oth)), reduce_b, me, chips, "grad_h", after=down.step(low_own)
    )
    half_values = ((rows, values_width // 2), bf16)
    half_mixed = ((rows, (values_width + z_width) // 2), bf16)
    grad_v, grad_r, gv_own, gv_oth, gr_own, gr_oth, dgains = kernel_call(
        functools.partial(attention_back_kernel, weight2, tile),
        [((rows, values_width), bf16), ((rows, values_width + z_width), bf16)] + [half_values] * 2 + [half_mixed] * 2
        + [((3, z_width), f32)],
        [me, middle_low, queries, keys, log_total, shared, value_pre, values, gate_pre, attended, seg_col, seg_row,
         valid_row, full_qg, full_kg, *weight2.arrays],
        [SM] + [VM] * 14 + any_of(weight2),
        scratch=[pltpu.VMEM(w2_shape, bf16), pltpu.VMEM((rows, rows), bf16), pltpu.VMEM((rows, rows), f32),
                 pltpu.VMEM((rows, z_width), bf16), dma],
        name="attention_back", micros=19, after=(heads.sent,) + gate.step(heads.sent),
    )
    grad_mix_rows, grad_norm_rows = kernel_call(
        functools.partial(sent_back_kernel, weight1),
        [((rows, width), bf16)] * 2,
        [me, grad_v, grad_r, *weight1.arrays],
        [SM, VM, VM] + any_of(weight1),
        scratch=[pltpu.VMEM(w1_shape, bf16), pltpu.SemaphoreType.DMA((2,))],
        name="sent_back", micros=11, after=up.step(gv_oth) + down.step(gv_oth),
    )
    gv_other, gr_other = other_core(gv_oth), other_core(gr_oth)
    drive, back_ends = kernel_call(
        back_ends_kernel, [((rows * SUB, LANES), f32), ((2 * ndim * SUB, LANES), f32)],
        [grad_mix_rows, mixed, a_flat, b_flat], name="back_ends", micros=12,
        after=heads.step(grad_mix_rows) + down.step(grad_mix_rows),
    )
    value = weight_grad((sent_norm, norm_other), (gv_own, gv_other), reduce_a, me, chips, "grad_v",
                        after=(back_ends, gr_other))
    both = merge(gate, up, back_ends)
    reset = weight_grad((sent_mix, mix_other), (gr_own, gr_other), reduce_b, me, chips, "grad_r",
                        after=(value.sent,) + both.pins + down.step(value.sent))
    hop_back = (par["hop"][0], -par["hop"][1])
    back_state = flat(
        state_before(back_ends.reshape(2 * ndim, SUB, LANES), hop_back, "seq", True,
                     {2: lambda: (value.sent,), 4: lambda: (reset.sent,)})
    )
    sums = jnp.zeros(((3 * ndim + 1) * SUB, LANES), f32)
    cuts = 4
    plan = [
        lambda done: heads.step(reset.sent) + both.step(reset.sent),
        lambda done: value.step(done) + heads.step(done),
        lambda done: reset.step(done) + both.step(done),
        lambda done: heads.step(done),
    ]
    last = []

    def merge_last(done):
        last.append(merge(value, reset, done))
        return last[0].pins

    done = back_state
    long = rows * SUB // cuts
    pieces_dx = []
    for cut in range(cuts - 1, -1, -1):
        block = pl.BlockSpec((long, LANES), lambda i, cut=cut: (cut, 0))
        keep_block = pl.BlockSpec((rows // SPAN // cuts, 2 * ndim * SUB, LANES), lambda i, cut=cut: (cut, 0, 0))
        dxs, back_state, sums = kernel_call(
            back_scan_kernel,
            [((long, LANES), f32), ((2 * ndim * SUB, LANES), f32), (((3 * ndim + 1) * SUB, LANES), f32)],
            [xs, drive, kept, back_state, sums, a_flat, b_flat, g_flat, par["skip"]],
            [block, block, keep_block] + [VM] * 6,
            scratch=[pltpu.VMEM((SPAN, 8 * SUB, LANES), f32)],
            name="back", micros=10, after=plan.pop(0)(done), grid=(1,), out_specs=[VM] * 3,
        )
        pieces_dx.insert(0, dxs)
        done = dxs
    pins = merge_last(done)
    last = last[0]
    dn, dgain, suffix, back_totals = kernel_call(
        back_norm_kernel,
        [((rows, width), f32), ((1, width), f32), ((rows, LANES), f32), ((DOCS, LANES), f32)],
        [*pieces_dx, grad_norm_rows, tokens[0], valid_col, seg_col, seg_row, prefix, carry, gain_row],
        name="back_norm", micros=6, after=pins,
    )
    sums = sums.reshape(3 * ndim + 1, SUB, LANES)
    d_params = ema_param_grads(par, sums)
    d_pack = jnp.concatenate(list(d_params) + [dgain.reshape(1, SUB, LANES), sums[3 * ndim :]], axis=0)
    d_pack = jnp.transpose(d_pack.reshape(4 * ndim + 2, seq_count, lanes), (1, 0, 2))
    owned = [dgains[i].reshape(devices, zs) for i in range(3)] + [dfg.reshape(devices, fs)]
    owned = jnp.concatenate(owned, axis=1).reshape(seq_count, -1)
    owned = jnp.pad(owned, ((0, 0), (0, extra * lanes - size))).reshape(seq_count, extra, lanes)
    own_pack, after_totals = exchange_end(jnp.concatenate([d_pack, owned], axis=1), tie(back_totals, *last.step(back_totals)), "seq")
    back_carry = lax.dynamic_slice_in_dim(after_totals, row_segs[rows - 1], 1)
    (input_grad,) = kernel_call(
        input_kernel, [((rows, width), f32)],
        [dn, suffix, back_carry, tokens[0], valid_col, seg_col, prefix, carry, grad_middle], name="input", micros=6,
        after=last.step(back_carry),
    )
    total = sum_over(sum_over(own_pack, "core"), "chip")
    mine = lax.dynamic_index_in_dim(total[4 * ndim + 2 :].reshape(-1)[:size].reshape(dp_count, -1), dp_index, 0, keepdims=False)
    (shard_down,) = down.finish(core, [part])
    shard_gate, shard_up = both.finish(core, [hidden_width // 2] * 2, done)
    (shard_h,) = heads.finish(core, [part], done)
    shard_v, shard_r, shard_z = last.finish(core, [values_width // 2, values_width // 2, z_width // 2])
    return (
        output[None], input_grad[None], shard_z, shard_v, shard_r, shard_h, shard_gate, shard_up, shard_down,
        mine[:zs], mine[zs : 2 * zs], mine[2 * zs : 3 * zs], mine[3 * zs :],
        total[4 * ndim], total[:ndim].T, total[ndim : 2 * ndim].T, total[2 * ndim : 3 * ndim].T,
        total[3 * ndim : 4 * ndim].T, total[4 * ndim + 1],
    )


def solution(mesh):
    shape = mesh.devices.shape
    whole = Mesh(mesh.devices.reshape(shape[0], shape[1] // 2, 2), AXES)
    by_token, by_group = P(("chip", "core"), "seq", None), P(("chip", "core"), None)
    by_row, by_owner = P(AXES, None), P(AXES)
    params = (by_row,) * 7 + (by_owner,) * 4 + (P("seq"),) + (P("seq", None),) * 4 + (P("seq"),)
    return jax.shard_map(
        on_device,
        mesh=whole,
        in_specs=(by_token, by_token, by_group, by_group) + params,
        out_specs=(by_token, by_token) + params,
        check_vma=False,
    )
```

```python
import functools
import math

import jax
import jax.numpy as jnp
from jax import lax
from jax.experimental import pallas as pl
from jax.experimental.pallas import tpu as pltpu
from jax.sharding import Mesh, PartitionSpec as P

AXES = ("seq", "chip", "core")
GROUP = 64
DOCS = 16
LANES = 128
SUB = 8
SPAN = 32
BAND = 64
bf16 = jnp.bfloat16
f32 = jnp.float32
VMEM_LIMIT = 60 * 1024 * 1024
PACE = 0.05


def split3(value):
    first = value.astype(bf16)
    rest = value - first.astype(f32)
    second = rest.astype(bf16)
    third = (rest - second.astype(f32)).astype(bf16)
    return first, second, third


def dot(left, right):
    return jnp.dot(left, right, preferred_element_type=f32)


def dot3(left, parts):
    return dot(left, parts[0]) + dot(left, parts[1]) + dot(left, parts[2])


def dot3_left(parts, right):
    return dot(parts[0], right) + dot(parts[1], right) + dot(parts[2], right)


def sigmoid(value):
    return 0.5 * jnp.tanh(0.5 * value) + 0.5


def iota(shape, axis):
    return lax.broadcasted_iota(jnp.int32, shape, axis)


def group_pick(width, shift):
    own = lax.shift_right_logical(iota((width, LANES), 0), GROUP.bit_length() - 1)
    return (own + shift == iota((width, LANES), 1)).astype(bf16)


def group_spread(groups, width):
    own = lax.shift_right_logical(iota((groups, width), 1), GROUP.bit_length() - 1)
    return (own == iota((groups, width), 0)).astype(bf16)


ANY = pl.BlockSpec(memory_space=pl.ANY)
VM = pl.BlockSpec(memory_space=pltpu.VMEM)
SM = pl.BlockSpec(memory_space=pltpu.SMEM)


def kernel_call(body, outs, args, specs=None, scratch=(), name=None, micros=10, after=(), grid=None, out_specs=None):
    specs = [VM] * len(args) if specs is None else specs
    count = len(args)

    def run(*refs):
        body(*refs[:count], *refs[count + len(after) :])

    more = {} if grid is None else dict(grid=grid, out_specs=tuple(out_specs))
    return pl.pallas_call(
        run,
        out_shape=tuple(jax.ShapeDtypeStruct(shape, dtype) for shape, dtype in outs),
        in_specs=list(specs) + [ANY] * len(after),
        scratch_shapes=list(scratch),
        compiler_params=pltpu.CompilerParams(vmem_limit_bytes=VMEM_LIMIT),
        cost_estimate=pl.CostEstimate(
            flops=int(micros * PACE * 1.0e9), bytes_accessed=int(micros * PACE * 3.0e6), transcendentals=0
        ),
        name=name,
        **more,
    )(*args, *after)


def grid_call(body, outs, args, steps, me, scratch=(), name=None, micros=10, after=()):
    def spec(shape, block, index):
        if block is None:
            return ANY
        if index is None:
            return pl.BlockSpec(shape, lambda g, me: (0,) * len(shape))
        return pl.BlockSpec(block, index)

    count = len(args)

    def run(*refs):
        body(*refs[: 1 + count], *refs[1 + count + len(after) :])

    return pl.pallas_call(
        run,
        out_shape=tuple(jax.ShapeDtypeStruct(shape, dtype) for shape, dtype, _, _ in outs),
        grid_spec=pltpu.PrefetchScalarGridSpec(
            num_scalar_prefetch=1,
            grid=(steps,),
            in_specs=[spec(array.shape, block, index) for array, block, index in args] + [ANY] * len(after),
            out_specs=tuple(spec(shape, block, index) for shape, _, block, index in outs),
            scratch_shapes=list(scratch),
        ),
        compiler_params=pltpu.CompilerParams(vmem_limit_bytes=VMEM_LIMIT),
        cost_estimate=pl.CostEstimate(
            flops=int(micros * PACE * 1.0e9), bytes_accessed=int(micros * PACE * 3.0e6), transcendentals=0
        ),
        name=name,
    )(me, *(array for array, _, _ in args), *after)


WHOLE = (1,)


def whole(array):
    return (array, WHOLE, None)


def columns_of(array, width, index=lambda g, me: (0, g)):
    return (array, (array.shape[0], width), index)


def tie(value, *after):
    def nothing(*refs):
        return None

    return pl.pallas_call(
        nothing,
        out_shape=jax.ShapeDtypeStruct(value.shape, value.dtype),
        in_specs=[ANY] * (1 + len(after)),
        out_specs=ANY,
        input_output_aliases={0: 0},
        name="tie",
    )(value, *after)


def zero_after(*after):
    return tie(jnp.zeros((1, 1, 1), bf16), *after)


def split_wide(value):
    return jnp.concatenate(split3(value), axis=1)


def spread_wide(groups, width, start):
    own = lax.shift_right_logical(iota((3 * groups, LANES), 1) + start, GROUP.bit_length() - 1)
    return (own == lax.rem(iota((3 * groups, LANES), 0), groups)).astype(bf16)


def moments(total, groups):
    counts = jnp.maximum(total[:, 2 * groups : 2 * groups + 1], 1.0) * float(GROUP)
    means = total[:, :groups] / counts
    variance = total[:, groups : 2 * groups] / counts - means * means
    return means, lax.rsqrt(variance + 1e-05), counts


def stats_kernel(tok_ref, valid_ref, segc_ref, segr_ref, prefix_ref, totals_ref):
    rows, width = tok_ref.shape
    groups = width // GROUP
    valid = valid_ref[...]
    masked = tok_ref[...].astype(f32) * valid
    low = masked.astype(bf16)
    square = masked * masked
    high = square.astype(bf16)
    rest = (square - high.astype(f32)).astype(bf16)
    second = group_pick(width, groups)
    sums = dot(low, group_pick(width, 0)) + dot(high, second) + dot(rest, second)
    sums = sums + jnp.where(iota((rows, LANES), 1) == 2 * groups, valid, 0.0)
    parts = split3(sums)
    earlier = (iota((rows, rows), 1) <= iota((rows, rows), 0)) & (segc_ref[...] == segr_ref[...])
    prefix_ref[...] = dot3(earlier.astype(f32).astype(bf16), parts)
    member = (iota((DOCS, rows), 0) == segr_ref[...]).astype(f32).astype(bf16)
    totals_ref[...] = dot3(member, parts)


def scan_ends(src_ref, a_ref, b_ref, end_ref, rows, ndim, reverse):
    half = ndim // 2
    for start in range(0, ndim, half):
        a = [a_ref[pl.ds((start + n) * SUB, SUB), :] for n in range(half)]
        b = [b_ref[pl.ds((start + n) * SUB, SUB), :] for n in range(half)]

        def step(i, state, a=a, b=b):
            t = rows - 1 - i if reverse else i
            x = src_ref[pl.ds(pl.multiple_of(t * SUB, SUB), SUB), :]
            fresh = []
            for n in range(half):
                re, im = state[2 * n], state[2 * n + 1]
                if reverse:
                    fresh += [a[n] * re + b[n] * im + x, a[n] * im - b[n] * re]
                else:
                    fresh += [a[n] * re - b[n] * im + x, a[n] * im + b[n] * re]
            return tuple(fresh)

        zero = jnp.zeros((SUB, LANES), f32)
        state = lax.fori_loop(0, rows, step, (zero,) * (2 * half), unroll=8)
        for n in range(half):
            end_ref[pl.ds((start + n) * SUB, SUB), :] = state[2 * n]
            end_ref[pl.ds((ndim + start + n) * SUB, SUB), :] = state[2 * n + 1]


def all_moments(prefix_ref, segc_ref, carry_ref, groups):
    total = prefix_ref[...] + jnp.where(segc_ref[...] == segc_ref[0:1, :], carry_ref[...], 0.0)
    return moments(total, groups)


def lane_rows(j, rows):
    return pl.ds(j, rows, stride=SUB)


def norm_kernel(tok_ref, valid_ref, segc_ref, prefix_ref, carry_ref, gain_ref, a_ref, b_ref,
                sent_ref, xs_ref, end_ref):
    rows, width = tok_ref.shape
    groups = width // GROUP
    ndim = a_ref.shape[0] // SUB
    means, scale, _ = all_moments(prefix_ref, segc_ref, carry_ref, groups)
    means, scale, valid = split_wide(means), split_wide(scale), valid_ref[...]
    for j in range(SUB):
        at = slice(j * LANES, (j + 1) * LANES)
        spread = spread_wide(groups, width, j * LANES)
        normed = (tok_ref[:, at].astype(f32) * valid - dot(means, spread)) * dot(scale, spread) * gain_ref[:, at]
        sent_ref[:, at] = normed.astype(bf16)
        xs_ref[lane_rows(j, rows), :] = normed
    scan_ends(xs_ref, a_ref, b_ref, end_ref, rows, ndim, False)


def mix_kernel(xs_ref, start_ref, a_ref, b_ref, g_ref, skip_ref, mixed_ref, sent_ref, keep_ref, state_ref):
    rows = xs_ref.shape[0] // SUB
    ndim = a_ref.shape[0] // SUB
    half = ndim // 2
    state_ref[...] = start_ref[...]

    def chunk(i, _):
        keep_ref[i] = state_ref[...]
        for start in range(0, ndim, half):
            re_at = [pl.ds((start + n) * SUB, SUB) for n in range(half)]
            im_at = [pl.ds((ndim + start + n) * SUB, SUB) for n in range(half)]
            a = [a_ref[at, :] for at in re_at]
            b = [b_ref[at, :] for at in re_at]
            g = [g_ref[at, :] for at in re_at]

            def step(k, state, start=start, a=a, b=b, g=g):
                at = pl.ds(pl.multiple_of((i * SPAN + k) * SUB, SUB), SUB)
                x = xs_ref[at, :]
                fresh, terms = [], []
                for n in range(half):
                    re, im = state[2 * n], state[2 * n + 1]
                    now = a[n] * re - b[n] * im + x
                    fresh += [now, a[n] * im + b[n] * re]
                    terms.append(g[n] * now)
                terms.append(skip_ref[...] * x if start == 0 else mixed_ref[at, :])
                while len(terms) > 1:
                    terms = [sum(terms[p : p + 2][1:], terms[p]) for p in range(0, len(terms), 2)]
                mixed_ref[at, :] = terms[0]
                return tuple(fresh)

            state = []
            for n in range(half):
                state += [state_ref[re_at[n], :], state_ref[im_at[n], :]]
            state = lax.fori_loop(0, SPAN, step, tuple(state), unroll=8)
            for n in range(half):
                state_ref[re_at[n], :] = state[2 * n]
                state_ref[im_at[n], :] = state[2 * n + 1]
        return 0

    lax.fori_loop(0, rows // SPAN, chunk, 0)

    def band(i, _):
        at = pl.ds(pl.multiple_of(i * BAND, BAND), BAND)
        for j in range(SUB):
            mixed = mixed_ref[pl.ds(i * (BAND * SUB) + j, BAND, stride=SUB), :]
            sent_ref[at, j * LANES : (j + 1) * LANES] = (mixed * sigmoid(mixed)).astype(bf16)
        return 0

    lax.fori_loop(0, rows // BAND, band, 0)


def back_ends_kernel(grad_ref, mixed_ref, a_ref, b_ref, drive_ref, end_ref):
    rows = grad_ref.shape[0]
    ndim = a_ref.shape[0] // SUB

    def band(i, _):
        at = pl.ds(pl.multiple_of(i * BAND, BAND), BAND)
        for j in range(SUB):
            where = pl.ds(i * (BAND * SUB) + j, BAND, stride=SUB)
            mixed = mixed_ref[where, :]
            sigma = sigmoid(mixed)
            slope = sigma * (1.0 + mixed * (1.0 - sigma))
            drive_ref[where, :] = grad_ref[at, j * LANES : (j + 1) * LANES].astype(f32) * slope
        return 0

    lax.fori_loop(0, rows // BAND, band, 0)
    scan_ends(drive_ref, a_ref, b_ref, end_ref, rows, ndim, True)


def back_scan_kernel(xs_ref, drive_ref, keep_ref, start_ref, sums_in_ref, a_ref, b_ref, g_ref, skip_ref,
                     dxs_ref, state_ref, sums_ref, hist_ref):
    ndim = a_ref.shape[0] // SUB
    rows = xs_ref.shape[0] // SUB
    part = 4
    count = rows // SPAN
    state_ref[...] = start_ref[...]
    sums_ref[...] = sums_in_ref[...]

    def chunk(c, _):
        i = count - 1 - c
        for start in range(0, ndim, part):
            re_at = [pl.ds((start + n) * SUB, SUB) for n in range(part)]
            im_at = [pl.ds((ndim + start + n) * SUB, SUB) for n in range(part)]
            last_at = [pl.ds((2 * ndim + start + n) * SUB, SUB) for n in range(part)]
            a = [a_ref[at, :] for at in re_at]
            b = [b_ref[at, :] for at in re_at]
            g = [g_ref[at, :] for at in re_at]

            def forward(k, state, a=a, b=b):
                x = xs_ref[pl.ds(pl.multiple_of((i * SPAN + k) * SUB, SUB), SUB), :]
                fresh = []
                for n in range(part):
                    re, im = state[2 * n], state[2 * n + 1]
                    hist_ref[k, pl.ds(2 * n * SUB, SUB), :] = re
                    hist_ref[k, pl.ds((2 * n + 1) * SUB, SUB), :] = im
                    fresh += [a[n] * re - b[n] * im + x, a[n] * im + b[n] * re]
                return tuple(fresh)

            state = []
            for n in range(part):
                state += [keep_ref[i, re_at[n], :], keep_ref[i, im_at[n], :]]
            lax.fori_loop(0, SPAN, forward, tuple(state), unroll=8)

            def backward(k, held, start=start, a=a, b=b, g=g):
                t = SPAN - 1 - k
                at = pl.ds(pl.multiple_of((i * SPAN + t) * SUB, SUB), SUB)
                x, drive = xs_ref[at, :], drive_ref[at, :]
                fresh, terms = [], []
                for n in range(part):
                    re, im, m_re, m_im, same = held[5 * n : 5 * n + 5]
                    now_re = a[n] * re + b[n] * im + drive
                    now_im = a[n] * im - b[n] * re
                    old_re = hist_ref[t, pl.ds(2 * n * SUB, SUB), :]
                    old_im = hist_ref[t, pl.ds((2 * n + 1) * SUB, SUB), :]
                    fresh += [
                        now_re,
                        now_im,
                        m_re + (now_re * old_re + now_im * old_im),
                        m_im + (now_im * old_re - now_re * old_im),
                        same + x * now_re,
                    ]
                    terms.append(g[n] * now_re)
                total = (terms[0] + terms[1]) + (terms[2] + terms[3])
                if start == 0:
                    dxs_ref[at, :] = total + skip_ref[...] * drive
                else:
                    dxs_ref[at, :] = total + dxs_ref[at, :]
                return tuple(fresh)

            held = []
            for n in range(part):
                held += [state_ref[re_at[n], :], state_ref[im_at[n], :]]
                held += [sums_ref[re_at[n], :], sums_ref[im_at[n], :], sums_ref[last_at[n], :]]
            held = lax.fori_loop(0, SPAN, backward, tuple(held), unroll=8)
            for n in range(part):
                state_ref[re_at[n], :] = held[5 * n]
                state_ref[im_at[n], :] = held[5 * n + 1]
                sums_ref[re_at[n], :] = held[5 * n + 2]
                sums_ref[im_at[n], :] = held[5 * n + 3]
                sums_ref[last_at[n], :] = held[5 * n + 4]
        return 0

    lax.fori_loop(0, count, chunk, 0)

    def skip_step(k, total):
        at = pl.ds(pl.multiple_of(k * SUB, SUB), SUB)
        return total + xs_ref[at, :] * drive_ref[at, :]

    last = pl.ds(3 * ndim * SUB, SUB)
    sums_ref[last, :] = lax.fori_loop(0, rows, skip_step, sums_ref[last, :], unroll=8)


def back_norm_kernel(*refs):
    dxs_refs, refs = refs[:-12], refs[-12:]
    (grad_ref, tok_ref, valid_ref, segc_ref, segr_ref, prefix_ref, carry_ref, gain_ref,
     dn_ref, dgain_ref, suffix_ref, totals_ref) = refs
    rows, width = tok_ref.shape
    groups = width // GROUP
    means, scale, counts = all_moments(prefix_ref, segc_ref, carry_ref, groups)
    wide_means, wide_scale, valid = split_wide(means), split_wide(scale), valid_ref[...]
    plain, leaning = jnp.zeros((rows, LANES), f32), jnp.zeros((rows, LANES), f32)
    for j in range(SUB):
        at = slice(j * LANES, (j + 1) * LANES)
        spread = spread_wide(groups, width, j * LANES)
        own = lax.shift_right_logical(iota((LANES, LANES), 0) + j * LANES, GROUP.bit_length() - 1)
        pick = (own == iota((LANES, LANES), 1)).astype(bf16)
        centred = tok_ref[:, at].astype(f32) * valid - dot(wide_means, spread)
        ema = [ref[lane_rows(j, ref.shape[0] // SUB), :] for ref in dxs_refs]
        dn = grad_ref[:, at].astype(f32) + jnp.concatenate(ema, axis=0)
        dgain_ref[:, at] = jnp.sum(dn * centred * dot(wide_scale, spread), axis=0, keepdims=True)
        dn = dn * gain_ref[:, at]
        dn_ref[:, at] = dn
        plain = plain + dot3_left(split3(dn), pick)
        leaning = leaning + dot3_left(split3(dn * centred), pick)
    plain, leaning = plain[:, :groups], leaning[:, :groups]
    d_variance = -0.5 * leaning * scale * scale * scale
    d_second = d_variance / counts
    d_first = (-scale * plain - 2.0 * means * d_variance) / counts
    flow = jnp.concatenate([d_first, d_second, jnp.zeros((rows, LANES - 2 * groups), f32)], axis=1)
    parts = split3(flow)
    later = (iota((rows, rows), 1) >= iota((rows, rows), 0)) & (segc_ref[...] == segr_ref[...])
    suffix_ref[...] = dot3(later.astype(f32).astype(bf16), parts)
    member = (iota((DOCS, rows), 0) == segr_ref[...]).astype(f32).astype(bf16)
    totals_ref[...] = dot3(member, parts)


def input_kernel(dn_ref, suffix_ref, back_ref, tok_ref, valid_ref, segc_ref, prefix_ref, carry_ref, middle_ref, out_ref):
    rows, width = tok_ref.shape
    groups = width // GROUP
    _, scale, _ = all_moments(prefix_ref, segc_ref, carry_ref, groups)
    flow = suffix_ref[...] + jnp.where(segc_ref[...] == segc_ref[rows - 1 : rows, :], back_ref[...], 0.0)
    scale, valid = split_wide(scale), valid_ref[...]
    first, second = split_wide(flow[:, :groups]), split_wide(flow[:, groups : 2 * groups])
    for j in range(SUB):
        at = slice(j * LANES, (j + 1) * LANES)
        spread = spread_wide(groups, width, j * LANES)
        masked = tok_ref[:, at].astype(f32) * valid
        grad = dn_ref[:, at] * dot(scale, spread) + dot(first, spread) + 2.0 * masked * dot(second, spread)
        out_ref[:, at] = valid * (middle_ref[:, at] + grad)


def swap(value, axis, bit):
    count = lax.axis_size(axis)
    return lax.ppermute(value, axis, [(i, i ^ bit) for i in range(count)])


def gather_small(value, axis):
    index, count = lax.axis_index(axis), lax.axis_size(axis)
    value, bit = value[None], 1
    while bit < count:
        other = swap(value, axis, bit)
        upper = (index & bit) != 0
        value = jnp.concatenate([jnp.where(upper, other, value), jnp.where(upper, value, other)], axis=0)
        bit *= 2
    return value


def cmul(left, right):
    return (left[0] * right[0] - left[1] * right[1], left[0] * right[1] + left[1] * right[0])


def state_before(ends, hop, axis, reverse, hold=None):
    index, count = lax.axis_index(axis), lax.axis_size(axis)
    if reverse:
        index = count - 1 - index
    half = ends.shape[0] // 2
    before = (jnp.zeros_like(ends[:half]), jnp.zeros_like(ends[:half]))
    reach = (jnp.ones_like(hop[0]), jnp.zeros_like(hop[1]))
    bit = 1
    while bit < count:
        waits = hold[bit]() if hold and bit in hold else ()
        other = swap(tie(ends, *waits) if waits else ends, axis, bit)
        upper = (index & bit) != 0
        far, own = (other[:half], other[half:]), (ends[:half], ends[half:])
        moved = cmul(reach, far)
        before = tuple(v + jnp.where(upper, w, 0.0) for v, w in zip(before, moved))
        if bit * 2 < count:
            lower = tuple(jnp.where(upper, v, w) for v, w in zip(far, own))
            higher = tuple(jnp.where(upper, w, v) for v, w in zip(far, own))
            carried = cmul(hop, lower)
            ends = jnp.concatenate([carried[0] + higher[0], carried[1] + higher[1]], axis=0)
            longer = cmul(reach, hop)
            reach = tuple(jnp.where(upper, v, w) for v, w in zip(longer, reach))
            hop = cmul(hop, hop)
        bit *= 2
    return jnp.concatenate(before, axis=0)


def ema_params(full, ndim, rows):
    full = jnp.transpose(full, (1, 0, 2))
    full = full.reshape(full.shape[0], SUB, -1)
    rate, angle, input_w, output_w = (full[i * ndim : (i + 1) * ndim] for i in range(4))
    gain, skip = full[4 * ndim], full[4 * ndim + 1]
    base = jnp.sqrt(rate * (2.0 - rate))
    cos, sin = jnp.cos(angle), jnp.sin(angle)
    a, b = (1.0 - rate) * cos, (1.0 - rate) * sin
    hop, steps = (a, b), 1
    while steps < rows:
        hop, steps = cmul(hop, hop), steps * 2
    return dict(rate=rate, input_w=input_w, output_w=output_w, gain=gain, skip=skip, base=base,
                cos=cos, sin=sin, a=a, b=b, coeff=base * input_w, hop=hop)


def ema_param_grads(par, sums):
    ndim = par["rate"].shape[0]
    m_re, m_im, same = sums[:ndim], sums[ndim : 2 * ndim], sums[2 * ndim : 3 * ndim]
    weight = par["output_w"] * par["coeff"]
    d_a, d_b = weight * m_re, weight * m_im
    d_coeff = par["output_w"] * same
    d_output = par["coeff"] * same
    d_input = par["base"] * d_coeff
    d_rate = d_coeff * par["input_w"] * (1.0 - par["rate"]) / par["base"] - par["cos"] * d_a - par["sin"] * d_b
    d_angle = par["a"] * d_b - par["b"] * d_a
    return d_rate, d_angle, d_input, d_output


def mul_t(left, right):
    return lax.dot_general(left, right, (((1,), (1,)), ((), ())), preferred_element_type=f32)


def t_mul(left, right):
    return lax.dot_general(left, right, (((0,), (0,)), ((), ())), preferred_element_type=f32)


def silu_grad(value):
    sigma = sigmoid(value)
    return sigma * (1.0 + value * (1.0 - sigma))


def bits_of(count):
    return count.bit_length() - 1


class Part:
    def __init__(self, source, take, width, rows, lower=0, column=0):
        self.arrays, self.owners, self.top = source.arrays, source.owners, source.top
        self.take, self.width, self.rows, self.lower, self.column = take, width, rows, lower, column

    def copies(self, refs, where, me, sem, span=None, near=None):
        made = []
        first, width = (0, self.width) if span is None else span
        for ref, owners in zip(refs, self.owners):
            block = ref.shape[1]
            for slot, owner in enumerate(owners):
                if near is not None and near != (owner < (1 << self.top)):
                    continue
                start = (me ^ owner) * self.rows + self.lower
                start = pl.multiple_of(start, math.gcd(self.rows, block)) if len(owners) > 1 else 0
                source = ref.at[slot, :, pl.ds(self.take + first, width)]
                to = where.at[pl.ds(start, block), pl.ds(self.column + first, width)]
                made.append(pltpu.make_async_copy(source, to, sem))
        return made


class Weight:
    def __init__(self, *parts):
        self.parts, self.arrays, self.places = parts, [], []
        self.split, self.top = len(parts[0].owners[0]) > 1, parts[0].top
        self.nears = (True, False) if self.split else (None,)
        for part in parts:
            place = []
            for array in part.arrays:
                same = [n for n, known in enumerate(self.arrays) if known is array]
                if not same:
                    self.arrays.append(array)
                place.append(same[0] if same else len(self.arrays) - 1)
            self.places.append(place)

    def copies(self, refs, where, me, sem, which=None, span=None, near=None):
        made = []
        for n, (part, place) in enumerate(zip(self.parts, self.places)):
            if which is None or which == n:
                made += part.copies([refs[n] for n in place], where, me, sem, span, near)
        return made


class Gather:
    def __init__(self, shard, order):
        self.order = order
        self.top = max(order or (0,))
        if order is None:
            full = lax.all_gather(shard, AXES, axis=0, tiled=True)
            self.arrays, self.owners = [full[None]], [[0]]
            return
        self.arrays, self.owners, self.place = [shard[None]], [[0]], 0

    def step(self, after=()):
        if self.order is None:
            return ()
        bit = self.order[self.place]
        mine = [tie(value, *after) for value in self.arrays] if after else self.arrays
        others = [swap_bit(value, bit) for value in mine]
        moved = [[owner ^ (1 << bit) for owner in row] for row in self.owners]
        if self.place < len(self.order) - 2:
            self.arrays = [jnp.concatenate([mine[0], others[0]], axis=0)]
            self.owners = [self.owners[0] + moved[0]]
        else:
            self.arrays, self.owners = mine + others, self.owners + moved
        self.place += 1
        return (self.arrays[-1],)

def swap_bit(value, bit):
    dp_bits = bits_of(lax.axis_size("chip")) + 1
    if bit == 0:
        return swap(value, "core", 1)
    if bit < dp_bits:
        return swap(value, "chip", 1 << (bit - 1))
    return swap(value, "seq", 1 << (bit - dp_bits))


def add_low(left, right, zero):
    return left + right + zero


class Reduce:
    def __init__(self, keep, send, order):
        self.keep, self.send, self.order, self.sent = keep, send, order, keep
        self.pins = () if order is None else (send,)
        self.left = list(order or ())
        self.other = None
        if order is None:
            self.keep = lax.psum_scatter(keep[0], ("seq", "chip"), scatter_dimension=0, tiled=True)[None]
        else:
            self.begin()

    def begin(self):
        self.other = swap_bit(self.send, self.left.pop(0)) if self.left else None

    def halves(self, after=()):
        half = self.keep.shape[0] // 2
        zero = zero_after(*after) if after else jnp.zeros((1, 1, 1), bf16)
        return add_low(self.keep[:half], self.other[:half], zero), add_low(self.keep[half:], self.other[half:], zero)

    def step(self, *after):
        if self.other is None:
            return ()
        if not self.left:
            zero = zero_after(*after) if after else 0.0
            self.keep = self.keep.astype(f32) + self.other.astype(f32) + zero
            self.other = None
            return (self.keep,)
        self.keep, self.send = self.halves(after)
        self.begin()
        return (self.send,)

    def finish(self, core, widths, *after):
        while self.other is not None:
            self.step(*after)
        chip_rows = self.keep[0].astype(f32)
        rows = chip_rows.shape[0] // 2
        lower, upper = chip_rows[:rows], chip_rows[rows:]
        own = jnp.where(core == 0, lower, upper)
        other = swap_bit(jnp.where(core == 0, upper, lower).astype(bf16), 0).astype(f32)
        outs, at = [], 0
        for width in widths:
            mine, theirs = own[:, at : at + width], other[:, at : at + width]
            outs.append(
                jnp.concatenate([jnp.where(core == 0, mine, theirs), jnp.where(core == 0, theirs, mine)], axis=1)
            )
            at += width
        return outs


def merge(first, second, *after):
    if first.order is None:
        both = Reduce.__new__(Reduce)
        both.keep = jnp.concatenate([first.keep, second.keep], axis=2)
        both.order, both.left, both.other, both.pins = None, [], None, ()
        return both
    parts = [first.halves(after), second.halves(after)]
    keep = jnp.concatenate([part[0] for part in parts], axis=2)
    send = jnp.concatenate([part[1] for part in parts], axis=2)
    return Reduce(keep, send, first.left)


def allowed_pairs(segc_ref, segr_ref, validr_ref):
    rows = segc_ref.shape[0]
    query, key = iota((rows, rows), 0), iota((rows, rows), 1)
    same = segc_ref[...] == segr_ref[...]
    usable = validr_ref[...] > 0.5
    return (key <= query) & same & (usable | (key == query))


def attention_kernel(weight1, tile, *refs):
    n1 = len(weight1.arrays)
    me_ref, norm_ref, mix_ref, segc_ref, segr_ref, validr_ref, qg_ref, qb_ref, kg_ref = refs[:9]
    w1_refs = refs[9 : 9 + n1]
    shared_ref, q_ref, k_ref, lse_ref, vpre_ref, values_ref, gpre_ref, att_ref, gated_ref, w1, probs_ref, sem1 = refs[9 + n1 :]
    me = me_ref[0]
    values_width = values_ref.shape[1]
    copies1 = weight1.copies(w1_refs, w1, me, sem1)
    for copy in copies1:
        copy.start()
    for copy in copies1:
        copy.wait()
    shared = dot(mix_ref[...], w1[:, 2 * values_width :])
    shared_ref[...] = shared
    queries = (shared * qg_ref[...] + qb_ref[...]).astype(bf16)
    keys = (shared * kg_ref[...]).astype(bf16)
    q_ref[...] = queries
    k_ref[...] = keys
    scores = mul_t(queries, keys) * (queries.shape[1] ** -0.5)
    masked = jnp.where(allowed_pairs(segc_ref, segr_ref, validr_ref), scores, -1e30)
    top = jnp.max(masked, axis=1, keepdims=True)
    weights = jnp.exp(masked - top)
    total = jnp.sum(weights, axis=1, keepdims=True)
    probs_ref[...] = (weights / total).astype(bf16)
    lse_ref[...] = top + jnp.log(total)

    def columns(i, _):
        at = pl.ds(pl.multiple_of(i * tile, tile), tile)
        value_pre = dot(norm_ref[...], w1[:, at])
        vpre_ref[:, at] = value_pre.astype(bf16)
        values = (value_pre * sigmoid(value_pre)).astype(bf16)
        values_ref[:, at] = values
        gate_pre = dot(mix_ref[...], w1[:, pl.ds(pl.multiple_of(values_width + i * tile, tile), tile)])
        gpre_ref[:, at] = gate_pre.astype(bf16)
        attended = dot(probs_ref[...], values)
        att_ref[:, at] = attended.astype(bf16)
        gated_ref[:, at] = (attended * (gate_pre * sigmoid(gate_pre))).astype(bf16)
        return 0

    lax.fori_loop(0, values_width // tile, columns, 0)


def project_kernel(weight2, *refs):
    n2 = len(weight2.arrays)
    me_ref, gated_ref, tok_ref, valid_ref, fg_ref = refs[:5]
    middle_ref, ffn_ref, inv_ref, w2, sems = refs[5 + n2 :]
    width = tok_ref.shape[1]
    edge = width // 2
    for part in range(2):
        for copy in weight2.copies(refs[5 : 5 + n2], w2, me_ref[0], sems.at[part], span=(part * edge, edge)):
            copy.start()
    square = jnp.zeros((tok_ref.shape[0], 1), f32)
    for part in range(2):
        for copy in weight2.copies(refs[5 : 5 + n2], w2, me_ref[0], sems.at[part], span=(part * edge, edge)):
            copy.wait()
        at = slice(part * edge, (part + 1) * edge)
        middle = tok_ref[:, at].astype(f32) * valid_ref[...] + dot(gated_ref[...], w2[:, at])
        middle_ref[:, at] = middle
        square = square + jnp.sum(middle * middle, axis=1, keepdims=True)
    inverse = lax.rsqrt(square * (1.0 / width) + 1e-05)
    inv_ref[...] = inverse
    ffn_ref[...] = (middle_ref[...] * inverse * fg_ref[...]).astype(bf16)


def hidden_kernel(weight3, weight4, me_ref, ffn_ref, cot_ref, *refs):
    n3, n4 = len(weight3.arrays), len(weight4.arrays)
    hid_ref, near_ref, far_ref, w3, w4, sems = refs[n3 + n4 :]
    step, core = pl.program_id(0), me_ref[1]
    half = hid_ref.shape[1]

    def copies(rel, n):
        base = pl.multiple_of((core ^ rel) * half, half)
        if n < 2:
            return weight3.copies(refs[:n3], w3, me_ref[0], sems.at[rel, n], n, (base, half))
        return weight4.copies(refs[n3 : n3 + n4], w4, me_ref[0], sems.at[rel, n], near=None)

    @pl.when(step == 0)
    def _():
        for rel, n in ((0, 0), (0, 1), (0, 2), (1, 0), (1, 1)):
            for copy in copies(rel, n):
                copy.start()

    def arrived(n):
        for rel in range(2):
            if (rel, n) != (1, 2):
                @pl.when(step == rel)
                def _():
                    for copy in copies(rel, n):
                        copy.wait()

    base = pl.multiple_of((core ^ step) * half, half)
    arrived(0)
    gate = dot(ffn_ref[...], w3[:, pl.ds(base, half)])
    sigma = sigmoid(gate)
    act = gate * sigma
    slope = sigma + act * (1.0 - sigma)
    arrived(1)
    up = dot(ffn_ref[...], w3[:, pl.ds(pl.multiple_of(base + 2 * half, half), half)])
    hid_ref[...] = (act * up).astype(bf16)
    arrived(2)
    grad = mul_t(cot_ref[...], w4[pl.ds(base, half), :])
    grad_gate = (grad * up * slope).astype(bf16)
    grad_up = (grad * act).astype(bf16)

    @pl.when(step == 0)
    def _():
        near_ref[:, :half] = grad_gate
        near_ref[:, half:] = grad_up

    @pl.when(step == 1)
    def _():
        far_ref[:, :half] = grad_gate
        far_ref[:, half:] = grad_up


def out_kernel(weight4, me_ref, hid_ref, middle_ref, *refs):
    n4 = len(weight4.arrays)
    out_ref, w4, sems = refs[n4:]
    width, half = middle_ref.shape[1], hid_ref.shape[1] // 2
    starts = [pl.multiple_of((me_ref[1] ^ rel) * half, half) for rel in range(2)]
    edge = width // 2
    for part in range(2):
        for copy in weight4.copies(refs[:n4], w4, me_ref[0], sems.at[part], span=(part * edge, edge)):
            copy.start()
    for part in range(2):
        for copy in weight4.copies(refs[:n4], w4, me_ref[0], sems.at[part], span=(part * edge, edge)):
            copy.wait()
        at = slice(part * edge, (part + 1) * edge)
        total = middle_ref[:, at]
        for rel in range(2):
            total = total + dot(hid_ref[:, rel * half : (rel + 1) * half], w4[pl.ds(starts[rel], half), at])
        out_ref[:, at] = total.astype(bf16)


def ffn_back_kernel(weight3, *refs):
    n3 = len(weight3.arrays)
    me_ref, near_ref, far_ref, middle_ref, inv_ref, cot_ref, fg_ref = refs[:7]
    gmid_ref, low_own, low_oth, low_ref, dfg_ref, w3, gin_ref, sems = refs[7 + n3 :]
    me, core = me_ref[0], me_ref[1]
    rows, width = middle_ref.shape
    half = near_ref.shape[1] // 2
    parts, edge = (2, width // 2) if weight3.split else (1, width)
    for part in range(parts):
        for copy in weight3.copies(refs[7 : 7 + n3], w3, me, sems.at[part], near=weight3.nears[part]):
            copy.start()
    starts = [pl.multiple_of((core ^ rel) * half, half) for rel in range(2)]
    lean = jnp.zeros((rows, 1), f32)
    for part in range(parts):
        for copy in weight3.copies(refs[7 : 7 + n3], w3, me, sems.at[part], near=weight3.nears[part]):
            copy.wait()
        base = pl.multiple_of((lax.shift_right_logical(me, weight3.top) ^ part) * edge, edge) if parts == 2 else 0
        at = pl.ds(base, edge)
        grad = jnp.zeros((rows, edge), f32)
        for rel, ref in enumerate((near_ref, far_ref)):
            grad = grad + mul_t(ref[:, :half], w3[at, pl.ds(starts[rel], half)])
            grad = grad + mul_t(ref[:, half:], w3[at, pl.ds(pl.multiple_of(starts[rel] + 2 * half, half), half)])
        normal = middle_ref[:, at] * inv_ref[...]
        dfg_ref[:, at] = jnp.sum(grad * normal, axis=0, keepdims=True)
        grad = grad * fg_ref[:, at]
        gin_ref[:, at] = grad
        lean = lean + jnp.sum(grad * normal, axis=1, keepdims=True)
    lean = lean * (1.0 / width)
    inverse = inv_ref[...]
    grad_middle = cot_ref[...].astype(f32) + inverse * (gin_ref[...] - middle_ref[...] * inverse * lean)
    gmid_ref[...] = grad_middle
    low_ref[...] = grad_middle.astype(bf16)
    part = width // 2
    low_own[...] = low_ref[:, pl.ds(pl.multiple_of(core * part, part), part)]
    low_oth[...] = low_ref[:, pl.ds(pl.multiple_of((1 - core) * part, part), part)]


def attention_back_kernel(weight2, tile, *refs):
    n2 = len(weight2.arrays)
    (me_ref, low_ref, q_ref, k_ref, lse_ref, shared_ref, vpre_ref, values_ref, gpre_ref, att_ref, segc_ref, segr_ref,
     validr_ref, qg_ref, kg_ref) = refs[:15]
    (gv_ref, gr_ref, gv_own, gv_oth, gr_own, gr_oth, dgain_ref, w2, low_probs_ref, gprobs_ref, gsh_ref, sem2) = refs[15 + n2 :]
    core = me_ref[1]
    rows = low_ref.shape[0]
    values_width = values_ref.shape[1]
    copies2 = weight2.copies(refs[15 : 15 + n2], w2, me_ref[0], sem2)
    for copy in copies2:
        copy.start()
    queries, keys = q_ref[...], k_ref[...]
    factor = queries.shape[1] ** -0.5
    scores = mul_t(queries, keys) * factor
    masked = jnp.where(allowed_pairs(segc_ref, segr_ref, validr_ref), scores, -1e30)
    probs = jnp.exp(masked - lse_ref[...])
    low_probs_ref[...] = probs.astype(bf16)
    gprobs_ref[...] = jnp.zeros((rows, rows), f32)
    for copy in copies2:
        copy.wait()

    def columns(i, _):
        at = pl.ds(pl.multiple_of(i * tile, tile), tile)
        grad = mul_t(low_ref[...], w2[at, :]).astype(bf16).astype(f32)
        gate_pre = gpre_ref[:, at].astype(f32)
        sigma = sigmoid(gate_pre)
        act = gate_pre * sigma
        grad_att = (grad * act).astype(bf16)
        gr_ref[:, at] = (grad * att_ref[:, at].astype(f32) * (sigma + act * (1.0 - sigma))).astype(bf16)
        gprobs_ref[...] += mul_t(grad_att, values_ref[:, at])
        grad_values = t_mul(low_probs_ref[...], grad_att)
        gv_ref[:, at] = (grad_values * silu_grad(vpre_ref[:, at].astype(f32))).astype(bf16)
        return 0

    lax.fori_loop(0, values_width // tile, columns, 0)
    grad_probs = gprobs_ref[...]
    grad_scores = (probs * (grad_probs - jnp.sum(probs * grad_probs, axis=1, keepdims=True))).astype(bf16)
    grad_queries = dot(grad_scores, keys) * factor
    grad_keys = t_mul(grad_scores, queries) * factor
    shared = shared_ref[...]
    dgain_ref[0:1, :] = jnp.sum(grad_queries * shared, axis=0, keepdims=True)
    dgain_ref[1:2, :] = jnp.sum(grad_queries, axis=0, keepdims=True)
    dgain_ref[2:3, :] = jnp.sum(grad_keys * shared, axis=0, keepdims=True)
    gsh_ref[...] = (grad_queries * qg_ref[...] + grad_keys * kg_ref[...]).astype(bf16)
    gr_ref[:, values_width:] = gsh_ref[...]
    for source, own, other, start in (
        (gv_ref, gv_own, gv_oth, 0), (gr_ref, gr_own, gr_oth, 0), (gsh_ref, gr_own, gr_oth, values_width // 2)
    ):
        part = (values_width if start == 0 else source.shape[1]) // 2
        own[:, start : start + part] = source[:, pl.ds(pl.multiple_of(core * part, part), part)]
        other[:, start : start + part] = source[:, pl.ds(pl.multiple_of((1 - core) * part, part), part)]


def sent_back_kernel(weight1, *refs):
    n1 = len(weight1.arrays)
    me_ref, gv_ref, gr_ref = refs[:3]
    gmix_ref, gnorm_ref, w1, sems = refs[3 + n1 :]
    me, width, values_width = me_ref[0], gmix_ref.shape[1], gv_ref.shape[1]
    parts, edge = (2, width // 2) if weight1.split else (1, width)
    for part in range(parts):
        for copy in weight1.copies(refs[3 : 3 + n1], w1, me, sems.at[part], near=weight1.nears[part]):
            copy.start()
    for part in range(parts):
        for copy in weight1.copies(refs[3 : 3 + n1], w1, me, sems.at[part], near=weight1.nears[part]):
            copy.wait()
        base = pl.multiple_of((lax.shift_right_logical(me, weight1.top) ^ part) * edge, edge) if parts == 2 else 0
        at = pl.ds(base, edge)
        gmix_ref[:, at] = mul_t(gr_ref[...], w1[at, values_width:]).astype(bf16)
        gnorm_ref[:, at] = mul_t(gv_ref[...], w1[at, :values_width]).astype(bf16)


def weight_grad_kernel(halves, order, blocks, block, me_ref, own, other, mine, theirs, *refs):
    keep, send = refs[0], refs[1]
    held, sems = refs[-2:]
    chip, core = lax.shift_right_logical(me_ref[0], 1), me_ref[1]
    tile, span = own.shape[1], mine.shape[1]
    step, steps = pl.program_id(0), pl.num_programs(0)
    strips = lax.div(steps, halves)
    rel = lax.div(step, strips)
    base = ((core ^ rel) if halves == 2 else rel) * (strips * tile) + lax.rem(step, strips) * tile
    slot = lax.rem(step, 2)
    parts = tile // block

    def done(slot):
        for s in range(parts):
            pltpu.make_async_copy(held.at[slot, pl.ds(s * block, block)], keep.at[0], sems.at[slot]).wait()

    @pl.when(step >= 2)
    def _():
        done(slot)

    out = t_mul(own[...], mine[...]) + t_mul(other[...], theirs[...])
    held[slot] = out.astype(bf16)
    for s in range(parts):
        rel_chip = (lax.div(base, block) + s) ^ chip
        place = 0
        for p, bit in enumerate(order):
            place = place | ((lax.shift_right_logical(rel_chip, bit - 1) & 1) << (len(order) - 1 - p))
        index = place & (blocks // 2 - 1)
        source = held.at[slot, pl.ds(s * block, block)]

        @pl.when(place < blocks // 2)
        def _():
            pltpu.make_async_copy(source, keep.at[index], sems.at[slot]).start()

        @pl.when(place >= blocks // 2)
        def _():
            pltpu.make_async_copy(source, send.at[index], sems.at[slot]).start()

    @pl.when(step == steps - 1)
    def _():
        done(slot)
        done(1 - slot)


def plain_grad_kernel(halves, me_ref, own, other, mine, theirs, keep):
    keep[0] = (t_mul(own[...], mine[...]) + t_mul(other[...], theirs[...])).astype(bf16)


def weight_grad(left, right, order, me, chips, name, halves=1, part=(0, 1), micros=6, after=()):
    total, span = left[0].shape[1], right[0].shape[1] // part[1]
    rows = left[0].shape[0]
    half = total // halves
    block = total // chips
    if order is None:
        tile = math.gcd(half, 256)
    else:
        tile = math.lcm(block, LANES)
        while tile < 512 and half % (2 * tile) == 0 and half // (2 * tile) >= 2 // halves:
            tile *= 2
    strips = half // tile
    far = (lambda g, me: (0, g)) if halves == 1 else (lambda g, me: (0, lax.rem(g + strips, 2 * strips)))
    args = [
        columns_of(left[0], tile), columns_of(left[1], tile, far), columns_of(right[0], span, lambda g, me: (0, part[0])),
        columns_of(right[1], span, lambda g, me: (0, part[0])),
    ]
    if order is None:
        place = (lambda g, me: (0, g, 0)) if halves == 1 else (
            lambda g, me: (0, (me[1] ^ lax.div(g, strips)) * strips + lax.rem(g, strips), 0))
        (keep,) = grid_call(
            functools.partial(plain_grad_kernel, halves), [((1, total, span), bf16, (1, tile, span), place)], args,
            halves * strips, me, name=name, micros=micros, after=after)
        return Reduce(keep, None, None)
    keep, send = grid_call(
        functools.partial(weight_grad_kernel, halves, order, chips, block),
        [((chips // 2, block, span), bf16, None, None)] * 2, args, halves * strips, me,
        scratch=[pltpu.VMEM((2, tile, span), bf16), pltpu.SemaphoreType.DMA((2,))], name=name, micros=micros, after=after)
    return Reduce(keep, send, order)


def exchange_start(pack, totals, axis, hold):
    index, count = lax.axis_index(axis), lax.axis_size(axis)
    lanes = pack.shape[1]
    rows = pack.shape[0]
    full, totals_shape = pack, totals.shape
    totals = totals.reshape(-1, lanes)
    before, bit = jnp.zeros_like(totals), 1
    while bit < count:
        goes = jnp.concatenate([totals, full], axis=0)
        other = swap(tie(goes, *hold) if hold and bit == 2 else goes, axis, bit)
        upper = (index & bit) != 0
        far_totals, far = other[: totals.shape[0]], other[totals.shape[0] :]
        before = before + jnp.where(upper, far_totals, 0.0)
        totals = totals + far_totals
        full = jnp.concatenate([jnp.where(upper, far, full), jnp.where(upper, full, far)], axis=0)
        bit *= 2
    return full.reshape(count, rows, lanes), before.reshape(totals_shape)


def exchange_end(pack, totals, axis):
    index, count = lax.axis_index(axis), lax.axis_size(axis)
    lanes = pack.shape[2]
    totals_shape = totals.shape
    totals = totals.reshape(-1, lanes)
    rows = totals.shape[0]
    after, bit = jnp.zeros_like(totals), 1
    while bit < count:
        upper = (index & bit) != 0
        pairs = pack.reshape((pack.shape[0] // 2, 2) + pack.shape[1:])
        goes = jnp.where(upper, pairs[:, 0], pairs[:, 1])
        stays = jnp.where(upper, pairs[:, 1], pairs[:, 0])
        other = swap(jnp.concatenate([totals, goes.reshape(-1, lanes)], axis=0), axis, bit)
        after = after + jnp.where(upper, 0.0, other[:rows])
        totals = totals + other[:rows]
        pack = stays + other[rows:].reshape(stays.shape)
        bit *= 2
    return pack[0], after.reshape(totals_shape)


def sum_over(value, axis):
    bit = 1
    while bit < lax.axis_size(axis):
        value = value + swap(value, axis, bit)
        bit *= 2
    return value


def on_device(tokens, cotangent, segment_ids, pad_mask, w_z, w_v, w_r, w_h, w_gate, w_up, w_down, q_gain, q_bias,
              k_gain, ffn_gain, norm_gain, ema_rate, ema_angle, ema_input, ema_output, ema_skip):
    rows, width = tokens.shape[1:]
    seq_count, dp_count = lax.axis_size("seq"), 2 * lax.axis_size("chip")
    seq_index, core = lax.axis_index("seq"), lax.axis_index("core")
    dp_index = lax.axis_index("chip") * 2 + core
    devices = seq_count * dp_count
    chips = devices // 2
    fits = all(value.shape[0] % 16 == 0 for value in (w_z, w_h, w_down))
    dp_bits, all_bits = bits_of(dp_count), bits_of(devices)
    inner = list(range(1, dp_bits))
    first_seq, rest_seq = [dp_bits], list(range(all_bits - 1, dp_bits, -1))
    if fits:
        gather_a = rest_seq + first_seq + inner + [0]
        gather_b = rest_seq + inner + first_seq + [0]
        gather_c = inner + first_seq + rest_seq + [0]
        reduce_a, reduce_b = gather_a[-2::-1], gather_b[-2::-1]
        me = jnp.stack([seq_index * dp_count + dp_index, core]).astype(jnp.int32)
    else:
        gather_a = gather_b = gather_c = reduce_a = reduce_b = None
        me = jnp.stack([core * 0, core]).astype(jnp.int32)
    values_width, hidden_width = w_v.shape[1], w_gate.shape[1]
    z_width = w_z.shape[1]
    low = lambda *parts: jnp.concatenate([part.astype(bf16) for part in parts], axis=1)
    short = w_v.shape[0]
    if fits:
        get_v = Gather(low(w_v, w_h[:short]), gather_a)
        get_r = Gather(low(w_r, w_z, w_h[short:]), gather_b)
    else:
        get_v, get_r = Gather(low(w_v), None), Gather(low(w_r, w_z), None)
    get_gate, get_up = Gather(low(w_gate), gather_a), Gather(low(w_up), gather_b)
    first_v, first_r = get_v.step(), get_r.step()
    get_down = Gather(low(w_down), gather_c)
    first_down = get_down.step()

    row_segs = lax.dynamic_slice_in_dim(segment_ids[0], seq_index * rows, rows)
    row_valid = lax.dynamic_slice_in_dim(pad_mask[0], seq_index * rows, rows).astype(f32)
    valid_col, seg_col, seg_row, valid_row = row_valid[:, None], row_segs[:, None], row_segs[None], row_valid[None]
    prefix, totals = kernel_call(
        stats_kernel, [((rows, LANES), f32), ((DOCS, LANES), f32)], [tokens[0], valid_col, seg_col, seg_row],
        name="stats", micros=5,
    )

    ndim, lanes = ema_rate.shape[1], norm_gain.shape[0]
    gains = jnp.concatenate([q_gain, q_bias, k_gain, ffn_gain])[None].astype(bf16).astype(f32)
    gains = gather_small(gather_small(gains, "core"), "chip").reshape(-1)
    size = gains.shape[0]
    extra = -(-size // lanes)
    gains = jnp.pad(gains, (0, extra * lanes - size)).reshape(extra, lanes)
    pack = jnp.concatenate(
        [ema_rate.T, ema_angle.T, ema_input.T, ema_output.T, norm_gain[None], ema_skip[None], gains], axis=0
    )
    full, before = exchange_start(pack, totals, "seq", first_v + first_r)
    carry = lax.dynamic_slice_in_dim(before, row_segs[0], 1)
    gains = full[:, 4 * ndim + 2 :].reshape(seq_count, -1)[:, :size].reshape(devices, -1)
    zs, fs = q_gain.shape[0], ffn_gain.shape[0]
    full_qg = gains[:, :zs].reshape(1, -1)
    full_qb = gains[:, zs : 2 * zs].reshape(1, -1)
    full_kg = gains[:, 2 * zs : 3 * zs].reshape(1, -1)
    full_fg = gains[:, 3 * zs :].reshape(1, -1)
    par = ema_params(full[:, : 4 * ndim + 2], ndim, rows)
    flat = lambda value: value.reshape(-1, LANES)
    a_flat, b_flat, g_flat = flat(par["a"]), flat(par["b"]), flat(par["output_w"] * par["coeff"])
    gain_row = par["gain"].reshape(1, width)
    seq_steps = len(rest_seq)
    for _ in range(seq_steps - 1):
        deep_v, deep_r = get_v.step(), get_r.step()
    for _ in inner[1:]:
        get_down.step()
    second_down = get_down.step(first_v)
    sent_norm, xs, ends = kernel_call(
        norm_kernel,
        [((rows, width), bf16), ((rows * SUB, LANES), f32), ((2 * ndim * SUB, LANES), f32)],
        [tokens[0], valid_col, seg_col, prefix, carry, gain_row, a_flat, b_flat],
        name="norm", micros=13, after=first_v + first_r + first_down,
    )
    middle_v, middle_r = get_v.step((ends,)), get_r.step((ends,))
    first_gate, first_up = get_gate.step(deep_v + (ends,)), get_up.step(deep_r + (ends,))
    start_state = state_before(
        tie(ends, *deep_v, *deep_r, *second_down).reshape(2 * ndim, SUB, LANES), par["hop"], "seq", False
    )
    start_state = tie(start_state, *middle_v, *middle_r, *first_gate, *first_up)
    for _ in range(seq_steps - 1):
        deep_gate, deep_up = get_gate.step((start_state,)), get_up.step((start_state,))
    get_down.step(deep_gate + deep_up)
    mixed, sent_mix, kept = kernel_call(
        mix_kernel,
        [((rows * SUB, LANES), f32), ((rows, width), bf16), ((rows // SPAN, 2 * ndim * SUB, LANES), f32)],
        [xs, flat(start_state), a_flat, b_flat, g_flat, par["skip"]],
        scratch=[pltpu.VMEM((2 * ndim * SUB, LANES), f32)],
        name="mix", micros=16, after=deep_gate + deep_up,
    )
    near_last = get_v.step((start_state,)) + get_r.step((start_state,))
    third_gate, third_up = get_gate.step((mixed,) + near_last), get_up.step((mixed,) + near_last)
    for getter in (get_v, get_r):
        while getter.order is not None and getter.place < all_bits:
            getter.step()
    weight1 = Weight(Part(get_v, 0, values_width, short), Part(get_r, 0, values_width + z_width, short, 0, values_width))
    if fits:
        tall = w_h.shape[0]
        weight2 = Weight(
            Part(get_v, values_width, width, tall), Part(get_r, values_width + z_width, width, tall, short)
        )
    else:
        weight2 = Weight(Part(Gather(low(w_h), None), 0, width, w_h.shape[0]))

    tile = 256
    w1_shape, w2_shape = (width, 2 * values_width + z_width), (values_width, width)
    w3_shape, w4_shape = (width, 2 * hidden_width), (hidden_width, width)
    dma = pltpu.SemaphoreType.DMA
    wide = ((rows, values_width), bf16)

    def other_core(value):
        return swap_bit(value, 0)

    norm_other = other_core(tie(sent_norm, mixed))

    def any_of(*groups):
        return [ANY] * sum(len(group.arrays) for group in groups)

    shared, queries, keys, log_total, value_pre, values, gate_pre, attended, gated = kernel_call(
        functools.partial(attention_kernel, weight1, tile),
        [((rows, z_width), f32), ((rows, z_width), bf16), ((rows, z_width), bf16), ((rows, 1), f32), wide, wide, wide,
         wide, wide],
        [me, sent_norm, sent_mix, seg_col, seg_row, valid_row, full_qg, full_qb, full_kg, *weight1.arrays],
        [SM] + [VM] * 8 + any_of(weight1),
        scratch=[pltpu.VMEM(w1_shape, bf16), pltpu.VMEM((rows, rows), bf16), dma],
        name="attention", micros=18, after=third_gate + third_up + (norm_other,),
    )
    middle, ffn_in, inverse = kernel_call(
        functools.partial(project_kernel, weight2),
        [((rows, width), f32), ((rows, width), bf16), ((rows, 1), f32)],
        [me, gated, tokens[0], valid_col, full_fg, *weight2.arrays],
        [SM] + [VM] * 4 + any_of(weight2),
        scratch=[pltpu.VMEM(w2_shape, bf16), pltpu.SemaphoreType.DMA((2,))],
        name="project", micros=6,
    )

    get_down.step(third_gate + third_up)
    for getter in (get_gate, get_up, get_down):
        while getter.order is not None and getter.place < all_bits - 1:
            getter.step()
        getter.step((ffn_in,))
    weight4 = Weight(Part(get_down, 0, width, w_down.shape[0]))
    weight3 = Weight(Part(get_gate, 0, hidden_width, short), Part(get_up, 0, hidden_width, short, 0, hidden_width))
    grad_low = cotangent[0]
    part = width // 2
    cot_own = lax.dynamic_slice_in_dim(grad_low, core * part, part, axis=1)
    cot_oth = other_core(tie(lax.dynamic_slice_in_dim(grad_low, (1 - core) * part, part, axis=1), mixed))
    gated_other, mix_other = other_core(gated), other_core(sent_mix)
    half = hidden_width // 2
    pair = ((rows, hidden_width), bf16, (rows, hidden_width), lambda g, me: (0, 0))
    hid, near, far = grid_call(
        functools.partial(hidden_kernel, weight3, weight4),
        [((rows, hidden_width), bf16, (rows, half), lambda g, me: (0, g)), pair, pair],
        [whole(ffn_in), whole(grad_low)] + [(array, None, None) for array in weight3.arrays + weight4.arrays],
        2, me,
        scratch=[pltpu.VMEM(w3_shape, bf16), pltpu.VMEM(w4_shape, bf16), pltpu.SemaphoreType.DMA((2, 3))],
        name="hidden", micros=15, after=(cot_oth, gated_other, mix_other),
    )
    ffn_other = other_core(ffn_in)
    (output,) = kernel_call(
        functools.partial(out_kernel, weight4),
        [((rows, width), bf16)],
        [me, hid, middle, *weight4.arrays],
        [SM, VM, VM] + any_of(weight4),
        scratch=[pltpu.VMEM(w4_shape, bf16), pltpu.SemaphoreType.DMA((2,))],
        name="out", micros=7,
    )
    hid_pair, ffn_pair = (hid, other_core(hid)), (ffn_in, ffn_other)
    far_other = other_core(far)
    down = weight_grad(hid_pair, (cot_own, cot_oth), reduce_a, me, chips, "grad_down", halves=2, after=(output,))
    gate = weight_grad(ffn_pair, (near, far_other), reduce_b, me, chips, "grad_gate", part=(0, 2), after=(down.sent,))
    up = weight_grad(
        ffn_pair, (near, far_other), reduce_a, me, chips, "grad_up", part=(1, 2), after=(gate.sent,)
    )
    grad_middle, low_own, low_oth, middle_low, dfg = kernel_call(
        functools.partial(ffn_back_kernel, weight3),
        [((rows, width), f32), ((rows, part), bf16), ((rows, part), bf16), ((rows, width), bf16), ((1, width), f32)],
        [me, near, far, middle, inverse, grad_low, full_fg, *weight3.arrays],
        [SM] + [VM] * 6 + any_of(weight3),
        scratch=[pltpu.VMEM(w3_shape, bf16), pltpu.VMEM((rows, width), f32), pltpu.SemaphoreType.DMA((2,))],
        name="ffn_back", micros=17, after=(up.sent,),
    )
    heads = weight_grad(
        (gated, gated_other), (low_own, other_core(low_oth)), reduce_b, me, chips, "grad_h", after=down.step(low_own)
    )
    half_values = ((rows, values_width // 2), bf16)
    half_mixed = ((rows, (values_width + z_width) // 2), bf16)
    grad_v, grad_r, gv_own, gv_oth, gr_own, gr_oth, dgains = kernel_call(
        functools.partial(attention_back_kernel, weight2, tile),
        [((rows, values_width), bf16), ((rows, values_width + z_width), bf16)] + [half_values] * 2 + [half_mixed] * 2
        + [((3, z_width), f32)],
        [me, middle_low, queries, keys, log_total, shared, value_pre, values, gate_pre, attended, seg_col, seg_row,
         valid_row, full_qg, full_kg, *weight2.arrays],
        [SM] + [VM] * 14 + any_of(weight2),
        scratch=[pltpu.VMEM(w2_shape, bf16), pltpu.VMEM((rows, rows), bf16), pltpu.VMEM((rows, rows), f32),
                 pltpu.VMEM((rows, z_width), bf16), dma],
        name="attention_back", micros=19, after=(heads.sent,) + gate.step(heads.sent),
    )
    grad_mix_rows, grad_norm_rows = kernel_call(
        functools.partial(sent_back_kernel, weight1),
        [((rows, width), bf16)] * 2,
        [me, grad_v, grad_r, *weight1.arrays],
        [SM, VM, VM] + any_of(weight1),
        scratch=[pltpu.VMEM(w1_shape, bf16), pltpu.SemaphoreType.DMA((2,))],
        name="sent_back", micros=11, after=up.step(gv_oth) + down.step(gv_oth),
    )
    gv_other, gr_other = other_core(gv_oth), other_core(gr_oth)
    drive, back_ends = kernel_call(
        back_ends_kernel, [((rows * SUB, LANES), f32), ((2 * ndim * SUB, LANES), f32)],
        [grad_mix_rows, mixed, a_flat, b_flat], name="back_ends", micros=12,
        after=heads.step(grad_mix_rows) + down.step(grad_mix_rows),
    )
    value = weight_grad((sent_norm, norm_other), (gv_own, gv_other), reduce_a, me, chips, "grad_v",
                        after=(back_ends, gr_other))
    both = merge(gate, up, back_ends)
    reset = weight_grad((sent_mix, mix_other), (gr_own, gr_other), reduce_b, me, chips, "grad_r",
                        after=(value.sent,) + both.pins + down.step(value.sent))
    hop_back = (par["hop"][0], -par["hop"][1])
    back_state = flat(
        state_before(back_ends.reshape(2 * ndim, SUB, LANES), hop_back, "seq", True,
                     {2: lambda: (value.sent,), 4: lambda: (reset.sent,)})
    )
    sums = jnp.zeros(((3 * ndim + 1) * SUB, LANES), f32)
    cuts = 4
    plan = [
        lambda done: heads.step(reset.sent) + both.step(reset.sent),
        lambda done: value.step(done) + heads.step(done),
        lambda done: reset.step(done) + both.step(done),
        lambda done: heads.step(done),
    ]
    last = []

    def merge_last(done):
        last.append(merge(value, reset, done))
        return last[0].pins

    done = back_state
    long = rows * SUB // cuts
    pieces_dx = []
    for cut in range(cuts - 1, -1, -1):
        block = pl.BlockSpec((long, LANES), lambda i, cut=cut: (cut, 0))
        keep_block = pl.BlockSpec((rows // SPAN // cuts, 2 * ndim * SUB, LANES), lambda i, cut=cut: (cut, 0, 0))
        dxs, back_state, sums = kernel_call(
            back_scan_kernel,
            [((long, LANES), f32), ((2 * ndim * SUB, LANES), f32), (((3 * ndim + 1) * SUB, LANES), f32)],
            [xs, drive, kept, back_state, sums, a_flat, b_flat, g_flat, par["skip"]],
            [block, block, keep_block] + [VM] * 6,
            scratch=[pltpu.VMEM((SPAN, 8 * SUB, LANES), f32)],
            name="back", micros=10, after=plan.pop(0)(done), grid=(1,), out_specs=[VM] * 3,
        )
        pieces_dx.insert(0, dxs)
        done = dxs
    pins = merge_last(done)
    last = last[0]
    dn, dgain, suffix, back_totals = kernel_call(
        back_norm_kernel,
        [((rows, width), f32), ((1, width), f32), ((rows, LANES), f32), ((DOCS, LANES), f32)],
        [*pieces_dx, grad_norm_rows, tokens[0], valid_col, seg_col, seg_row, prefix, carry, gain_row],
        name="back_norm", micros=6, after=pins,
    )
    sums = sums.reshape(3 * ndim + 1, SUB, LANES)
    d_params = ema_param_grads(par, sums)
    d_pack = jnp.concatenate(list(d_params) + [dgain.reshape(1, SUB, LANES), sums[3 * ndim :]], axis=0)
    d_pack = jnp.transpose(d_pack.reshape(4 * ndim + 2, seq_count, lanes), (1, 0, 2))
    owned = [dgains[i].reshape(devices, zs) for i in range(3)] + [dfg.reshape(devices, fs)]
    owned = jnp.concatenate(owned, axis=1).reshape(seq_count, -1)
    owned = jnp.pad(owned, ((0, 0), (0, extra * lanes - size))).reshape(seq_count, extra, lanes)
    own_pack, after_totals = exchange_end(jnp.concatenate([d_pack, owned], axis=1), tie(back_totals, *last.step(back_totals)), "seq")
    back_carry = lax.dynamic_slice_in_dim(after_totals, row_segs[rows - 1], 1)
    (input_grad,) = kernel_call(
        input_kernel, [((rows, width), f32)],
        [dn, suffix, back_carry, tokens[0], valid_col, seg_col, prefix, carry, grad_middle], name="input", micros=6,
        after=last.step(back_carry),
    )
    total = sum_over(sum_over(own_pack, "core"), "chip")
    mine = lax.dynamic_index_in_dim(total[4 * ndim + 2 :].reshape(-1)[:size].reshape(dp_count, -1), dp_index, 0, keepdims=False)
    (shard_down,) = down.finish(core, [part])
    shard_gate, shard_up = both.finish(core, [hidden_width // 2] * 2, done)
    (shard_h,) = heads.finish(core, [part], done)
    shard_v, shard_r, shard_z = last.finish(core, [values_width // 2, values_width // 2, z_width // 2])
    return (
        output[None], input_grad[None], shard_z, shard_v, shard_r, shard_h, shard_gate, shard_up, shard_down,
        mine[:zs], mine[zs : 2 * zs], mine[2 * zs : 3 * zs], mine[3 * zs :],
        total[4 * ndim], total[:ndim].T, total[ndim : 2 * ndim].T, total[2 * ndim : 3 * ndim].T,
        total[3 * ndim : 4 * ndim].T, total[4 * ndim + 1],
    )


def solution(mesh):
    shape = mesh.devices.shape
    whole = Mesh(mesh.devices.reshape(shape[0], shape[1] // 2, 2), AXES)
    by_token, by_group = P(("chip", "core"), "seq", None), P(("chip", "core"), None)
    by_row, by_owner = P(AXES, None), P(AXES)
    params = (by_row,) * 7 + (by_owner,) * 4 + (P("seq"),) + (P("seq", None),) * 4 + (P("seq"),)
    return jax.shard_map(
        on_device,
        mesh=whole,
        in_specs=(by_token, by_token, by_group, by_group) + params,
        out_specs=(by_token, by_token) + params,
        check_vma=False,
    )
```

```python
import functools
import math

import jax
import jax.numpy as jnp
from jax import lax
from jax.experimental import pallas as pl
from jax.experimental.pallas import tpu as pltpu
from jax.sharding import Mesh, PartitionSpec as P

AXES = ("seq", "chip", "core")
GROUP = 64
DOCS = 16
LANES = 128
SUB = 8
SPAN = 32
BAND = 64
bf16 = jnp.bfloat16
f32 = jnp.float32
VMEM_LIMIT = 60 * 1024 * 1024
PACE = 0.05


def split3(value):
    first = value.astype(bf16)
    rest = value - first.astype(f32)
    second = rest.astype(bf16)
    third = (rest - second.astype(f32)).astype(bf16)
    return first, second, third


def dot(left, right):
    return jnp.dot(left, right, preferred_element_type=f32)


def dot3(left, parts):
    return dot(left, parts[0]) + dot(left, parts[1]) + dot(left, parts[2])


def dot3_left(parts, right):
    return dot(parts[0], right) + dot(parts[1], right) + dot(parts[2], right)


def sigmoid(value):
    return 0.5 * jnp.tanh(0.5 * value) + 0.5


def iota(shape, axis):
    return lax.broadcasted_iota(jnp.int32, shape, axis)


def group_pick(width, shift):
    own = lax.shift_right_logical(iota((width, LANES), 0), GROUP.bit_length() - 1)
    return (own + shift == iota((width, LANES), 1)).astype(bf16)


def group_spread(groups, width):
    own = lax.shift_right_logical(iota((groups, width), 1), GROUP.bit_length() - 1)
    return (own == iota((groups, width), 0)).astype(bf16)


ANY = pl.BlockSpec(memory_space=pl.ANY)
VM = pl.BlockSpec(memory_space=pltpu.VMEM)
SM = pl.BlockSpec(memory_space=pltpu.SMEM)


def kernel_call(body, outs, args, specs=None, scratch=(), name=None, micros=10, after=(), grid=None, out_specs=None):
    specs = [VM] * len(args) if specs is None else specs
    count = len(args)

    def run(*refs):
        body(*refs[:count], *refs[count + len(after) :])

    more = {} if grid is None else dict(grid=grid, out_specs=tuple(out_specs))
    return pl.pallas_call(
        run,
        out_shape=tuple(jax.ShapeDtypeStruct(shape, dtype) for shape, dtype in outs),
        in_specs=list(specs) + [ANY] * len(after),
        scratch_shapes=list(scratch),
        compiler_params=pltpu.CompilerParams(vmem_limit_bytes=VMEM_LIMIT),
        cost_estimate=pl.CostEstimate(
            flops=int(micros * PACE * 1.0e9), bytes_accessed=int(micros * PACE * 3.0e6), transcendentals=0
        ),
        name=name,
        **more,
    )(*args, *after)


def grid_call(body, outs, args, steps, me, scratch=(), name=None, micros=10, after=()):
    def spec(shape, block, index):
        if block is None:
            return ANY
        if index is None:
            return pl.BlockSpec(shape, lambda g, me: (0,) * len(shape))
        return pl.BlockSpec(block, index)

    count = len(args)

    def run(*refs):
        body(*refs[: 1 + count], *refs[1 + count + len(after) :])

    return pl.pallas_call(
        run,
        out_shape=tuple(jax.ShapeDtypeStruct(shape, dtype) for shape, dtype, _, _ in outs),
        grid_spec=pltpu.PrefetchScalarGridSpec(
            num_scalar_prefetch=1,
            grid=(steps,),
            in_specs=[spec(array.shape, block, index) for array, block, index in args] + [ANY] * len(after),
            out_specs=tuple(spec(shape, block, index) for shape, _, block, index in outs),
            scratch_shapes=list(scratch),
        ),
        compiler_params=pltpu.CompilerParams(vmem_limit_bytes=VMEM_LIMIT),
        cost_estimate=pl.CostEstimate(
            flops=int(micros * PACE * 1.0e9), bytes_accessed=int(micros * PACE * 3.0e6), transcendentals=0
        ),
        name=name,
    )(me, *(array for array, _, _ in args), *after)


WHOLE = (1,)


def whole(array):
    return (array, WHOLE, None)


def columns_of(array, width, index=lambda g, me: (0, g)):
    return (array, (array.shape[0], width), index)


def tie(value, *after):
    def nothing(*refs):
        return None

    return pl.pallas_call(
        nothing,
        out_shape=jax.ShapeDtypeStruct(value.shape, value.dtype),
        in_specs=[ANY] * (1 + len(after)),
        out_specs=ANY,
        input_output_aliases={0: 0},
        name="tie",
    )(value, *after)


def zero_after(*after):
    return tie(jnp.zeros((1, 1, 1), bf16), *after)


def split_wide(value):
    return jnp.concatenate(split3(value), axis=1)


def spread_wide(groups, width, start):
    own = lax.shift_right_logical(iota((3 * groups, LANES), 1) + start, GROUP.bit_length() - 1)
    return (own == lax.rem(iota((3 * groups, LANES), 0), groups)).astype(bf16)


def moments(total, groups):
    counts = jnp.maximum(total[:, 2 * groups : 2 * groups + 1], 1.0) * float(GROUP)
    means = total[:, :groups] / counts
    variance = total[:, groups : 2 * groups] / counts - means * means
    return means, lax.rsqrt(variance + 1e-05), counts


def stats_kernel(tok_ref, valid_ref, segc_ref, segr_ref, prefix_ref, totals_ref):
    rows, width = tok_ref.shape
    groups = width // GROUP
    valid = valid_ref[...]
    masked = tok_ref[...].astype(f32) * valid
    low = masked.astype(bf16)
    square = masked * masked
    high = square.astype(bf16)
    rest = (square - high.astype(f32)).astype(bf16)
    second = group_pick(width, groups)
    sums = dot(low, group_pick(width, 0)) + dot(high, second) + dot(rest, second)
    sums = sums + jnp.where(iota((rows, LANES), 1) == 2 * groups, valid, 0.0)
    parts = split3(sums)
    earlier = (iota((rows, rows), 1) <= iota((rows, rows), 0)) & (segc_ref[...] == segr_ref[...])
    prefix_ref[...] = dot3(earlier.astype(f32).astype(bf16), parts)
    member = (iota((DOCS, rows), 0) == segr_ref[...]).astype(f32).astype(bf16)
    totals_ref[...] = dot3(member, parts)


def scan_ends(src_ref, a_ref, b_ref, end_ref, rows, ndim, reverse):
    half = ndim // 2
    for start in range(0, ndim, half):
        a = [a_ref[pl.ds((start + n) * SUB, SUB), :] for n in range(half)]
        b = [b_ref[pl.ds((start + n) * SUB, SUB), :] for n in range(half)]

        def step(i, state, a=a, b=b):
            t = rows - 1 - i if reverse else i
            x = src_ref[pl.ds(pl.multiple_of(t * SUB, SUB), SUB), :]
            fresh = []
            for n in range(half):
                re, im = state[2 * n], state[2 * n + 1]
                if reverse:
                    fresh += [a[n] * re + b[n] * im + x, a[n] * im - b[n] * re]
                else:
                    fresh += [a[n] * re - b[n] * im + x, a[n] * im + b[n] * re]
            return tuple(fresh)

        zero = jnp.zeros((SUB, LANES), f32)
        state = lax.fori_loop(0, rows, step, (zero,) * (2 * half), unroll=32)
        for n in range(half):
            end_ref[pl.ds((start + n) * SUB, SUB), :] = state[2 * n]
            end_ref[pl.ds((ndim + start + n) * SUB, SUB), :] = state[2 * n + 1]


def all_moments(prefix_ref, segc_ref, carry_ref, groups):
    total = prefix_ref[...] + jnp.where(segc_ref[...] == segc_ref[0:1, :], carry_ref[...], 0.0)
    return moments(total, groups)


def lane_rows(j, rows):
    return pl.ds(j, rows, stride=SUB)


def norm_kernel(tok_ref, valid_ref, segc_ref, prefix_ref, carry_ref, gain_ref, a_ref, b_ref,
                sent_ref, xs_ref, end_ref):
    rows, width = tok_ref.shape
    groups = width // GROUP
    ndim = a_ref.shape[0] // SUB
    means, scale, _ = all_moments(prefix_ref, segc_ref, carry_ref, groups)
    means, scale, valid = split_wide(means), split_wide(scale), valid_ref[...]
    for j in range(SUB):
        at = slice(j * LANES, (j + 1) * LANES)
        spread = spread_wide(groups, width, j * LANES)
        normed = (tok_ref[:, at].astype(f32) * valid - dot(means, spread)) * dot(scale, spread) * gain_ref[:, at]
        sent_ref[:, at] = normed.astype(bf16)
        xs_ref[lane_rows(j, rows), :] = normed
    scan_ends(xs_ref, a_ref, b_ref, end_ref, rows, ndim, False)


def mix_kernel(xs_ref, start_ref, a_ref, b_ref, g_ref, skip_ref, mixed_ref, sent_ref, keep_ref, state_ref):
    rows = xs_ref.shape[0] // SUB
    ndim = a_ref.shape[0] // SUB
    half = ndim // 2
    state_ref[...] = start_ref[...]

    def chunk(i, _):
        keep_ref[i] = state_ref[...]
        for start in range(0, ndim, half):
            re_at = [pl.ds((start + n) * SUB, SUB) for n in range(half)]
            im_at = [pl.ds((ndim + start + n) * SUB, SUB) for n in range(half)]
            a = [a_ref[at, :] for at in re_at]
            b = [b_ref[at, :] for at in re_at]
            g = [g_ref[at, :] for at in re_at]

            def step(k, state, start=start, a=a, b=b, g=g):
                at = pl.ds(pl.multiple_of((i * SPAN + k) * SUB, SUB), SUB)
                x = xs_ref[at, :]
                fresh, terms = [], []
                for n in range(half):
                    re, im = state[2 * n], state[2 * n + 1]
                    now = a[n] * re - b[n] * im + x
                    fresh += [now, a[n] * im + b[n] * re]
                    terms.append(g[n] * now)
                terms.append(skip_ref[...] * x if start == 0 else mixed_ref[at, :])
                while len(terms) > 1:
                    terms = [sum(terms[p : p + 2][1:], terms[p]) for p in range(0, len(terms), 2)]
                mixed_ref[at, :] = terms[0]
                return tuple(fresh)

            state = []
            for n in range(half):
                state += [state_ref[re_at[n], :], state_ref[im_at[n], :]]
            state = lax.fori_loop(0, SPAN, step, tuple(state), unroll=SPAN)
            for n in range(half):
                state_ref[re_at[n], :] = state[2 * n]
                state_ref[im_at[n], :] = state[2 * n + 1]
        return 0

    lax.fori_loop(0, rows // SPAN, chunk, 0)

    def band(i, _):
        at = pl.ds(pl.multiple_of(i * BAND, BAND), BAND)
        for j in range(SUB):
            mixed = mixed_ref[pl.ds(i * (BAND * SUB) + j, BAND, stride=SUB), :]
            sent_ref[at, j * LANES : (j + 1) * LANES] = (mixed * sigmoid(mixed)).astype(bf16)
        return 0

    lax.fori_loop(0, rows // BAND, band, 0)


def back_ends_kernel(grad_ref, mixed_ref, a_ref, b_ref, drive_ref, end_ref):
    rows = grad_ref.shape[0]
    ndim = a_ref.shape[0] // SUB

    def band(i, _):
        at = pl.ds(pl.multiple_of(i * BAND, BAND), BAND)
        for j in range(SUB):
            where = pl.ds(i * (BAND * SUB) + j, BAND, stride=SUB)
            mixed = mixed_ref[where, :]
            sigma = sigmoid(mixed)
            slope = sigma * (1.0 + mixed * (1.0 - sigma))
            drive_ref[where, :] = grad_ref[at, j * LANES : (j + 1) * LANES].astype(f32) * slope
        return 0

    lax.fori_loop(0, rows // BAND, band, 0)
    scan_ends(drive_ref, a_ref, b_ref, end_ref, rows, ndim, True)


def back_scan_kernel(xs_ref, drive_ref, keep_ref, start_ref, sums_in_ref, a_ref, b_ref, g_ref, skip_ref,
                     dxs_ref, state_ref, sums_ref, hist_ref):
    ndim = a_ref.shape[0] // SUB
    rows = xs_ref.shape[0] // SUB
    part = 4
    count = rows // SPAN
    state_ref[...] = start_ref[...]
    sums_ref[...] = sums_in_ref[...]

    def chunk(c, _):
        i = count - 1 - c
        for start in range(0, ndim, part):
            re_at = [pl.ds((start + n) * SUB, SUB) for n in range(part)]
            im_at = [pl.ds((ndim + start + n) * SUB, SUB) for n in range(part)]
            last_at = [pl.ds((2 * ndim + start + n) * SUB, SUB) for n in range(part)]
            a = [a_ref[at, :] for at in re_at]
            b = [b_ref[at, :] for at in re_at]
            g = [g_ref[at, :] for at in re_at]

            def forward(k, state, a=a, b=b):
                x = xs_ref[pl.ds(pl.multiple_of((i * SPAN + k) * SUB, SUB), SUB), :]
                fresh = []
                for n in range(part):
                    re, im = state[2 * n], state[2 * n + 1]
                    hist_ref[k, pl.ds(2 * n * SUB, SUB), :] = re
                    hist_ref[k, pl.ds((2 * n + 1) * SUB, SUB), :] = im
                    fresh += [a[n] * re - b[n] * im + x, a[n] * im + b[n] * re]
                return tuple(fresh)

            state = []
            for n in range(part):
                state += [keep_ref[i, re_at[n], :], keep_ref[i, im_at[n], :]]
            lax.fori_loop(0, SPAN, forward, tuple(state), unroll=SPAN)

            def backward(k, held, start=start, a=a, b=b, g=g):
                t = SPAN - 1 - k
                at = pl.ds(pl.multiple_of((i * SPAN + t) * SUB, SUB), SUB)
                x, drive = xs_ref[at, :], drive_ref[at, :]
                fresh, terms = [], []
                for n in range(part):
                    re, im, m_re, m_im, same = held[5 * n : 5 * n + 5]
                    now_re = a[n] * re + b[n] * im + drive
                    now_im = a[n] * im - b[n] * re
                    old_re = hist_ref[t, pl.ds(2 * n * SUB, SUB), :]
                    old_im = hist_ref[t, pl.ds((2 * n + 1) * SUB, SUB), :]
                    fresh += [
                        now_re,
                        now_im,
                        m_re + (now_re * old_re + now_im * old_im),
                        m_im + (now_im * old_re - now_re * old_im),
                        same + x * now_re,
                    ]
                    terms.append(g[n] * now_re)
                total = (terms[0] + terms[1]) + (terms[2] + terms[3])
                if start == 0:
                    dxs_ref[at, :] = total + skip_ref[...] * drive
                else:
                    dxs_ref[at, :] = total + dxs_ref[at, :]
                return tuple(fresh)

            held = []
            for n in range(part):
                held += [state_ref[re_at[n], :], state_ref[im_at[n], :]]
                held += [sums_ref[re_at[n], :], sums_ref[im_at[n], :], sums_ref[last_at[n], :]]
            held = lax.fori_loop(0, SPAN, backward, tuple(held), unroll=SPAN)
            for n in range(part):
                state_ref[re_at[n], :] = held[5 * n]
                state_ref[im_at[n], :] = held[5 * n + 1]
                sums_ref[re_at[n], :] = held[5 * n + 2]
                sums_ref[im_at[n], :] = held[5 * n + 3]
                sums_ref[last_at[n], :] = held[5 * n + 4]
        return 0

    lax.fori_loop(0, count, chunk, 0)

    def skip_step(k, total):
        at = pl.ds(pl.multiple_of(k * SUB, SUB), SUB)
        return total + xs_ref[at, :] * drive_ref[at, :]

    last = pl.ds(3 * ndim * SUB, SUB)
    sums_ref[last, :] = lax.fori_loop(0, rows, skip_step, sums_ref[last, :], unroll=8)


def back_norm_kernel(*refs):
    dxs_refs, refs = refs[:-12], refs[-12:]
    (grad_ref, tok_ref, valid_ref, segc_ref, segr_ref, prefix_ref, carry_ref, gain_ref,
     dn_ref, dgain_ref, suffix_ref, totals_ref) = refs
    rows, width = tok_ref.shape
    groups = width // GROUP
    means, scale, counts = all_moments(prefix_ref, segc_ref, carry_ref, groups)
    wide_means, wide_scale, valid = split_wide(means), split_wide(scale), valid_ref[...]
    plain, leaning = jnp.zeros((rows, LANES), f32), jnp.zeros((rows, LANES), f32)
    for j in range(SUB):
        at = slice(j * LANES, (j + 1) * LANES)
        spread = spread_wide(groups, width, j * LANES)
        own = lax.shift_right_logical(iota((LANES, LANES), 0) + j * LANES, GROUP.bit_length() - 1)
        pick = (own == iota((LANES, LANES), 1)).astype(bf16)
        centred = tok_ref[:, at].astype(f32) * valid - dot(wide_means, spread)
        ema = [ref[lane_rows(j, ref.shape[0] // SUB), :] for ref in dxs_refs]
        dn = grad_ref[:, at].astype(f32) + jnp.concatenate(ema, axis=0)
        dgain_ref[:, at] = jnp.sum(dn * centred * dot(wide_scale, spread), axis=0, keepdims=True)
        dn = dn * gain_ref[:, at]
        dn_ref[:, at] = dn
        plain = plain + dot3_left(split3(dn), pick)
        leaning = leaning + dot3_left(split3(dn * centred), pick)
    plain, leaning = plain[:, :groups], leaning[:, :groups]
    d_variance = -0.5 * leaning * scale * scale * scale
    d_second = d_variance / counts
    d_first = (-scale * plain - 2.0 * means * d_variance) / counts
    flow = jnp.concatenate([d_first, d_second, jnp.zeros((rows, LANES - 2 * groups), f32)], axis=1)
    parts = split3(flow)
    later = (iota((rows, rows), 1) >= iota((rows, rows), 0)) & (segc_ref[...] == segr_ref[...])
    suffix_ref[...] = dot3(later.astype(f32).astype(bf16), parts)
    member = (iota((DOCS, rows), 0) == segr_ref[...]).astype(f32).astype(bf16)
    totals_ref[...] = dot3(member, parts)


def input_kernel(dn_ref, suffix_ref, back_ref, tok_ref, valid_ref, segc_ref, prefix_ref, carry_ref, middle_ref, out_ref):
    rows, width = tok_ref.shape
    groups = width // GROUP
    _, scale, _ = all_moments(prefix_ref, segc_ref, carry_ref, groups)
    flow = suffix_ref[...] + jnp.where(segc_ref[...] == segc_ref[rows - 1 : rows, :], back_ref[...], 0.0)
    scale, valid = split_wide(scale), valid_ref[...]
    first, second = split_wide(flow[:, :groups]), split_wide(flow[:, groups : 2 * groups])
    for j in range(SUB):
        at = slice(j * LANES, (j + 1) * LANES)
        spread = spread_wide(groups, width, j * LANES)
        masked = tok_ref[:, at].astype(f32) * valid
        grad = dn_ref[:, at] * dot(scale, spread) + dot(first, spread) + 2.0 * masked * dot(second, spread)
        out_ref[:, at] = valid * (middle_ref[:, at] + grad)


def swap(value, axis, bit):
    count = lax.axis_size(axis)
    return lax.ppermute(value, axis, [(i, i ^ bit) for i in range(count)])


def gather_small(value, axis):
    index, count = lax.axis_index(axis), lax.axis_size(axis)
    value, bit = value[None], 1
    while bit < count:
        other = swap(value, axis, bit)
        upper = (index & bit) != 0
        value = jnp.concatenate([jnp.where(upper, other, value), jnp.where(upper, value, other)], axis=0)
        bit *= 2
    return value


def cmul(left, right):
    return (left[0] * right[0] - left[1] * right[1], left[0] * right[1] + left[1] * right[0])


def state_before(ends, hop, axis, reverse, hold=None):
    index, count = lax.axis_index(axis), lax.axis_size(axis)
    if reverse:
        index = count - 1 - index
    half = ends.shape[0] // 2
    before = (jnp.zeros_like(ends[:half]), jnp.zeros_like(ends[:half]))
    reach = (jnp.ones_like(hop[0]), jnp.zeros_like(hop[1]))
    bit = 1
    while bit < count:
        waits = hold[bit]() if hold and bit in hold else ()
        other = swap(tie(ends, *waits) if waits else ends, axis, bit)
        upper = (index & bit) != 0
        far, own = (other[:half], other[half:]), (ends[:half], ends[half:])
        moved = cmul(reach, far)
        before = tuple(v + jnp.where(upper, w, 0.0) for v, w in zip(before, moved))
        if bit * 2 < count:
            lower = tuple(jnp.where(upper, v, w) for v, w in zip(far, own))
            higher = tuple(jnp.where(upper, w, v) for v, w in zip(far, own))
            carried = cmul(hop, lower)
            ends = jnp.concatenate([carried[0] + higher[0], carried[1] + higher[1]], axis=0)
            longer = cmul(reach, hop)
            reach = tuple(jnp.where(upper, v, w) for v, w in zip(longer, reach))
            hop = cmul(hop, hop)
        bit *= 2
    return jnp.concatenate(before, axis=0)


def ema_params(full, ndim, rows):
    full = jnp.transpose(full, (1, 0, 2))
    full = full.reshape(full.shape[0], SUB, -1)
    rate, angle, input_w, output_w = (full[i * ndim : (i + 1) * ndim] for i in range(4))
    gain, skip = full[4 * ndim], full[4 * ndim + 1]
    base = jnp.sqrt(rate * (2.0 - rate))
    cos, sin = jnp.cos(angle), jnp.sin(angle)
    a, b = (1.0 - rate) * cos, (1.0 - rate) * sin
    hop, steps = (a, b), 1
    while steps < rows:
        hop, steps = cmul(hop, hop), steps * 2
    return dict(rate=rate, input_w=input_w, output_w=output_w, gain=gain, skip=skip, base=base,
                cos=cos, sin=sin, a=a, b=b, coeff=base * input_w, hop=hop)


def ema_param_grads(par, sums):
    ndim = par["rate"].shape[0]
    m_re, m_im, same = sums[:ndim], sums[ndim : 2 * ndim], sums[2 * ndim : 3 * ndim]
    weight = par["output_w"] * par["coeff"]
    d_a, d_b = weight * m_re, weight * m_im
    d_coeff = par["output_w"] * same
    d_output = par["coeff"] * same
    d_input = par["base"] * d_coeff
    d_rate = d_coeff * par["input_w"] * (1.0 - par["rate"]) / par["base"] - par["cos"] * d_a - par["sin"] * d_b
    d_angle = par["a"] * d_b - par["b"] * d_a
    return d_rate, d_angle, d_input, d_output


def mul_t(left, right):
    return lax.dot_general(left, right, (((1,), (1,)), ((), ())), preferred_element_type=f32)


def t_mul(left, right):
    return lax.dot_general(left, right, (((0,), (0,)), ((), ())), preferred_element_type=f32)


def silu_grad(value):
    sigma = sigmoid(value)
    return sigma * (1.0 + value * (1.0 - sigma))


def bits_of(count):
    return count.bit_length() - 1


class Part:
    def __init__(self, source, take, width, rows, lower=0, column=0):
        self.arrays, self.owners, self.top = source.arrays, source.owners, source.top
        self.take, self.width, self.rows, self.lower, self.column = take, width, rows, lower, column

    def copies(self, refs, where, me, sem, span=None, near=None):
        made = []
        first, width = (0, self.width) if span is None else span
        for ref, owners in zip(refs, self.owners):
            block = ref.shape[1]
            for slot, owner in enumerate(owners):
                if near is not None and near != (owner < (1 << self.top)):
                    continue
                start = (me ^ owner) * self.rows + self.lower
                start = pl.multiple_of(start, math.gcd(self.rows, block)) if len(owners) > 1 else 0
                source = ref.at[slot, :, pl.ds(self.take + first, width)]
                to = where.at[pl.ds(start, block), pl.ds(self.column + first, width)]
                made.append(pltpu.make_async_copy(source, to, sem))
        return made


class Weight:
    def __init__(self, *parts):
        self.parts, self.arrays, self.places = parts, [], []
        self.split, self.top = len(parts[0].owners[0]) > 1, parts[0].top
        self.nears = (True, False) if self.split else (None,)
        for part in parts:
            place = []
            for array in part.arrays:
                same = [n for n, known in enumerate(self.arrays) if known is array]
                if not same:
                    self.arrays.append(array)
                place.append(same[0] if same else len(self.arrays) - 1)
            self.places.append(place)

    def copies(self, refs, where, me, sem, which=None, span=None, near=None):
        made = []
        for n, (part, place) in enumerate(zip(self.parts, self.places)):
            if which is None or which == n:
                made += part.copies([refs[n] for n in place], where, me, sem, span, near)
        return made


class Gather:
    def __init__(self, shard, order):
        self.order = order
        self.top = max(order or (0,))
        if order is None:
            full = lax.all_gather(shard, AXES, axis=0, tiled=True)
            self.arrays, self.owners = [full[None]], [[0]]
            return
        self.arrays, self.owners, self.place = [shard[None]], [[0]], 0

    def step(self, after=()):
        if self.order is None:
            return ()
        bit = self.order[self.place]
        mine = [tie(value, *after) for value in self.arrays] if after else self.arrays
        others = [swap_bit(value, bit) for value in mine]
        moved = [[owner ^ (1 << bit) for owner in row] for row in self.owners]
        if self.place < len(self.order) - 2:
            self.arrays = [jnp.concatenate([mine[0], others[0]], axis=0)]
            self.owners = [self.owners[0] + moved[0]]
        else:
            self.arrays, self.owners = mine + others, self.owners + moved
        self.place += 1
        return (self.arrays[-1],)

def swap_bit(value, bit):
    dp_bits = bits_of(lax.axis_size("chip")) + 1
    if bit == 0:
        return swap(value, "core", 1)
    if bit < dp_bits:
        return swap(value, "chip", 1 << (bit - 1))
    return swap(value, "seq", 1 << (bit - dp_bits))


def add_low(left, right, zero):
    return left + right + zero


class Reduce:
    def __init__(self, keep, send, order):
        self.keep, self.send, self.order, self.sent = keep, send, order, keep
        self.pins = () if order is None else (send,)
        self.left = list(order or ())
        self.other = None
        if order is None:
            self.keep = lax.psum_scatter(keep[0], ("seq", "chip"), scatter_dimension=0, tiled=True)[None]
        else:
            self.begin()

    def begin(self):
        self.other = swap_bit(self.send, self.left.pop(0)) if self.left else None

    def halves(self, after=()):
        half = self.keep.shape[0] // 2
        zero = zero_after(*after) if after else jnp.zeros((1, 1, 1), bf16)
        return add_low(self.keep[:half], self.other[:half], zero), add_low(self.keep[half:], self.other[half:], zero)

    def step(self, *after):
        if self.other is None:
            return ()
        if not self.left:
            zero = zero_after(*after) if after else 0.0
            self.keep = self.keep.astype(f32) + self.other.astype(f32) + zero
            self.other = None
            return (self.keep,)
        self.keep, self.send = self.halves(after)
        self.begin()
        return (self.send,)

    def finish(self, core, widths, *after):
        while self.other is not None:
            self.step(*after)
        chip_rows = self.keep[0].astype(f32)
        rows = chip_rows.shape[0] // 2
        lower, upper = chip_rows[:rows], chip_rows[rows:]
        own = jnp.where(core == 0, lower, upper)
        other = swap_bit(jnp.where(core == 0, upper, lower).astype(bf16), 0).astype(f32)
        outs, at = [], 0
        for width in widths:
            mine, theirs = own[:, at : at + width], other[:, at : at + width]
            outs.append(
                jnp.concatenate([jnp.where(core == 0, mine, theirs), jnp.where(core == 0, theirs, mine)], axis=1)
            )
            at += width
        return outs


def merge(first, second, *after):
    if first.order is None:
        both = Reduce.__new__(Reduce)
        both.keep = jnp.concatenate([first.keep, second.keep], axis=2)
        both.order, both.left, both.other, both.pins = None, [], None, ()
        return both
    parts = [first.halves(after), second.halves(after)]
    keep = jnp.concatenate([part[0] for part in parts], axis=2)
    send = jnp.concatenate([part[1] for part in parts], axis=2)
    return Reduce(keep, send, first.left)


def allowed_pairs(segc_ref, segr_ref, validr_ref):
    rows = segc_ref.shape[0]
    query, key = iota((rows, rows), 0), iota((rows, rows), 1)
    same = segc_ref[...] == segr_ref[...]
    usable = validr_ref[...] > 0.5
    return (key <= query) & same & (usable | (key == query))


def attention_kernel(weight1, tile, me_ref, norm_ref, mix_ref, segc_ref, segr_ref, validr_ref, qg_ref, qb_ref, kg_ref,
                     *refs):
    n1 = len(weight1.arrays)
    shared_ref, q_ref, k_ref, lse_ref, vpre_ref, values_ref, gpre_ref, att_ref, gated_ref, w1, probs_ref, sems = refs[n1:]
    step, steps = pl.program_id(0), pl.num_programs(0)
    values_width = tile * weight1.tiles
    half = values_width // 2

    def copies(n):
        made = []
        if n == 0:
            made += weight1.copies(refs[:n1], w1, me_ref[0], sems.at[0], 1, (values_width, w1.shape[1] - 2 * values_width))
        for part in range(2):
            made += weight1.copies(refs[:n1], w1, me_ref[0], sems.at[n], part, (n * half, half))
        return made

    @pl.when(step == 0)
    def _():
        for n in range(2):
            for copy in copies(n):
                copy.start()
        for copy in copies(0):
            copy.wait()
        shared = dot(mix_ref[...], w1[:, 2 * values_width :])
        shared_ref[...] = shared
        queries = (shared * qg_ref[...] + qb_ref[...]).astype(bf16)
        keys = (shared * kg_ref[...]).astype(bf16)
        q_ref[...] = queries
        k_ref[...] = keys
        scores = mul_t(queries, keys) * (queries.shape[1] ** -0.5)
        masked = jnp.where(allowed_pairs(segc_ref, segr_ref, validr_ref), scores, -1e30)
        top = jnp.max(masked, axis=1, keepdims=True)
        weights = jnp.exp(masked - top)
        total = jnp.sum(weights, axis=1, keepdims=True)
        probs_ref[...] = (weights / total).astype(bf16)
        lse_ref[...] = top + jnp.log(total)

    @pl.when(step == lax.div(steps, 2))
    def _():
        for copy in copies(1):
            copy.wait()

    value_pre = dot(norm_ref[...], w1[:, pl.ds(pl.multiple_of(step * tile, tile), tile)])
    vpre_ref[...] = value_pre.astype(bf16)
    values = (value_pre * sigmoid(value_pre)).astype(bf16)
    values_ref[...] = values
    gate_pre = dot(mix_ref[...], w1[:, pl.ds(pl.multiple_of(values_width + step * tile, tile), tile)])
    gpre_ref[...] = gate_pre.astype(bf16)
    attended = dot(probs_ref[...], values)
    att_ref[...] = attended.astype(bf16)
    gated_ref[...] = (attended * (gate_pre * sigmoid(gate_pre))).astype(bf16)


def project_kernel(weight2, *refs):
    n2 = len(weight2.arrays)
    me_ref, gated_ref, tok_ref, valid_ref, fg_ref = refs[:5]
    middle_ref, ffn_ref, inv_ref, w2, sems = refs[5 + n2 :]
    width = tok_ref.shape[1]
    edge = width // 2
    for part in range(2):
        for copy in weight2.copies(refs[5 : 5 + n2], w2, me_ref[0], sems.at[part], span=(part * edge, edge)):
            copy.start()
    square = jnp.zeros((tok_ref.shape[0], 1), f32)
    for part in range(2):
        for copy in weight2.copies(refs[5 : 5 + n2], w2, me_ref[0], sems.at[part], span=(part * edge, edge)):
            copy.wait()
        at = slice(part * edge, (part + 1) * edge)
        middle = tok_ref[:, at].astype(f32) * valid_ref[...] + dot(gated_ref[...], w2[:, at])
        middle_ref[:, at] = middle
        square = square + jnp.sum(middle * middle, axis=1, keepdims=True)
    inverse = lax.rsqrt(square * (1.0 / width) + 1e-05)
    inv_ref[...] = inverse
    ffn_ref[...] = (middle_ref[...] * inverse * fg_ref[...]).astype(bf16)


def hidden_kernel(weight3, weight4, me_ref, ffn_ref, cot_ref, *refs):
    n3, n4 = len(weight3.arrays), len(weight4.arrays)
    hid_ref, near_ref, far_ref, w3, w4, sems = refs[n3 + n4 :]
    step, core = pl.program_id(0), me_ref[1]
    half = hid_ref.shape[1]

    def copies(rel, n):
        base = pl.multiple_of((core ^ rel) * half, half)
        if n < 2:
            return weight3.copies(refs[:n3], w3, me_ref[0], sems.at[rel, n], n, (base, half))
        return weight4.copies(refs[n3 : n3 + n4], w4, me_ref[0], sems.at[rel, n], near=None)

    @pl.when(step == 0)
    def _():
        for rel, n in ((0, 0), (0, 1), (0, 2), (1, 0), (1, 1)):
            for copy in copies(rel, n):
                copy.start()

    def arrived(n):
        for rel in range(2):
            if (rel, n) != (1, 2):
                @pl.when(step == rel)
                def _():
                    for copy in copies(rel, n):
                        copy.wait()

    base = pl.multiple_of((core ^ step) * half, half)
    arrived(0)
    gate = dot(ffn_ref[...], w3[:, pl.ds(base, half)])
    sigma = sigmoid(gate)
    act = gate * sigma
    slope = sigma + act * (1.0 - sigma)
    arrived(1)
    up = dot(ffn_ref[...], w3[:, pl.ds(pl.multiple_of(base + 2 * half, half), half)])
    hid_ref[...] = (act * up).astype(bf16)
    arrived(2)
    grad = mul_t(cot_ref[...], w4[pl.ds(base, half), :])
    grad_gate = (grad * up * slope).astype(bf16)
    grad_up = (grad * act).astype(bf16)

    @pl.when(step == 0)
    def _():
        near_ref[:, :half] = grad_gate
        near_ref[:, half:] = grad_up

    @pl.when(step == 1)
    def _():
        far_ref[:, :half] = grad_gate
        far_ref[:, half:] = grad_up


def out_kernel(weight4, me_ref, hid_ref, middle_ref, *refs):
    n4 = len(weight4.arrays)
    out_ref, w4, sems = refs[n4:]
    width, half = middle_ref.shape[1], hid_ref.shape[1] // 2
    starts = [pl.multiple_of((me_ref[1] ^ rel) * half, half) for rel in range(2)]
    edge = width // 2
    for part in range(2):
        for copy in weight4.copies(refs[:n4], w4, me_ref[0], sems.at[part], span=(part * edge, edge)):
            copy.start()
    for part in range(2):
        for copy in weight4.copies(refs[:n4], w4, me_ref[0], sems.at[part], span=(part * edge, edge)):
            copy.wait()
        at = slice(part * edge, (part + 1) * edge)
        total = middle_ref[:, at]
        for rel in range(2):
            total = total + dot(hid_ref[:, rel * half : (rel + 1) * half], w4[pl.ds(starts[rel], half), at])
        out_ref[:, at] = total.astype(bf16)


def ffn_back_kernel(weight3, *refs):
    n3 = len(weight3.arrays)
    me_ref, near_ref, far_ref, middle_ref, inv_ref, cot_ref, fg_ref = refs[:7]
    gmid_ref, low_own, low_oth, low_ref, dfg_ref, w3, gin_ref, sems = refs[7 + n3 :]
    me, core = me_ref[0], me_ref[1]
    rows, width = middle_ref.shape
    half = near_ref.shape[1] // 2
    parts, edge = (2, width // 2) if weight3.split else (1, width)
    for part in range(parts):
        for copy in weight3.copies(refs[7 : 7 + n3], w3, me, sems.at[part], near=weight3.nears[part]):
            copy.start()
    starts = [pl.multiple_of((core ^ rel) * half, half) for rel in range(2)]
    lean = jnp.zeros((rows, 1), f32)
    for part in range(parts):
        for copy in weight3.copies(refs[7 : 7 + n3], w3, me, sems.at[part], near=weight3.nears[part]):
            copy.wait()
        base = pl.multiple_of((lax.shift_right_logical(me, weight3.top) ^ part) * edge, edge) if parts == 2 else 0
        at = pl.ds(base, edge)
        grad = jnp.zeros((rows, edge), f32)
        for rel, ref in enumerate((near_ref, far_ref)):
            grad = grad + mul_t(ref[:, :half], w3[at, pl.ds(starts[rel], half)])
            grad = grad + mul_t(ref[:, half:], w3[at, pl.ds(pl.multiple_of(starts[rel] + 2 * half, half), half)])
        normal = middle_ref[:, at] * inv_ref[...]
        dfg_ref[:, at] = jnp.sum(grad * normal, axis=0, keepdims=True)
        grad = grad * fg_ref[:, at]
        gin_ref[:, at] = grad
        lean = lean + jnp.sum(grad * normal, axis=1, keepdims=True)
    lean = lean * (1.0 / width)
    inverse = inv_ref[...]
    grad_middle = cot_ref[...].astype(f32) + inverse * (gin_ref[...] - middle_ref[...] * inverse * lean)
    gmid_ref[...] = grad_middle
    low_ref[...] = grad_middle.astype(bf16)
    part = width // 2
    low_own[...] = low_ref[:, pl.ds(pl.multiple_of(core * part, part), part)]
    low_oth[...] = low_ref[:, pl.ds(pl.multiple_of((1 - core) * part, part), part)]


def attention_back_kernel(weight2, tile, me_ref, low_ref, q_ref, k_ref, lse_ref, shared_ref, segc_ref, segr_ref,
                          validr_ref, qg_ref, kg_ref, vpre_ref, values_ref, gpre_ref, att_ref, *refs):
    n2 = len(weight2.arrays)
    (gv_ref, gr_ref, gv_own, gv_oth, gr_own, gr_oth, gsh_ref, dgain_ref, w2, probs_ref, low_probs_ref, gprobs_ref,
     sems) = refs[n2:]
    core = me_ref[1]
    rows = low_ref.shape[0]
    step, steps = pl.program_id(0), pl.num_programs(0)
    strips = steps // 2
    values_width = gv_own.shape[1] * 2
    factor = q_ref.shape[1] ** -0.5

    def copies(n):
        return weight2.copies(refs[:n2], w2, me_ref[0], sems.at[n], near=weight2.nears[n])

    @pl.when(step == 0)
    def _():
        for n in range(len(weight2.nears)):
            for copy in copies(n):
                copy.start()
        scores = mul_t(q_ref[...], k_ref[...]) * factor
        masked = jnp.where(allowed_pairs(segc_ref, segr_ref, validr_ref), scores, -1e30)
        probs = jnp.exp(masked - lse_ref[...])
        probs_ref[...] = probs
        low_probs_ref[...] = probs.astype(bf16)
        gprobs_ref[...] = jnp.zeros((rows, rows), f32)
        for copy in copies(0):
            copy.wait()

    if len(weight2.nears) > 1:

        @pl.when(step == strips)
        def _():
            for copy in copies(1):
                copy.wait()

    tile_at = tile_order(weight2, step, strips, me_ref)
    grad = mul_t(low_ref[...], w2[pl.ds(pl.multiple_of(tile_at * tile, tile), tile), :]).astype(bf16).astype(f32)
    gate_pre = gpre_ref[...].astype(f32)
    sigma = sigmoid(gate_pre)
    act = gate_pre * sigma
    grad_att = (grad * act).astype(bf16)
    grad_gate = (grad * att_ref[...].astype(f32) * (sigma + act * (1.0 - sigma))).astype(bf16)
    gr_ref[...] = grad_gate
    gprobs_ref[...] += mul_t(grad_att, values_ref[...])
    grad_values = (t_mul(low_probs_ref[...], grad_att) * silu_grad(vpre_ref[...].astype(f32))).astype(bf16)
    gv_ref[...] = grad_values
    inside = pl.ds(pl.multiple_of(lax.rem(tile_at, strips) * tile, tile), tile)
    mine = lax.div(tile_at, strips) == core

    @pl.when(mine)
    def _():
        gv_own[:, inside] = grad_values
        gr_own[:, inside] = grad_gate

    @pl.when(jnp.logical_not(mine))
    def _():
        gv_oth[:, inside] = grad_values
        gr_oth[:, inside] = grad_gate

    @pl.when(step == steps - 1)
    def _():
        probs, grad_probs = probs_ref[...], gprobs_ref[...]
        grad_scores = (probs * (grad_probs - jnp.sum(probs * grad_probs, axis=1, keepdims=True))).astype(bf16)
        grad_queries = dot(grad_scores, k_ref[...]) * factor
        grad_keys = t_mul(grad_scores, q_ref[...]) * factor
        shared = shared_ref[...]
        dgain_ref[0:1, :] = jnp.sum(grad_queries * shared, axis=0, keepdims=True)
        dgain_ref[1:2, :] = jnp.sum(grad_queries, axis=0, keepdims=True)
        dgain_ref[2:3, :] = jnp.sum(grad_keys * shared, axis=0, keepdims=True)
        gsh_ref[...] = (grad_queries * qg_ref[...] + grad_keys * kg_ref[...]).astype(bf16)
        part = gsh_ref.shape[1] // 2
        start = values_width // 2
        gr_own[:, start:] = gsh_ref[:, pl.ds(pl.multiple_of(core * part, part), part)]
        gr_oth[:, start:] = gsh_ref[:, pl.ds(pl.multiple_of((1 - core) * part, part), part)]


def tile_order(weight, step, strips, me):
    if len(weight.nears) == 1:
        return step
    return (lax.shift_right_logical(me[0], weight.top) ^ lax.div(step, strips)) * strips + lax.rem(step, strips)


def sent_back_kernel(weight1, *refs):
    n1 = len(weight1.arrays)
    me_ref, gv_ref, gr_ref, gsh_ref = refs[:4]
    gmix_ref, gnorm_ref, w1, sems = refs[4 + n1 :]
    me, width, values_width = me_ref[0], gmix_ref.shape[1], gv_ref.shape[1]
    parts, edge = (2, width // 2) if weight1.split else (1, width)
    for part in range(parts):
        for copy in weight1.copies(refs[4 : 4 + n1], w1, me, sems.at[part], near=weight1.nears[part]):
            copy.start()
    for part in range(parts):
        for copy in weight1.copies(refs[4 : 4 + n1], w1, me, sems.at[part], near=weight1.nears[part]):
            copy.wait()
        base = pl.multiple_of((lax.shift_right_logical(me, weight1.top) ^ part) * edge, edge) if parts == 2 else 0
        at = pl.ds(base, edge)
        gmix_ref[:, at] = (
            mul_t(gr_ref[...], w1[at, values_width : 2 * values_width]) + mul_t(gsh_ref[...], w1[at, 2 * values_width :])
        ).astype(bf16)
        gnorm_ref[:, at] = mul_t(gv_ref[...], w1[at, :values_width]).astype(bf16)


def weight_grad_kernel(halves, order, blocks, block, me_ref, own, other, mine, theirs, *refs):
    keep, send = refs[0], refs[1]
    held, sems = refs[-2:]
    chip, core = lax.shift_right_logical(me_ref[0], 1), me_ref[1]
    tile, span = own.shape[1], mine.shape[1]
    step, steps = pl.program_id(0), pl.num_programs(0)
    strips = lax.div(steps, halves)
    rel = lax.div(step, strips)
    base = ((core ^ rel) if halves == 2 else rel) * (strips * tile) + lax.rem(step, strips) * tile
    slot = lax.rem(step, 2)
    parts = tile // block

    def done(slot):
        for s in range(parts):
            pltpu.make_async_copy(held.at[slot, pl.ds(s * block, block)], keep.at[0], sems.at[slot]).wait()

    @pl.when(step >= 2)
    def _():
        done(slot)

    out = t_mul(own[...], mine[...]) + t_mul(other[...], theirs[...])
    held[slot] = out.astype(bf16)
    for s in range(parts):
        rel_chip = (lax.div(base, block) + s) ^ chip
        place = 0
        for p, bit in enumerate(order):
            place = place | ((lax.shift_right_logical(rel_chip, bit - 1) & 1) << (len(order) - 1 - p))
        index = place & (blocks // 2 - 1)
        source = held.at[slot, pl.ds(s * block, block)]

        @pl.when(place < blocks // 2)
        def _():
            pltpu.make_async_copy(source, keep.at[index], sems.at[slot]).start()

        @pl.when(place >= blocks // 2)
        def _():
            pltpu.make_async_copy(source, send.at[index], sems.at[slot]).start()

    @pl.when(step == steps - 1)
    def _():
        done(slot)
        done(1 - slot)


def plain_grad_kernel(halves, me_ref, own, other, mine, theirs, keep):
    keep[0] = (t_mul(own[...], mine[...]) + t_mul(other[...], theirs[...])).astype(bf16)


def weight_grad(left, right, order, me, chips, name, halves=1, part=(0, 1), micros=6, after=()):
    total, span = left[0].shape[1], right[0].shape[1] // part[1]
    rows = left[0].shape[0]
    half = total // halves
    block = total // chips
    if order is None:
        tile = math.gcd(half, 256)
    else:
        tile = math.lcm(block, LANES)
        while tile < 512 and half % (2 * tile) == 0 and half // (2 * tile) >= 2 // halves:
            tile *= 2
    strips = half // tile
    far = (lambda g, me: (0, g)) if halves == 1 else (lambda g, me: (0, lax.rem(g + strips, 2 * strips)))
    args = [
        columns_of(left[0], tile), columns_of(left[1], tile, far), columns_of(right[0], span, lambda g, me: (0, part[0])),
        columns_of(right[1], span, lambda g, me: (0, part[0])),
    ]
    if order is None:
        place = (lambda g, me: (0, g, 0)) if halves == 1 else (
            lambda g, me: (0, (me[1] ^ lax.div(g, strips)) * strips + lax.rem(g, strips), 0))
        (keep,) = grid_call(
            functools.partial(plain_grad_kernel, halves), [((1, total, span), bf16, (1, tile, span), place)], args,
            halves * strips, me, name=name, micros=micros, after=after)
        return Reduce(keep, None, None)
    keep, send = grid_call(
        functools.partial(weight_grad_kernel, halves, order, chips, block),
        [((chips // 2, block, span), bf16, None, None)] * 2, args, halves * strips, me,
        scratch=[pltpu.VMEM((2, tile, span), bf16), pltpu.SemaphoreType.DMA((2,))], name=name, micros=micros, after=after)
    return Reduce(keep, send, order)


def exchange_start(pack, totals, axis, hold):
    index, count = lax.axis_index(axis), lax.axis_size(axis)
    lanes = pack.shape[1]
    rows = pack.shape[0]
    full, totals_shape = pack, totals.shape
    totals = totals.reshape(-1, lanes)
    before, bit = jnp.zeros_like(totals), 1
    while bit < count:
        goes = jnp.concatenate([totals, full], axis=0)
        other = swap(tie(goes, *hold) if hold and bit == 2 else goes, axis, bit)
        upper = (index & bit) != 0
        far_totals, far = other[: totals.shape[0]], other[totals.shape[0] :]
        before = before + jnp.where(upper, far_totals, 0.0)
        totals = totals + far_totals
        full = jnp.concatenate([jnp.where(upper, far, full), jnp.where(upper, full, far)], axis=0)
        bit *= 2
    return full.reshape(count, rows, lanes), before.reshape(totals_shape)


def exchange_end(pack, totals, axis):
    index, count = lax.axis_index(axis), lax.axis_size(axis)
    lanes = pack.shape[2]
    totals_shape = totals.shape
    totals = totals.reshape(-1, lanes)
    rows = totals.shape[0]
    after, bit = jnp.zeros_like(totals), 1
    while bit < count:
        upper = (index & bit) != 0
        pairs = pack.reshape((pack.shape[0] // 2, 2) + pack.shape[1:])
        goes = jnp.where(upper, pairs[:, 0], pairs[:, 1])
        stays = jnp.where(upper, pairs[:, 1], pairs[:, 0])
        other = swap(jnp.concatenate([totals, goes.reshape(-1, lanes)], axis=0), axis, bit)
        after = after + jnp.where(upper, 0.0, other[:rows])
        totals = totals + other[:rows]
        pack = stays + other[rows:].reshape(stays.shape)
        bit *= 2
    return pack[0], after.reshape(totals_shape)


def sum_over(value, axis):
    bit = 1
    while bit < lax.axis_size(axis):
        value = value + swap(value, axis, bit)
        bit *= 2
    return value


def on_device(tokens, cotangent, segment_ids, pad_mask, w_z, w_v, w_r, w_h, w_gate, w_up, w_down, q_gain, q_bias,
              k_gain, ffn_gain, norm_gain, ema_rate, ema_angle, ema_input, ema_output, ema_skip):
    rows, width = tokens.shape[1:]
    seq_count, dp_count = lax.axis_size("seq"), 2 * lax.axis_size("chip")
    seq_index, core = lax.axis_index("seq"), lax.axis_index("core")
    dp_index = lax.axis_index("chip") * 2 + core
    devices = seq_count * dp_count
    chips = devices // 2
    fits = all(value.shape[0] % 16 == 0 for value in (w_z, w_h, w_down))
    dp_bits, all_bits = bits_of(dp_count), bits_of(devices)
    inner = list(range(1, dp_bits))
    first_seq, rest_seq = [dp_bits], list(range(all_bits - 1, dp_bits, -1))
    if fits:
        gather_a = rest_seq + first_seq + inner + [0]
        gather_b = rest_seq + inner + first_seq + [0]
        gather_c = inner + first_seq + rest_seq + [0]
        reduce_a, reduce_b = gather_a[-2::-1], gather_b[-2::-1]
        me = jnp.stack([seq_index * dp_count + dp_index, core]).astype(jnp.int32)
    else:
        gather_a = gather_b = gather_c = reduce_a = reduce_b = None
        me = jnp.stack([core * 0, core]).astype(jnp.int32)
    values_width, hidden_width = w_v.shape[1], w_gate.shape[1]
    z_width = w_z.shape[1]
    low = lambda *parts: jnp.concatenate([part.astype(bf16) for part in parts], axis=1)
    short = w_v.shape[0]
    if fits:
        get_v = Gather(low(w_v, w_h[:short]), gather_a)
        get_r = Gather(low(w_r, w_z, w_h[short:]), gather_b)
    else:
        get_v, get_r = Gather(low(w_v), None), Gather(low(w_r, w_z), None)
    get_gate, get_up = Gather(low(w_gate), gather_a), Gather(low(w_up), gather_b)
    first_v, first_r = get_v.step(), get_r.step()
    get_down = Gather(low(w_down), gather_c)
    first_down = get_down.step()

    row_segs = lax.dynamic_slice_in_dim(segment_ids[0], seq_index * rows, rows)
    row_valid = lax.dynamic_slice_in_dim(pad_mask[0], seq_index * rows, rows).astype(f32)
    valid_col, seg_col, seg_row, valid_row = row_valid[:, None], row_segs[:, None], row_segs[None], row_valid[None]
    prefix, totals = kernel_call(
        stats_kernel, [((rows, LANES), f32), ((DOCS, LANES), f32)], [tokens[0], valid_col, seg_col, seg_row],
        name="stats", micros=5,
    )

    ndim, lanes = ema_rate.shape[1], norm_gain.shape[0]
    gains = jnp.concatenate([q_gain, q_bias, k_gain, ffn_gain])[None].astype(bf16).astype(f32)
    gains = gather_small(gather_small(gains, "core"), "chip").reshape(-1)
    size = gains.shape[0]
    extra = -(-size // lanes)
    gains = jnp.pad(gains, (0, extra * lanes - size)).reshape(extra, lanes)
    pack = jnp.concatenate(
        [ema_rate.T, ema_angle.T, ema_input.T, ema_output.T, norm_gain[None], ema_skip[None], gains], axis=0
    )
    full, before = exchange_start(pack, totals, "seq", first_v + first_r)
    carry = lax.dynamic_slice_in_dim(before, row_segs[0], 1)
    gains = full[:, 4 * ndim + 2 :].reshape(seq_count, -1)[:, :size].reshape(devices, -1)
    zs, fs = q_gain.shape[0], ffn_gain.shape[0]
    full_qg = gains[:, :zs].reshape(1, -1)
    full_qb = gains[:, zs : 2 * zs].reshape(1, -1)
    full_kg = gains[:, 2 * zs : 3 * zs].reshape(1, -1)
    full_fg = gains[:, 3 * zs :].reshape(1, -1)
    par = ema_params(full[:, : 4 * ndim + 2], ndim, rows)
    flat = lambda value: value.reshape(-1, LANES)
    a_flat, b_flat, g_flat = flat(par["a"]), flat(par["b"]), flat(par["output_w"] * par["coeff"])
    gain_row = par["gain"].reshape(1, width)
    seq_steps = len(rest_seq)
    for _ in range(seq_steps - 1):
        deep_v, deep_r = get_v.step(), get_r.step()
    for _ in inner[1:]:
        get_down.step()
    second_down = get_down.step(first_v)
    sent_norm, xs, ends = kernel_call(
        norm_kernel,
        [((rows, width), bf16), ((rows * SUB, LANES), f32), ((2 * ndim * SUB, LANES), f32)],
        [tokens[0], valid_col, seg_col, prefix, carry, gain_row, a_flat, b_flat],
        name="norm", micros=13, after=first_v + first_r + first_down,
    )
    middle_v, middle_r = get_v.step((ends,)), get_r.step((ends,))
    first_gate, first_up = get_gate.step(deep_v + (ends,)), get_up.step(deep_r + (ends,))
    start_state = state_before(
        tie(ends, *deep_v, *deep_r, *second_down).reshape(2 * ndim, SUB, LANES), par["hop"], "seq", False
    )
    start_state = tie(start_state, *middle_v, *middle_r, *first_gate, *first_up)
    for _ in range(seq_steps - 1):
        deep_gate, deep_up = get_gate.step((start_state,)), get_up.step((start_state,))
    get_down.step(deep_gate + deep_up)
    mixed, sent_mix, kept = kernel_call(
        mix_kernel,
        [((rows * SUB, LANES), f32), ((rows, width), bf16), ((rows // SPAN, 2 * ndim * SUB, LANES), f32)],
        [xs, flat(start_state), a_flat, b_flat, g_flat, par["skip"]],
        scratch=[pltpu.VMEM((2 * ndim * SUB, LANES), f32)],
        name="mix", micros=16, after=deep_gate + deep_up,
    )
    near_last = get_v.step((start_state,)) + get_r.step((start_state,))
    third_gate, third_up = get_gate.step((mixed,) + near_last), get_up.step((mixed,) + near_last)
    for getter in (get_v, get_r):
        while getter.order is not None and getter.place < all_bits:
            getter.step()
    weight1 = Weight(Part(get_v, 0, values_width, short), Part(get_r, 0, values_width + z_width, short, 0, values_width))
    if fits:
        tall = w_h.shape[0]
        weight2 = Weight(
            Part(get_v, values_width, width, tall), Part(get_r, values_width + z_width, width, tall, short)
        )
    else:
        weight2 = Weight(Part(Gather(low(w_h), None), 0, width, w_h.shape[0]))

    tile = 256
    w1_shape, w2_shape = (width, 2 * values_width + z_width), (values_width, width)
    w3_shape, w4_shape = (width, 2 * hidden_width), (hidden_width, width)
    dma = pltpu.SemaphoreType.DMA
    wide = ((rows, values_width), bf16)

    def other_core(value):
        return swap_bit(value, 0)

    norm_other = other_core(tie(sent_norm, mixed))

    def any_of(*groups):
        return [ANY] * sum(len(group.arrays) for group in groups)

    tile = 512
    weight1.tiles = values_width // tile
    strip = ((rows, values_width), bf16, (rows, tile), lambda g, me: (0, g))

    def still(shape, dtype):
        return (shape, dtype, shape, lambda g, me: (0, 0))

    def loose(*groups):
        return [(array, None, None) for group in groups for array in group.arrays]

    shared, queries, keys, log_total, value_pre, values, gate_pre, attended, gated = grid_call(
        functools.partial(attention_kernel, weight1, tile),
        [still((rows, z_width), f32), still((rows, z_width), bf16), still((rows, z_width), bf16), still((rows, 1), f32)]
        + [strip] * 5,
        [whole(array) for array in (sent_norm, sent_mix, seg_col, seg_row, valid_row, full_qg, full_qb, full_kg)]
        + loose(weight1),
        weight1.tiles, me,
        scratch=[pltpu.VMEM(w1_shape, bf16), pltpu.VMEM((rows, rows), bf16), pltpu.SemaphoreType.DMA((2,))],
        name="attention", micros=15, after=third_gate + third_up + (norm_other,),
    )
    middle, ffn_in, inverse = kernel_call(
        functools.partial(project_kernel, weight2),
        [((rows, width), f32), ((rows, width), bf16), ((rows, 1), f32)],
        [me, gated, tokens[0], valid_col, full_fg, *weight2.arrays],
        [SM] + [VM] * 4 + any_of(weight2),
        scratch=[pltpu.VMEM(w2_shape, bf16), pltpu.SemaphoreType.DMA((2,))],
        name="project", micros=6,
    )

    get_down.step(third_gate + third_up)
    for getter in (get_gate, get_up, get_down):
        while getter.order is not None and getter.place < all_bits - 1:
            getter.step()
        getter.step((ffn_in,))
    weight4 = Weight(Part(get_down, 0, width, w_down.shape[0]))
    weight3 = Weight(Part(get_gate, 0, hidden_width, short), Part(get_up, 0, hidden_width, short, 0, hidden_width))
    grad_low = cotangent[0]
    part = width // 2
    cot_own = lax.dynamic_slice_in_dim(grad_low, core * part, part, axis=1)
    cot_oth = other_core(tie(lax.dynamic_slice_in_dim(grad_low, (1 - core) * part, part, axis=1), mixed))
    gated_other, mix_other = other_core(gated), other_core(sent_mix)
    half = hidden_width // 2
    pair = ((rows, hidden_width), bf16, (rows, hidden_width), lambda g, me: (0, 0))
    hid, near, far = grid_call(
        functools.partial(hidden_kernel, weight3, weight4),
        [((rows, hidden_width), bf16, (rows, half), lambda g, me: (0, g)), pair, pair],
        [whole(ffn_in), whole(grad_low)] + [(array, None, None) for array in weight3.arrays + weight4.arrays],
        2, me,
        scratch=[pltpu.VMEM(w3_shape, bf16), pltpu.VMEM(w4_shape, bf16), pltpu.SemaphoreType.DMA((2, 3))],
        name="hidden", micros=15, after=(cot_oth, gated_other, mix_other),
    )
    ffn_other = other_core(ffn_in)
    (output,) = kernel_call(
        functools.partial(out_kernel, weight4),
        [((rows, width), bf16)],
        [me, hid, middle, *weight4.arrays],
        [SM, VM, VM] + any_of(weight4),
        scratch=[pltpu.VMEM(w4_shape, bf16), pltpu.SemaphoreType.DMA((2,))],
        name="out", micros=7,
    )
    hid_pair, ffn_pair = (hid, other_core(hid)), (ffn_in, ffn_other)
    far_other = other_core(far)
    down = weight_grad(hid_pair, (cot_own, cot_oth), reduce_a, me, chips, "grad_down", halves=2, after=(output,))
    gate = weight_grad(ffn_pair, (near, far_other), reduce_b, me, chips, "grad_gate", part=(0, 2), after=(down.sent,))
    up = weight_grad(
        ffn_pair, (near, far_other), reduce_a, me, chips, "grad_up", part=(1, 2), after=(gate.sent,)
    )
    grad_middle, low_own, low_oth, middle_low, dfg = kernel_call(
        functools.partial(ffn_back_kernel, weight3),
        [((rows, width), f32), ((rows, part), bf16), ((rows, part), bf16), ((rows, width), bf16), ((1, width), f32)],
        [me, near, far, middle, inverse, grad_low, full_fg, *weight3.arrays],
        [SM] + [VM] * 6 + any_of(weight3),
        scratch=[pltpu.VMEM(w3_shape, bf16), pltpu.VMEM((rows, width), f32), pltpu.SemaphoreType.DMA((2,))],
        name="ffn_back", micros=17, after=(up.sent,),
    )
    heads = weight_grad(
        (gated, gated_other), (low_own, other_core(low_oth)), reduce_b, me, chips, "grad_h", after=down.step(low_own)
    )
    half_values = still((rows, values_width // 2), bf16)
    half_mixed = still((rows, (values_width + z_width) // 2), bf16)
    strips = values_width // tile // 2

    def turn(g, me):
        return (0, tile_order(weight2, g, strips, me))

    strip = ((rows, values_width), bf16, (rows, tile), turn)
    grad_v, grad_r, gv_own, gv_oth, gr_own, gr_oth, grad_z, dgains = grid_call(
        functools.partial(attention_back_kernel, weight2, tile),
        [strip, strip] + [half_values] * 2 + [half_mixed] * 2
        + [still((rows, z_width), bf16), still((3, z_width), f32)],
        [whole(array) for array in (middle_low, queries, keys, log_total, shared, seg_col, seg_row, valid_row, full_qg,
                                    full_kg)]
        + [columns_of(array, tile, turn) for array in (value_pre, values, gate_pre, attended)] + loose(weight2),
        2 * strips, me,
        scratch=[pltpu.VMEM(w2_shape, bf16), pltpu.VMEM((rows, rows), f32), pltpu.VMEM((rows, rows), bf16),
                 pltpu.VMEM((rows, rows), f32), pltpu.SemaphoreType.DMA((2,))],
        name="attention_back", micros=19, after=(heads.sent,) + gate.step(heads.sent),
    )
    grad_mix_rows, grad_norm_rows = kernel_call(
        functools.partial(sent_back_kernel, weight1),
        [((rows, width), bf16)] * 2,
        [me, grad_v, grad_r, grad_z, *weight1.arrays],
        [SM, VM, VM, VM] + any_of(weight1),
        scratch=[pltpu.VMEM(w1_shape, bf16), pltpu.SemaphoreType.DMA((2,))],
        name="sent_back", micros=11, after=up.step(gv_oth) + down.step(gv_oth),
    )
    gv_other, gr_other = other_core(gv_oth), other_core(gr_oth)
    drive, back_ends = kernel_call(
        back_ends_kernel, [((rows * SUB, LANES), f32), ((2 * ndim * SUB, LANES), f32)],
        [grad_mix_rows, mixed, a_flat, b_flat], name="back_ends", micros=12,
        after=heads.step(grad_mix_rows) + down.step(grad_mix_rows),
    )
    value = weight_grad((sent_norm, norm_other), (gv_own, gv_other), reduce_a, me, chips, "grad_v",
                        after=(back_ends, gr_other))
    both = merge(gate, up, back_ends)
    reset = weight_grad((sent_mix, mix_other), (gr_own, gr_other), reduce_b, me, chips, "grad_r",
                        after=(value.sent,) + both.pins + down.step(value.sent))
    hop_back = (par["hop"][0], -par["hop"][1])
    back_state = flat(
        state_before(back_ends.reshape(2 * ndim, SUB, LANES), hop_back, "seq", True,
                     {2: lambda: (value.sent,), 4: lambda: (reset.sent,)})
    )
    sums = jnp.zeros(((3 * ndim + 1) * SUB, LANES), f32)
    cuts = 4
    plan = [
        lambda done: heads.step(reset.sent) + both.step(reset.sent),
        lambda done: value.step(done) + heads.step(done),
        lambda done: reset.step(done) + both.step(done),
        lambda done: heads.step(done),
    ]
    last = []

    def merge_last(done):
        last.append(merge(value, reset, done))
        return last[0].pins

    done = back_state
    long = rows * SUB // cuts
    pieces_dx = []
    for cut in range(cuts - 1, -1, -1):
        block = pl.BlockSpec((long, LANES), lambda i, cut=cut: (cut, 0))
        keep_block = pl.BlockSpec((rows // SPAN // cuts, 2 * ndim * SUB, LANES), lambda i, cut=cut: (cut, 0, 0))
        dxs, back_state, sums = kernel_call(
            back_scan_kernel,
            [((long, LANES), f32), ((2 * ndim * SUB, LANES), f32), (((3 * ndim + 1) * SUB, LANES), f32)],
            [xs, drive, kept, back_state, sums, a_flat, b_flat, g_flat, par["skip"]],
            [block, block, keep_block] + [VM] * 6,
            scratch=[pltpu.VMEM((SPAN, 8 * SUB, LANES), f32)],
            name="back", micros=10, after=plan.pop(0)(done), grid=(1,), out_specs=[VM] * 3,
        )
        pieces_dx.insert(0, dxs)
        done = dxs
    pins = merge_last(done)
    last = last[0]
    dn, dgain, suffix, back_totals = kernel_call(
        back_norm_kernel,
        [((rows, width), f32), ((1, width), f32), ((rows, LANES), f32), ((DOCS, LANES), f32)],
        [*pieces_dx, grad_norm_rows, tokens[0], valid_col, seg_col, seg_row, prefix, carry, gain_row],
        name="back_norm", micros=6, after=pins,
    )
    sums = sums.reshape(3 * ndim + 1, SUB, LANES)
    d_params = ema_param_grads(par, sums)
    d_pack = jnp.concatenate(list(d_params) + [dgain.reshape(1, SUB, LANES), sums[3 * ndim :]], axis=0)
    d_pack = jnp.transpose(d_pack.reshape(4 * ndim + 2, seq_count, lanes), (1, 0, 2))
    owned = [dgains[i].reshape(devices, zs) for i in range(3)] + [dfg.reshape(devices, fs)]
    owned = jnp.concatenate(owned, axis=1).reshape(seq_count, -1)
    owned = jnp.pad(owned, ((0, 0), (0, extra * lanes - size))).reshape(seq_count, extra, lanes)
    own_pack, after_totals = exchange_end(jnp.concatenate([d_pack, owned], axis=1), tie(back_totals, *last.step(back_totals)), "seq")
    back_carry = lax.dynamic_slice_in_dim(after_totals, row_segs[rows - 1], 1)
    (input_grad,) = kernel_call(
        input_kernel, [((rows, width), f32)],
        [dn, suffix, back_carry, tokens[0], valid_col, seg_col, prefix, carry, grad_middle], name="input", micros=6,
        after=last.step(back_carry),
    )
    total = sum_over(sum_over(own_pack, "core"), "chip")
    mine = lax.dynamic_index_in_dim(total[4 * ndim + 2 :].reshape(-1)[:size].reshape(dp_count, -1), dp_index, 0, keepdims=False)
    (shard_down,) = down.finish(core, [part])
    shard_gate, shard_up = both.finish(core, [hidden_width // 2] * 2, done)
    (shard_h,) = heads.finish(core, [part], done)
    shard_v, shard_r, shard_z = last.finish(core, [values_width // 2, values_width // 2, z_width // 2])
    return (
        output[None], input_grad[None], shard_z, shard_v, shard_r, shard_h, shard_gate, shard_up, shard_down,
        mine[:zs], mine[zs : 2 * zs], mine[2 * zs : 3 * zs], mine[3 * zs :],
        total[4 * ndim], total[:ndim].T, total[ndim : 2 * ndim].T, total[2 * ndim : 3 * ndim].T,
        total[3 * ndim : 4 * ndim].T, total[4 * ndim + 1],
    )


def solution(mesh):
    shape = mesh.devices.shape
    whole = Mesh(mesh.devices.reshape(shape[0], shape[1] // 2, 2), AXES)
    by_token, by_group = P(("chip", "core"), "seq", None), P(("chip", "core"), None)
    by_row, by_owner = P(AXES, None), P(AXES)
    params = (by_row,) * 7 + (by_owner,) * 4 + (P("seq"),) + (P("seq", None),) * 4 + (P("seq"),)
    return jax.shard_map(
        on_device,
        mesh=whole,
        in_specs=(by_token, by_token, by_group, by_group) + params,
        out_specs=(by_token, by_token) + params,
        check_vma=False,
    )
```

```python
import functools
import math

import jax
import jax.numpy as jnp
from jax import lax
from jax.experimental import pallas as pl
from jax.experimental.pallas import tpu as pltpu
from jax.sharding import Mesh, PartitionSpec as P

AXES = ("seq", "chip", "core")
GROUP = 64
DOCS = 16
LANES = 128
SUB = 8
SPAN = 32
BAND = 64
bf16 = jnp.bfloat16
f32 = jnp.float32
VMEM_LIMIT = 60 * 1024 * 1024
PACE = 0.1


def split3(value):
    first = value.astype(bf16)
    rest = value - first.astype(f32)
    second = rest.astype(bf16)
    third = (rest - second.astype(f32)).astype(bf16)
    return first, second, third


def dot(left, right):
    return jnp.dot(left, right, preferred_element_type=f32)


def dot3(left, parts):
    return dot(left, parts[0]) + dot(left, parts[1]) + dot(left, parts[2])


def dot3_left(parts, right):
    return dot(parts[0], right) + dot(parts[1], right) + dot(parts[2], right)


def sigmoid(value):
    return 0.5 * jnp.tanh(0.5 * value) + 0.5


def iota(shape, axis):
    return lax.broadcasted_iota(jnp.int32, shape, axis)


def group_pick(width, shift):
    own = lax.shift_right_logical(iota((width, LANES), 0), GROUP.bit_length() - 1)
    return (own + shift == iota((width, LANES), 1)).astype(bf16)


def group_spread(groups, width):
    own = lax.shift_right_logical(iota((groups, width), 1), GROUP.bit_length() - 1)
    return (own == iota((groups, width), 0)).astype(bf16)


ANY = pl.BlockSpec(memory_space=pl.ANY)
VM = pl.BlockSpec(memory_space=pltpu.VMEM)
SM = pl.BlockSpec(memory_space=pltpu.SMEM)


def kernel_call(body, outs, args, specs=None, scratch=(), name=None, micros=10, after=(), grid=None, out_specs=None):
    specs = [VM] * len(args) if specs is None else specs
    count = len(args)

    def run(*refs):
        body(*refs[:count], *refs[count + len(after) :])

    more = {} if grid is None else dict(grid=grid, out_specs=tuple(out_specs))
    return pl.pallas_call(
        run,
        out_shape=tuple(jax.ShapeDtypeStruct(shape, dtype) for shape, dtype in outs),
        in_specs=list(specs) + [ANY] * len(after),
        scratch_shapes=list(scratch),
        compiler_params=pltpu.CompilerParams(vmem_limit_bytes=VMEM_LIMIT),
        cost_estimate=pl.CostEstimate(
            flops=int(micros * PACE * 1.0e9), bytes_accessed=int(micros * PACE * 3.0e6), transcendentals=0
        ),
        name=name,
        **more,
    )(*args, *after)


def grid_call(body, outs, args, steps, me, scratch=(), name=None, micros=10, after=()):
    def spec(shape, block, index):
        if block is None:
            return ANY
        if index is None:
            return pl.BlockSpec(shape, lambda g, me: (0,) * len(shape))
        return pl.BlockSpec(block, index)

    count = len(args)

    def run(*refs):
        body(*refs[: 1 + count], *refs[1 + count + len(after) :])

    return pl.pallas_call(
        run,
        out_shape=tuple(jax.ShapeDtypeStruct(shape, dtype) for shape, dtype, _, _ in outs),
        grid_spec=pltpu.PrefetchScalarGridSpec(
            num_scalar_prefetch=1,
            grid=(steps,),
            in_specs=[spec(array.shape, block, index) for array, block, index in args] + [ANY] * len(after),
            out_specs=tuple(spec(shape, block, index) for shape, _, block, index in outs),
            scratch_shapes=list(scratch),
        ),
        compiler_params=pltpu.CompilerParams(vmem_limit_bytes=VMEM_LIMIT),
        cost_estimate=pl.CostEstimate(
            flops=int(micros * PACE * 1.0e9), bytes_accessed=int(micros * PACE * 3.0e6), transcendentals=0
        ),
        name=name,
    )(me, *(array for array, _, _ in args), *after)


WHOLE = (1,)


def whole(array):
    return (array, WHOLE, None)


def columns_of(array, width, index=lambda g, me: (0, g)):
    return (array, (array.shape[0], width), index)


def tie(value, *after):
    def nothing(*refs):
        return None

    return pl.pallas_call(
        nothing,
        out_shape=jax.ShapeDtypeStruct(value.shape, value.dtype),
        in_specs=[ANY] * (1 + len(after)),
        out_specs=ANY,
        input_output_aliases={0: 0},
        name="tie",
    )(value, *after)


def zero_after(*after):
    return tie(jnp.zeros((1, 1, 1), bf16), *after)


def split_wide(value):
    return jnp.concatenate(split3(value), axis=1)


def spread_wide(groups, width, start):
    own = lax.shift_right_logical(iota((3 * groups, LANES), 1) + start, GROUP.bit_length() - 1)
    return (own == lax.rem(iota((3 * groups, LANES), 0), groups)).astype(bf16)


def moments(total, groups):
    counts = jnp.maximum(total[:, 2 * groups : 2 * groups + 1], 1.0) * float(GROUP)
    means = total[:, :groups] / counts
    variance = total[:, groups : 2 * groups] / counts - means * means
    return means, lax.rsqrt(variance + 1e-05), counts


def stats_kernel(tok_ref, valid_ref, segc_ref, segr_ref, prefix_ref, totals_ref):
    rows, width = tok_ref.shape
    groups = width // GROUP
    valid = valid_ref[...]
    masked = tok_ref[...].astype(f32) * valid
    low = masked.astype(bf16)
    square = masked * masked
    high = square.astype(bf16)
    rest = (square - high.astype(f32)).astype(bf16)
    second = group_pick(width, groups)
    sums = dot(low, group_pick(width, 0)) + dot(high, second) + dot(rest, second)
    sums = sums + jnp.where(iota((rows, LANES), 1) == 2 * groups, valid, 0.0)
    parts = split3(sums)
    earlier = (iota((rows, rows), 1) <= iota((rows, rows), 0)) & (segc_ref[...] == segr_ref[...])
    prefix_ref[...] = dot3(earlier.astype(f32).astype(bf16), parts)
    member = (iota((DOCS, rows), 0) == segr_ref[...]).astype(f32).astype(bf16)
    totals_ref[...] = dot3(member, parts)


def scan_ends(src_ref, a_ref, b_ref, end_ref, rows, ndim, reverse):
    half = ndim // 2
    for start in range(0, ndim, half):
        a = [a_ref[pl.ds((start + n) * SUB, SUB), :] for n in range(half)]
        b = [b_ref[pl.ds((start + n) * SUB, SUB), :] for n in range(half)]

        def step(i, state, a=a, b=b):
            t = rows - 1 - i if reverse else i
            x = src_ref[pl.ds(pl.multiple_of(t * SUB, SUB), SUB), :]
            fresh = []
            for n in range(half):
                re, im = state[2 * n], state[2 * n + 1]
                if reverse:
                    fresh += [a[n] * re + b[n] * im + x, a[n] * im - b[n] * re]
                else:
                    fresh += [a[n] * re - b[n] * im + x, a[n] * im + b[n] * re]
            return tuple(fresh)

        zero = jnp.zeros((SUB, LANES), f32)
        state = lax.fori_loop(0, rows, step, (zero,) * (2 * half), unroll=32)
        for n in range(half):
            end_ref[pl.ds((start + n) * SUB, SUB), :] = state[2 * n]
            end_ref[pl.ds((ndim + start + n) * SUB, SUB), :] = state[2 * n + 1]


def all_moments(prefix_ref, segc_ref, carry_ref, groups):
    total = prefix_ref[...] + jnp.where(segc_ref[...] == segc_ref[0:1, :], carry_ref[...], 0.0)
    return moments(total, groups)


def lane_rows(j, rows):
    return pl.ds(j, rows, stride=SUB)


def norm_kernel(tok_ref, valid_ref, segc_ref, prefix_ref, carry_ref, gain_ref, a_ref, b_ref,
                sent_ref, xs_ref, end_ref):
    rows, width = tok_ref.shape
    groups = width // GROUP
    ndim = a_ref.shape[0] // SUB
    means, scale, _ = all_moments(prefix_ref, segc_ref, carry_ref, groups)
    means, scale, valid = split_wide(means), split_wide(scale), valid_ref[...]
    for j in range(SUB):
        at = slice(j * LANES, (j + 1) * LANES)
        spread = spread_wide(groups, width, j * LANES)
        normed = (tok_ref[:, at].astype(f32) * valid - dot(means, spread)) * dot(scale, spread) * gain_ref[:, at]
        sent_ref[:, at] = normed.astype(bf16)
        xs_ref[lane_rows(j, rows), :] = normed
    scan_ends(xs_ref, a_ref, b_ref, end_ref, rows, ndim, False)


def mix_kernel(xs_ref, start_ref, a_ref, b_ref, g_ref, skip_ref, mixed_ref, sent_ref, keep_ref, state_ref):
    rows = xs_ref.shape[0] // SUB
    ndim = a_ref.shape[0] // SUB
    half = ndim // 2
    state_ref[...] = start_ref[...]

    def chunk(i, _):
        keep_ref[i] = state_ref[...]
        for start in range(0, ndim, half):
            re_at = [pl.ds((start + n) * SUB, SUB) for n in range(half)]
            im_at = [pl.ds((ndim + start + n) * SUB, SUB) for n in range(half)]
            a = [a_ref[at, :] for at in re_at]
            b = [b_ref[at, :] for at in re_at]
            g = [g_ref[at, :] for at in re_at]

            def step(k, state, start=start, a=a, b=b, g=g):
                at = pl.ds(pl.multiple_of((i * SPAN + k) * SUB, SUB), SUB)
                x = xs_ref[at, :]
                fresh, terms = [], []
                for n in range(half):
                    re, im = state[2 * n], state[2 * n + 1]
                    now = a[n] * re - b[n] * im + x
                    fresh += [now, a[n] * im + b[n] * re]
                    terms.append(g[n] * now)
                terms.append(skip_ref[...] * x if start == 0 else mixed_ref[at, :])
                while len(terms) > 1:
                    terms = [sum(terms[p : p + 2][1:], terms[p]) for p in range(0, len(terms), 2)]
                mixed_ref[at, :] = terms[0]
                return tuple(fresh)

            state = []
            for n in range(half):
                state += [state_ref[re_at[n], :], state_ref[im_at[n], :]]
            state = lax.fori_loop(0, SPAN, step, tuple(state), unroll=SPAN)
            for n in range(half):
                state_ref[re_at[n], :] = state[2 * n]
                state_ref[im_at[n], :] = state[2 * n + 1]
        return 0

    lax.fori_loop(0, rows // SPAN, chunk, 0)

    def band(i, _):
        at = pl.ds(pl.multiple_of(i * BAND, BAND), BAND)
        for j in range(SUB):
            mixed = mixed_ref[pl.ds(i * (BAND * SUB) + j, BAND, stride=SUB), :]
            sent_ref[at, j * LANES : (j + 1) * LANES] = (mixed * sigmoid(mixed)).astype(bf16)
        return 0

    lax.fori_loop(0, rows // BAND, band, 0)


def back_ends_kernel(grad_ref, mixed_ref, a_ref, b_ref, drive_ref, end_ref):
    rows = grad_ref.shape[0]
    ndim = a_ref.shape[0] // SUB

    def band(i, _):
        at = pl.ds(pl.multiple_of(i * BAND, BAND), BAND)
        for j in range(SUB):
            where = pl.ds(i * (BAND * SUB) + j, BAND, stride=SUB)
            mixed = mixed_ref[where, :]
            sigma = sigmoid(mixed)
            slope = sigma * (1.0 + mixed * (1.0 - sigma))
            drive_ref[where, :] = grad_ref[at, j * LANES : (j + 1) * LANES].astype(f32) * slope
        return 0

    lax.fori_loop(0, rows // BAND, band, 0)
    scan_ends(drive_ref, a_ref, b_ref, end_ref, rows, ndim, True)


def back_scan_kernel(xs_ref, drive_ref, keep_ref, start_ref, sums_in_ref, a_ref, b_ref, g_ref, skip_ref,
                     dxs_ref, state_ref, sums_ref, hist_ref):
    ndim = a_ref.shape[0] // SUB
    rows = xs_ref.shape[0] // SUB
    part = 4
    count = rows // SPAN
    state_ref[...] = start_ref[...]
    sums_ref[...] = sums_in_ref[...]

    def chunk(c, _):
        i = count - 1 - c
        for start in range(0, ndim, part):
            re_at = [pl.ds((start + n) * SUB, SUB) for n in range(part)]
            im_at = [pl.ds((ndim + start + n) * SUB, SUB) for n in range(part)]
            last_at = [pl.ds((2 * ndim + start + n) * SUB, SUB) for n in range(part)]
            a = [a_ref[at, :] for at in re_at]
            b = [b_ref[at, :] for at in re_at]
            g = [g_ref[at, :] for at in re_at]

            def forward(k, state, a=a, b=b):
                x = xs_ref[pl.ds(pl.multiple_of((i * SPAN + k) * SUB, SUB), SUB), :]
                fresh = []
                for n in range(part):
                    re, im = state[2 * n], state[2 * n + 1]
                    hist_ref[k, pl.ds(2 * n * SUB, SUB), :] = re
                    hist_ref[k, pl.ds((2 * n + 1) * SUB, SUB), :] = im
                    fresh += [a[n] * re - b[n] * im + x, a[n] * im + b[n] * re]
                return tuple(fresh)

            state = []
            for n in range(part):
                state += [keep_ref[i, re_at[n], :], keep_ref[i, im_at[n], :]]
            lax.fori_loop(0, SPAN, forward, tuple(state), unroll=SPAN)

            def backward(k, held, start=start, a=a, b=b, g=g):
                t = SPAN - 1 - k
                at = pl.ds(pl.multiple_of((i * SPAN + t) * SUB, SUB), SUB)
                x, drive = xs_ref[at, :], drive_ref[at, :]
                fresh, terms = [], []
                for n in range(part):
                    re, im, m_re, m_im, same = held[5 * n : 5 * n + 5]
                    now_re = a[n] * re + b[n] * im + drive
                    now_im = a[n] * im - b[n] * re
                    old_re = hist_ref[t, pl.ds(2 * n * SUB, SUB), :]
                    old_im = hist_ref[t, pl.ds((2 * n + 1) * SUB, SUB), :]
                    fresh += [
                        now_re,
                        now_im,
                        m_re + (now_re * old_re + now_im * old_im),
                        m_im + (now_im * old_re - now_re * old_im),
                        same + x * now_re,
                    ]
                    terms.append(g[n] * now_re)
                total = (terms[0] + terms[1]) + (terms[2] + terms[3])
                if start == 0:
                    dxs_ref[at, :] = total + skip_ref[...] * drive
                else:
                    dxs_ref[at, :] = total + dxs_ref[at, :]
                return tuple(fresh)

            held = []
            for n in range(part):
                held += [state_ref[re_at[n], :], state_ref[im_at[n], :]]
                held += [sums_ref[re_at[n], :], sums_ref[im_at[n], :], sums_ref[last_at[n], :]]
            held = lax.fori_loop(0, SPAN, backward, tuple(held), unroll=SPAN)
            for n in range(part):
                state_ref[re_at[n], :] = held[5 * n]
                state_ref[im_at[n], :] = held[5 * n + 1]
                sums_ref[re_at[n], :] = held[5 * n + 2]
                sums_ref[im_at[n], :] = held[5 * n + 3]
                sums_ref[last_at[n], :] = held[5 * n + 4]
        return 0

    lax.fori_loop(0, count, chunk, 0)

    def skip_step(k, total):
        at = pl.ds(pl.multiple_of(k * SUB, SUB), SUB)
        return total + xs_ref[at, :] * drive_ref[at, :]

    last = pl.ds(3 * ndim * SUB, SUB)
    sums_ref[last, :] = lax.fori_loop(0, rows, skip_step, sums_ref[last, :], unroll=8)


def back_norm_kernel(*refs):
    dxs_refs, refs = refs[:-12], refs[-12:]
    (grad_ref, tok_ref, valid_ref, segc_ref, segr_ref, prefix_ref, carry_ref, gain_ref,
     dn_ref, dgain_ref, suffix_ref, totals_ref) = refs
    rows, width = tok_ref.shape
    groups = width // GROUP
    means, scale, counts = all_moments(prefix_ref, segc_ref, carry_ref, groups)
    wide_means, wide_scale, valid = split_wide(means), split_wide(scale), valid_ref[...]
    plain, leaning = jnp.zeros((rows, LANES), f32), jnp.zeros((rows, LANES), f32)
    for j in range(SUB):
        at = slice(j * LANES, (j + 1) * LANES)
        spread = spread_wide(groups, width, j * LANES)
        own = lax.shift_right_logical(iota((LANES, LANES), 0) + j * LANES, GROUP.bit_length() - 1)
        pick = (own == iota((LANES, LANES), 1)).astype(bf16)
        centred = tok_ref[:, at].astype(f32) * valid - dot(wide_means, spread)
        ema = [ref[lane_rows(j, ref.shape[0] // SUB), :] for ref in dxs_refs]
        dn = grad_ref[:, at].astype(f32) + jnp.concatenate(ema, axis=0)
        dgain_ref[:, at] = jnp.sum(dn * centred * dot(wide_scale, spread), axis=0, keepdims=True)
        dn = dn * gain_ref[:, at]
        dn_ref[:, at] = dn
        plain = plain + dot3_left(split3(dn), pick)
        leaning = leaning + dot3_left(split3(dn * centred), pick)
    plain, leaning = plain[:, :groups], leaning[:, :groups]
    d_variance = -0.5 * leaning * scale * scale * scale
    d_second = d_variance / counts
    d_first = (-scale * plain - 2.0 * means * d_variance) / counts
    flow = jnp.concatenate([d_first, d_second, jnp.zeros((rows, LANES - 2 * groups), f32)], axis=1)
    parts = split3(flow)
    later = (iota((rows, rows), 1) >= iota((rows, rows), 0)) & (segc_ref[...] == segr_ref[...])
    suffix_ref[...] = dot3(later.astype(f32).astype(bf16), parts)
    member = (iota((DOCS, rows), 0) == segr_ref[...]).astype(f32).astype(bf16)
    totals_ref[...] = dot3(member, parts)


def input_kernel(dn_ref, suffix_ref, back_ref, tok_ref, valid_ref, segc_ref, prefix_ref, carry_ref, middle_ref, out_ref):
    rows, width = tok_ref.shape
    groups = width // GROUP
    _, scale, _ = all_moments(prefix_ref, segc_ref, carry_ref, groups)
    flow = suffix_ref[...] + jnp.where(segc_ref[...] == segc_ref[rows - 1 : rows, :], back_ref[...], 0.0)
    scale, valid = split_wide(scale), valid_ref[...]
    first, second = split_wide(flow[:, :groups]), split_wide(flow[:, groups : 2 * groups])
    for j in range(SUB):
        at = slice(j * LANES, (j + 1) * LANES)
        spread = spread_wide(groups, width, j * LANES)
        masked = tok_ref[:, at].astype(f32) * valid
        grad = dn_ref[:, at] * dot(scale, spread) + dot(first, spread) + 2.0 * masked * dot(second, spread)
        out_ref[:, at] = valid * (middle_ref[:, at] + grad)


def swap(value, axis, bit):
    count = lax.axis_size(axis)
    return lax.ppermute(value, axis, [(i, i ^ bit) for i in range(count)])


def gather_small(value, axis):
    index, count = lax.axis_index(axis), lax.axis_size(axis)
    value, bit = value[None], 1
    while bit < count:
        other = swap(value, axis, bit)
        upper = (index & bit) != 0
        value = jnp.concatenate([jnp.where(upper, other, value), jnp.where(upper, value, other)], axis=0)
        bit *= 2
    return value


def cmul(left, right):
    return (left[0] * right[0] - left[1] * right[1], left[0] * right[1] + left[1] * right[0])


def state_before(ends, hop, axis, reverse, hold=None):
    index, count = lax.axis_index(axis), lax.axis_size(axis)
    if reverse:
        index = count - 1 - index
    half = ends.shape[0] // 2
    before = (jnp.zeros_like(ends[:half]), jnp.zeros_like(ends[:half]))
    reach = (jnp.ones_like(hop[0]), jnp.zeros_like(hop[1]))
    bit = 1
    while bit < count:
        waits = hold[bit]() if hold and bit in hold else ()
        other = swap(tie(ends, *waits) if waits else ends, axis, bit)
        upper = (index & bit) != 0
        far, own = (other[:half], other[half:]), (ends[:half], ends[half:])
        moved = cmul(reach, far)
        before = tuple(v + jnp.where(upper, w, 0.0) for v, w in zip(before, moved))
        if bit * 2 < count:
            lower = tuple(jnp.where(upper, v, w) for v, w in zip(far, own))
            higher = tuple(jnp.where(upper, w, v) for v, w in zip(far, own))
            carried = cmul(hop, lower)
            ends = jnp.concatenate([carried[0] + higher[0], carried[1] + higher[1]], axis=0)
            longer = cmul(reach, hop)
            reach = tuple(jnp.where(upper, v, w) for v, w in zip(longer, reach))
            hop = cmul(hop, hop)
        bit *= 2
    return jnp.concatenate(before, axis=0)


def ema_params(full, ndim, rows):
    full = jnp.transpose(full, (1, 0, 2))
    full = full.reshape(full.shape[0], SUB, -1)
    rate, angle, input_w, output_w = (full[i * ndim : (i + 1) * ndim] for i in range(4))
    gain, skip = full[4 * ndim], full[4 * ndim + 1]
    base = jnp.sqrt(rate * (2.0 - rate))
    cos, sin = jnp.cos(angle), jnp.sin(angle)
    a, b = (1.0 - rate) * cos, (1.0 - rate) * sin
    hop, steps = (a, b), 1
    while steps < rows:
        hop, steps = cmul(hop, hop), steps * 2
    return dict(rate=rate, input_w=input_w, output_w=output_w, gain=gain, skip=skip, base=base,
                cos=cos, sin=sin, a=a, b=b, coeff=base * input_w, hop=hop)


def ema_param_grads(par, sums):
    ndim = par["rate"].shape[0]
    m_re, m_im, same = sums[:ndim], sums[ndim : 2 * ndim], sums[2 * ndim : 3 * ndim]
    weight = par["output_w"] * par["coeff"]
    d_a, d_b = weight * m_re, weight * m_im
    d_coeff = par["output_w"] * same
    d_output = par["coeff"] * same
    d_input = par["base"] * d_coeff
    d_rate = d_coeff * par["input_w"] * (1.0 - par["rate"]) / par["base"] - par["cos"] * d_a - par["sin"] * d_b
    d_angle = par["a"] * d_b - par["b"] * d_a
    return d_rate, d_angle, d_input, d_output


def mul_t(left, right):
    return lax.dot_general(left, right, (((1,), (1,)), ((), ())), preferred_element_type=f32)


def t_mul(left, right):
    return lax.dot_general(left, right, (((0,), (0,)), ((), ())), preferred_element_type=f32)


def silu_grad(value):
    sigma = sigmoid(value)
    return sigma * (1.0 + value * (1.0 - sigma))


def bits_of(count):
    return count.bit_length() - 1


class Part:
    def __init__(self, source, take, width, rows, lower=0, column=0):
        self.arrays, self.owners, self.top = source.arrays, source.owners, source.top
        self.take, self.width, self.rows, self.lower, self.column = take, width, rows, lower, column

    def copies(self, refs, where, me, sem, span=None, near=None):
        made = []
        first, width = (0, self.width) if span is None else span
        for ref, owners in zip(refs, self.owners):
            block = ref.shape[1]
            for slot, owner in enumerate(owners):
                if near is not None and near != (owner < (1 << self.top)):
                    continue
                start = (me ^ owner) * self.rows + self.lower
                start = pl.multiple_of(start, math.gcd(self.rows, block)) if len(owners) > 1 else 0
                source = ref.at[slot, :, pl.ds(self.take + first, width)]
                to = where.at[pl.ds(start, block), pl.ds(self.column + first, width)]
                made.append(pltpu.make_async_copy(source, to, sem))
        return made


class Weight:
    def __init__(self, *parts):
        self.parts, self.arrays, self.places = parts, [], []
        self.split, self.top = len(parts[0].owners[0]) > 1, parts[0].top
        self.nears = (True, False) if self.split else (None,)
        for part in parts:
            place = []
            for array in part.arrays:
                same = [n for n, known in enumerate(self.arrays) if known is array]
                if not same:
                    self.arrays.append(array)
                place.append(same[0] if same else len(self.arrays) - 1)
            self.places.append(place)

    def copies(self, refs, where, me, sem, which=None, span=None, near=None):
        made = []
        for n, (part, place) in enumerate(zip(self.parts, self.places)):
            if which is None or which == n:
                made += part.copies([refs[n] for n in place], where, me, sem, span, near)
        return made


class Gather:
    def __init__(self, shard, order):
        self.order = order
        self.top = max(order or (0,))
        if order is None:
            full = lax.all_gather(shard, AXES, axis=0, tiled=True)
            self.arrays, self.owners = [full[None]], [[0]]
            return
        self.arrays, self.owners, self.place = [shard[None]], [[0]], 0

    def step(self, after=()):
        if self.order is None:
            return ()
        bit = self.order[self.place]
        mine = [tie(value, *after) for value in self.arrays] if after else self.arrays
        others = [swap_bit(value, bit) for value in mine]
        moved = [[owner ^ (1 << bit) for owner in row] for row in self.owners]
        if self.place < len(self.order) - 2:
            self.arrays = [jnp.concatenate([mine[0], others[0]], axis=0)]
            self.owners = [self.owners[0] + moved[0]]
        else:
            self.arrays, self.owners = mine + others, self.owners + moved
        self.place += 1
        return (self.arrays[-1],)

def swap_bit(value, bit):
    dp_bits = bits_of(lax.axis_size("chip")) + 1
    if bit == 0:
        return swap(value, "core", 1)
    if bit < dp_bits:
        return swap(value, "chip", 1 << (bit - 1))
    return swap(value, "seq", 1 << (bit - dp_bits))


def add_low(left, right, zero):
    return left + right + zero


class Reduce:
    def __init__(self, keep, send, order):
        self.keep, self.send, self.order, self.sent = keep, send, order, keep
        self.pins = () if order is None else (send,)
        self.left = list(order or ())
        self.other = None
        if order is None:
            self.keep = lax.psum_scatter(keep[0], ("seq", "chip"), scatter_dimension=0, tiled=True)[None]
        else:
            self.begin()

    def begin(self):
        self.other = swap_bit(self.send, self.left.pop(0)) if self.left else None

    def halves(self, after=()):
        half = self.keep.shape[0] // 2
        zero = zero_after(*after) if after else jnp.zeros((1, 1, 1), bf16)
        return add_low(self.keep[:half], self.other[:half], zero), add_low(self.keep[half:], self.other[half:], zero)

    def step(self, *after):
        if self.other is None:
            return ()
        if not self.left:
            zero = zero_after(*after) if after else 0.0
            self.keep = self.keep.astype(f32) + self.other.astype(f32) + zero
            self.other = None
            return (self.keep,)
        self.keep, self.send = self.halves(after)
        self.begin()
        return (self.send,)

    def finish(self, core, widths, *after):
        while self.other is not None:
            self.step(*after)
        chip_rows = self.keep[0].astype(f32)
        rows = chip_rows.shape[0] // 2
        lower, upper = chip_rows[:rows], chip_rows[rows:]
        own = jnp.where(core == 0, lower, upper)
        other = swap_bit(jnp.where(core == 0, upper, lower).astype(bf16), 0).astype(f32)
        outs, at = [], 0
        for width in widths:
            mine, theirs = own[:, at : at + width], other[:, at : at + width]
            outs.append(
                jnp.concatenate([jnp.where(core == 0, mine, theirs), jnp.where(core == 0, theirs, mine)], axis=1)
            )
            at += width
        return outs


def merge(first, second, *after):
    if first.order is None:
        both = Reduce.__new__(Reduce)
        both.keep = jnp.concatenate([first.keep, second.keep], axis=2)
        both.order, both.left, both.other, both.pins = None, [], None, ()
        return both
    parts = [first.halves(after), second.halves(after)]
    keep = jnp.concatenate([part[0] for part in parts], axis=2)
    send = jnp.concatenate([part[1] for part in parts], axis=2)
    return Reduce(keep, send, first.left)


def allowed_pairs(segc_ref, segr_ref, validr_ref):
    rows = segc_ref.shape[0]
    query, key = iota((rows, rows), 0), iota((rows, rows), 1)
    same = segc_ref[...] == segr_ref[...]
    usable = validr_ref[...] > 0.5
    return (key <= query) & same & (usable | (key == query))


def attention_kernel(weight1, tile, me_ref, norm_ref, mix_ref, segc_ref, segr_ref, validr_ref, qg_ref, qb_ref, kg_ref,
                     *refs):
    n1 = len(weight1.arrays)
    shared_ref, q_ref, k_ref, lse_ref, vpre_ref, values_ref, gpre_ref, att_ref, gated_ref, w1, probs_ref, sems = refs[n1:]
    step, steps = pl.program_id(0), pl.num_programs(0)
    values_width = tile * weight1.tiles
    half = values_width // 2

    def copies(n):
        made = []
        if n == 0:
            made += weight1.copies(refs[:n1], w1, me_ref[0], sems.at[0], 1, (values_width, w1.shape[1] - 2 * values_width))
        for part in range(2):
            made += weight1.copies(refs[:n1], w1, me_ref[0], sems.at[n], part, (n * half, half))
        return made

    @pl.when(step == 0)
    def _():
        for n in range(2):
            for copy in copies(n):
                copy.start()
        for copy in copies(0):
            copy.wait()
        shared = dot(mix_ref[...], w1[:, 2 * values_width :])
        shared_ref[...] = shared
        queries = (shared * qg_ref[...] + qb_ref[...]).astype(bf16)
        keys = (shared * kg_ref[...]).astype(bf16)
        q_ref[...] = queries
        k_ref[...] = keys
        scores = mul_t(queries, keys) * (queries.shape[1] ** -0.5)
        masked = jnp.where(allowed_pairs(segc_ref, segr_ref, validr_ref), scores, -1e30)
        top = jnp.max(masked, axis=1, keepdims=True)
        weights = jnp.exp(masked - top)
        total = jnp.sum(weights, axis=1, keepdims=True)
        probs_ref[...] = (weights / total).astype(bf16)
        lse_ref[...] = top + jnp.log(total)

    @pl.when(step == lax.div(steps, 2))
    def _():
        for copy in copies(1):
            copy.wait()

    value_pre = dot(norm_ref[...], w1[:, pl.ds(pl.multiple_of(step * tile, tile), tile)])
    vpre_ref[...] = value_pre.astype(bf16)
    values = (value_pre * sigmoid(value_pre)).astype(bf16)
    values_ref[...] = values
    gate_pre = dot(mix_ref[...], w1[:, pl.ds(pl.multiple_of(values_width + step * tile, tile), tile)])
    gpre_ref[...] = gate_pre.astype(bf16)
    attended = dot(probs_ref[...], values)
    att_ref[...] = attended.astype(bf16)
    gated_ref[...] = (attended * (gate_pre * sigmoid(gate_pre))).astype(bf16)


def project_kernel(weight2, *refs):
    n2 = len(weight2.arrays)
    me_ref, gated_ref, tok_ref, valid_ref, fg_ref = refs[:5]
    middle_ref, ffn_ref, inv_ref, w2, sems = refs[5 + n2 :]
    width = tok_ref.shape[1]
    edge = width // 2
    for part in range(2):
        for copy in weight2.copies(refs[5 : 5 + n2], w2, me_ref[0], sems.at[part], span=(part * edge, edge)):
            copy.start()
    square = jnp.zeros((tok_ref.shape[0], 1), f32)
    for part in range(2):
        for copy in weight2.copies(refs[5 : 5 + n2], w2, me_ref[0], sems.at[part], span=(part * edge, edge)):
            copy.wait()
        at = slice(part * edge, (part + 1) * edge)
        middle = tok_ref[:, at].astype(f32) * valid_ref[...] + dot(gated_ref[...], w2[:, at])
        middle_ref[:, at] = middle
        square = square + jnp.sum(middle * middle, axis=1, keepdims=True)
    inverse = lax.rsqrt(square * (1.0 / width) + 1e-05)
    inv_ref[...] = inverse
    ffn_ref[...] = (middle_ref[...] * inverse * fg_ref[...]).astype(bf16)


def hidden_kernel(weight3, weight4, me_ref, ffn_ref, cot_ref, *refs):
    n3, n4 = len(weight3.arrays), len(weight4.arrays)
    hid_ref, near_ref, far_ref, w3, w4, sems = refs[n3 + n4 :]
    step, core = pl.program_id(0), me_ref[1]
    half = hid_ref.shape[1]

    def copies(rel, n):
        base = pl.multiple_of((core ^ rel) * half, half)
        if n < 2:
            return weight3.copies(refs[:n3], w3, me_ref[0], sems.at[rel, n], n, (base, half))
        return weight4.copies(refs[n3 : n3 + n4], w4, me_ref[0], sems.at[rel, n], near=None)

    @pl.when(step == 0)
    def _():
        for rel, n in ((0, 0), (0, 1), (0, 2), (1, 0), (1, 1)):
            for copy in copies(rel, n):
                copy.start()

    def arrived(n):
        for rel in range(2):
            if (rel, n) != (1, 2):
                @pl.when(step == rel)
                def _():
                    for copy in copies(rel, n):
                        copy.wait()

    base = pl.multiple_of((core ^ step) * half, half)
    arrived(0)
    gate = dot(ffn_ref[...], w3[:, pl.ds(base, half)])
    sigma = sigmoid(gate)
    act = gate * sigma
    slope = sigma + act * (1.0 - sigma)
    arrived(1)
    up = dot(ffn_ref[...], w3[:, pl.ds(pl.multiple_of(base + 2 * half, half), half)])
    hid_ref[...] = (act * up).astype(bf16)
    arrived(2)
    grad = mul_t(cot_ref[...], w4[pl.ds(base, half), :])
    grad_gate = (grad * up * slope).astype(bf16)
    grad_up = (grad * act).astype(bf16)

    @pl.when(step == 0)
    def _():
        near_ref[:, :half] = grad_gate
        near_ref[:, half:] = grad_up

    @pl.when(step == 1)
    def _():
        far_ref[:, :half] = grad_gate
        far_ref[:, half:] = grad_up


def out_kernel(weight4, me_ref, hid_ref, middle_ref, *refs):
    n4 = len(weight4.arrays)
    out_ref, w4, sems = refs[n4:]
    width, half = middle_ref.shape[1], hid_ref.shape[1] // 2
    starts = [pl.multiple_of((me_ref[1] ^ rel) * half, half) for rel in range(2)]
    edge = width // 2
    for part in range(2):
        for copy in weight4.copies(refs[:n4], w4, me_ref[0], sems.at[part], span=(part * edge, edge)):
            copy.start()
    for part in range(2):
        for copy in weight4.copies(refs[:n4], w4, me_ref[0], sems.at[part], span=(part * edge, edge)):
            copy.wait()
        at = slice(part * edge, (part + 1) * edge)
        total = middle_ref[:, at]
        for rel in range(2):
            total = total + dot(hid_ref[:, rel * half : (rel + 1) * half], w4[pl.ds(starts[rel], half), at])
        out_ref[:, at] = total.astype(bf16)


def ffn_back_kernel(weight3, *refs):
    n3 = len(weight3.arrays)
    me_ref, near_ref, far_ref, middle_ref, inv_ref, cot_ref, fg_ref = refs[:7]
    gmid_ref, low_own, low_oth, low_ref, dfg_ref, w3, gin_ref, sems = refs[7 + n3 :]
    me, core = me_ref[0], me_ref[1]
    rows, width = middle_ref.shape
    half = near_ref.shape[1] // 2
    parts, edge = (2, width // 2) if weight3.split else (1, width)
    for part in range(parts):
        for copy in weight3.copies(refs[7 : 7 + n3], w3, me, sems.at[part], near=weight3.nears[part]):
            copy.start()
    starts = [pl.multiple_of((core ^ rel) * half, half) for rel in range(2)]
    lean = jnp.zeros((rows, 1), f32)
    for part in range(parts):
        for copy in weight3.copies(refs[7 : 7 + n3], w3, me, sems.at[part], near=weight3.nears[part]):
            copy.wait()
        base = pl.multiple_of((lax.shift_right_logical(me, weight3.top) ^ part) * edge, edge) if parts == 2 else 0
        at = pl.ds(base, edge)
        grad = jnp.zeros((rows, edge), f32)
        for rel, ref in enumerate((near_ref, far_ref)):
            grad = grad + mul_t(ref[:, :half], w3[at, pl.ds(starts[rel], half)])
            grad = grad + mul_t(ref[:, half:], w3[at, pl.ds(pl.multiple_of(starts[rel] + 2 * half, half), half)])
        normal = middle_ref[:, at] * inv_ref[...]
        dfg_ref[:, at] = jnp.sum(grad * normal, axis=0, keepdims=True)
        grad = grad * fg_ref[:, at]
        gin_ref[:, at] = grad
        lean = lean + jnp.sum(grad * normal, axis=1, keepdims=True)
    lean = lean * (1.0 / width)
    inverse = inv_ref[...]
    grad_middle = cot_ref[...].astype(f32) + inverse * (gin_ref[...] - middle_ref[...] * inverse * lean)
    gmid_ref[...] = grad_middle
    low_ref[...] = grad_middle.astype(bf16)
    part = width // 2
    low_own[...] = low_ref[:, pl.ds(pl.multiple_of(core * part, part), part)]
    low_oth[...] = low_ref[:, pl.ds(pl.multiple_of((1 - core) * part, part), part)]


def attention_back_kernel(weight2, tile, me_ref, low_ref, q_ref, k_ref, lse_ref, shared_ref, segc_ref, segr_ref,
                          validr_ref, qg_ref, kg_ref, vpre_ref, values_ref, gpre_ref, att_ref, *refs):
    n2 = len(weight2.arrays)
    (gv_ref, gr_ref, gv_own, gv_oth, gr_own, gr_oth, gsh_ref, dgain_ref, w2, probs_ref, low_probs_ref, gprobs_ref,
     sems) = refs[n2:]
    core = me_ref[1]
    rows = low_ref.shape[0]
    step, steps = pl.program_id(0), pl.num_programs(0)
    strips = steps // 2
    values_width = gv_own.shape[1] * 2
    factor = q_ref.shape[1] ** -0.5

    def copies(n):
        return weight2.copies(refs[:n2], w2, me_ref[0], sems.at[n], near=weight2.nears[n])

    @pl.when(step == 0)
    def _():
        for n in range(len(weight2.nears)):
            for copy in copies(n):
                copy.start()
        scores = mul_t(q_ref[...], k_ref[...]) * factor
        masked = jnp.where(allowed_pairs(segc_ref, segr_ref, validr_ref), scores, -1e30)
        probs = jnp.exp(masked - lse_ref[...])
        probs_ref[...] = probs
        low_probs_ref[...] = probs.astype(bf16)
        gprobs_ref[...] = jnp.zeros((rows, rows), f32)
        for copy in copies(0):
            copy.wait()

    if len(weight2.nears) > 1:

        @pl.when(step == strips)
        def _():
            for copy in copies(1):
                copy.wait()

    tile_at = tile_order(weight2, step, strips, me_ref)
    grad = mul_t(low_ref[...], w2[pl.ds(pl.multiple_of(tile_at * tile, tile), tile), :]).astype(bf16).astype(f32)
    gate_pre = gpre_ref[...].astype(f32)
    sigma = sigmoid(gate_pre)
    act = gate_pre * sigma
    grad_att = (grad * act).astype(bf16)
    grad_gate = (grad * att_ref[...].astype(f32) * (sigma + act * (1.0 - sigma))).astype(bf16)
    gr_ref[...] = grad_gate
    gprobs_ref[...] += mul_t(grad_att, values_ref[...])
    grad_values = (t_mul(low_probs_ref[...], grad_att) * silu_grad(vpre_ref[...].astype(f32))).astype(bf16)
    gv_ref[...] = grad_values
    inside = pl.ds(pl.multiple_of(lax.rem(tile_at, strips) * tile, tile), tile)
    mine = lax.div(tile_at, strips) == core

    @pl.when(mine)
    def _():
        gv_own[:, inside] = grad_values
        gr_own[:, inside] = grad_gate

    @pl.when(jnp.logical_not(mine))
    def _():
        gv_oth[:, inside] = grad_values
        gr_oth[:, inside] = grad_gate

    @pl.when(step == steps - 1)
    def _():
        probs, grad_probs = probs_ref[...], gprobs_ref[...]
        grad_scores = (probs * (grad_probs - jnp.sum(probs * grad_probs, axis=1, keepdims=True))).astype(bf16)
        grad_queries = dot(grad_scores, k_ref[...]) * factor
        grad_keys = t_mul(grad_scores, q_ref[...]) * factor
        shared = shared_ref[...]
        dgain_ref[0:1, :] = jnp.sum(grad_queries * shared, axis=0, keepdims=True)
        dgain_ref[1:2, :] = jnp.sum(grad_queries, axis=0, keepdims=True)
        dgain_ref[2:3, :] = jnp.sum(grad_keys * shared, axis=0, keepdims=True)
        gsh_ref[...] = (grad_queries * qg_ref[...] + grad_keys * kg_ref[...]).astype(bf16)
        part = gsh_ref.shape[1] // 2
        start = values_width // 2
        gr_own[:, start:] = gsh_ref[:, pl.ds(pl.multiple_of(core * part, part), part)]
        gr_oth[:, start:] = gsh_ref[:, pl.ds(pl.multiple_of((1 - core) * part, part), part)]


def tile_order(weight, step, strips, me):
    if len(weight.nears) == 1:
        return step
    return (lax.shift_right_logical(me[0], weight.top) ^ lax.div(step, strips)) * strips + lax.rem(step, strips)


def sent_back_kernel(weight1, *refs):
    n1 = len(weight1.arrays)
    me_ref, gv_ref, gr_ref, gsh_ref = refs[:4]
    gmix_ref, gnorm_ref, w1, sems = refs[4 + n1 :]
    me, width, values_width = me_ref[0], gmix_ref.shape[1], gv_ref.shape[1]
    parts, edge = (2, width // 2) if weight1.split else (1, width)
    for part in range(parts):
        for copy in weight1.copies(refs[4 : 4 + n1], w1, me, sems.at[part], near=weight1.nears[part]):
            copy.start()
    for part in range(parts):
        for copy in weight1.copies(refs[4 : 4 + n1], w1, me, sems.at[part], near=weight1.nears[part]):
            copy.wait()
        base = pl.multiple_of((lax.shift_right_logical(me, weight1.top) ^ part) * edge, edge) if parts == 2 else 0
        at = pl.ds(base, edge)
        gmix_ref[:, at] = (
            mul_t(gr_ref[...], w1[at, values_width : 2 * values_width]) + mul_t(gsh_ref[...], w1[at, 2 * values_width :])
        ).astype(bf16)
        gnorm_ref[:, at] = mul_t(gv_ref[...], w1[at, :values_width]).astype(bf16)


def weight_grad_kernel(halves, order, blocks, block, me_ref, own, other, mine, theirs, *refs):
    keep, send = refs[0], refs[1]
    held, sems = refs[-2:]
    chip, core = lax.shift_right_logical(me_ref[0], 1), me_ref[1]
    tile, span = own.shape[1], mine.shape[1]
    step, steps = pl.program_id(0), pl.num_programs(0)
    strips = lax.div(steps, halves)
    rel = lax.div(step, strips)
    base = ((core ^ rel) if halves == 2 else rel) * (strips * tile) + lax.rem(step, strips) * tile
    slot = lax.rem(step, 2)
    parts = tile // block

    def done(slot):
        for s in range(parts):
            pltpu.make_async_copy(held.at[slot, pl.ds(s * block, block)], keep.at[0], sems.at[slot]).wait()

    @pl.when(step >= 2)
    def _():
        done(slot)

    out = t_mul(own[...], mine[...]) + t_mul(other[...], theirs[...])
    held[slot] = out.astype(bf16)
    for s in range(parts):
        rel_chip = (lax.div(base, block) + s) ^ chip
        place = 0
        for p, bit in enumerate(order):
            place = place | ((lax.shift_right_logical(rel_chip, bit - 1) & 1) << (len(order) - 1 - p))
        index = place & (blocks // 2 - 1)
        source = held.at[slot, pl.ds(s * block, block)]

        @pl.when(place < blocks // 2)
        def _():
            pltpu.make_async_copy(source, keep.at[index], sems.at[slot]).start()

        @pl.when(place >= blocks // 2)
        def _():
            pltpu.make_async_copy(source, send.at[index], sems.at[slot]).start()

    @pl.when(step == steps - 1)
    def _():
        done(slot)
        done(1 - slot)


def plain_grad_kernel(halves, me_ref, own, other, mine, theirs, keep):
    keep[0] = (t_mul(own[...], mine[...]) + t_mul(other[...], theirs[...])).astype(bf16)


def weight_grad(left, right, order, me, chips, name, halves=1, part=(0, 1), micros=6, after=()):
    total, span = left[0].shape[1], right[0].shape[1] // part[1]
    rows = left[0].shape[0]
    half = total // halves
    block = total // chips
    if order is None:
        tile = math.gcd(half, 256)
    else:
        tile = math.lcm(block, LANES)
        while tile < 512 and half % (2 * tile) == 0 and half // (2 * tile) >= 2 // halves:
            tile *= 2
    strips = half // tile
    far = (lambda g, me: (0, g)) if halves == 1 else (lambda g, me: (0, lax.rem(g + strips, 2 * strips)))
    args = [
        columns_of(left[0], tile), columns_of(left[1], tile, far), columns_of(right[0], span, lambda g, me: (0, part[0])),
        columns_of(right[1], span, lambda g, me: (0, part[0])),
    ]
    if order is None:
        place = (lambda g, me: (0, g, 0)) if halves == 1 else (
            lambda g, me: (0, (me[1] ^ lax.div(g, strips)) * strips + lax.rem(g, strips), 0))
        (keep,) = grid_call(
            functools.partial(plain_grad_kernel, halves), [((1, total, span), bf16, (1, tile, span), place)], args,
            halves * strips, me, name=name, micros=micros, after=after)
        return Reduce(keep, None, None)
    keep, send = grid_call(
        functools.partial(weight_grad_kernel, halves, order, chips, block),
        [((chips // 2, block, span), bf16, None, None)] * 2, args, halves * strips, me,
        scratch=[pltpu.VMEM((2, tile, span), bf16), pltpu.SemaphoreType.DMA((2,))], name=name, micros=micros, after=after)
    return Reduce(keep, send, order)


def exchange_start(pack, totals, axis, hold):
    index, count = lax.axis_index(axis), lax.axis_size(axis)
    lanes = pack.shape[1]
    rows = pack.shape[0]
    full, totals_shape = pack, totals.shape
    totals = totals.reshape(-1, lanes)
    before, bit = jnp.zeros_like(totals), 1
    while bit < count:
        goes = jnp.concatenate([totals, full], axis=0)
        other = swap(tie(goes, *hold) if hold and bit == 2 else goes, axis, bit)
        upper = (index & bit) != 0
        far_totals, far = other[: totals.shape[0]], other[totals.shape[0] :]
        before = before + jnp.where(upper, far_totals, 0.0)
        totals = totals + far_totals
        full = jnp.concatenate([jnp.where(upper, far, full), jnp.where(upper, full, far)], axis=0)
        bit *= 2
    return full.reshape(count, rows, lanes), before.reshape(totals_shape)


def exchange_end(pack, totals, axis):
    index, count = lax.axis_index(axis), lax.axis_size(axis)
    lanes = pack.shape[2]
    totals_shape = totals.shape
    totals = totals.reshape(-1, lanes)
    rows = totals.shape[0]
    after, bit = jnp.zeros_like(totals), 1
    while bit < count:
        upper = (index & bit) != 0
        pairs = pack.reshape((pack.shape[0] // 2, 2) + pack.shape[1:])
        goes = jnp.where(upper, pairs[:, 0], pairs[:, 1])
        stays = jnp.where(upper, pairs[:, 1], pairs[:, 0])
        other = swap(jnp.concatenate([totals, goes.reshape(-1, lanes)], axis=0), axis, bit)
        after = after + jnp.where(upper, 0.0, other[:rows])
        totals = totals + other[:rows]
        pack = stays + other[rows:].reshape(stays.shape)
        bit *= 2
    return pack[0], after.reshape(totals_shape)


def sum_over(value, axis):
    bit = 1
    while bit < lax.axis_size(axis):
        value = value + swap(value, axis, bit)
        bit *= 2
    return value


def on_device(tokens, cotangent, segment_ids, pad_mask, w_z, w_v, w_r, w_h, w_gate, w_up, w_down, q_gain, q_bias,
              k_gain, ffn_gain, norm_gain, ema_rate, ema_angle, ema_input, ema_output, ema_skip):
    rows, width = tokens.shape[1:]
    seq_count, dp_count = lax.axis_size("seq"), 2 * lax.axis_size("chip")
    seq_index, core = lax.axis_index("seq"), lax.axis_index("core")
    dp_index = lax.axis_index("chip") * 2 + core
    devices = seq_count * dp_count
    chips = devices // 2
    fits = all(value.shape[0] % 16 == 0 for value in (w_z, w_h, w_down))
    dp_bits, all_bits = bits_of(dp_count), bits_of(devices)
    inner = list(range(1, dp_bits))
    first_seq, rest_seq = [dp_bits], list(range(all_bits - 1, dp_bits, -1))
    if fits:
        gather_a = rest_seq + first_seq + inner + [0]
        gather_b = rest_seq + inner + first_seq + [0]
        gather_c = inner + first_seq + rest_seq + [0]
        reduce_a, reduce_b = gather_a[-2::-1], gather_b[-2::-1]
        me = jnp.stack([seq_index * dp_count + dp_index, core]).astype(jnp.int32)
    else:
        gather_a = gather_b = gather_c = reduce_a = reduce_b = None
        me = jnp.stack([core * 0, core]).astype(jnp.int32)
    values_width, hidden_width = w_v.shape[1], w_gate.shape[1]
    z_width = w_z.shape[1]
    low = lambda *parts: jnp.concatenate([part.astype(bf16) for part in parts], axis=1)
    short = w_v.shape[0]
    if fits:
        get_v = Gather(low(w_v, w_h[:short]), gather_a)
        get_r = Gather(low(w_r, w_z, w_h[short:]), gather_b)
    else:
        get_v, get_r = Gather(low(w_v), None), Gather(low(w_r, w_z), None)
    get_gate, get_up = Gather(low(w_gate), gather_a), Gather(low(w_up), gather_b)
    first_v, first_r = get_v.step(), get_r.step()
    get_down = Gather(low(w_down), gather_c)
    first_down = get_down.step()

    row_segs = lax.dynamic_slice_in_dim(segment_ids[0], seq_index * rows, rows)
    row_valid = lax.dynamic_slice_in_dim(pad_mask[0], seq_index * rows, rows).astype(f32)
    valid_col, seg_col, seg_row, valid_row = row_valid[:, None], row_segs[:, None], row_segs[None], row_valid[None]
    prefix, totals = kernel_call(
        stats_kernel, [((rows, LANES), f32), ((DOCS, LANES), f32)], [tokens[0], valid_col, seg_col, seg_row],
        name="stats", micros=5,
    )

    ndim, lanes = ema_rate.shape[1], norm_gain.shape[0]
    gains = jnp.concatenate([q_gain, q_bias, k_gain, ffn_gain])[None].astype(bf16).astype(f32)
    gains = gather_small(gather_small(gains, "core"), "chip").reshape(-1)
    size = gains.shape[0]
    extra = -(-size // lanes)
    gains = jnp.pad(gains, (0, extra * lanes - size)).reshape(extra, lanes)
    pack = jnp.concatenate(
        [ema_rate.T, ema_angle.T, ema_input.T, ema_output.T, norm_gain[None], ema_skip[None], gains], axis=0
    )
    full, before = exchange_start(pack, totals, "seq", first_v + first_r)
    carry = lax.dynamic_slice_in_dim(before, row_segs[0], 1)
    gains = full[:, 4 * ndim + 2 :].reshape(seq_count, -1)[:, :size].reshape(devices, -1)
    zs, fs = q_gain.shape[0], ffn_gain.shape[0]
    full_qg = gains[:, :zs].reshape(1, -1)
    full_qb = gains[:, zs : 2 * zs].reshape(1, -1)
    full_kg = gains[:, 2 * zs : 3 * zs].reshape(1, -1)
    full_fg = gains[:, 3 * zs :].reshape(1, -1)
    par = ema_params(full[:, : 4 * ndim + 2], ndim, rows)
    flat = lambda value: value.reshape(-1, LANES)
    a_flat, b_flat, g_flat = flat(par["a"]), flat(par["b"]), flat(par["output_w"] * par["coeff"])
    gain_row = par["gain"].reshape(1, width)
    seq_steps = len(rest_seq)
    for _ in range(seq_steps - 1):
        deep_v, deep_r = get_v.step(), get_r.step()
    for _ in inner[1:]:
        get_down.step()
    second_down = get_down.step(first_v)
    sent_norm, xs, ends = kernel_call(
        norm_kernel,
        [((rows, width), bf16), ((rows * SUB, LANES), f32), ((2 * ndim * SUB, LANES), f32)],
        [tokens[0], valid_col, seg_col, prefix, carry, gain_row, a_flat, b_flat],
        name="norm", micros=13, after=first_v + first_r + first_down,
    )
    middle_v, middle_r = get_v.step((ends,)), get_r.step((ends,))
    first_gate, first_up = get_gate.step(deep_v + (ends,)), get_up.step(deep_r + (ends,))
    start_state = state_before(
        tie(ends, *deep_v, *deep_r, *second_down).reshape(2 * ndim, SUB, LANES), par["hop"], "seq", False
    )
    start_state = tie(start_state, *middle_v, *middle_r, *first_gate, *first_up)
    for _ in range(seq_steps - 1):
        deep_gate, deep_up = get_gate.step((start_state,)), get_up.step((start_state,))
    get_down.step(deep_gate + deep_up)
    mixed, sent_mix, kept = kernel_call(
        mix_kernel,
        [((rows * SUB, LANES), f32), ((rows, width), bf16), ((rows // SPAN, 2 * ndim * SUB, LANES), f32)],
        [xs, flat(start_state), a_flat, b_flat, g_flat, par["skip"]],
        scratch=[pltpu.VMEM((2 * ndim * SUB, LANES), f32)],
        name="mix", micros=16, after=deep_gate + deep_up,
    )
    near_last = get_v.step((start_state,)) + get_r.step((start_state,))
    third_gate, third_up = get_gate.step((mixed,) + near_last), get_up.step((mixed,) + near_last)
    for getter in (get_v, get_r):
        while getter.order is not None and getter.place < all_bits:
            getter.step()
    weight1 = Weight(Part(get_v, 0, values_width, short), Part(get_r, 0, values_width + z_width, short, 0, values_width))
    if fits:
        tall = w_h.shape[0]
        weight2 = Weight(
            Part(get_v, values_width, width, tall), Part(get_r, values_width + z_width, width, tall, short)
        )
    else:
        weight2 = Weight(Part(Gather(low(w_h), None), 0, width, w_h.shape[0]))

    tile = 256
    w1_shape, w2_shape = (width, 2 * values_width + z_width), (values_width, width)
    w3_shape, w4_shape = (width, 2 * hidden_width), (hidden_width, width)
    dma = pltpu.SemaphoreType.DMA
    wide = ((rows, values_width), bf16)

    def other_core(value):
        return swap_bit(value, 0)

    norm_other = other_core(tie(sent_norm, mixed))

    def any_of(*groups):
        return [ANY] * sum(len(group.arrays) for group in groups)

    tile = 512
    weight1.tiles = values_width // tile
    strip = ((rows, values_width), bf16, (rows, tile), lambda g, me: (0, g))

    def still(shape, dtype):
        return (shape, dtype, shape, lambda g, me: (0, 0))

    def loose(*groups):
        return [(array, None, None) for group in groups for array in group.arrays]

    shared, queries, keys, log_total, value_pre, values, gate_pre, attended, gated = grid_call(
        functools.partial(attention_kernel, weight1, tile),
        [still((rows, z_width), f32), still((rows, z_width), bf16), still((rows, z_width), bf16), still((rows, 1), f32)]
        + [strip] * 5,
        [whole(array) for array in (sent_norm, sent_mix, seg_col, seg_row, valid_row, full_qg, full_qb, full_kg)]
        + loose(weight1),
        weight1.tiles, me,
        scratch=[pltpu.VMEM(w1_shape, bf16), pltpu.VMEM((rows, rows), bf16), pltpu.SemaphoreType.DMA((2,))],
        name="attention", micros=15, after=third_gate + third_up + (norm_other,),
    )
    middle, ffn_in, inverse = kernel_call(
        functools.partial(project_kernel, weight2),
        [((rows, width), f32), ((rows, width), bf16), ((rows, 1), f32)],
        [me, gated, tokens[0], valid_col, full_fg, *weight2.arrays],
        [SM] + [VM] * 4 + any_of(weight2),
        scratch=[pltpu.VMEM(w2_shape, bf16), pltpu.SemaphoreType.DMA((2,))],
        name="project", micros=6,
    )

    get_down.step(third_gate + third_up)
    for getter in (get_gate, get_up, get_down):
        while getter.order is not None and getter.place < all_bits - 1:
            getter.step()
        getter.step((ffn_in,))
    weight4 = Weight(Part(get_down, 0, width, w_down.shape[0]))
    weight3 = Weight(Part(get_gate, 0, hidden_width, short), Part(get_up, 0, hidden_width, short, 0, hidden_width))
    grad_low = cotangent[0]
    part = width // 2
    cot_own = lax.dynamic_slice_in_dim(grad_low, core * part, part, axis=1)
    cot_oth = other_core(tie(lax.dynamic_slice_in_dim(grad_low, (1 - core) * part, part, axis=1), mixed))
    gated_other, mix_other = other_core(gated), other_core(sent_mix)
    half = hidden_width // 2
    pair = ((rows, hidden_width), bf16, (rows, hidden_width), lambda g, me: (0, 0))
    hid, near, far = grid_call(
        functools.partial(hidden_kernel, weight3, weight4),
        [((rows, hidden_width), bf16, (rows, half), lambda g, me: (0, g)), pair, pair],
        [whole(ffn_in), whole(grad_low)] + [(array, None, None) for array in weight3.arrays + weight4.arrays],
        2, me,
        scratch=[pltpu.VMEM(w3_shape, bf16), pltpu.VMEM(w4_shape, bf16), pltpu.SemaphoreType.DMA((2, 3))],
        name="hidden", micros=15, after=(cot_oth, gated_other, mix_other),
    )
    ffn_other = other_core(ffn_in)
    (output,) = kernel_call(
        functools.partial(out_kernel, weight4),
        [((rows, width), bf16)],
        [me, hid, middle, *weight4.arrays],
        [SM, VM, VM] + any_of(weight4),
        scratch=[pltpu.VMEM(w4_shape, bf16), pltpu.SemaphoreType.DMA((2,))],
        name="out", micros=7,
    )
    hid_pair, ffn_pair = (hid, other_core(hid)), (ffn_in, ffn_other)
    far_other = other_core(far)
    down = weight_grad(hid_pair, (cot_own, cot_oth), reduce_a, me, chips, "grad_down", halves=2, after=(output,))
    gate = weight_grad(ffn_pair, (near, far_other), reduce_b, me, chips, "grad_gate", part=(0, 2), after=(down.sent,))
    up = weight_grad(
        ffn_pair, (near, far_other), reduce_a, me, chips, "grad_up", part=(1, 2), after=(gate.sent,)
    )
    grad_middle, low_own, low_oth, middle_low, dfg = kernel_call(
        functools.partial(ffn_back_kernel, weight3),
        [((rows, width), f32), ((rows, part), bf16), ((rows, part), bf16), ((rows, width), bf16), ((1, width), f32)],
        [me, near, far, middle, inverse, grad_low, full_fg, *weight3.arrays],
        [SM] + [VM] * 6 + any_of(weight3),
        scratch=[pltpu.VMEM(w3_shape, bf16), pltpu.VMEM((rows, width), f32), pltpu.SemaphoreType.DMA((2,))],
        name="ffn_back", micros=17, after=(up.sent,),
    )
    heads = weight_grad(
        (gated, gated_other), (low_own, other_core(low_oth)), reduce_b, me, chips, "grad_h", after=down.step(low_own)
    )
    half_values = still((rows, values_width // 2), bf16)
    half_mixed = still((rows, (values_width + z_width) // 2), bf16)
    strips = values_width // tile // 2

    def turn(g, me):
        return (0, tile_order(weight2, g, strips, me))

    strip = ((rows, values_width), bf16, (rows, tile), turn)
    grad_v, grad_r, gv_own, gv_oth, gr_own, gr_oth, grad_z, dgains = grid_call(
        functools.partial(attention_back_kernel, weight2, tile),
        [strip, strip] + [half_values] * 2 + [half_mixed] * 2
        + [still((rows, z_width), bf16), still((3, z_width), f32)],
        [whole(array) for array in (middle_low, queries, keys, log_total, shared, seg_col, seg_row, valid_row, full_qg,
                                    full_kg)]
        + [columns_of(array, tile, turn) for array in (value_pre, values, gate_pre, attended)] + loose(weight2),
        2 * strips, me,
        scratch=[pltpu.VMEM(w2_shape, bf16), pltpu.VMEM((rows, rows), f32), pltpu.VMEM((rows, rows), bf16),
                 pltpu.VMEM((rows, rows), f32), pltpu.SemaphoreType.DMA((2,))],
        name="attention_back", micros=19, after=(heads.sent,) + gate.step(heads.sent),
    )
    grad_mix_rows, grad_norm_rows = kernel_call(
        functools.partial(sent_back_kernel, weight1),
        [((rows, width), bf16)] * 2,
        [me, grad_v, grad_r, grad_z, *weight1.arrays],
        [SM, VM, VM, VM] + any_of(weight1),
        scratch=[pltpu.VMEM(w1_shape, bf16), pltpu.SemaphoreType.DMA((2,))],
        name="sent_back", micros=11, after=up.step(gv_oth) + down.step(gv_oth),
    )
    gv_other, gr_other = other_core(gv_oth), other_core(gr_oth)
    drive, back_ends = kernel_call(
        back_ends_kernel, [((rows * SUB, LANES), f32), ((2 * ndim * SUB, LANES), f32)],
        [grad_mix_rows, mixed, a_flat, b_flat], name="back_ends", micros=12,
        after=heads.step(grad_mix_rows) + down.step(grad_mix_rows),
    )
    value = weight_grad((sent_norm, norm_other), (gv_own, gv_other), reduce_a, me, chips, "grad_v",
                        after=(back_ends, gr_other))
    both = merge(gate, up, back_ends)
    reset = weight_grad((sent_mix, mix_other), (gr_own, gr_other), reduce_b, me, chips, "grad_r",
                        after=(value.sent,) + both.pins + down.step(value.sent))
    hop_back = (par["hop"][0], -par["hop"][1])
    back_state = flat(
        state_before(back_ends.reshape(2 * ndim, SUB, LANES), hop_back, "seq", True,
                     {2: lambda: (value.sent,), 4: lambda: (reset.sent,)})
    )
    sums = jnp.zeros(((3 * ndim + 1) * SUB, LANES), f32)
    cuts = 4
    plan = [
        lambda done: heads.step(reset.sent) + both.step(reset.sent),
        lambda done: value.step(done) + heads.step(done),
        lambda done: reset.step(done) + both.step(done),
        lambda done: heads.step(done),
    ]
    last = []

    def merge_last(done):
        last.append(merge(value, reset, done))
        return last[0].pins

    done = back_state
    long = rows * SUB // cuts
    pieces_dx = []
    for cut in range(cuts - 1, -1, -1):
        block = pl.BlockSpec((long, LANES), lambda i, cut=cut: (cut, 0))
        keep_block = pl.BlockSpec((rows // SPAN // cuts, 2 * ndim * SUB, LANES), lambda i, cut=cut: (cut, 0, 0))
        dxs, back_state, sums = kernel_call(
            back_scan_kernel,
            [((long, LANES), f32), ((2 * ndim * SUB, LANES), f32), (((3 * ndim + 1) * SUB, LANES), f32)],
            [xs, drive, kept, back_state, sums, a_flat, b_flat, g_flat, par["skip"]],
            [block, block, keep_block] + [VM] * 6,
            scratch=[pltpu.VMEM((SPAN, 8 * SUB, LANES), f32)],
            name="back", micros=10, after=plan.pop(0)(done), grid=(1,), out_specs=[VM] * 3,
        )
        pieces_dx.insert(0, dxs)
        done = dxs
    pins = merge_last(done)
    last = last[0]
    dn, dgain, suffix, back_totals = kernel_call(
        back_norm_kernel,
        [((rows, width), f32), ((1, width), f32), ((rows, LANES), f32), ((DOCS, LANES), f32)],
        [*pieces_dx, grad_norm_rows, tokens[0], valid_col, seg_col, seg_row, prefix, carry, gain_row],
        name="back_norm", micros=6, after=pins,
    )
    sums = sums.reshape(3 * ndim + 1, SUB, LANES)
    d_params = ema_param_grads(par, sums)
    d_pack = jnp.concatenate(list(d_params) + [dgain.reshape(1, SUB, LANES), sums[3 * ndim :]], axis=0)
    d_pack = jnp.transpose(d_pack.reshape(4 * ndim + 2, seq_count, lanes), (1, 0, 2))
    owned = [dgains[i].reshape(devices, zs) for i in range(3)] + [dfg.reshape(devices, fs)]
    owned = jnp.concatenate(owned, axis=1).reshape(seq_count, -1)
    owned = jnp.pad(owned, ((0, 0), (0, extra * lanes - size))).reshape(seq_count, extra, lanes)
    own_pack, after_totals = exchange_end(jnp.concatenate([d_pack, owned], axis=1), tie(back_totals, *last.step(back_totals)), "seq")
    back_carry = lax.dynamic_slice_in_dim(after_totals, row_segs[rows - 1], 1)
    (input_grad,) = kernel_call(
        input_kernel, [((rows, width), f32)],
        [dn, suffix, back_carry, tokens[0], valid_col, seg_col, prefix, carry, grad_middle], name="input", micros=6,
        after=last.step(back_carry),
    )
    total = sum_over(sum_over(own_pack, "core"), "chip")
    mine = lax.dynamic_index_in_dim(total[4 * ndim + 2 :].reshape(-1)[:size].reshape(dp_count, -1), dp_index, 0, keepdims=False)
    (shard_down,) = down.finish(core, [part])
    shard_gate, shard_up = both.finish(core, [hidden_width // 2] * 2, done)
    (shard_h,) = heads.finish(core, [part], done)
    shard_v, shard_r, shard_z = last.finish(core, [values_width // 2, values_width // 2, z_width // 2])
    return (
        output[None], input_grad[None], shard_z, shard_v, shard_r, shard_h, shard_gate, shard_up, shard_down,
        mine[:zs], mine[zs : 2 * zs], mine[2 * zs : 3 * zs], mine[3 * zs :],
        total[4 * ndim], total[:ndim].T, total[ndim : 2 * ndim].T, total[2 * ndim : 3 * ndim].T,
        total[3 * ndim : 4 * ndim].T, total[4 * ndim + 1],
    )


def solution(mesh):
    shape = mesh.devices.shape
    whole = Mesh(mesh.devices.reshape(shape[0], shape[1] // 2, 2), AXES)
    by_token, by_group = P(("chip", "core"), "seq", None), P(("chip", "core"), None)
    by_row, by_owner = P(AXES, None), P(AXES)
    params = (by_row,) * 7 + (by_owner,) * 4 + (P("seq"),) + (P("seq", None),) * 4 + (P("seq"),)
    return jax.shard_map(
        on_device,
        mesh=whole,
        in_specs=(by_token, by_token, by_group, by_group) + params,
        out_specs=(by_token, by_token) + params,
        check_vma=False,
    )
```

```python
import functools
import math

import jax
import jax.numpy as jnp
from jax import lax
from jax.experimental import pallas as pl
from jax.experimental.pallas import tpu as pltpu
from jax.sharding import Mesh, PartitionSpec as P

AXES = ("seq", "chip", "core")
GROUP = 64
DOCS = 16
LANES = 128
SUB = 8
SPAN = 32
BAND = 64
bf16 = jnp.bfloat16
f32 = jnp.float32
VMEM_LIMIT = 60 * 1024 * 1024
PACE = 0.1


def split3(value):
    first = value.astype(bf16)
    rest = value - first.astype(f32)
    second = rest.astype(bf16)
    third = (rest - second.astype(f32)).astype(bf16)
    return first, second, third


def dot(left, right):
    return jnp.dot(left, right, preferred_element_type=f32)


def dot3(left, parts):
    return dot(left, parts[0]) + dot(left, parts[1]) + dot(left, parts[2])


def dot3_left(parts, right):
    return dot(parts[0], right) + dot(parts[1], right) + dot(parts[2], right)


def sigmoid(value):
    return 0.5 * jnp.tanh(0.5 * value) + 0.5


def iota(shape, axis):
    return lax.broadcasted_iota(jnp.int32, shape, axis)


def group_pick(width, shift):
    own = lax.shift_right_logical(iota((width, LANES), 0), GROUP.bit_length() - 1)
    return (own + shift == iota((width, LANES), 1)).astype(bf16)


def group_spread(groups, width):
    own = lax.shift_right_logical(iota((groups, width), 1), GROUP.bit_length() - 1)
    return (own == iota((groups, width), 0)).astype(bf16)


ANY = pl.BlockSpec(memory_space=pl.ANY)
VM = pl.BlockSpec(memory_space=pltpu.VMEM)
SM = pl.BlockSpec(memory_space=pltpu.SMEM)


def kernel_call(body, outs, args, specs=None, scratch=(), name=None, micros=10, after=(), grid=None, out_specs=None):
    specs = [VM] * len(args) if specs is None else specs
    count = len(args)

    def run(*refs):
        body(*refs[:count], *refs[count + len(after) :])

    more = {} if grid is None else dict(grid=grid, out_specs=tuple(out_specs))
    return pl.pallas_call(
        run,
        out_shape=tuple(jax.ShapeDtypeStruct(shape, dtype) for shape, dtype in outs),
        in_specs=list(specs) + [ANY] * len(after),
        scratch_shapes=list(scratch),
        compiler_params=pltpu.CompilerParams(vmem_limit_bytes=VMEM_LIMIT),
        cost_estimate=pl.CostEstimate(
            flops=int(micros * PACE * 1.0e9), bytes_accessed=int(micros * PACE * 3.0e6), transcendentals=0
        ),
        name=name,
        **more,
    )(*args, *after)


def grid_call(body, outs, args, steps, me, scratch=(), name=None, micros=10, after=()):
    def spec(shape, block, index):
        if block is None:
            return ANY
        if index is None:
            return pl.BlockSpec(shape, lambda g, me: (0,) * len(shape))
        return pl.BlockSpec(block, index)

    count = len(args)

    def run(*refs):
        body(*refs[: 1 + count], *refs[1 + count + len(after) :])

    return pl.pallas_call(
        run,
        out_shape=tuple(jax.ShapeDtypeStruct(shape, dtype) for shape, dtype, _, _ in outs),
        grid_spec=pltpu.PrefetchScalarGridSpec(
            num_scalar_prefetch=1,
            grid=(steps,),
            in_specs=[spec(array.shape, block, index) for array, block, index in args] + [ANY] * len(after),
            out_specs=tuple(spec(shape, block, index) for shape, _, block, index in outs),
            scratch_shapes=list(scratch),
        ),
        compiler_params=pltpu.CompilerParams(vmem_limit_bytes=VMEM_LIMIT),
        cost_estimate=pl.CostEstimate(
            flops=int(micros * PACE * 1.0e9), bytes_accessed=int(micros * PACE * 3.0e6), transcendentals=0
        ),
        name=name,
    )(me, *(array for array, _, _ in args), *after)


WHOLE = (1,)


def whole(array):
    return (array, WHOLE, None)


def columns_of(array, width, index=lambda g, me: (0, g)):
    return (array, (array.shape[0], width), index)


def tie(value, *after):
    def nothing(*refs):
        return None

    return pl.pallas_call(
        nothing,
        out_shape=jax.ShapeDtypeStruct(value.shape, value.dtype),
        in_specs=[ANY] * (1 + len(after)),
        out_specs=ANY,
        input_output_aliases={0: 0},
        name="tie",
    )(value, *after)


def zero_after(*after):
    return tie(jnp.zeros((1, 1, 1), bf16), *after)


def split_wide(value):
    return jnp.concatenate(split3(value), axis=1)


def spread_wide(groups, width, start):
    own = lax.shift_right_logical(iota((3 * groups, LANES), 1) + start, GROUP.bit_length() - 1)
    return (own == lax.rem(iota((3 * groups, LANES), 0), groups)).astype(bf16)


def moments(total, groups):
    counts = jnp.maximum(total[:, 2 * groups : 2 * groups + 1], 1.0) * float(GROUP)
    means = total[:, :groups] / counts
    variance = total[:, groups : 2 * groups] / counts - means * means
    return means, lax.rsqrt(variance + 1e-05), counts


def stats_kernel(tok_ref, valid_ref, segc_ref, segr_ref, prefix_ref, totals_ref):
    rows, width = tok_ref.shape
    groups = width // GROUP
    valid = valid_ref[...]
    masked = tok_ref[...].astype(f32) * valid
    low = masked.astype(bf16)
    square = masked * masked
    high = square.astype(bf16)
    rest = (square - high.astype(f32)).astype(bf16)
    second = group_pick(width, groups)
    sums = dot(low, group_pick(width, 0)) + dot(high, second) + dot(rest, second)
    sums = sums + jnp.where(iota((rows, LANES), 1) == 2 * groups, valid, 0.0)
    parts = split3(sums)
    earlier = (iota((rows, rows), 1) <= iota((rows, rows), 0)) & (segc_ref[...] == segr_ref[...])
    prefix_ref[...] = dot3(earlier.astype(f32).astype(bf16), parts)
    member = (iota((DOCS, rows), 0) == segr_ref[...]).astype(f32).astype(bf16)
    totals_ref[...] = dot3(member, parts)


def scan_ends(src_ref, a_ref, b_ref, end_ref, rows, ndim, reverse):
    half = ndim // 2
    for start in range(0, ndim, half):
        a = [a_ref[pl.ds((start + n) * SUB, SUB), :] for n in range(half)]
        b = [b_ref[pl.ds((start + n) * SUB, SUB), :] for n in range(half)]

        def step(i, state, a=a, b=b):
            t = rows - 1 - i if reverse else i
            x = src_ref[pl.ds(pl.multiple_of(t * SUB, SUB), SUB), :]
            fresh = []
            for n in range(half):
                re, im = state[2 * n], state[2 * n + 1]
                if reverse:
                    fresh += [a[n] * re + b[n] * im + x, a[n] * im - b[n] * re]
                else:
                    fresh += [a[n] * re - b[n] * im + x, a[n] * im + b[n] * re]
            return tuple(fresh)

        zero = jnp.zeros((SUB, LANES), f32)
        state = lax.fori_loop(0, rows, step, (zero,) * (2 * half), unroll=32)
        for n in range(half):
            end_ref[pl.ds((start + n) * SUB, SUB), :] = state[2 * n]
            end_ref[pl.ds((ndim + start + n) * SUB, SUB), :] = state[2 * n + 1]


def all_moments(prefix_ref, segc_ref, carry_ref, groups):
    total = prefix_ref[...] + jnp.where(segc_ref[...] == segc_ref[0:1, :], carry_ref[...], 0.0)
    return moments(total, groups)


def lane_rows(j, rows):
    return pl.ds(j, rows, stride=SUB)


def norm_kernel(tok_ref, valid_ref, segc_ref, prefix_ref, carry_ref, gain_ref, a_ref, b_ref,
                sent_ref, xs_ref, end_ref):
    rows, width = tok_ref.shape
    groups = width // GROUP
    ndim = a_ref.shape[0] // SUB
    means, scale, _ = all_moments(prefix_ref, segc_ref, carry_ref, groups)
    means, scale, valid = split_wide(means), split_wide(scale), valid_ref[...]
    for j in range(SUB):
        at = slice(j * LANES, (j + 1) * LANES)
        spread = spread_wide(groups, width, j * LANES)
        normed = (tok_ref[:, at].astype(f32) * valid - dot(means, spread)) * dot(scale, spread) * gain_ref[:, at]
        sent_ref[:, at] = normed.astype(bf16)
        xs_ref[lane_rows(j, rows), :] = normed
    scan_ends(xs_ref, a_ref, b_ref, end_ref, rows, ndim, False)


def mix_kernel(xs_ref, start_ref, a_ref, b_ref, g_ref, skip_ref, mixed_ref, sent_ref, keep_ref, state_ref):
    rows = xs_ref.shape[0] // SUB
    ndim = a_ref.shape[0] // SUB
    half = ndim // 2
    state_ref[...] = start_ref[...]

    def chunk(i, _):
        keep_ref[i] = state_ref[...]
        for start in range(0, ndim, half):
            re_at = [pl.ds((start + n) * SUB, SUB) for n in range(half)]
            im_at = [pl.ds((ndim + start + n) * SUB, SUB) for n in range(half)]
            a = [a_ref[at, :] for at in re_at]
            b = [b_ref[at, :] for at in re_at]
            g = [g_ref[at, :] for at in re_at]

            def step(k, state, start=start, a=a, b=b, g=g):
                at = pl.ds(pl.multiple_of((i * SPAN + k) * SUB, SUB), SUB)
                x = xs_ref[at, :]
                fresh, terms = [], []
                for n in range(half):
                    re, im = state[2 * n], state[2 * n + 1]
                    now = a[n] * re - b[n] * im + x
                    fresh += [now, a[n] * im + b[n] * re]
                    terms.append(g[n] * now)
                terms.append(skip_ref[...] * x if start == 0 else mixed_ref[at, :])
                while len(terms) > 1:
                    terms = [sum(terms[p : p + 2][1:], terms[p]) for p in range(0, len(terms), 2)]
                mixed_ref[at, :] = terms[0]
                return tuple(fresh)

            state = []
            for n in range(half):
                state += [state_ref[re_at[n], :], state_ref[im_at[n], :]]
            state = lax.fori_loop(0, SPAN, step, tuple(state), unroll=SPAN)
            for n in range(half):
                state_ref[re_at[n], :] = state[2 * n]
                state_ref[im_at[n], :] = state[2 * n + 1]
        return 0

    lax.fori_loop(0, rows // SPAN, chunk, 0)

    def band(i, _):
        at = pl.ds(pl.multiple_of(i * BAND, BAND), BAND)
        for j in range(SUB):
            mixed = mixed_ref[pl.ds(i * (BAND * SUB) + j, BAND, stride=SUB), :]
            sent_ref[at, j * LANES : (j + 1) * LANES] = (mixed * sigmoid(mixed)).astype(bf16)
        return 0

    lax.fori_loop(0, rows // BAND, band, 0)


def back_ends_kernel(grad_ref, mixed_ref, a_ref, b_ref, drive_ref, end_ref):
    rows = grad_ref.shape[0]
    ndim = a_ref.shape[0] // SUB

    def band(i, _):
        at = pl.ds(pl.multiple_of(i * BAND, BAND), BAND)
        for j in range(SUB):
            where = pl.ds(i * (BAND * SUB) + j, BAND, stride=SUB)
            mixed = mixed_ref[where, :]
            sigma = sigmoid(mixed)
            slope = sigma * (1.0 + mixed * (1.0 - sigma))
            drive_ref[where, :] = grad_ref[at, j * LANES : (j + 1) * LANES].astype(f32) * slope
        return 0

    lax.fori_loop(0, rows // BAND, band, 0)
    scan_ends(drive_ref, a_ref, b_ref, end_ref, rows, ndim, True)


def back_scan_kernel(xs_ref, drive_ref, keep_ref, start_ref, sums_in_ref, a_ref, b_ref, g_ref, skip_ref,
                     dxs_ref, state_ref, sums_ref, hist_ref):
    ndim = a_ref.shape[0] // SUB
    rows = xs_ref.shape[0] // SUB
    part = 4
    count = rows // SPAN
    state_ref[...] = start_ref[...]
    sums_ref[...] = sums_in_ref[...]

    def chunk(c, _):
        i = count - 1 - c
        for start in range(0, ndim, part):
            re_at = [pl.ds((start + n) * SUB, SUB) for n in range(part)]
            im_at = [pl.ds((ndim + start + n) * SUB, SUB) for n in range(part)]
            last_at = [pl.ds((2 * ndim + start + n) * SUB, SUB) for n in range(part)]
            a = [a_ref[at, :] for at in re_at]
            b = [b_ref[at, :] for at in re_at]
            g = [g_ref[at, :] for at in re_at]

            def forward(k, state, a=a, b=b):
                x = xs_ref[pl.ds(pl.multiple_of((i * SPAN + k) * SUB, SUB), SUB), :]
                fresh = []
                for n in range(part):
                    re, im = state[2 * n], state[2 * n + 1]
                    hist_ref[k, pl.ds(2 * n * SUB, SUB), :] = re
                    hist_ref[k, pl.ds((2 * n + 1) * SUB, SUB), :] = im
                    fresh += [a[n] * re - b[n] * im + x, a[n] * im + b[n] * re]
                return tuple(fresh)

            state = []
            for n in range(part):
                state += [keep_ref[i, re_at[n], :], keep_ref[i, im_at[n], :]]
            lax.fori_loop(0, SPAN, forward, tuple(state), unroll=SPAN)

            def backward(k, held, start=start, a=a, b=b, g=g):
                t = SPAN - 1 - k
                at = pl.ds(pl.multiple_of((i * SPAN + t) * SUB, SUB), SUB)
                x, drive = xs_ref[at, :], drive_ref[at, :]
                fresh, terms = [], []
                for n in range(part):
                    re, im, m_re, m_im, same = held[5 * n : 5 * n + 5]
                    now_re = a[n] * re + b[n] * im + drive
                    now_im = a[n] * im - b[n] * re
                    old_re = hist_ref[t, pl.ds(2 * n * SUB, SUB), :]
                    old_im = hist_ref[t, pl.ds((2 * n + 1) * SUB, SUB), :]
                    fresh += [
                        now_re,
                        now_im,
                        m_re + (now_re * old_re + now_im * old_im),
                        m_im + (now_im * old_re - now_re * old_im),
                        same + x * now_re,
                    ]
                    terms.append(g[n] * now_re)
                total = (terms[0] + terms[1]) + (terms[2] + terms[3])
                if start == 0:
                    dxs_ref[at, :] = total + skip_ref[...] * drive
                else:
                    dxs_ref[at, :] = total + dxs_ref[at, :]
                return tuple(fresh)

            held = []
            for n in range(part):
                held += [state_ref[re_at[n], :], state_ref[im_at[n], :]]
                held += [sums_ref[re_at[n], :], sums_ref[im_at[n], :], sums_ref[last_at[n], :]]
            held = lax.fori_loop(0, SPAN, backward, tuple(held), unroll=SPAN)
            for n in range(part):
                state_ref[re_at[n], :] = held[5 * n]
                state_ref[im_at[n], :] = held[5 * n + 1]
                sums_ref[re_at[n], :] = held[5 * n + 2]
                sums_ref[im_at[n], :] = held[5 * n + 3]
                sums_ref[last_at[n], :] = held[5 * n + 4]
        return 0

    lax.fori_loop(0, count, chunk, 0)

    def skip_step(k, total):
        at = pl.ds(pl.multiple_of(k * SUB, SUB), SUB)
        return total + xs_ref[at, :] * drive_ref[at, :]

    last = pl.ds(3 * ndim * SUB, SUB)
    sums_ref[last, :] = lax.fori_loop(0, rows, skip_step, sums_ref[last, :], unroll=32)


def back_norm_kernel(*refs):
    dxs_refs, refs = refs[:-12], refs[-12:]
    (grad_ref, tok_ref, valid_ref, segc_ref, segr_ref, prefix_ref, carry_ref, gain_ref,
     dn_ref, dgain_ref, suffix_ref, totals_ref) = refs
    rows, width = tok_ref.shape
    groups = width // GROUP
    means, scale, counts = all_moments(prefix_ref, segc_ref, carry_ref, groups)
    wide_means, wide_scale, valid = split_wide(means), split_wide(scale), valid_ref[...]
    plain, leaning = jnp.zeros((rows, LANES), f32), jnp.zeros((rows, LANES), f32)
    for j in range(SUB):
        at = slice(j * LANES, (j + 1) * LANES)
        spread = spread_wide(groups, width, j * LANES)
        own = lax.shift_right_logical(iota((LANES, LANES), 0) + j * LANES, GROUP.bit_length() - 1)
        pick = (own == iota((LANES, LANES), 1)).astype(bf16)
        centred = tok_ref[:, at].astype(f32) * valid - dot(wide_means, spread)
        ema = [ref[lane_rows(j, ref.shape[0] // SUB), :] for ref in dxs_refs]
        dn = grad_ref[:, at].astype(f32) + jnp.concatenate(ema, axis=0)
        dgain_ref[:, at] = jnp.sum(dn * centred * dot(wide_scale, spread), axis=0, keepdims=True)
        dn = dn * gain_ref[:, at]
        dn_ref[:, at] = dn
        plain = plain + dot3_left(split3(dn), pick)
        leaning = leaning + dot3_left(split3(dn * centred), pick)
    plain, leaning = plain[:, :groups], leaning[:, :groups]
    d_variance = -0.5 * leaning * scale * scale * scale
    d_second = d_variance / counts
    d_first = (-scale * plain - 2.0 * means * d_variance) / counts
    flow = jnp.concatenate([d_first, d_second, jnp.zeros((rows, LANES - 2 * groups), f32)], axis=1)
    parts = split3(flow)
    later = (iota((rows, rows), 1) >= iota((rows, rows), 0)) & (segc_ref[...] == segr_ref[...])
    suffix_ref[...] = dot3(later.astype(f32).astype(bf16), parts)
    member = (iota((DOCS, rows), 0) == segr_ref[...]).astype(f32).astype(bf16)
    totals_ref[...] = dot3(member, parts)


def input_kernel(dn_ref, suffix_ref, back_ref, tok_ref, valid_ref, segc_ref, prefix_ref, carry_ref, middle_ref, out_ref):
    rows, width = tok_ref.shape
    groups = width // GROUP
    _, scale, _ = all_moments(prefix_ref, segc_ref, carry_ref, groups)
    flow = suffix_ref[...] + jnp.where(segc_ref[...] == segc_ref[rows - 1 : rows, :], back_ref[...], 0.0)
    scale, valid = split_wide(scale), valid_ref[...]
    first, second = split_wide(flow[:, :groups]), split_wide(flow[:, groups : 2 * groups])
    for j in range(SUB):
        at = slice(j * LANES, (j + 1) * LANES)
        spread = spread_wide(groups, width, j * LANES)
        masked = tok_ref[:, at].astype(f32) * valid
        grad = dn_ref[:, at] * dot(scale, spread) + dot(first, spread) + 2.0 * masked * dot(second, spread)
        out_ref[:, at] = valid * (middle_ref[:, at] + grad)


def swap(value, axis, bit):
    count = lax.axis_size(axis)
    return lax.ppermute(value, axis, [(i, i ^ bit) for i in range(count)])


def gather_small(value, axis):
    index, count = lax.axis_index(axis), lax.axis_size(axis)
    value, bit = value[None], 1
    while bit < count:
        other = swap(value, axis, bit)
        upper = (index & bit) != 0
        value = jnp.concatenate([jnp.where(upper, other, value), jnp.where(upper, value, other)], axis=0)
        bit *= 2
    return value


def cmul(left, right):
    return (left[0] * right[0] - left[1] * right[1], left[0] * right[1] + left[1] * right[0])


def state_before(ends, hop, axis, reverse, hold=None):
    index, count = lax.axis_index(axis), lax.axis_size(axis)
    if reverse:
        index = count - 1 - index
    half = ends.shape[0] // 2
    before = (jnp.zeros_like(ends[:half]), jnp.zeros_like(ends[:half]))
    reach = (jnp.ones_like(hop[0]), jnp.zeros_like(hop[1]))
    bit = 1
    while bit < count:
        waits = hold[bit]() if hold and bit in hold else ()
        other = swap(tie(ends, *waits) if waits else ends, axis, bit)
        upper = (index & bit) != 0
        far, own = (other[:half], other[half:]), (ends[:half], ends[half:])
        moved = cmul(reach, far)
        before = tuple(v + jnp.where(upper, w, 0.0) for v, w in zip(before, moved))
        if bit * 2 < count:
            lower = tuple(jnp.where(upper, v, w) for v, w in zip(far, own))
            higher = tuple(jnp.where(upper, w, v) for v, w in zip(far, own))
            carried = cmul(hop, lower)
            ends = jnp.concatenate([carried[0] + higher[0], carried[1] + higher[1]], axis=0)
            longer = cmul(reach, hop)
            reach = tuple(jnp.where(upper, v, w) for v, w in zip(longer, reach))
            hop = cmul(hop, hop)
        bit *= 2
    return jnp.concatenate(before, axis=0)


def ema_params(full, ndim, rows):
    full = jnp.transpose(full, (1, 0, 2))
    full = full.reshape(full.shape[0], SUB, -1)
    rate, angle, input_w, output_w = (full[i * ndim : (i + 1) * ndim] for i in range(4))
    gain, skip = full[4 * ndim], full[4 * ndim + 1]
    base = jnp.sqrt(rate * (2.0 - rate))
    cos, sin = jnp.cos(angle), jnp.sin(angle)
    a, b = (1.0 - rate) * cos, (1.0 - rate) * sin
    hop, steps = (a, b), 1
    while steps < rows:
        hop, steps = cmul(hop, hop), steps * 2
    return dict(rate=rate, input_w=input_w, output_w=output_w, gain=gain, skip=skip, base=base,
                cos=cos, sin=sin, a=a, b=b, coeff=base * input_w, hop=hop)


def ema_param_grads(par, sums):
    ndim = par["rate"].shape[0]
    m_re, m_im, same = sums[:ndim], sums[ndim : 2 * ndim], sums[2 * ndim : 3 * ndim]
    weight = par["output_w"] * par["coeff"]
    d_a, d_b = weight * m_re, weight * m_im
    d_coeff = par["output_w"] * same
    d_output = par["coeff"] * same
    d_input = par["base"] * d_coeff
    d_rate = d_coeff * par["input_w"] * (1.0 - par["rate"]) / par["base"] - par["cos"] * d_a - par["sin"] * d_b
    d_angle = par["a"] * d_b - par["b"] * d_a
    return d_rate, d_angle, d_input, d_output


def mul_t(left, right):
    return lax.dot_general(left, right, (((1,), (1,)), ((), ())), preferred_element_type=f32)


def t_mul(left, right):
    return lax.dot_general(left, right, (((0,), (0,)), ((), ())), preferred_element_type=f32)


def silu_grad(value):
    sigma = sigmoid(value)
    return sigma * (1.0 + value * (1.0 - sigma))


def bits_of(count):
    return count.bit_length() - 1


class Part:
    def __init__(self, source, take, width, rows, lower=0, column=0):
        self.arrays, self.owners, self.top = source.arrays, source.owners, source.top
        self.take, self.width, self.rows, self.lower, self.column = take, width, rows, lower, column

    def copies(self, refs, where, me, sem, span=None, near=None):
        made = []
        first, width = (0, self.width) if span is None else span
        for ref, owners in zip(refs, self.owners):
            block = ref.shape[1]
            for slot, owner in enumerate(owners):
                if near is not None and near != (owner < (1 << self.top)):
                    continue
                start = (me ^ owner) * self.rows + self.lower
                start = pl.multiple_of(start, math.gcd(self.rows, block)) if len(owners) > 1 else 0
                source = ref.at[slot, :, pl.ds(self.take + first, width)]
                to = where.at[pl.ds(start, block), pl.ds(self.column + first, width)]
                made.append(pltpu.make_async_copy(source, to, sem))
        return made


class Weight:
    def __init__(self, *parts):
        self.parts, self.arrays, self.places = parts, [], []
        self.split, self.top = len(parts[0].owners[0]) > 1, parts[0].top
        self.nears = (True, False) if self.split else (None,)
        for part in parts:
            place = []
            for array in part.arrays:
                same = [n for n, known in enumerate(self.arrays) if known is array]
                if not same:
                    self.arrays.append(array)
                place.append(same[0] if same else len(self.arrays) - 1)
            self.places.append(place)

    def copies(self, refs, where, me, sem, which=None, span=None, near=None):
        made = []
        for n, (part, place) in enumerate(zip(self.parts, self.places)):
            if which is None or which == n:
                made += part.copies([refs[n] for n in place], where, me, sem, span, near)
        return made


class Gather:
    def __init__(self, shard, order):
        self.order = order
        self.top = max(order or (0,))
        if order is None:
            full = lax.all_gather(shard, AXES, axis=0, tiled=True)
            self.arrays, self.owners = [full[None]], [[0]]
            return
        self.arrays, self.owners, self.place = [shard[None]], [[0]], 0

    def step(self, after=()):
        if self.order is None:
            return ()
        bit = self.order[self.place]
        mine = [tie(value, *after) for value in self.arrays] if after else self.arrays
        others = [swap_bit(value, bit) for value in mine]
        moved = [[owner ^ (1 << bit) for owner in row] for row in self.owners]
        if self.place < len(self.order) - 2:
            self.arrays = [jnp.concatenate([mine[0], others[0]], axis=0)]
            self.owners = [self.owners[0] + moved[0]]
        else:
            self.arrays, self.owners = mine + others, self.owners + moved
        self.place += 1
        return (self.arrays[-1],)

def swap_bit(value, bit):
    dp_bits = bits_of(lax.axis_size("chip")) + 1
    if bit == 0:
        return swap(value, "core", 1)
    if bit < dp_bits:
        return swap(value, "chip", 1 << (bit - 1))
    return swap(value, "seq", 1 << (bit - dp_bits))


def add_low(left, right, zero):
    return left + right + zero


class Reduce:
    def __init__(self, keep, send, order):
        self.keep, self.send, self.order, self.sent = keep, send, order, keep
        self.pins = () if order is None else (send,)
        self.left = list(order or ())
        self.other = None
        if order is None:
            self.keep = lax.psum_scatter(keep[0], ("seq", "chip"), scatter_dimension=0, tiled=True)[None]
        else:
            self.begin()

    def begin(self):
        self.other = swap_bit(self.send, self.left.pop(0)) if self.left else None

    def halves(self, after=()):
        half = self.keep.shape[0] // 2
        zero = zero_after(*after) if after else jnp.zeros((1, 1, 1), bf16)
        return add_low(self.keep[:half], self.other[:half], zero), add_low(self.keep[half:], self.other[half:], zero)

    def step(self, *after):
        if self.other is None:
            return ()
        if not self.left:
            zero = zero_after(*after) if after else 0.0
            self.keep = self.keep.astype(f32) + self.other.astype(f32) + zero
            self.other = None
            return (self.keep,)
        self.keep, self.send = self.halves(after)
        self.begin()
        return (self.send,)

    def finish(self, core, widths, *after):
        while self.other is not None:
            self.step(*after)
        chip_rows = self.keep[0].astype(f32)
        rows = chip_rows.shape[0] // 2
        lower, upper = chip_rows[:rows], chip_rows[rows:]
        own = jnp.where(core == 0, lower, upper)
        other = swap_bit(jnp.where(core == 0, upper, lower).astype(bf16), 0).astype(f32)
        outs, at = [], 0
        for width in widths:
            mine, theirs = own[:, at : at + width], other[:, at : at + width]
            outs.append(
                jnp.concatenate([jnp.where(core == 0, mine, theirs), jnp.where(core == 0, theirs, mine)], axis=1)
            )
            at += width
        return outs


def merge(first, second, *after):
    if first.order is None:
        both = Reduce.__new__(Reduce)
        both.keep = jnp.concatenate([first.keep, second.keep], axis=2)
        both.order, both.left, both.other, both.pins = None, [], None, ()
        return both
    parts = [first.halves(after), second.halves(after)]
    keep = jnp.concatenate([part[0] for part in parts], axis=2)
    send = jnp.concatenate([part[1] for part in parts], axis=2)
    return Reduce(keep, send, first.left)


def allowed_pairs(segc_ref, segr_ref, validr_ref):
    rows = segc_ref.shape[0]
    query, key = iota((rows, rows), 0), iota((rows, rows), 1)
    same = segc_ref[...] == segr_ref[...]
    usable = validr_ref[...] > 0.5
    return (key <= query) & same & (usable | (key == query))


def attention_kernel(weight1, tile, me_ref, norm_ref, mix_ref, segc_ref, segr_ref, validr_ref, qg_ref, qb_ref, kg_ref,
                     *refs):
    n1 = len(weight1.arrays)
    shared_ref, q_ref, k_ref, lse_ref, vpre_ref, values_ref, gpre_ref, att_ref, gated_ref, w1, probs_ref, sems = refs[n1:]
    step, steps = pl.program_id(0), pl.num_programs(0)
    values_width = tile * weight1.tiles
    half = values_width // 2

    def copies(n):
        made = []
        if n == 0:
            made += weight1.copies(refs[:n1], w1, me_ref[0], sems.at[0], 1, (values_width, w1.shape[1] - 2 * values_width))
        for part in range(2):
            made += weight1.copies(refs[:n1], w1, me_ref[0], sems.at[n], part, (n * half, half))
        return made

    @pl.when(step == 0)
    def _():
        for n in range(2):
            for copy in copies(n):
                copy.start()
        for copy in copies(0):
            copy.wait()
        shared = dot(mix_ref[...], w1[:, 2 * values_width :])
        shared_ref[...] = shared
        queries = (shared * qg_ref[...] + qb_ref[...]).astype(bf16)
        keys = (shared * kg_ref[...]).astype(bf16)
        q_ref[...] = queries
        k_ref[...] = keys
        scores = mul_t(queries, keys) * (queries.shape[1] ** -0.5)
        masked = jnp.where(allowed_pairs(segc_ref, segr_ref, validr_ref), scores, -1e30)
        top = jnp.max(masked, axis=1, keepdims=True)
        weights = jnp.exp(masked - top)
        total = jnp.sum(weights, axis=1, keepdims=True)
        probs_ref[...] = (weights / total).astype(bf16)
        lse_ref[...] = top + jnp.log(total)

    @pl.when(step == lax.div(steps, 2))
    def _():
        for copy in copies(1):
            copy.wait()

    value_pre = dot(norm_ref[...], w1[:, pl.ds(pl.multiple_of(step * tile, tile), tile)])
    vpre_ref[...] = value_pre.astype(bf16)
    values = (value_pre * sigmoid(value_pre)).astype(bf16)
    values_ref[...] = values
    gate_pre = dot(mix_ref[...], w1[:, pl.ds(pl.multiple_of(values_width + step * tile, tile), tile)])
    gpre_ref[...] = gate_pre.astype(bf16)
    attended = dot(probs_ref[...], values)
    att_ref[...] = attended.astype(bf16)
    gated_ref[...] = (attended * (gate_pre * sigmoid(gate_pre))).astype(bf16)


def project_kernel(weight2, *refs):
    n2 = len(weight2.arrays)
    me_ref, gated_ref, tok_ref, valid_ref, fg_ref = refs[:5]
    middle_ref, ffn_ref, inv_ref, w2, sems = refs[5 + n2 :]
    width = tok_ref.shape[1]
    edge = width // 2
    for part in range(2):
        for copy in weight2.copies(refs[5 : 5 + n2], w2, me_ref[0], sems.at[part], span=(part * edge, edge)):
            copy.start()
    square = jnp.zeros((tok_ref.shape[0], 1), f32)
    for part in range(2):
        for copy in weight2.copies(refs[5 : 5 + n2], w2, me_ref[0], sems.at[part], span=(part * edge, edge)):
            copy.wait()
        at = slice(part * edge, (part + 1) * edge)
        middle = tok_ref[:, at].astype(f32) * valid_ref[...] + dot(gated_ref[...], w2[:, at])
        middle_ref[:, at] = middle
        square = square + jnp.sum(middle * middle, axis=1, keepdims=True)
    inverse = lax.rsqrt(square * (1.0 / width) + 1e-05)
    inv_ref[...] = inverse
    ffn_ref[...] = (middle_ref[...] * inverse * fg_ref[...]).astype(bf16)


def hidden_kernel(weight3, weight4, me_ref, ffn_ref, cot_ref, *refs):
    n3, n4 = len(weight3.arrays), len(weight4.arrays)
    hid_ref, near_ref, far_ref, w3, w4, sems = refs[n3 + n4 :]
    step, core = pl.program_id(0), me_ref[1]
    half = hid_ref.shape[1]

    def copies(rel, n):
        base = pl.multiple_of((core ^ rel) * half, half)
        if n < 2:
            return weight3.copies(refs[:n3], w3, me_ref[0], sems.at[rel, n], n, (base, half))
        return weight4.copies(refs[n3 : n3 + n4], w4, me_ref[0], sems.at[rel, n], near=None)

    @pl.when(step == 0)
    def _():
        for rel, n in ((0, 0), (0, 1), (0, 2), (1, 0), (1, 1)):
            for copy in copies(rel, n):
                copy.start()

    def arrived(n):
        for rel in range(2):
            if (rel, n) != (1, 2):
                @pl.when(step == rel)
                def _():
                    for copy in copies(rel, n):
                        copy.wait()

    base = pl.multiple_of((core ^ step) * half, half)
    arrived(0)
    gate = dot(ffn_ref[...], w3[:, pl.ds(base, half)])
    sigma = sigmoid(gate)
    act = gate * sigma
    slope = sigma + act * (1.0 - sigma)
    arrived(1)
    up = dot(ffn_ref[...], w3[:, pl.ds(pl.multiple_of(base + 2 * half, half), half)])
    hid_ref[...] = (act * up).astype(bf16)
    arrived(2)
    grad = mul_t(cot_ref[...], w4[pl.ds(base, half), :])
    grad_gate = (grad * up * slope).astype(bf16)
    grad_up = (grad * act).astype(bf16)

    @pl.when(step == 0)
    def _():
        near_ref[:, :half] = grad_gate
        near_ref[:, half:] = grad_up

    @pl.when(step == 1)
    def _():
        far_ref[:, :half] = grad_gate
        far_ref[:, half:] = grad_up


def out_kernel(weight4, me_ref, hid_ref, middle_ref, *refs):
    n4 = len(weight4.arrays)
    out_ref, w4, sems = refs[n4:]
    width, half = middle_ref.shape[1], hid_ref.shape[1] // 2
    starts = [pl.multiple_of((me_ref[1] ^ rel) * half, half) for rel in range(2)]
    edge = width // 2
    for part in range(2):
        for copy in weight4.copies(refs[:n4], w4, me_ref[0], sems.at[part], span=(part * edge, edge)):
            copy.start()
    for part in range(2):
        for copy in weight4.copies(refs[:n4], w4, me_ref[0], sems.at[part], span=(part * edge, edge)):
            copy.wait()
        at = slice(part * edge, (part + 1) * edge)
        total = middle_ref[:, at]
        for rel in range(2):
            total = total + dot(hid_ref[:, rel * half : (rel + 1) * half], w4[pl.ds(starts[rel], half), at])
        out_ref[:, at] = total.astype(bf16)


def ffn_back_kernel(weight3, *refs):
    n3 = len(weight3.arrays)
    me_ref, near_ref, far_ref, middle_ref, inv_ref, cot_ref, fg_ref = refs[:7]
    gmid_ref, low_own, low_oth, low_ref, dfg_ref, w3, gin_ref, sems = refs[7 + n3 :]
    me, core = me_ref[0], me_ref[1]
    rows, width = middle_ref.shape
    half = near_ref.shape[1] // 2
    parts, edge = (2, width // 2) if weight3.split else (1, width)
    for part in range(parts):
        for copy in weight3.copies(refs[7 : 7 + n3], w3, me, sems.at[part], near=weight3.nears[part]):
            copy.start()
    starts = [pl.multiple_of((core ^ rel) * half, half) for rel in range(2)]
    lean = jnp.zeros((rows, 1), f32)
    for part in range(parts):
        for copy in weight3.copies(refs[7 : 7 + n3], w3, me, sems.at[part], near=weight3.nears[part]):
            copy.wait()
        base = pl.multiple_of((lax.shift_right_logical(me, weight3.top) ^ part) * edge, edge) if parts == 2 else 0
        at = pl.ds(base, edge)
        grad = jnp.zeros((rows, edge), f32)
        for rel, ref in enumerate((near_ref, far_ref)):
            grad = grad + mul_t(ref[:, :half], w3[at, pl.ds(starts[rel], half)])
            grad = grad + mul_t(ref[:, half:], w3[at, pl.ds(pl.multiple_of(starts[rel] + 2 * half, half), half)])
        normal = middle_ref[:, at] * inv_ref[...]
        dfg_ref[:, at] = jnp.sum(grad * normal, axis=0, keepdims=True)
        grad = grad * fg_ref[:, at]
        gin_ref[:, at] = grad
        lean = lean + jnp.sum(grad * normal, axis=1, keepdims=True)
    lean = lean * (1.0 / width)
    inverse = inv_ref[...]
    grad_middle = cot_ref[...].astype(f32) + inverse * (gin_ref[...] - middle_ref[...] * inverse * lean)
    gmid_ref[...] = grad_middle
    low_ref[...] = grad_middle.astype(bf16)
    part = width // 2
    low_own[...] = low_ref[:, pl.ds(pl.multiple_of(core * part, part), part)]
    low_oth[...] = low_ref[:, pl.ds(pl.multiple_of((1 - core) * part, part), part)]


def attention_back_kernel(weight2, tile, me_ref, low_ref, q_ref, k_ref, lse_ref, shared_ref, segc_ref, segr_ref,
                          validr_ref, qg_ref, kg_ref, vpre_ref, values_ref, gpre_ref, att_ref, *refs):
    n2 = len(weight2.arrays)
    (gv_ref, gr_ref, gv_own, gv_oth, gr_own, gr_oth, gsh_ref, dgain_ref, w2, probs_ref, low_probs_ref, gprobs_ref,
     sems) = refs[n2:]
    core = me_ref[1]
    rows = low_ref.shape[0]
    step, steps = pl.program_id(0), pl.num_programs(0)
    strips = steps // 2
    values_width = gv_own.shape[1] * 2
    factor = q_ref.shape[1] ** -0.5

    def copies(n):
        return weight2.copies(refs[:n2], w2, me_ref[0], sems.at[n], near=weight2.nears[n])

    @pl.when(step == 0)
    def _():
        for n in range(len(weight2.nears)):
            for copy in copies(n):
                copy.start()
        scores = mul_t(q_ref[...], k_ref[...]) * factor
        masked = jnp.where(allowed_pairs(segc_ref, segr_ref, validr_ref), scores, -1e30)
        probs = jnp.exp(masked - lse_ref[...])
        probs_ref[...] = probs
        low_probs_ref[...] = probs.astype(bf16)
        gprobs_ref[...] = jnp.zeros((rows, rows), f32)
        for copy in copies(0):
            copy.wait()

    if len(weight2.nears) > 1:

        @pl.when(step == strips)
        def _():
            for copy in copies(1):
                copy.wait()

    tile_at = tile_order(weight2, step, strips, me_ref)
    grad = mul_t(low_ref[...], w2[pl.ds(pl.multiple_of(tile_at * tile, tile), tile), :]).astype(bf16).astype(f32)
    gate_pre = gpre_ref[...].astype(f32)
    sigma = sigmoid(gate_pre)
    act = gate_pre * sigma
    grad_att = (grad * act).astype(bf16)
    grad_gate = (grad * att_ref[...].astype(f32) * (sigma + act * (1.0 - sigma))).astype(bf16)
    gr_ref[...] = grad_gate
    gprobs_ref[...] += mul_t(grad_att, values_ref[...])
    grad_values = (t_mul(low_probs_ref[...], grad_att) * silu_grad(vpre_ref[...].astype(f32))).astype(bf16)
    gv_ref[...] = grad_values
    inside = pl.ds(pl.multiple_of(lax.rem(tile_at, strips) * tile, tile), tile)
    mine = lax.div(tile_at, strips) == core

    @pl.when(mine)
    def _():
        gv_own[:, inside] = grad_values
        gr_own[:, inside] = grad_gate

    @pl.when(jnp.logical_not(mine))
    def _():
        gv_oth[:, inside] = grad_values
        gr_oth[:, inside] = grad_gate

    @pl.when(step == steps - 1)
    def _():
        probs, grad_probs = probs_ref[...], gprobs_ref[...]
        grad_scores = (probs * (grad_probs - jnp.sum(probs * grad_probs, axis=1, keepdims=True))).astype(bf16)
        grad_queries = dot(grad_scores, k_ref[...]) * factor
        grad_keys = t_mul(grad_scores, q_ref[...]) * factor
        shared = shared_ref[...]
        dgain_ref[0:1, :] = jnp.sum(grad_queries * shared, axis=0, keepdims=True)
        dgain_ref[1:2, :] = jnp.sum(grad_queries, axis=0, keepdims=True)
        dgain_ref[2:3, :] = jnp.sum(grad_keys * shared, axis=0, keepdims=True)
        gsh_ref[...] = (grad_queries * qg_ref[...] + grad_keys * kg_ref[...]).astype(bf16)
        part = gsh_ref.shape[1] // 2
        start = values_width // 2
        gr_own[:, start:] = gsh_ref[:, pl.ds(pl.multiple_of(core * part, part), part)]
        gr_oth[:, start:] = gsh_ref[:, pl.ds(pl.multiple_of((1 - core) * part, part), part)]


def tile_order(weight, step, strips, me):
    if len(weight.nears) == 1:
        return step
    return (lax.shift_right_logical(me[0], weight.top) ^ lax.div(step, strips)) * strips + lax.rem(step, strips)


def sent_back_kernel(weight1, *refs):
    n1 = len(weight1.arrays)
    me_ref, gv_ref, gr_ref, gsh_ref = refs[:4]
    gmix_ref, gnorm_ref, w1, sems = refs[4 + n1 :]
    me, width, values_width = me_ref[0], gmix_ref.shape[1], gv_ref.shape[1]
    parts, edge = (2, width // 2) if weight1.split else (1, width)
    for part in range(parts):
        for copy in weight1.copies(refs[4 : 4 + n1], w1, me, sems.at[part], near=weight1.nears[part]):
            copy.start()
    for part in range(parts):
        for copy in weight1.copies(refs[4 : 4 + n1], w1, me, sems.at[part], near=weight1.nears[part]):
            copy.wait()
        base = pl.multiple_of((lax.shift_right_logical(me, weight1.top) ^ part) * edge, edge) if parts == 2 else 0
        at = pl.ds(base, edge)
        gmix_ref[:, at] = (
            mul_t(gr_ref[...], w1[at, values_width : 2 * values_width]) + mul_t(gsh_ref[...], w1[at, 2 * values_width :])
        ).astype(bf16)
        gnorm_ref[:, at] = mul_t(gv_ref[...], w1[at, :values_width]).astype(bf16)


def weight_grad_kernel(halves, order, blocks, block, me_ref, own, other, mine, theirs, *refs):
    keep, send = refs[0], refs[1]
    held, sems = refs[-2:]
    chip, core = lax.shift_right_logical(me_ref[0], 1), me_ref[1]
    tile, span = own.shape[1], mine.shape[1]
    step, steps = pl.program_id(0), pl.num_programs(0)
    strips = lax.div(steps, halves)
    rel = lax.div(step, strips)
    base = ((core ^ rel) if halves == 2 else rel) * (strips * tile) + lax.rem(step, strips) * tile
    slot = lax.rem(step, 2)
    parts = tile // block

    def done(slot):
        for s in range(parts):
            pltpu.make_async_copy(held.at[slot, pl.ds(s * block, block)], keep.at[0], sems.at[slot]).wait()

    @pl.when(step >= 2)
    def _():
        done(slot)

    out = t_mul(own[...], mine[...]) + t_mul(other[...], theirs[...])
    held[slot] = out.astype(bf16)
    for s in range(parts):
        rel_chip = (lax.div(base, block) + s) ^ chip
        place = 0
        for p, bit in enumerate(order):
            place = place | ((lax.shift_right_logical(rel_chip, bit - 1) & 1) << (len(order) - 1 - p))
        index = place & (blocks // 2 - 1)
        source = held.at[slot, pl.ds(s * block, block)]

        @pl.when(place < blocks // 2)
        def _():
            pltpu.make_async_copy(source, keep.at[index], sems.at[slot]).start()

        @pl.when(place >= blocks // 2)
        def _():
            pltpu.make_async_copy(source, send.at[index], sems.at[slot]).start()

    @pl.when(step == steps - 1)
    def _():
        done(slot)
        done(1 - slot)


def plain_grad_kernel(halves, me_ref, own, other, mine, theirs, keep):
    keep[0] = (t_mul(own[...], mine[...]) + t_mul(other[...], theirs[...])).astype(bf16)


def weight_grad(left, right, order, me, chips, name, halves=1, part=(0, 1), micros=6, after=()):
    total, span = left[0].shape[1], right[0].shape[1] // part[1]
    rows = left[0].shape[0]
    half = total // halves
    block = total // chips
    if order is None:
        tile = math.gcd(half, 256)
    else:
        tile = math.lcm(block, LANES)
        while tile < 512 and half % (2 * tile) == 0 and half // (2 * tile) >= 2 // halves:
            tile *= 2
    strips = half // tile
    far = (lambda g, me: (0, g)) if halves == 1 else (lambda g, me: (0, lax.rem(g + strips, 2 * strips)))
    args = [
        columns_of(left[0], tile), columns_of(left[1], tile, far), columns_of(right[0], span, lambda g, me: (0, part[0])),
        columns_of(right[1], span, lambda g, me: (0, part[0])),
    ]
    if order is None:
        place = (lambda g, me: (0, g, 0)) if halves == 1 else (
            lambda g, me: (0, (me[1] ^ lax.div(g, strips)) * strips + lax.rem(g, strips), 0))
        (keep,) = grid_call(
            functools.partial(plain_grad_kernel, halves), [((1, total, span), bf16, (1, tile, span), place)], args,
            halves * strips, me, name=name, micros=micros, after=after)
        return Reduce(keep, None, None)
    keep, send = grid_call(
        functools.partial(weight_grad_kernel, halves, order, chips, block),
        [((chips // 2, block, span), bf16, None, None)] * 2, args, halves * strips, me,
        scratch=[pltpu.VMEM((2, tile, span), bf16), pltpu.SemaphoreType.DMA((2,))], name=name, micros=micros, after=after)
    return Reduce(keep, send, order)


def exchange_start(pack, totals, axis, hold):
    index, count = lax.axis_index(axis), lax.axis_size(axis)
    lanes = pack.shape[1]
    rows = pack.shape[0]
    full, totals_shape = pack, totals.shape
    totals = totals.reshape(-1, lanes)
    before, bit = jnp.zeros_like(totals), 1
    while bit < count:
        goes = jnp.concatenate([totals, full], axis=0)
        other = swap(tie(goes, *hold) if hold and bit == 2 else goes, axis, bit)
        upper = (index & bit) != 0
        far_totals, far = other[: totals.shape[0]], other[totals.shape[0] :]
        before = before + jnp.where(upper, far_totals, 0.0)
        totals = totals + far_totals
        full = jnp.concatenate([jnp.where(upper, far, full), jnp.where(upper, full, far)], axis=0)
        bit *= 2
    return full.reshape(count, rows, lanes), before.reshape(totals_shape)


def exchange_end(pack, totals, axis):
    index, count = lax.axis_index(axis), lax.axis_size(axis)
    lanes = pack.shape[2]
    totals_shape = totals.shape
    totals = totals.reshape(-1, lanes)
    rows = totals.shape[0]
    after, bit = jnp.zeros_like(totals), 1
    while bit < count:
        upper = (index & bit) != 0
        pairs = pack.reshape((pack.shape[0] // 2, 2) + pack.shape[1:])
        goes = jnp.where(upper, pairs[:, 0], pairs[:, 1])
        stays = jnp.where(upper, pairs[:, 1], pairs[:, 0])
        other = swap(jnp.concatenate([totals, goes.reshape(-1, lanes)], axis=0), axis, bit)
        after = after + jnp.where(upper, 0.0, other[:rows])
        totals = totals + other[:rows]
        pack = stays + other[rows:].reshape(stays.shape)
        bit *= 2
    return pack[0], after.reshape(totals_shape)


def sum_over(value, axis):
    bit = 1
    while bit < lax.axis_size(axis):
        value = value + swap(value, axis, bit)
        bit *= 2
    return value


def on_device(tokens, cotangent, segment_ids, pad_mask, w_z, w_v, w_r, w_h, w_gate, w_up, w_down, q_gain, q_bias,
              k_gain, ffn_gain, norm_gain, ema_rate, ema_angle, ema_input, ema_output, ema_skip):
    rows, width = tokens.shape[1:]
    seq_count, dp_count = lax.axis_size("seq"), 2 * lax.axis_size("chip")
    seq_index, core = lax.axis_index("seq"), lax.axis_index("core")
    dp_index = lax.axis_index("chip") * 2 + core
    devices = seq_count * dp_count
    chips = devices // 2
    fits = all(value.shape[0] % 16 == 0 for value in (w_z, w_h, w_down))
    dp_bits, all_bits = bits_of(dp_count), bits_of(devices)
    inner = list(range(1, dp_bits))
    first_seq, rest_seq = [dp_bits], list(range(all_bits - 1, dp_bits, -1))
    if fits:
        gather_a = rest_seq + first_seq + inner + [0]
        gather_b = rest_seq + inner + first_seq + [0]
        gather_c = inner + first_seq + rest_seq + [0]
        reduce_a, reduce_b = gather_a[-2::-1], gather_b[-2::-1]
        me = jnp.stack([seq_index * dp_count + dp_index, core]).astype(jnp.int32)
    else:
        gather_a = gather_b = gather_c = reduce_a = reduce_b = None
        me = jnp.stack([core * 0, core]).astype(jnp.int32)
    values_width, hidden_width = w_v.shape[1], w_gate.shape[1]
    z_width = w_z.shape[1]
    low = lambda *parts: jnp.concatenate([part.astype(bf16) for part in parts], axis=1)
    short = w_v.shape[0]
    if fits:
        get_v = Gather(low(w_v, w_h[:short]), gather_a)
        get_r = Gather(low(w_r, w_z, w_h[short:]), gather_b)
    else:
        get_v, get_r = Gather(low(w_v), None), Gather(low(w_r, w_z), None)
    get_gate, get_up = Gather(low(w_gate), gather_a), Gather(low(w_up), gather_b)
    first_v, first_r = get_v.step(), get_r.step()
    get_down = Gather(low(w_down), gather_c)
    first_down = get_down.step()

    row_segs = lax.dynamic_slice_in_dim(segment_ids[0], seq_index * rows, rows)
    row_valid = lax.dynamic_slice_in_dim(pad_mask[0], seq_index * rows, rows).astype(f32)
    valid_col, seg_col, seg_row, valid_row = row_valid[:, None], row_segs[:, None], row_segs[None], row_valid[None]
    prefix, totals = kernel_call(
        stats_kernel, [((rows, LANES), f32), ((DOCS, LANES), f32)], [tokens[0], valid_col, seg_col, seg_row],
        name="stats", micros=5,
    )

    ndim, lanes = ema_rate.shape[1], norm_gain.shape[0]
    gains = jnp.concatenate([q_gain, q_bias, k_gain, ffn_gain])[None].astype(bf16).astype(f32)
    gains = gather_small(gather_small(gains, "core"), "chip").reshape(-1)
    size = gains.shape[0]
    extra = -(-size // lanes)
    gains = jnp.pad(gains, (0, extra * lanes - size)).reshape(extra, lanes)
    pack = jnp.concatenate(
        [ema_rate.T, ema_angle.T, ema_input.T, ema_output.T, norm_gain[None], ema_skip[None], gains], axis=0
    )
    full, before = exchange_start(pack, totals, "seq", first_v + first_r)
    carry = lax.dynamic_slice_in_dim(before, row_segs[0], 1)
    gains = full[:, 4 * ndim + 2 :].reshape(seq_count, -1)[:, :size].reshape(devices, -1)
    zs, fs = q_gain.shape[0], ffn_gain.shape[0]
    full_qg = gains[:, :zs].reshape(1, -1)
    full_qb = gains[:, zs : 2 * zs].reshape(1, -1)
    full_kg = gains[:, 2 * zs : 3 * zs].reshape(1, -1)
    full_fg = gains[:, 3 * zs :].reshape(1, -1)
    par = ema_params(full[:, : 4 * ndim + 2], ndim, rows)
    flat = lambda value: value.reshape(-1, LANES)
    a_flat, b_flat, g_flat = flat(par["a"]), flat(par["b"]), flat(par["output_w"] * par["coeff"])
    gain_row = par["gain"].reshape(1, width)
    seq_steps = len(rest_seq)
    for _ in range(seq_steps - 1):
        deep_v, deep_r = get_v.step(), get_r.step()
    for _ in inner[1:]:
        get_down.step()
    second_down = get_down.step(first_v)
    sent_norm, xs, ends = kernel_call(
        norm_kernel,
        [((rows, width), bf16), ((rows * SUB, LANES), f32), ((2 * ndim * SUB, LANES), f32)],
        [tokens[0], valid_col, seg_col, prefix, carry, gain_row, a_flat, b_flat],
        name="norm", micros=13, after=first_v + first_r + first_down,
    )
    middle_v, middle_r = get_v.step((ends,)), get_r.step((ends,))
    first_gate, first_up = get_gate.step(deep_v + (ends,)), get_up.step(deep_r + (ends,))
    start_state = state_before(
        tie(ends, *deep_v, *deep_r, *second_down).reshape(2 * ndim, SUB, LANES), par["hop"], "seq", False
    )
    start_state = tie(start_state, *middle_v, *middle_r, *first_gate, *first_up)
    for _ in range(seq_steps - 1):
        deep_gate, deep_up = get_gate.step((start_state,)), get_up.step((start_state,))
    get_down.step(deep_gate + deep_up)
    mixed, sent_mix, kept = kernel_call(
        mix_kernel,
        [((rows * SUB, LANES), f32), ((rows, width), bf16), ((rows // SPAN, 2 * ndim * SUB, LANES), f32)],
        [xs, flat(start_state), a_flat, b_flat, g_flat, par["skip"]],
        scratch=[pltpu.VMEM((2 * ndim * SUB, LANES), f32)],
        name="mix", micros=16, after=deep_gate + deep_up,
    )
    near_last = get_v.step((start_state,)) + get_r.step((start_state,))
    third_gate, third_up = get_gate.step((mixed,) + near_last), get_up.step((mixed,) + near_last)
    for getter in (get_v, get_r):
        while getter.order is not None and getter.place < all_bits:
            getter.step()
    weight1 = Weight(Part(get_v, 0, values_width, short), Part(get_r, 0, values_width + z_width, short, 0, values_width))
    if fits:
        tall = w_h.shape[0]
        weight2 = Weight(
            Part(get_v, values_width, width, tall), Part(get_r, values_width + z_width, width, tall, short)
        )
    else:
        weight2 = Weight(Part(Gather(low(w_h), None), 0, width, w_h.shape[0]))

    tile = 256
    w1_shape, w2_shape = (width, 2 * values_width + z_width), (values_width, width)
    w3_shape, w4_shape = (width, 2 * hidden_width), (hidden_width, width)
    dma = pltpu.SemaphoreType.DMA
    wide = ((rows, values_width), bf16)

    def other_core(value):
        return swap_bit(value, 0)

    norm_other = other_core(tie(sent_norm, mixed))

    def any_of(*groups):
        return [ANY] * sum(len(group.arrays) for group in groups)

    tile = 512
    weight1.tiles = values_width // tile
    strip = ((rows, values_width), bf16, (rows, tile), lambda g, me: (0, g))

    def still(shape, dtype):
        return (shape, dtype, shape, lambda g, me: (0, 0))

    def loose(*groups):
        return [(array, None, None) for group in groups for array in group.arrays]

    grad_low = cotangent[0]
    part = width // 2
    cot_own = lax.dynamic_slice_in_dim(grad_low, core * part, part, axis=1)
    cot_oth = other_core(tie(lax.dynamic_slice_in_dim(grad_low, (1 - core) * part, part, axis=1), mixed))
    shared, queries, keys, log_total, value_pre, values, gate_pre, attended, gated = grid_call(
        functools.partial(attention_kernel, weight1, tile),
        [still((rows, z_width), f32), still((rows, z_width), bf16), still((rows, z_width), bf16), still((rows, 1), f32)]
        + [strip] * 5,
        [whole(array) for array in (sent_norm, sent_mix, seg_col, seg_row, valid_row, full_qg, full_qb, full_kg)]
        + loose(weight1),
        weight1.tiles, me,
        scratch=[pltpu.VMEM(w1_shape, bf16), pltpu.VMEM((rows, rows), bf16), pltpu.SemaphoreType.DMA((2,))],
        name="attention", micros=15, after=third_gate + third_up + (norm_other, cot_oth),
    )
    middle, ffn_in, inverse = kernel_call(
        functools.partial(project_kernel, weight2),
        [((rows, width), f32), ((rows, width), bf16), ((rows, 1), f32)],
        [me, gated, tokens[0], valid_col, full_fg, *weight2.arrays],
        [SM] + [VM] * 4 + any_of(weight2),
        scratch=[pltpu.VMEM(w2_shape, bf16), pltpu.SemaphoreType.DMA((2,))],
        name="project", micros=6,
    )

    get_down.step(third_gate + third_up)
    for getter in (get_gate, get_up, get_down):
        while getter.order is not None and getter.place < all_bits - 1:
            getter.step()
        getter.step((ffn_in,))
    weight4 = Weight(Part(get_down, 0, width, w_down.shape[0]))
    weight3 = Weight(Part(get_gate, 0, hidden_width, short), Part(get_up, 0, hidden_width, short, 0, hidden_width))
    gated_other, mix_other = other_core(gated), other_core(sent_mix)
    half = hidden_width // 2
    pair = ((rows, hidden_width), bf16, (rows, hidden_width), lambda g, me: (0, 0))
    hid, near, far = grid_call(
        functools.partial(hidden_kernel, weight3, weight4),
        [((rows, hidden_width), bf16, (rows, half), lambda g, me: (0, g)), pair, pair],
        [whole(ffn_in), whole(grad_low)] + [(array, None, None) for array in weight3.arrays + weight4.arrays],
        2, me,
        scratch=[pltpu.VMEM(w3_shape, bf16), pltpu.VMEM(w4_shape, bf16), pltpu.SemaphoreType.DMA((2, 3))],
        name="hidden", micros=15, after=(gated_other, mix_other),
    )
    ffn_other = other_core(ffn_in)
    (output,) = kernel_call(
        functools.partial(out_kernel, weight4),
        [((rows, width), bf16)],
        [me, hid, middle, *weight4.arrays],
        [SM, VM, VM] + any_of(weight4),
        scratch=[pltpu.VMEM(w4_shape, bf16), pltpu.SemaphoreType.DMA((2,))],
        name="out", micros=7,
    )
    hid_pair, ffn_pair = (hid, other_core(hid)), (ffn_in, ffn_other)
    far_other = other_core(far)
    down = weight_grad(hid_pair, (cot_own, cot_oth), reduce_a, me, chips, "grad_down", halves=2, after=(output,))
    gate = weight_grad(ffn_pair, (near, far_other), reduce_b, me, chips, "grad_gate", part=(0, 2), after=(down.sent,))
    up = weight_grad(
        ffn_pair, (near, far_other), reduce_a, me, chips, "grad_up", part=(1, 2), after=(gate.sent,)
    )
    grad_middle, low_own, low_oth, middle_low, dfg = kernel_call(
        functools.partial(ffn_back_kernel, weight3),
        [((rows, width), f32), ((rows, part), bf16), ((rows, part), bf16), ((rows, width), bf16), ((1, width), f32)],
        [me, near, far, middle, inverse, grad_low, full_fg, *weight3.arrays],
        [SM] + [VM] * 6 + any_of(weight3),
        scratch=[pltpu.VMEM(w3_shape, bf16), pltpu.VMEM((rows, width), f32), pltpu.SemaphoreType.DMA((2,))],
        name="ffn_back", micros=17, after=(up.sent,),
    )
    heads = weight_grad(
        (gated, gated_other), (low_own, other_core(low_oth)), reduce_b, me, chips, "grad_h", after=down.step(low_own)
    )
    half_values = still((rows, values_width // 2), bf16)
    half_mixed = still((rows, (values_width + z_width) // 2), bf16)
    strips = values_width // tile // 2

    def turn(g, me):
        return (0, tile_order(weight2, g, strips, me))

    strip = ((rows, values_width), bf16, (rows, tile), turn)
    grad_v, grad_r, gv_own, gv_oth, gr_own, gr_oth, grad_z, dgains = grid_call(
        functools.partial(attention_back_kernel, weight2, tile),
        [strip, strip] + [half_values] * 2 + [half_mixed] * 2
        + [still((rows, z_width), bf16), still((3, z_width), f32)],
        [whole(array) for array in (middle_low, queries, keys, log_total, shared, seg_col, seg_row, valid_row, full_qg,
                                    full_kg)]
        + [columns_of(array, tile, turn) for array in (value_pre, values, gate_pre, attended)] + loose(weight2),
        2 * strips, me,
        scratch=[pltpu.VMEM(w2_shape, bf16), pltpu.VMEM((rows, rows), f32), pltpu.VMEM((rows, rows), bf16),
                 pltpu.VMEM((rows, rows), f32), pltpu.SemaphoreType.DMA((2,))],
        name="attention_back", micros=19, after=(heads.sent,) + gate.step(heads.sent),
    )
    grad_mix_rows, grad_norm_rows = kernel_call(
        functools.partial(sent_back_kernel, weight1),
        [((rows, width), bf16)] * 2,
        [me, grad_v, grad_r, grad_z, *weight1.arrays],
        [SM, VM, VM, VM] + any_of(weight1),
        scratch=[pltpu.VMEM(w1_shape, bf16), pltpu.SemaphoreType.DMA((2,))],
        name="sent_back", micros=11, after=up.step(gv_oth) + down.step(gv_oth),
    )
    gv_other, gr_other = other_core(gv_oth), other_core(gr_oth)
    drive, back_ends = kernel_call(
        back_ends_kernel, [((rows * SUB, LANES), f32), ((2 * ndim * SUB, LANES), f32)],
        [grad_mix_rows, mixed, a_flat, b_flat], name="back_ends", micros=12,
        after=heads.step(grad_mix_rows) + down.step(grad_mix_rows),
    )
    value = weight_grad((sent_norm, norm_other), (gv_own, gv_other), reduce_a, me, chips, "grad_v",
                        after=(back_ends, gr_other))
    both = merge(gate, up, back_ends)
    reset = weight_grad((sent_mix, mix_other), (gr_own, gr_other), reduce_b, me, chips, "grad_r",
                        after=(value.sent,) + both.pins + down.step(value.sent))
    hop_back = (par["hop"][0], -par["hop"][1])
    back_state = flat(
        state_before(back_ends.reshape(2 * ndim, SUB, LANES), hop_back, "seq", True,
                     {2: lambda: (value.sent,), 4: lambda: (reset.sent,)})
    )
    sums = jnp.zeros(((3 * ndim + 1) * SUB, LANES), f32)
    cuts = 4
    plan = [
        lambda done: heads.step(reset.sent) + both.step(reset.sent),
        lambda done: value.step(done) + heads.step(done),
        lambda done: reset.step(done) + both.step(done),
        lambda done: heads.step(done),
    ]
    last = []

    def merge_last(done):
        last.append(merge(value, reset, done))
        return last[0].pins

    done = back_state
    long = rows * SUB // cuts
    pieces_dx = []
    for cut in range(cuts - 1, -1, -1):
        block = pl.BlockSpec((long, LANES), lambda i, cut=cut: (cut, 0))
        keep_block = pl.BlockSpec((rows // SPAN // cuts, 2 * ndim * SUB, LANES), lambda i, cut=cut: (cut, 0, 0))
        dxs, back_state, sums = kernel_call(
            back_scan_kernel,
            [((long, LANES), f32), ((2 * ndim * SUB, LANES), f32), (((3 * ndim + 1) * SUB, LANES), f32)],
            [xs, drive, kept, back_state, sums, a_flat, b_flat, g_flat, par["skip"]],
            [block, block, keep_block] + [VM] * 6,
            scratch=[pltpu.VMEM((SPAN, 8 * SUB, LANES), f32)],
            name="back", micros=10, after=plan.pop(0)(done), grid=(1,), out_specs=[VM] * 3,
        )
        pieces_dx.insert(0, dxs)
        done = dxs
    pins = merge_last(done)
    last = last[0]
    dn, dgain, suffix, back_totals = kernel_call(
        back_norm_kernel,
        [((rows, width), f32), ((1, width), f32), ((rows, LANES), f32), ((DOCS, LANES), f32)],
        [*pieces_dx, grad_norm_rows, tokens[0], valid_col, seg_col, seg_row, prefix, carry, gain_row],
        name="back_norm", micros=6, after=pins,
    )
    sums = sums.reshape(3 * ndim + 1, SUB, LANES)
    d_params = ema_param_grads(par, sums)
    d_pack = jnp.concatenate(list(d_params) + [dgain.reshape(1, SUB, LANES), sums[3 * ndim :]], axis=0)
    d_pack = jnp.transpose(d_pack.reshape(4 * ndim + 2, seq_count, lanes), (1, 0, 2))
    owned = [dgains[i].reshape(devices, zs) for i in range(3)] + [dfg.reshape(devices, fs)]
    owned = jnp.concatenate(owned, axis=1).reshape(seq_count, -1)
    owned = jnp.pad(owned, ((0, 0), (0, extra * lanes - size))).reshape(seq_count, extra, lanes)
    own_pack, after_totals = exchange_end(jnp.concatenate([d_pack, owned], axis=1), tie(back_totals, *last.step(back_totals)), "seq")
    back_carry = lax.dynamic_slice_in_dim(after_totals, row_segs[rows - 1], 1)
    (input_grad,) = kernel_call(
        input_kernel, [((rows, width), f32)],
        [dn, suffix, back_carry, tokens[0], valid_col, seg_col, prefix, carry, grad_middle], name="input", micros=6,
    )
    total = sum_over(sum_over(own_pack, "core"), "chip")
    mine = lax.dynamic_index_in_dim(total[4 * ndim + 2 :].reshape(-1)[:size].reshape(dp_count, -1), dp_index, 0, keepdims=False)
    (shard_down,) = down.finish(core, [part])
    shard_gate, shard_up = both.finish(core, [hidden_width // 2] * 2, done)
    (shard_h,) = heads.finish(core, [part], done)
    shard_v, shard_r, shard_z = last.finish(core, [values_width // 2, values_width // 2, z_width // 2])
    return (
        output[None], input_grad[None], shard_z, shard_v, shard_r, shard_h, shard_gate, shard_up, shard_down,
        mine[:zs], mine[zs : 2 * zs], mine[2 * zs : 3 * zs], mine[3 * zs :],
        total[4 * ndim], total[:ndim].T, total[ndim : 2 * ndim].T, total[2 * ndim : 3 * ndim].T,
        total[3 * ndim : 4 * ndim].T, total[4 * ndim + 1],
    )


def solution(mesh):
    shape = mesh.devices.shape
    whole = Mesh(mesh.devices.reshape(shape[0], shape[1] // 2, 2), AXES)
    by_token, by_group = P(("chip", "core"), "seq", None), P(("chip", "core"), None)
    by_row, by_owner = P(AXES, None), P(AXES)
    params = (by_row,) * 7 + (by_owner,) * 4 + (P("seq"),) + (P("seq", None),) * 4 + (P("seq"),)
    return jax.shard_map(
        on_device,
        mesh=whole,
        in_specs=(by_token, by_token, by_group, by_group) + params,
        out_specs=(by_token, by_token) + params,
        check_vma=False,
    )
```
